32 devices in a mesh: bead: 8 (over z, x), space: 4 (over y, core).
Axes of the slice: x: 2, y: 2, z: 4, core: 2. Of those that a mesh axis runs over, the one named last changes fastest.
Arguments:
- positions: float32 [32, 64, 3, 128], P('bead', 'space'), may hold values from 0 to 1
- momenta: float32 [32, 64, 3, 128], P('bead', 'space'), may hold values from -3 to 3
- noise: float32 [32, 64, 3, 128], P('bead', 'space'), may hold values from -6 to 6
- atom_types: int32 [64, 128], P('space'), may hold values from 0 to 3
- occupancy: int32 [64], P('space'), may hold values from 64 to 128, as said below
- type_sigma: float32 [4], replicated, may hold values from 0.2 to 0.4
- type_eps: float32 [4], replicated, may hold values from 0.5 to 2
- type_mass: float32 [4], replicated, may hold values from 1 to 4
Outputs:
- new_positions: float32 [32, 64, 3, 128], P('bead', 'space')
- new_momenta: float32 [32, 64, 3, 128], P('bead', 'space')
The draws below stay inside these ranges and needn't reach their ends.
Inputs may be any that keep to these rules, and one draw needn't show every extreme that they name: `occupancy`: in each domain of 16 consecutive cells some cell holds 128 atoms.
All inputs are finite; a program needn't handle non-finite values.
Results may differ from the reference program's by a relative error of at most 0.0002.
Values sent between devices are 32-bit elements; how exact they have to be, the bound alone decides.
No kernel may reach another device: no remote copies, remote signals or barrier semaphores. Data moves between devices by JAX's collectives and lax.ppermute only.
A program may use at most 64 MiB of HBM per device.

```python
import math
import jax
import jax.numpy as jnp
from jax import lax

P_SIZE = 32
PC = 8
A = 128
NTYPES = 4
GY = 4
GZ = 4
CELLS_ALL = 64
N_SPACE = 4


def draw_occupancy(key, part):
    per_domain = GY * GZ
    counts = jax.random.randint(jax.random.fold_in(key, 21), (CELLS_ALL,), A // 2, A + 1)
    fullest = jax.random.randint(jax.random.fold_in(key, 22), (CELLS_ALL // per_domain,), 0, per_domain)
    marked = jnp.arange(CELLS_ALL) % per_domain == jnp.repeat(fullest, per_domain)
    return jnp.where(marked, A, counts).astype(jnp.int32)


def with_ends(values, key, smallest, top_value):
    longest = values.shape.index(max(values.shape))
    spots = []
    for shift in (0, 1):
        where = [jax.random.randint(jax.random.fold_in(key, axis), (), 0, length) for axis, length in enumerate(values.shape)]
        where[longest] = (where[longest] + shift) % values.shape[longest]
        spots.append(tuple(where))
    return values.at[spots[0]].set(smallest).at[spots[1]].set(top_value)


def shard_levels(stream_key, dims, split, smallest, top_value):
    def one(position, parts):
        steps = jax.random.uniform(jax.random.fold_in(jax.random.fold_in(stream_key, 6), position), (parts,), jnp.float32, smallest / len(split), top_value / len(split))
        return jnp.repeat(jnp.exp(steps), dims[position] // parts).reshape((-1,) + (1,) * (len(dims) - position - 1))

    factor_of = one(*split[0])
    for cut in split[1:]:
        factor_of = factor_of * one(*cut)
    return factor_of


def gaussian(rng, shape, spread, most, pieces=(), kind=jnp.bfloat16):
    entries = jax.random.normal(rng, shape, jnp.float32) * spread
    if len(pieces) > 0:
        entries = shard_levels(rng, shape, pieces, -0.22, 0.18) * entries
    return jnp.clip(entries, min=-most, max=most).astype(kind)


def setup_inputs(seed: int = 0) -> dict:
    splits = jax.random.split(jax.random.key(seed), 9)
    positions = jnp.clip(1.0 * jax.random.uniform(splits[0], (P_SIZE, CELLS_ALL, 3, A), jnp.float32) ** shard_levels(splits[0], (P_SIZE, CELLS_ALL, 3, A), ((0, 8), (1, 4)), -0.2, 0.2), 0.0, 1.0)
    momenta = gaussian(splits[1], (P_SIZE, CELLS_ALL, 3, A), 0.5, 3.0, ((0, 8), (1, 4)), jnp.float32)
    noise = gaussian(splits[2], (P_SIZE, CELLS_ALL, 3, A), 1.0, 6.0, ((0, 8), (1, 4)), jnp.float32)
    atom_types = with_ends(jax.random.randint(splits[3], (CELLS_ALL, A), 0, NTYPES), jax.random.fold_in(splits[3], 1), 0, NTYPES - 1).astype(jnp.int32)
    occupancy = draw_occupancy(jax.random.fold_in(splits[8], 71), 0)
    type_sigma = jnp.clip(jax.random.uniform(splits[5], (NTYPES,), jnp.float32, 0.2, 0.4), 0.2, 0.4)
    type_eps = jnp.clip(jnp.exp(jax.random.uniform(splits[6], (NTYPES,), jnp.float32, math.log(0.5), math.log(2.0))), 0.5, 2.0)
    type_mass = jnp.clip(jnp.exp(jax.random.uniform(splits[7], (NTYPES,), jnp.float32, math.log(1.0), math.log(4.0))), 1.0, 4.0)
    return dict(positions=positions, momenta=momenta, noise=noise, atom_types=atom_types, occupancy=occupancy, type_sigma=type_sigma, type_eps=type_eps, type_mass=type_mass)


TIME_STEP = 0.05
INVERSE_TEMP = 32.0
CENTROID_FRICTION = 1.0
INNER_CUT = 0.5
OUTER_CUT = 1.0
precise = lax.Precision.HIGHEST

def stencil_table(cell_total, per_domain, depth_z, height_y):
    in_domain = jnp.arange(cell_total) % per_domain
    across = in_domain // depth_z
    upward = in_domain % depth_z
    offsets = jnp.arange(27)
    step_x = offsets // 9 - 1
    step_y = offsets // 3 % 3 - 1
    step_z = offsets % 3 - 1
    target_y = across[:, None] + step_y[None, :]
    target_z = upward[:, None] + step_z[None, :]
    inside = (target_y >= 0) & (target_y < height_y) & (target_z >= 0) & (target_z < depth_z)
    entry = (step_x[None, :] + 1) * per_domain + target_y * depth_z + target_z
    return jnp.where(inside, entry, 3 * per_domain).astype(jnp.int32)

def mode_table(number):
    bead_rows = jnp.arange(number, dtype=jnp.float32)[:, None]
    column = jnp.arange(number, dtype=jnp.float32)[None, :]
    phases = 2.0 * jnp.pi * bead_rows * column / number
    factor = jnp.sqrt(2.0 / number)
    middle = jnp.cos(jnp.pi * bead_rows) / jnp.sqrt(float(number))
    matrix = jnp.where(column < number / 2, factor * jnp.cos(phases), factor * jnp.sin(phases))
    matrix = jnp.where(column == number / 2, middle, matrix)
    matrix = jnp.where(column == 0, 1.0 / jnp.sqrt(float(number)), matrix)
    return matrix.astype(jnp.float32)

def contract_table(full_count, reduced):
    selected = jnp.arange(reduced)
    selected = jnp.where(selected <= reduced // 2, selected, selected + full_count - reduced)
    chosen = mode_table(full_count)[:, selected]
    product = jnp.dot(mode_table(reduced), chosen.T, precision=precise, preferred_element_type=jnp.float32)
    return jnp.sqrt(reduced / full_count) * product

def propagate(position_modes, momentum_modes, noise_modes):
    number = position_modes.shape[0]
    mode_index = jnp.arange(number)
    frequency = 2.0 * (number / INVERSE_TEMP) * jnp.sin(jnp.pi * mode_index.astype(jnp.float32) / number)
    friction = jnp.where(mode_index == 0, CENTROID_FRICTION, 2.0 * frequency)
    damping = jnp.exp(-friction * TIME_STEP)
    kicking = jnp.sqrt((1.0 - damping * damping) / INVERSE_TEMP)
    cosine = jnp.cos(frequency * TIME_STEP)
    sine_term = jnp.sin(frequency * TIME_STEP)
    drift_factor = jnp.where(mode_index == 0, TIME_STEP, sine_term / jnp.where(mode_index == 0, 1.0, frequency))
    spring = frequency * sine_term
    trailing = (number,) + (1,) * (position_modes.ndim - 1)
    damping = damping.reshape(trailing)
    kicking = kicking.reshape(trailing)
    cosine = cosine.reshape(trailing)
    drift_factor = drift_factor.reshape(trailing)
    spring = spring.reshape(trailing)
    momentum = damping * momentum_modes + kicking * noise_modes
    next_position = cosine * position_modes + drift_factor * momentum
    next_momentum = cosine * momentum - spring * position_modes
    return (next_position, next_momentum)

def atom_table(atom_types, occupancy, type_sigma, type_eps, type_mass):
    type_codes = jnp.arange(type_sigma.shape[0])
    onehot = (atom_types[..., None] == type_codes).astype(jnp.float32)
    sigma_atom = lax.optimization_barrier(jnp.sum(onehot * type_sigma, -1))
    energy_root = jnp.sqrt(lax.optimization_barrier(jnp.sum(onehot * type_eps, -1)))
    mass_atom = lax.optimization_barrier(jnp.sum(onehot * type_mass, -1))
    slot_index = jnp.arange(atom_types.shape[-1])
    living = (slot_index[None, :] < occupancy[:, None]).astype(jnp.float32)
    return (jnp.stack([sigma_atom, energy_root, living], 1), mass_atom)

def anchor_of(ext_index, domain_cells, slab_depth):
    slab_layer = ext_index // domain_cells - 1
    within = ext_index % domain_cells
    return jnp.stack([slab_layer, within // slab_depth, within % slab_depth], -1).astype(jnp.float32)

def taper(radius_sq, cutoff):
    margin = jnp.maximum(0.0, 1.0 - radius_sq / (cutoff * cutoff))
    return (margin * margin, -2.0 * margin / (cutoff * cutoff))

def pair_force(left_position, left_param, right_position, right_param, longer):
    separation = left_position[:, :, None] - right_position[:, None, :]
    radius_sq = lax.optimization_barrier(jnp.sum(separation * separation, 0))
    sigma_pair = 0.5 * (left_param[0][:, None] + right_param[0][None, :])
    sigma_sq = sigma_pair * sigma_pair
    energy = left_param[1][:, None] * right_param[1][None, :]
    shifted = radius_sq + sigma_sq
    quotient = sigma_sq / shifted
    sixth_power = quotient * quotient * quotient
    potential = 4.0 * energy * (sixth_power * sixth_power - sixth_power)
    derivative = -12.0 * energy * (2.0 * sixth_power - 1.0) * sixth_power / shifted
    outer_value, outer_slope = taper(radius_sq, OUTER_CUT)
    inner_value, inner_slope = taper(radius_sq, INNER_CUT)
    if longer:
        switch = outer_value - inner_value
        switch_slope = outer_slope - inner_slope
    else:
        switch = inner_value
        switch_slope = inner_slope
    weight = -2.0 * (derivative * switch + potential * switch_slope)
    weight = weight * left_param[2][:, None] * right_param[2][None, :]
    return lax.optimization_barrier(jnp.sum(weight[None] * separation, 2))

def reference(positions, momenta, noise, atom_types, occupancy, type_sigma, type_eps, type_mass):
    total_beads = positions.shape[0]
    all_cells = positions.shape[1]
    domain_cells = GY * GZ
    neighbours = stencil_table(all_cells, domain_cells, GZ, GY)
    params, mass_atom = atom_table(atom_types, occupancy, type_sigma, type_eps, type_mass)
    root_mass = jnp.sqrt(mass_atom)[None, :, None, :]
    domain = jnp.arange(all_cells) // domain_cells
    within = jnp.arange(all_cells) % domain_cells
    missing = neighbours == 3 * domain_cells
    source = (domain[:, None] + neighbours // domain_cells - 1) % N_SPACE * domain_cells + neighbours % domain_cells
    source = jnp.where(missing, all_cells, source).astype(jnp.int32)
    right_anchor = anchor_of(neighbours, domain_cells, GZ)
    left_anchor = anchor_of(within + domain_cells, domain_cells, GZ)
    param_padded = jnp.concatenate([params, jnp.zeros_like(params[:1])], 0)

    def field(coords, longer):
        padded = jnp.concatenate([coords, jnp.zeros_like(coords[:, :1])], 1)
        bead_total = coords.shape[0]

        def one_cell(cell_index):
            listing = source[cell_index]
            left_all = coords[:, cell_index] + left_anchor[cell_index][None, :, None]
            right_all = padded[:, listing] + right_anchor[cell_index][None, :, :, None]
            right_all = jnp.transpose(right_all, (0, 2, 1, 3)).reshape(bead_total, 3, -1)
            right_param = jnp.transpose(param_padded[listing], (1, 0, 2)).reshape(3, -1)
            left_param = params[cell_index]

            def per_bead(left_position, right_position):
                return pair_force(left_position, left_param, right_position, right_param, longer)
            return jax.vmap(per_bead)(left_all, right_all)
        result = lax.map(one_cell, jnp.arange(all_cells))
        return jnp.transpose(result, (1, 0, 2, 3))
    short_force = field(positions, False)
    kicked = momenta + 0.5 * TIME_STEP * short_force
    matrix = mode_table(total_beads)
    position_modes = jnp.einsum('kn,kcda->ncda', matrix, positions * root_mass, precision=precise)
    momentum_modes = jnp.einsum('kn,kcda->ncda', matrix, kicked / root_mass, precision=precise)
    noise_modes = jnp.einsum('kn,kcda->ncda', matrix, noise, precision=precise)
    moved_position, moved_momentum = propagate(position_modes, momentum_modes, noise_modes)
    new_positions = jnp.einsum('kn,ncda->kcda', matrix, moved_position, precision=precise) / root_mass
    free_momenta = jnp.einsum('kn,ncda->kcda', matrix, moved_momentum, precision=precise) * root_mass
    weights = contract_table(total_beads, PC)
    contracted = jnp.einsum('rk,kcda->rcda', weights, new_positions, precision=precise)
    slow_force = field(contracted, True)
    spread_force = total_beads / PC * jnp.einsum('rk,rcda->kcda', weights, slow_force, precision=precise)
    new_momenta = free_momenta + 0.5 * TIME_STEP * spread_force
    return (new_positions, new_momenta)
```

```python
import functools

import jax
import jax.numpy as jnp
import numpy as np
from jax import lax
from jax.experimental import pallas as pl
from jax.experimental.pallas import tpu as pltpu
from jax.sharding import PartitionSpec as P

PC = 8
GY = 4
GZ = 4

TIME_STEP = 0.05
INVERSE_TEMP = 32.0
CENTROID_FRICTION = 1.0
INNER_CUT = 0.5
OUTER_CUT = 1.0
CUBE_ROOT_TWO = 2.0 ** (1.0 / 3.0)
F32 = jnp.float32
BF16 = jnp.bfloat16
VMEM_LIMIT = 48 * 1024 * 1024


def mode_matrix(number):
    rows = np.arange(number, dtype=np.float64)[:, None]
    column = np.arange(number, dtype=np.float64)[None, :]
    phases = 2.0 * np.pi * rows * column / number
    factor = np.sqrt(2.0 / number)
    middle = np.cos(np.pi * rows) / np.sqrt(number)
    matrix = np.where(column < number / 2, factor * np.cos(phases), factor * np.sin(phases))
    matrix = np.where(column == number / 2, middle, matrix)
    return np.where(column == 0, 1.0 / np.sqrt(number), matrix)


def contract_matrix(full_count, reduced):
    selected = np.arange(reduced)
    selected = np.where(selected <= reduced // 2, selected, selected + full_count - reduced)
    chosen = mode_matrix(full_count)[:, selected]
    return np.sqrt(reduced / full_count) * (mode_matrix(reduced) @ chosen.T)


def step_matrices(number):
    index = np.arange(number, dtype=np.float64)
    frequency = 2.0 * (number / INVERSE_TEMP) * np.sin(np.pi * index / number)
    friction = np.where(index == 0, CENTROID_FRICTION, 2.0 * frequency)
    damping = np.exp(-friction * TIME_STEP)
    kicking = np.sqrt((1.0 - damping * damping) / INVERSE_TEMP)
    cosine = np.cos(frequency * TIME_STEP)
    sine = np.sin(frequency * TIME_STEP)
    drift = np.where(index == 0, TIME_STEP, sine / np.where(index == 0, 1.0, frequency))
    modes = mode_matrix(number)

    def over_beads(diagonal):
        return (modes * diagonal[None, :]) @ modes.T

    return np.array(
        [
            [over_beads(cosine), over_beads(drift * damping), over_beads(drift * kicking)],
            [
                over_beads(-frequency * sine),
                over_beads(cosine * damping),
                over_beads(cosine * kicking),
            ],
        ]
    )


def cell_pairs(domain_cells):
    inside, across = [], []
    for one in range(domain_cells):
        for two in range(domain_cells):
            if abs(one // GZ - two // GZ) <= 1 and abs(one % GZ - two % GZ) <= 1:
                across.append((one, two))
                if one < two:
                    inside.append((one, two))
    return np.array(inside, np.int32), np.array(across, np.int32)


def split_three(value):
    high = value.astype(BF16).astype(F32)
    rest = value - high
    middle = rest.astype(BF16).astype(F32)
    return high, middle, rest - middle


def dot(left, right, contract=((1,), (0,))):
    return lax.dot_general(left, right, (contract, ((), ())), preferred_element_type=F32)


def cell_vector(position, half_sigma, layer, cell):
    row = lax.broadcasted_iota(jnp.int32, (8, position.shape[-1]), 0)
    block = jnp.concatenate(
        [position, half_sigma, jnp.zeros((4, position.shape[-1]), F32)], axis=0
    )
    corner = jnp.where(
        row == 0,
        float(layer - 1),
        jnp.where(
            row == 1,
            (cell // GZ).astype(F32) - GY / 2,
            jnp.where(row == 2, (cell % GZ).astype(F32) - GZ / 2, 0.0),
        ),
    )
    return block + corner, row


def right_side(vector, row):
    norm = jnp.sum(vector * vector, axis=0, keepdims=True)
    full = jnp.where(row == 4, norm, jnp.where(row == 5, 1.0, vector))
    high, middle, low = split_three(full)
    return jnp.concatenate([high, middle, high, low, high, middle], axis=0)


def left_side(vector, row):
    norm = jnp.sum(vector * vector, axis=0, keepdims=True)
    full = jnp.where(
        row < 3,
        -2.0 * vector,
        jnp.where(
            row == 3, 2.0 * vector, jnp.where(row == 4, 1.0, jnp.where(row == 5, norm, 0.0))
        ),
    )
    high, middle, low = split_three(full)
    return jnp.concatenate([high, high, middle, high, low, middle], axis=0)


def source_rows(vector, row, strength):
    full = strength * jnp.where(row == 3, 1.0, vector)
    high, middle, low = split_three(full)
    return jnp.concatenate([high, middle, low, jnp.zeros_like(low)], axis=0)


def pair_weight(h, s2, longer):
    guess = pl.reciprocal(h, approx=True)
    inverse = guess * (2.0 - h * guess)
    if longer:
        quotient = s2 * inverse
        sixth = quotient * quotient * quotient
        radius_sq = h - s2
        outer = jnp.maximum(1.0 - radius_sq, 0.0)
        inner = jnp.maximum(1.0 - 4.0 * radius_sq, 0.0)
        switch = outer * outer - inner * inner
        slope = outer - 4.0 * inner
        return sixth * (
            (6.0 * sixth - 3.0) * (switch * inverse) + (2.0 * sixth - 2.0) * slope
        )
    scaled, reach = s2
    quotient = scaled * inverse
    twice = quotient * quotient * quotient
    edge = jnp.maximum(reach * inverse - 1.0, 2.0)
    bracket = edge * (twice - 1.0) - twice
    return (twice * bracket) * ((edge - 2.0) * h)


def pair_block(left, right, source_left, source_right, s2, longer, reaction):
    h = dot(left, right)
    chunk = 32
    highs, lows = [], []
    for start in range(0, h.shape[0], chunk):
        piece = slice(start, start + chunk)
        if longer:
            terms = s2[piece]
        else:
            terms = (s2[0][piece], s2[1][piece])
        weight = pair_weight(h[piece], terms, longer)
        high = weight.astype(BF16)
        highs.append(high)
        lows.append((weight - high.astype(F32)).astype(BF16))
    high = jnp.concatenate(highs, axis=0)
    low = jnp.concatenate(lows, axis=0)

    def fold(total):
        return total[0:8] + total[8:16] + total[16:24]

    on_right = fold(dot(source_left, high) + dot(source_left, low))
    if not reaction:
        return on_right, None
    across = ((1,), (1,))
    on_left = fold(dot(source_right, high, across) + dot(source_right, low, across))
    return on_right, on_left


def size_terms(s2, longer):
    if longer:
        return s2
    return CUBE_ROOT_TWO * s2, 0.75 + 3.0 * s2


def force_of(total, vector, strength, factor):
    return (factor * strength) * (vector[0:3] * total[3:4] - total[0:3])


def weight_factor(longer):
    return 8.0 if longer else 64.0 / 3.0


def prepare(read, params, layer, beads, cells, left_ref, right_ref, source_ref, size_left, size_right):
    lanes = params.shape[-1]

    def one(bead, cell):
        half_sigma = params[cell, 0:1, :]
        strength = params[cell, 1:2, :]
        vector, row = cell_vector(read(bead, cell), half_sigma, layer, cell)
        if left_ref is not None:
            left_ref[bead, cell] = left_side(vector, row).T.astype(BF16)
        if right_ref is not None:
            right_ref[bead, cell] = right_side(vector, row).astype(BF16)
        source_ref[bead, cell] = source_rows(vector, row, strength).astype(BF16)

    def sizes(cell):
        half_sigma = params[cell, 0:1, :]
        row = lax.broadcasted_iota(jnp.int32, (8, lanes), 0)
        vector = jnp.where(row == 3, half_sigma, 0.0)
        if left_ref is not None:
            size_left[cell] = left_side(vector, row).T.astype(BF16)
        if right_ref is not None:
            size_right[cell] = right_side(vector, row).astype(BF16)

    def per_cell(cell, carry):
        sizes(cell)
        for bead in range(beads):
            one(bead, cell)
        return carry

    lax.fori_loop(0, cells, per_cell, 0)


def inside_kernel(longer, pairs_ref, position, params, total_ref, left_ref, right_ref, source_ref, size_left, size_right):
    beads, cells = position.shape[:2]
    prepare(
        lambda bead, cell: position[bead, cell],
        params,
        0,
        beads,
        cells,
        left_ref,
        right_ref,
        source_ref,
        size_left,
        size_right,
    )

    def own(cell, carry):
        s2 = size_terms(dot(size_left[cell], size_right[cell]), longer)
        for bead in range(beads):
            source = source_ref[bead, cell]
            total, _ = pair_block(
                left_ref[bead, cell], right_ref[bead, cell], source, source, s2, longer, False
            )
            total_ref[bead, cell] = total
        return carry

    lax.fori_loop(0, cells, own, 0)

    def pair(index, carry):
        one = pairs_ref[index, 0]
        two = pairs_ref[index, 1]
        s2 = size_terms(dot(size_left[one], size_right[two]), longer)
        for bead in range(beads):
            on_two, on_one = pair_block(
                left_ref[bead, one],
                right_ref[bead, two],
                source_ref[bead, one],
                source_ref[bead, two],
                s2,
                longer,
                True,
            )
            total_ref[bead, two] += on_two
            total_ref[bead, one] += on_one
        return carry

    lax.fori_loop(0, pairs_ref.shape[0], pair, 0)


def across_kernel(
    longer, pairs_ref, position, params, next_position, next_params, held, force_ref, back_ref,
    total_ref, next_total, left_ref, right_ref, source_ref, next_source, size_left, size_right,
):
    beads, cells = position.shape[:2]
    prepare(
        lambda bead, cell: position[bead, cell],
        params, 0, beads, cells, None, right_ref, source_ref, None, size_right,
    )
    prepare(
        lambda bead, cell: next_position[bead, cell],
        next_params, 1, beads, cells, left_ref, None, next_source, size_left, None,
    )
    total_ref[...] = held[...]
    next_total[...] = jnp.zeros_like(next_total)

    def pair(index, carry):
        one = pairs_ref[index, 0]
        two = pairs_ref[index, 1]
        s2 = size_terms(dot(size_left[one], size_right[two]), longer)
        for bead in range(beads):
            on_two, on_one = pair_block(
                left_ref[bead, one],
                right_ref[bead, two],
                next_source[bead, one],
                source_ref[bead, two],
                s2,
                longer,
                True,
            )
            total_ref[bead, two] += on_two
            next_total[bead, one] += on_one
        return carry

    lax.fori_loop(0, pairs_ref.shape[0], pair, 0)

    def finish(cell, carry):
        for bead in range(beads):
            for layer, place, values, total, out in (
                (0, position, params, total_ref, force_ref),
                (1, next_position, next_params, next_total, back_ref),
            ):
                vector, _ = cell_vector(place[bead, cell], values[cell, 0:1, :], layer, cell)
                out[bead, cell] = force_of(
                    total[bead, cell], vector, values[cell, 1:2, :], weight_factor(longer)
                )
        return carry

    lax.fori_loop(0, cells, finish, 0)


def call(kernel, inputs, smem, outputs, scratch, flops):
    return pl.pallas_call(
        kernel,
        out_shape=outputs,
        in_specs=[
            pl.BlockSpec(memory_space=pltpu.SMEM if place < smem else pltpu.VMEM)
            for place in range(len(inputs))
        ],
        scratch_shapes=scratch,
        compiler_params=pltpu.CompilerParams(vmem_limit_bytes=VMEM_LIMIT),
        cost_estimate=pl.CostEstimate(flops=flops, bytes_accessed=1 << 18, transcendentals=0),
    )(*inputs)


PAIR_FLOPS = 40 * 128 * 128


def pair_scratch(beads, cells, lanes):
    return dict(
        left=pltpu.VMEM((beads, cells, lanes, 48), BF16),
        right=pltpu.VMEM((beads, cells, 48, lanes), BF16),
        source=pltpu.VMEM((beads, cells, 32, lanes), BF16),
        size_left=pltpu.VMEM((cells, lanes, 48), BF16),
        size_right=pltpu.VMEM((cells, 48, lanes), BF16),
        total=pltpu.VMEM((beads, cells, 8, lanes), F32),
    )


def pair_forces(position, params, next_position, next_params, longer):
    beads, cells, _, lanes = position.shape
    inside, across = cell_pairs(cells)
    room = pair_scratch(beads, cells, lanes)
    held = call(
        functools.partial(inside_kernel, longer),
        (jnp.asarray(inside), position, params),
        1,
        jax.ShapeDtypeStruct((beads, cells, 8, lanes), F32),
        [room["left"], room["right"], room["source"], room["size_left"], room["size_right"]],
        PAIR_FLOPS * beads * (len(inside) + cells),
    )
    forces = jax.ShapeDtypeStruct((beads, cells, 3, lanes), F32)
    return call(
        functools.partial(across_kernel, longer),
        (jnp.asarray(across), position, params, next_position, next_params, held),
        1,
        (forces, forces),
        [
            room["total"], room["total"], room["left"], room["right"], room["source"],
            room["source"], room["size_left"], room["size_right"],
        ],
        PAIR_FLOPS * beads * len(across),
    )


def kick_kernel(
    piece_rows, groups, table, rank, position, momenta, noise, force, back, params, partial_ref, piece_ref
):
    beads, cells = position.shape[:2]
    holders = piece_ref.shape[0]
    reduced = table.shape[0]
    first = rank[0] * beads
    if holders * piece_rows > 3 * cells:
        piece_ref[...] = jnp.zeros_like(piece_ref)
    for cell in range(cells):
        mass = params[cell, 2:3, :]
        per_mass = 1.0 / mass
        per_root = lax.rsqrt(mass)
        per_root = per_root * (1.5 - 0.5 * mass * per_root * per_root)
        inputs = []
        for bead in range(beads):
            kicked = momenta[bead, cell] + 0.5 * TIME_STEP * (force[bead, cell] + back[bead, cell])
            inputs.append((position[bead, cell], kicked * per_mass, noise[bead, cell] * per_root))
        for bead in range(beads):
            for kind in range(3):
                base = (kind * beads + bead) * piece_rows
                if piece_rows % 3 == 0:
                    owner, row = divmod(3 * cell, piece_rows)
                    piece_ref[owner, base + row : base + row + 3, :] = inputs[bead][kind]
                else:
                    for axis in range(3):
                        owner, row = divmod(3 * cell + axis, piece_rows)
                        piece_ref[owner, base + row : base + row + 1, :] = inputs[bead][kind][
                            axis : axis + 1
                        ]
        for group in range(reduced):
            total = None
            for bead in range(beads):
                for kind in range(3):
                    term = table[group, kind * holders * beads + first + bead] * inputs[bead][kind]
                    total = term if total is None else total + term
            for copy in range(groups):
                partial_ref[group * groups + copy, 3 * cell : 3 * cell + 3, :] = total


def move_kernel(piece_rows, beads, matrix, arrived, out_ref, gathered):
    holders = arrived.shape[0]
    taken = 3 * beads
    given = 2 * beads
    for row in range(piece_rows):
        for holder in range(holders):
            gathered[row, holder * taken : (holder + 1) * taken, :] = arrived[
                holder, pl.ds(row, taken, stride=piece_rows), :
            ]
        moved = lax.dot_general(
            matrix[...],
            gathered[row],
            (((1,), (0,)), ((), ())),
            precision=lax.Precision.HIGHEST,
            preferred_element_type=F32,
        )
        for holder in range(holders):
            out_ref[holder, row * given : (row + 1) * given, :] = moved[
                holder * given : (holder + 1) * given
            ]


def finish_kernel(piece_rows, groups, table, rank, moved, slow, params, position_ref, momentum_ref):
    beads, cells = position_ref.shape[:2]
    given = 2 * beads
    reduced = table.shape[0]
    first = rank[0] * beads
    for cell in range(cells):
        mass = params[cell, 2:3, :]
        for bead in range(beads):
            def taken(kind):
                if piece_rows % 3 == 0:
                    owner, row = divmod(3 * cell, piece_rows)
                    return moved[owner, pl.ds(row * given + kind * beads + bead, 3, stride=given), :]
                rows = []
                for axis in range(3):
                    owner, row = divmod(3 * cell + axis, piece_rows)
                    place = row * given + kind * beads + bead
                    rows.append(moved[owner, place : place + 1, :])
                return jnp.concatenate(rows, axis=0)

            position_ref[bead, cell] = taken(0)
            total = mass * taken(1)
            for group in range(reduced):
                total = total + table[group, first + bead] * slow[
                    group * groups, 3 * cell : 3 * cell + 3, :
                ]
            momentum_ref[bead, cell] = total


def shards(positions, momenta, noise, atom_types, occupancy, type_sigma, type_eps, type_mass):
    beads, cells, _, lanes = positions.shape
    holders = lax.axis_size("bead")
    domains = lax.axis_size("space")
    rank = lax.axis_index("bead")
    total_beads = beads * holders
    rows = 3 * cells
    piece_rows = -(-rows // holders)
    held = max(1, PC // holders)
    groups = max(1, holders // PC)
    contract = contract_matrix(total_beads, PC)
    steps = step_matrices(total_beads)
    rank_table = rank.astype(jnp.int32).reshape(1)
    one_back = [((i + 1) % domains, i) for i in range(domains)]
    one_on = [(i, (i + 1) % domains) for i in range(domains)]

    codes = jnp.arange(type_sigma.shape[0])
    onehot = atom_types[..., None] == codes
    living = jnp.arange(lanes)[None, :] < occupancy[:, None]
    half_sigma = 0.5 * jnp.sum(jnp.where(onehot, type_sigma, 0.0), -1)
    root_eps = jnp.sqrt(jnp.sum(jnp.where(onehot, type_eps, 0.0), -1))
    mass = jnp.sum(jnp.where(onehot, type_mass, 0.0), -1)
    params = jnp.stack([half_sigma, jnp.where(living, root_eps, 0.0), mass], 1)

    stacked = jnp.concatenate([positions, params[None]], 0)
    next_stacked = lax.ppermute(stacked, "space", one_back)
    next_params = next_stacked[beads]
    force, back = pair_forces(positions, params, next_stacked[:beads], next_params, False)
    back = lax.ppermute(back, "space", one_on)

    position_map = np.concatenate([contract @ steps[0, kind] for kind in range(3)], axis=1)
    partial, pieces = call(
        functools.partial(kick_kernel, piece_rows, groups),
        (
            jnp.asarray(position_map, F32), rank_table, positions, momenta, noise, force, back,
            params,
        ),
        2,
        (
            jax.ShapeDtypeStruct((PC * groups, rows, lanes), F32),
            jax.ShapeDtypeStruct((holders, 3 * beads * piece_rows, lanes), F32),
        ),
        [],
        1 << 22,
    )
    arrived = lax.all_to_all(
        partial.reshape(holders, held * rows, lanes), "bead", split_axis=0, concat_axis=0, tiled=True
    )
    contracted = jnp.sum(arrived, 0).reshape(held, cells, 3, lanes)
    next_contracted = lax.ppermute(contracted, "space", one_back)
    pieces = lax.all_to_all(pieces, "bead", split_axis=0, concat_axis=0, tiled=True)
    slow, slow_back = pair_forces(contracted, params, next_contracted, next_params, True)
    slow = slow + lax.ppermute(slow_back, "space", one_on)

    order = steps.reshape(2, 3, holders, beads, holders, beads).transpose(2, 0, 3, 4, 1, 5)
    order = order.reshape(2 * total_beads, 3 * total_beads)
    moved = call(
        functools.partial(move_kernel, piece_rows, beads),
        (jnp.asarray(order, F32), pieces),
        0,
        jax.ShapeDtypeStruct((holders, 2 * beads * piece_rows, lanes), F32),
        [pltpu.VMEM((piece_rows, 3 * total_beads, lanes), F32)],
        1 << 23,
    )
    moved_rows = 2 * beads * piece_rows
    sent = jnp.concatenate(
        [
            moved,
            jnp.broadcast_to(slow.reshape(1, held * rows, lanes), (holders, held * rows, lanes)),
        ],
        1,
    )
    got = lax.all_to_all(sent, "bead", split_axis=0, concat_axis=0, tiled=True)
    spread = 0.5 * TIME_STEP * (total_beads / PC) * contract
    shape = jax.ShapeDtypeStruct(positions.shape, F32)
    return call(
        functools.partial(finish_kernel, piece_rows, groups),
        (
            jnp.asarray(spread, F32), rank_table, got[:, :moved_rows],
            got[:, moved_rows:].reshape(holders * held, rows, lanes), params,
        ),
        2,
        (shape, shape),
        [],
        1 << 20,
    )


def solution(mesh):
    placed = (
        P("bead", "space", None, None),
        P("bead", "space", None, None),
        P("bead", "space", None, None),
        P("space", None),
        P("space"),
        P(),
        P(),
        P(),
    )
    return jax.shard_map(
        shards,
        mesh=mesh,
        in_specs=placed,
        out_specs=(P("bead", "space", None, None), P("bead", "space", None, None)),
        check_vma=False,
    )
```

```python
import functools

import jax
import jax.numpy as jnp
import numpy as np
from jax import lax
from jax.experimental import pallas as pl
from jax.experimental.pallas import tpu as pltpu
from jax.sharding import PartitionSpec as P

PC = 8
GY = 4
GZ = 4

TIME_STEP = 0.05
INVERSE_TEMP = 32.0
CENTROID_FRICTION = 1.0
INNER_CUT = 0.5
OUTER_CUT = 1.0
CUBE_ROOT_TWO = 2.0 ** (1.0 / 3.0)
F32 = jnp.float32
VMEM_LIMIT = 48 * 1024 * 1024


def mode_matrix(number):
    rows = np.arange(number, dtype=np.float64)[:, None]
    column = np.arange(number, dtype=np.float64)[None, :]
    phases = 2.0 * np.pi * rows * column / number
    factor = np.sqrt(2.0 / number)
    middle = np.cos(np.pi * rows) / np.sqrt(number)
    matrix = np.where(column < number / 2, factor * np.cos(phases), factor * np.sin(phases))
    matrix = np.where(column == number / 2, middle, matrix)
    return np.where(column == 0, 1.0 / np.sqrt(number), matrix)


def contract_matrix(full_count, reduced):
    selected = np.arange(reduced)
    selected = np.where(selected <= reduced // 2, selected, selected + full_count - reduced)
    chosen = mode_matrix(full_count)[:, selected]
    return np.sqrt(reduced / full_count) * (mode_matrix(reduced) @ chosen.T)


def step_matrices(number):
    index = np.arange(number, dtype=np.float64)
    frequency = 2.0 * (number / INVERSE_TEMP) * np.sin(np.pi * index / number)
    friction = np.where(index == 0, CENTROID_FRICTION, 2.0 * frequency)
    damping = np.exp(-friction * TIME_STEP)
    kicking = np.sqrt((1.0 - damping * damping) / INVERSE_TEMP)
    cosine = np.cos(frequency * TIME_STEP)
    sine = np.sin(frequency * TIME_STEP)
    drift = np.where(index == 0, TIME_STEP, sine / np.where(index == 0, 1.0, frequency))
    modes = mode_matrix(number)

    def over_beads(diagonal):
        return (modes * diagonal[None, :]) @ modes.T

    return np.array(
        [
            [over_beads(cosine), over_beads(drift * damping), over_beads(drift * kicking)],
            [
                over_beads(-frequency * sine),
                over_beads(cosine * damping),
                over_beads(cosine * kicking),
            ],
        ]
    )


def partner_lists(domain_cells):
    inside, across = [], []
    for one in range(domain_cells):
        near = []
        for two in range(domain_cells):
            step_y, step_z = two // GZ - one // GZ, two % GZ - one % GZ
            if abs(step_y) <= 1 and abs(step_z) <= 1:
                near.append((two, step_y, step_z))
        across.append(near)
        inside.append([entry for entry in near if entry[0] > one])
    return inside, across


def flat(lists):
    starts = np.cumsum([0] + [len(entries) for entries in lists]).astype(np.int32)
    return starts, np.array([value for entries in lists for entry in entries for value in entry], np.int32)


def pair_weight(h, radius_sq, terms, longer):
    inverse = pl.reciprocal(h, approx=True)
    if longer:
        quotient = terms[0] * inverse
        sixth = quotient * quotient * quotient
        outer = jnp.maximum(1.0 - radius_sq, 0.0)
        inner = jnp.maximum(1.0 - 4.0 * radius_sq, 0.0)
        switch = outer * outer - inner * inner
        slope = outer - 4.0 * inner
        return sixth * (
            (6.0 * sixth - 3.0) * (switch * inverse) + (2.0 * sixth - 2.0) * slope
        )
    quotient = terms[1] * inverse
    twice = quotient * quotient * quotient
    edge = jnp.maximum(terms[2] * inverse - 1.0, 2.0)
    bracket = edge * (twice - 1.0) - twice
    return (twice * bracket) * ((edge - 2.0) * h)


def weight_factor(longer):
    return 8.0 if longer else 64.0 / 3.0


def columns(block):
    few, lanes = block.shape
    return jnp.concatenate([block, jnp.zeros((8 - few, lanes), F32)], axis=0).T


def spread_rows(position, params, cell, beads, rows_ref, size_ref):
    lanes = position.shape[-1]
    sizes = columns(params[cell, 0:2, :])
    for kind in range(2):
        size_ref[kind] = jnp.broadcast_to(sizes[:, kind : kind + 1], (lanes, lanes))
    for bead in range(beads):
        block = columns(position[bead, cell])
        for axis in range(3):
            rows_ref[bead, axis] = jnp.broadcast_to(block[:, axis : axis + 1], (lanes, lanes))


def meet(
    longer, span, first, offset, partner, position, params, rows_ref, size_ref, total_ref, back_ref
):
    beads = position.shape[0]
    lanes = position.shape[-1]
    here = pl.ds(first, span)
    half = size_ref[0, here, :] + params[partner, 0:1, :]
    s2 = half * half
    terms = (s2,) if longer else (s2, CUBE_ROOT_TWO * s2, 0.75 + 3.0 * s2)
    depth = size_ref[1, here, :] * params[partner, 1:2, :]
    for bead in range(beads):
        place = position[bead, partner]
        apart = []
        for axis in range(3):
            other = place[axis : axis + 1, :] + offset[axis]
            apart.append(other - rows_ref[bead, axis, here, :])
        radius_sq = apart[0] * apart[0] + apart[1] * apart[1] + apart[2] * apart[2]
        weight = depth * pair_weight(radius_sq + s2, radius_sq, terms, longer)
        for axis in range(3):
            push = weight * apart[axis]
            total_ref[bead, partner, axis] += jnp.sum(push.reshape(span // 8, 8, lanes), axis=0)
            if back_ref is not None:
                back_ref[bead, axis, here, :] -= push


def fold_back(back_ref, bead):
    lanes = back_ref.shape[-1]
    column = lax.broadcasted_iota(jnp.int32, (lanes, 8), 1)
    sums = [jnp.sum(back_ref[bead, axis], axis=1, keepdims=True) for axis in range(3)]
    block = jnp.where(
        column == 0, sums[0], jnp.where(column == 1, sums[1], jnp.where(column == 2, sums[2], 0.0))
    )
    return block.T[0:3]


def fold_total(total_ref, bead, cell):
    return jnp.concatenate(
        [jnp.sum(total_ref[bead, cell, axis], axis=0, keepdims=True) for axis in range(3)], axis=0
    )


def pairs_kernel(
    longer, span, across, starts, partners, occupied, position, params, *rest
):
    if across:
        spread, spread_params, held, force_ref, other_ref = rest[:5]
    else:
        spread, spread_params, held = position, params, None
        force_ref = rest[0]
        other_ref = None
    total_ref, back_ref, rows_ref, size_ref = rest[-4:]
    beads, cells = position.shape[:2]
    total_ref[...] = jnp.zeros_like(total_ref)

    def per_cell(cell, carry):
        spread_rows(spread, spread_params, cell, beads, rows_ref, size_ref)
        back_ref[...] = jnp.zeros_like(back_ref)

        def per_span(index, carry):
            first = pl.multiple_of(index * span, span)
            common = (position, params, rows_ref, size_ref, total_ref)
            if not across:
                meet(longer, span, first, (0.0, 0.0, 0.0), cell, *common, None)

            def per_partner(entry, carry):
                offset = (
                    -1.0 if across else 0.0,
                    partners[3 * entry + 1].astype(F32),
                    partners[3 * entry + 2].astype(F32),
                )
                meet(longer, span, first, offset, partners[3 * entry], *common, back_ref)
                return carry

            return lax.fori_loop(starts[cell], starts[cell + 1], per_partner, carry)

        lax.fori_loop(0, lax.div(occupied[cell] + (span - 1), span), per_span, 0)
        for bead in range(beads):
            if across:
                other_ref[bead, cell] = weight_factor(longer) * fold_back(back_ref, bead)
            else:
                force_ref[bead, cell] = fold_back(back_ref, bead)
        return carry

    lax.fori_loop(0, cells, per_cell, 0)

    def finish(cell, carry):
        for bead in range(beads):
            total = fold_total(total_ref, bead, cell)
            if across:
                force_ref[bead, cell] = weight_factor(longer) * total + held[bead, cell]
            else:
                force_ref[bead, cell] = weight_factor(longer) * (total + force_ref[bead, cell])
        return carry

    lax.fori_loop(0, cells, finish, 0)


def call(kernel, inputs, smem, outputs, scratch, flops):
    return pl.pallas_call(
        kernel,
        out_shape=outputs,
        in_specs=[
            pl.BlockSpec(memory_space=pltpu.SMEM if place < smem else pltpu.VMEM)
            for place in range(len(inputs))
        ],
        scratch_shapes=scratch,
        compiler_params=pltpu.CompilerParams(vmem_limit_bytes=VMEM_LIMIT),
        cost_estimate=pl.CostEstimate(flops=flops, bytes_accessed=1 << 18, transcendentals=0),
    )(*inputs)


PAIR_FLOPS = 40 * 128 * 128


def pair_forces(position, params, occupied, next_position, next_params, next_occupied, longer):
    beads, cells, _, lanes = position.shape
    inside, across = partner_lists(cells)
    span = lanes // 2 if longer else lanes // 4
    scratch = [
        pltpu.VMEM((beads, cells, 3, 8, lanes), F32),
        pltpu.VMEM((beads, 3, lanes, lanes), F32),
        pltpu.VMEM((beads, 3, lanes, lanes), F32),
        pltpu.VMEM((2, lanes, lanes), F32),
    ]
    forces = jax.ShapeDtypeStruct((beads, cells, 3, lanes), F32)
    starts, entries = flat(inside)
    held = call(
        functools.partial(pairs_kernel, longer, span, False),
        (jnp.asarray(starts), jnp.asarray(entries), occupied, position, params),
        3,
        forces,
        scratch,
        PAIR_FLOPS * beads * (len(entries) // 3 + cells),
    )
    starts, entries = flat(across)
    return call(
        functools.partial(pairs_kernel, longer, span, True),
        (
            jnp.asarray(starts), jnp.asarray(entries), next_occupied, position, params,
            next_position, next_params, held,
        ),
        3,
        (forces, forces),
        scratch,
        PAIR_FLOPS * beads * (len(entries) // 3),
    )


def kick_kernel(
    piece_rows, groups, table, rank, position, momenta, noise, force, back, params, partial_ref, piece_ref
):
    beads, cells = position.shape[:2]
    holders = piece_ref.shape[0]
    reduced = table.shape[0]
    first = rank[0] * beads
    if holders * piece_rows > 3 * cells:
        piece_ref[...] = jnp.zeros_like(piece_ref)
    for cell in range(cells):
        mass = params[cell, 2:3, :]
        per_mass = 1.0 / mass
        per_root = lax.rsqrt(mass)
        per_root = per_root * (1.5 - 0.5 * mass * per_root * per_root)
        inputs = []
        for bead in range(beads):
            kicked = momenta[bead, cell] + 0.5 * TIME_STEP * (force[bead, cell] + back[bead, cell])
            inputs.append((position[bead, cell], kicked * per_mass, noise[bead, cell] * per_root))
        for bead in range(beads):
            for kind in range(3):
                base = (kind * beads + bead) * piece_rows
                if piece_rows % 3 == 0:
                    owner, row = divmod(3 * cell, piece_rows)
                    piece_ref[owner, base + row : base + row + 3, :] = inputs[bead][kind]
                else:
                    for axis in range(3):
                        owner, row = divmod(3 * cell + axis, piece_rows)
                        piece_ref[owner, base + row : base + row + 1, :] = inputs[bead][kind][
                            axis : axis + 1
                        ]
        for group in range(reduced):
            total = None
            for bead in range(beads):
                for kind in range(3):
                    term = table[group, kind * holders * beads + first + bead] * inputs[bead][kind]
                    total = term if total is None else total + term
            for copy in range(groups):
                partial_ref[group * groups + copy, 3 * cell : 3 * cell + 3, :] = total


def move_kernel(piece_rows, beads, matrix, arrived, out_ref, gathered):
    holders = arrived.shape[0]
    taken = 3 * beads
    given = 2 * beads
    for row in range(piece_rows):
        for holder in range(holders):
            gathered[row, holder * taken : (holder + 1) * taken, :] = arrived[
                holder, pl.ds(row, taken, stride=piece_rows), :
            ]
        moved = lax.dot_general(
            matrix[...],
            gathered[row],
            (((1,), (0,)), ((), ())),
            precision=lax.Precision.HIGHEST,
            preferred_element_type=F32,
        )
        for holder in range(holders):
            out_ref[holder, row * given : (row + 1) * given, :] = moved[
                holder * given : (holder + 1) * given
            ]


def finish_kernel(piece_rows, groups, table, rank, moved, slow, params, position_ref, momentum_ref):
    beads, cells = position_ref.shape[:2]
    given = 2 * beads
    reduced = table.shape[0]
    first = rank[0] * beads
    for cell in range(cells):
        mass = params[cell, 2:3, :]
        for bead in range(beads):
            def taken(kind):
                if piece_rows % 3 == 0:
                    owner, row = divmod(3 * cell, piece_rows)
                    return moved[owner, pl.ds(row * given + kind * beads + bead, 3, stride=given), :]
                rows = []
                for axis in range(3):
                    owner, row = divmod(3 * cell + axis, piece_rows)
                    place = row * given + kind * beads + bead
                    rows.append(moved[owner, place : place + 1, :])
                return jnp.concatenate(rows, axis=0)

            position_ref[bead, cell] = taken(0)
            total = mass * taken(1)
            for group in range(reduced):
                total = total + table[group, first + bead] * slow[
                    group * groups, 3 * cell : 3 * cell + 3, :
                ]
            momentum_ref[bead, cell] = total


def shards(positions, momenta, noise, atom_types, occupancy, type_sigma, type_eps, type_mass):
    beads, cells, _, lanes = positions.shape
    holders = lax.axis_size("bead")
    domains = lax.axis_size("space")
    rank = lax.axis_index("bead")
    total_beads = beads * holders
    rows = 3 * cells
    piece_rows = -(-rows // holders)
    held = max(1, PC // holders)
    groups = max(1, holders // PC)
    contract = contract_matrix(total_beads, PC)
    steps = step_matrices(total_beads)
    rank_table = rank.astype(jnp.int32).reshape(1)
    one_back = [((i + 1) % domains, i) for i in range(domains)]
    one_on = [(i, (i + 1) % domains) for i in range(domains)]

    codes = jnp.arange(type_sigma.shape[0])
    onehot = atom_types[..., None] == codes
    living = jnp.arange(lanes)[None, :] < occupancy[:, None]
    half_sigma = 0.5 * jnp.sum(jnp.where(onehot, type_sigma, 0.0), -1)
    root_eps = jnp.sqrt(jnp.sum(jnp.where(onehot, type_eps, 0.0), -1))
    mass = jnp.sum(jnp.where(onehot, type_mass, 0.0), -1)
    params = jnp.stack([half_sigma, jnp.where(living, root_eps, 0.0), mass], 1)

    stacked = jnp.concatenate([positions, params[None]], 0)
    next_stacked = lax.ppermute(stacked, "space", one_back)
    next_params = next_stacked[beads]
    next_occupied = jnp.sum((next_params[:, 1] > 0.0).astype(jnp.int32), -1)
    force, back = pair_forces(
        positions, params, occupancy, next_stacked[:beads], next_params, next_occupied, False
    )
    back = lax.ppermute(back, "space", one_on)

    position_map = np.concatenate([contract @ steps[0, kind] for kind in range(3)], axis=1)
    partial, pieces = call(
        functools.partial(kick_kernel, piece_rows, groups),
        (
            jnp.asarray(position_map, F32), rank_table, positions, momenta, noise, force, back,
            params,
        ),
        2,
        (
            jax.ShapeDtypeStruct((PC * groups, rows, lanes), F32),
            jax.ShapeDtypeStruct((holders, 3 * beads * piece_rows, lanes), F32),
        ),
        [],
        1 << 22,
    )
    arrived = lax.all_to_all(
        partial.reshape(holders, held * rows, lanes), "bead", split_axis=0, concat_axis=0, tiled=True
    )
    contracted = jnp.sum(arrived, 0).reshape(held, cells, 3, lanes)
    next_contracted = lax.ppermute(contracted, "space", one_back)
    pieces = lax.all_to_all(pieces, "bead", split_axis=0, concat_axis=0, tiled=True)
    slow, slow_back = pair_forces(
        contracted, params, occupancy, next_contracted, next_params, next_occupied, True
    )
    slow = slow + lax.ppermute(slow_back, "space", one_on)

    order = steps.reshape(2, 3, holders, beads, holders, beads).transpose(2, 0, 3, 4, 1, 5)
    order = order.reshape(2 * total_beads, 3 * total_beads)
    moved = call(
        functools.partial(move_kernel, piece_rows, beads),
        (jnp.asarray(order, F32), pieces),
        0,
        jax.ShapeDtypeStruct((holders, 2 * beads * piece_rows, lanes), F32),
        [pltpu.VMEM((piece_rows, 3 * total_beads, lanes), F32)],
        1 << 23,
    )
    moved_rows = 2 * beads * piece_rows
    sent = jnp.concatenate(
        [
            moved,
            jnp.broadcast_to(slow.reshape(1, held * rows, lanes), (holders, held * rows, lanes)),
        ],
        1,
    )
    got = lax.all_to_all(sent, "bead", split_axis=0, concat_axis=0, tiled=True)
    spread = 0.5 * TIME_STEP * (total_beads / PC) * contract
    shape = jax.ShapeDtypeStruct(positions.shape, F32)
    return call(
        functools.partial(finish_kernel, piece_rows, groups),
        (
            jnp.asarray(spread, F32), rank_table, got[:, :moved_rows],
            got[:, moved_rows:].reshape(holders * held, rows, lanes), params,
        ),
        2,
        (shape, shape),
        [],
        1 << 20,
    )


def solution(mesh):
    placed = (
        P("bead", "space", None, None),
        P("bead", "space", None, None),
        P("bead", "space", None, None),
        P("space", None),
        P("space"),
        P(),
        P(),
        P(),
    )
    return jax.shard_map(
        shards,
        mesh=mesh,
        in_specs=placed,
        out_specs=(P("bead", "space", None, None), P("bead", "space", None, None)),
        check_vma=False,
    )
```

```python
import functools

import jax
import jax.numpy as jnp
import numpy as np
from jax import lax
from jax.experimental import pallas as pl
from jax.experimental.pallas import tpu as pltpu
from jax.sharding import PartitionSpec as P

PC = 8
GY = 4
GZ = 4

TIME_STEP = 0.05
INVERSE_TEMP = 32.0
CENTROID_FRICTION = 1.0
INNER_CUT = 0.5
OUTER_CUT = 1.0
CUBE_ROOT_TWO = 2.0 ** (1.0 / 3.0)
F32 = jnp.float32
SPAN = 32
VMEM_LIMIT = 48 * 1024 * 1024


def mode_matrix(number):
    rows = np.arange(number, dtype=np.float64)[:, None]
    column = np.arange(number, dtype=np.float64)[None, :]
    phases = 2.0 * np.pi * rows * column / number
    factor = np.sqrt(2.0 / number)
    middle = np.cos(np.pi * rows) / np.sqrt(number)
    matrix = np.where(column < number / 2, factor * np.cos(phases), factor * np.sin(phases))
    matrix = np.where(column == number / 2, middle, matrix)
    return np.where(column == 0, 1.0 / np.sqrt(number), matrix)


def contract_matrix(full_count, reduced):
    selected = np.arange(reduced)
    selected = np.where(selected <= reduced // 2, selected, selected + full_count - reduced)
    chosen = mode_matrix(full_count)[:, selected]
    return np.sqrt(reduced / full_count) * (mode_matrix(reduced) @ chosen.T)


def step_matrices(number):
    index = np.arange(number, dtype=np.float64)
    frequency = 2.0 * (number / INVERSE_TEMP) * np.sin(np.pi * index / number)
    friction = np.where(index == 0, CENTROID_FRICTION, 2.0 * frequency)
    damping = np.exp(-friction * TIME_STEP)
    kicking = np.sqrt((1.0 - damping * damping) / INVERSE_TEMP)
    cosine = np.cos(frequency * TIME_STEP)
    sine = np.sin(frequency * TIME_STEP)
    drift = np.where(index == 0, TIME_STEP, sine / np.where(index == 0, 1.0, frequency))
    modes = mode_matrix(number)

    def over_beads(diagonal):
        return (modes * diagonal[None, :]) @ modes.T

    return np.array(
        [
            [over_beads(cosine), over_beads(drift * damping), over_beads(drift * kicking)],
            [
                over_beads(-frequency * sine),
                over_beads(cosine * damping),
                over_beads(cosine * kicking),
            ],
        ]
    )


def partner_lists(domain_cells):
    lists = []
    for one in range(domain_cells):
        near = []
        for two in range(domain_cells):
            step_y, step_z = two // GZ - one // GZ, two % GZ - one % GZ
            if abs(step_y) <= 1 and abs(step_z) <= 1:
                near.append((two, step_y, step_z))
        later = [entry for entry in near if entry[0] > one]
        lists.append(later + [(two + domain_cells, y, z) for two, y, z in near])
    starts = np.cumsum([0] + [len(entries) for entries in lists]).astype(np.int32)
    return starts, np.array([value for entries in lists for entry in entries for value in entry], np.int32)


def pair_weight(h, radius_sq, terms, longer):
    inverse = pl.reciprocal(h, approx=True)
    if longer:
        quotient = terms[0] * inverse
        sixth = quotient * quotient * quotient
        outer = jnp.maximum(1.0 - radius_sq, 0.0)
        inner = jnp.maximum(1.0 - 4.0 * radius_sq, 0.0)
        switch = outer * outer - inner * inner
        slope = outer - 4.0 * inner
        return sixth * (
            (6.0 * sixth - 3.0) * (switch * inverse) + (2.0 * sixth - 2.0) * slope
        )
    quotient = terms[1] * inverse
    twice = quotient * quotient * quotient
    edge = jnp.maximum(terms[2] * inverse - 1.0, 2.0)
    bracket = edge * (twice - 1.0) - twice
    return (twice * bracket) * ((edge - 2.0) * h)


def weight_factor(longer):
    return 8.0 if longer else 64.0 / 3.0


def columns(block):
    few, lanes = block.shape
    return jnp.concatenate([block, jnp.zeros((8 - few, lanes), F32)], axis=0).T


def spread_rows(position, params, cell, rows_ref, size_ref):
    beads, lanes = position.shape[0], position.shape[-1]
    sizes = columns(params[cell, 0:2, :])
    for kind in range(2):
        size_ref[cell, kind] = jnp.broadcast_to(sizes[:, kind : kind + 1], (lanes, lanes))
    for bead in range(beads):
        block = columns(position[bead, cell])
        for axis in range(3):
            rows_ref[cell, bead, axis] = jnp.broadcast_to(
                block[:, axis : axis + 1], (lanes, lanes)
            )


def meet(longer, cell, first, partners, refs):
    lanes_ref, sizes_ref, rows_ref, size_ref, total_ref, back_ref = refs
    beads, lanes = lanes_ref.shape[0], lanes_ref.shape[-1]
    here = pl.ds(first, SPAN)
    row_half, row_root = size_ref[cell, 0, here, :], size_ref[cell, 1, here, :]
    known = []
    for partner, _, _ in partners:
        half = row_half + sizes_ref[partner, 0:1, :]
        s2 = half * half
        terms = (s2,) if longer else (s2, CUBE_ROOT_TWO * s2, 0.75 + 3.0 * s2)
        known.append((s2, terms, row_root * sizes_ref[partner, 1:2, :]))
    for bead in range(beads):
        rows = [rows_ref[cell, bead, axis, here, :] for axis in range(3)]
        back = [None, None, None]
        for (partner, step_y, step_z), (s2, terms, depth) in zip(partners, known):
            place = lanes_ref[bead, partner]
            apart = [
                place[0:1] - rows[0], (place[1:2] + step_y) - rows[1], (place[2:3] + step_z) - rows[2]
            ]
            radius_sq = apart[0] * apart[0] + apart[1] * apart[1] + apart[2] * apart[2]
            weight = depth * pair_weight(radius_sq + s2, radius_sq, terms, longer)
            for axis in range(3):
                push = weight * apart[axis]
                back[axis] = push if back[axis] is None else back[axis] + push
                if total_ref is not None:
                    total_ref[partner, bead, axis] += jnp.sum(
                        push.reshape(SPAN // 8, 8, lanes), axis=0
                    )
        for axis in range(3):
            if total_ref is None:
                back_ref[cell, bead, axis, here, :] = back[axis]
            else:
                back_ref[cell, bead, axis, here, :] += back[axis]


def fold_back(back_ref, cell, bead):
    lanes = back_ref.shape[-1]
    column = lax.broadcasted_iota(jnp.int32, (lanes, 8), 1)
    sums = [jnp.sum(back_ref[cell, bead, axis], axis=1, keepdims=True) for axis in range(3)]
    block = jnp.where(
        column == 0, sums[0], jnp.where(column == 1, sums[1], jnp.where(column == 2, sums[2], 0.0))
    )
    return block.T[0:3]


def fold_total(total_ref, cell, bead):
    return jnp.concatenate(
        [jnp.sum(total_ref[cell, bead, axis], axis=0, keepdims=True) for axis in range(3)], axis=0
    )


def pairs_kernel(
    longer, parts, starts, partners, occupied, position, params, next_position, next_params,
    force_ref, other_ref, lanes_ref, sizes_ref, rows_ref, size_ref, total_ref, back_ref,
):
    beads, cells, _, lanes = position.shape
    factor = weight_factor(longer)
    together = max(1, 4 // beads)
    axis_row = lax.broadcasted_iota(jnp.int32, (3, lanes), 0)
    layer = jnp.where(axis_row == 0, 1.0, 0.0)
    for bead in range(beads):
        lanes_ref[bead, 0:cells] = position[bead]
        lanes_ref[bead, cells : 2 * cells] = next_position[bead] + layer[None]
    sizes_ref[0:cells] = params[:, 0:2, :]
    sizes_ref[cells : 2 * cells] = next_params[:, 0:2, :]
    total_ref[...] = jnp.zeros_like(total_ref)

    def spread(index, carry):
        for shift in range(together):
            spread_rows(position, params, index * together + shift, rows_ref, size_ref)
        return carry

    lax.fori_loop(0, cells // together, spread, 0)
    refs = (lanes_ref, sizes_ref, rows_ref, size_ref)

    def entry_of(entry):
        return (
            partners[3 * entry],
            partners[3 * entry + 1].astype(F32),
            partners[3 * entry + 2].astype(F32),
        )

    def per_cell(cell, carry):
        begin, end = starts[cell], starts[cell + 1]
        odd = lax.rem(end - begin, 2)

        def per_span(index, carry):
            firsts = [
                pl.multiple_of((index * parts + part) * SPAN, SPAN) for part in range(parts)
            ]
            for first in firsts:
                meet(longer, cell, first, [(cell, 0.0, 0.0)], refs + (None, back_ref))

            def single(entry, carry):
                for first in firsts:
                    meet(longer, cell, first, [entry_of(entry)], refs + (total_ref, back_ref))
                return carry

            def double(step, carry):
                entry = begin + odd + 2 * step
                both = [entry_of(entry), entry_of(entry + 1)]
                for first in firsts:
                    meet(longer, cell, first, both, refs + (total_ref, back_ref))
                return carry

            carry = lax.fori_loop(begin, begin + odd, single, carry)
            return lax.fori_loop(0, lax.div(end - begin, 2), double, carry)

        span = SPAN * parts
        return lax.fori_loop(0, lax.div(occupied[cell] + (span - 1), span), per_span, carry)

    lax.fori_loop(0, cells, per_cell, 0)

    def finish(index, carry):
        for shift in range(together):
            cell = index * together + shift
            alive = params[cell, 1:2, :] > 0.0
            for bead in range(beads):
                total = fold_total(total_ref, cell, bead) - fold_back(back_ref, cell, bead)
                force_ref[bead, cell] = jnp.where(alive, factor * total, 0.0)
                other_ref[bead, cell] = factor * fold_total(total_ref, cell + cells, bead)
        return carry

    lax.fori_loop(0, cells // together, finish, 0)


def call(kernel, inputs, smem, outputs, scratch, flops):
    return pl.pallas_call(
        kernel,
        out_shape=outputs,
        in_specs=[
            pl.BlockSpec(memory_space=pltpu.SMEM if place < smem else pltpu.VMEM)
            for place in range(len(inputs))
        ],
        scratch_shapes=scratch,
        compiler_params=pltpu.CompilerParams(vmem_limit_bytes=VMEM_LIMIT),
        cost_estimate=pl.CostEstimate(flops=flops, bytes_accessed=1 << 18, transcendentals=0),
    )(*inputs)


PAIR_FLOPS = 40 * 128 * 128


def pair_forces(position, params, occupied, next_position, next_params, longer):
    beads, cells, _, lanes = position.shape
    starts, entries = partner_lists(cells)
    forces = jax.ShapeDtypeStruct((beads, cells, 3, lanes), F32)
    return call(
        functools.partial(pairs_kernel, longer, lanes // SPAN if longer else 1),
        (
            jnp.asarray(starts), jnp.asarray(entries), occupied, position, params, next_position,
            next_params,
        ),
        3,
        (forces, forces),
        [
            pltpu.VMEM((beads, 2 * cells, 3, lanes), F32),
            pltpu.VMEM((2 * cells, 2, lanes), F32),
            pltpu.VMEM((cells, beads, 3, lanes, lanes), F32),
            pltpu.VMEM((cells, 2, lanes, lanes), F32),
            pltpu.VMEM((2 * cells, beads, 3, 8, lanes), F32),
            pltpu.VMEM((cells, beads, 3, lanes, lanes), F32),
        ],
        PAIR_FLOPS * beads * (len(entries) // 3 + cells),
    )


def kick_kernel(
    piece_rows, groups, table, rank, position, momenta, noise, force, back, params, partial_ref, piece_ref
):
    beads, cells = position.shape[:2]
    holders = piece_ref.shape[0]
    reduced = table.shape[0]
    first = rank[0] * beads
    if holders * piece_rows > 3 * cells:
        piece_ref[...] = jnp.zeros_like(piece_ref)
    for cell in range(cells):
        mass = params[cell, 2:3, :]
        per_mass = 1.0 / mass
        per_root = lax.rsqrt(mass)
        per_root = per_root * (1.5 - 0.5 * mass * per_root * per_root)
        inputs = []
        for bead in range(beads):
            kicked = momenta[bead, cell] + 0.5 * TIME_STEP * (force[bead, cell] + back[bead, cell])
            inputs.append((position[bead, cell], kicked * per_mass, noise[bead, cell] * per_root))
        for bead in range(beads):
            for kind in range(3):
                base = (kind * beads + bead) * piece_rows
                if piece_rows % 3 == 0:
                    owner, row = divmod(3 * cell, piece_rows)
                    piece_ref[owner, base + row : base + row + 3, :] = inputs[bead][kind]
                else:
                    for axis in range(3):
                        owner, row = divmod(3 * cell + axis, piece_rows)
                        piece_ref[owner, base + row : base + row + 1, :] = inputs[bead][kind][
                            axis : axis + 1
                        ]
        for group in range(reduced):
            total = None
            for bead in range(beads):
                for kind in range(3):
                    term = table[group, kind * holders * beads + first + bead] * inputs[bead][kind]
                    total = term if total is None else total + term
            for copy in range(groups):
                partial_ref[group * groups + copy, 3 * cell : 3 * cell + 3, :] = total


def move_kernel(piece_rows, beads, matrix, arrived, out_ref, gathered):
    holders = arrived.shape[0]
    taken = 3 * beads
    given = 2 * beads
    for row in range(piece_rows):
        for holder in range(holders):
            gathered[row, holder * taken : (holder + 1) * taken, :] = arrived[
                holder, pl.ds(row, taken, stride=piece_rows), :
            ]
        moved = lax.dot_general(
            matrix[...],
            gathered[row],
            (((1,), (0,)), ((), ())),
            precision=lax.Precision.HIGHEST,
            preferred_element_type=F32,
        )
        for holder in range(holders):
            out_ref[holder, row * given : (row + 1) * given, :] = moved[
                holder * given : (holder + 1) * given
            ]


def finish_kernel(piece_rows, groups, table, rank, moved, slow, params, position_ref, momentum_ref):
    beads, cells = position_ref.shape[:2]
    given = 2 * beads
    reduced = table.shape[0]
    first = rank[0] * beads
    for cell in range(cells):
        mass = params[cell, 2:3, :]
        for bead in range(beads):
            def taken(kind):
                if piece_rows % 3 == 0:
                    owner, row = divmod(3 * cell, piece_rows)
                    return moved[owner, pl.ds(row * given + kind * beads + bead, 3, stride=given), :]
                rows = []
                for axis in range(3):
                    owner, row = divmod(3 * cell + axis, piece_rows)
                    place = row * given + kind * beads + bead
                    rows.append(moved[owner, place : place + 1, :])
                return jnp.concatenate(rows, axis=0)

            position_ref[bead, cell] = taken(0)
            total = mass * taken(1)
            for group in range(reduced):
                total = total + table[group, first + bead] * slow[
                    group * groups, 3 * cell : 3 * cell + 3, :
                ]
            momentum_ref[bead, cell] = total


def shards(positions, momenta, noise, atom_types, occupancy, type_sigma, type_eps, type_mass):
    beads, cells, _, lanes = positions.shape
    holders = lax.axis_size("bead")
    domains = lax.axis_size("space")
    rank = lax.axis_index("bead")
    total_beads = beads * holders
    rows = 3 * cells
    piece_rows = -(-rows // holders)
    held = max(1, PC // holders)
    groups = max(1, holders // PC)
    contract = contract_matrix(total_beads, PC)
    steps = step_matrices(total_beads)
    rank_table = rank.astype(jnp.int32).reshape(1)
    one_back = [((i + 1) % domains, i) for i in range(domains)]
    one_on = [(i, (i + 1) % domains) for i in range(domains)]

    codes = jnp.arange(type_sigma.shape[0])
    onehot = atom_types[..., None] == codes
    living = jnp.arange(lanes)[None, :] < occupancy[:, None]
    half_sigma = 0.5 * jnp.sum(jnp.where(onehot, type_sigma, 0.0), -1)
    root_eps = jnp.sqrt(jnp.sum(jnp.where(onehot, type_eps, 0.0), -1))
    mass = jnp.sum(jnp.where(onehot, type_mass, 0.0), -1)
    params = jnp.stack([half_sigma, jnp.where(living, root_eps, 0.0), mass], 1)

    stacked = jnp.concatenate([positions, params[None]], 0)
    next_stacked = lax.ppermute(stacked, "space", one_back)
    next_params = next_stacked[beads]
    force, back = pair_forces(
        positions, params, occupancy, next_stacked[:beads], next_params, False
    )
    back = lax.ppermute(back, "space", one_on)

    position_map = np.concatenate([contract @ steps[0, kind] for kind in range(3)], axis=1)
    partial, pieces = call(
        functools.partial(kick_kernel, piece_rows, groups),
        (
            jnp.asarray(position_map, F32), rank_table, positions, momenta, noise, force, back,
            params,
        ),
        2,
        (
            jax.ShapeDtypeStruct((PC * groups, rows, lanes), F32),
            jax.ShapeDtypeStruct((holders, 3 * beads * piece_rows, lanes), F32),
        ),
        [],
        1 << 22,
    )
    arrived = lax.all_to_all(
        partial.reshape(holders, held * rows, lanes), "bead", split_axis=0, concat_axis=0, tiled=True
    )
    contracted = jnp.sum(arrived, 0).reshape(held, cells, 3, lanes)
    next_contracted = lax.ppermute(contracted, "space", one_back)
    pieces = lax.all_to_all(pieces, "bead", split_axis=0, concat_axis=0, tiled=True)
    slow, slow_back = pair_forces(
        contracted, params, occupancy, next_contracted, next_params, True
    )
    slow = slow + lax.ppermute(slow_back, "space", one_on)

    order = steps.reshape(2, 3, holders, beads, holders, beads).transpose(2, 0, 3, 4, 1, 5)
    order = order.reshape(2 * total_beads, 3 * total_beads)
    moved = call(
        functools.partial(move_kernel, piece_rows, beads),
        (jnp.asarray(order, F32), pieces),
        0,
        jax.ShapeDtypeStruct((holders, 2 * beads * piece_rows, lanes), F32),
        [pltpu.VMEM((piece_rows, 3 * total_beads, lanes), F32)],
        1 << 23,
    )
    moved_rows = 2 * beads * piece_rows
    sent = jnp.concatenate(
        [
            moved,
            jnp.broadcast_to(slow.reshape(1, held * rows, lanes), (holders, held * rows, lanes)),
        ],
        1,
    )
    got = lax.all_to_all(sent, "bead", split_axis=0, concat_axis=0, tiled=True)
    spread = 0.5 * TIME_STEP * (total_beads / PC) * contract
    shape = jax.ShapeDtypeStruct(positions.shape, F32)
    return call(
        functools.partial(finish_kernel, piece_rows, groups),
        (
            jnp.asarray(spread, F32), rank_table, got[:, :moved_rows],
            got[:, moved_rows:].reshape(holders * held, rows, lanes), params,
        ),
        2,
        (shape, shape),
        [],
        1 << 20,
    )


def solution(mesh):
    placed = (
        P("bead", "space", None, None),
        P("bead", "space", None, None),
        P("bead", "space", None, None),
        P("space", None),
        P("space"),
        P(),
        P(),
        P(),
    )
    return jax.shard_map(
        shards,
        mesh=mesh,
        in_specs=placed,
        out_specs=(P("bead", "space", None, None), P("bead", "space", None, None)),
        check_vma=False,
    )
```

```python
import functools

import jax
import jax.numpy as jnp
import numpy as np
from jax import lax
from jax.experimental import pallas as pl
from jax.experimental.pallas import tpu as pltpu
from jax.sharding import PartitionSpec as P

PC = 8
GY = 4
GZ = 4

TIME_STEP = 0.05
INVERSE_TEMP = 32.0
CENTROID_FRICTION = 1.0
INNER_CUT = 0.5
OUTER_CUT = 1.0
CUBE_ROOT_TWO = 2.0 ** (1.0 / 3.0)
F32 = jnp.float32
BF16 = jnp.bfloat16
SPAN = 32
VMEM_LIMIT = 48 * 1024 * 1024


def mode_matrix(number):
    rows = np.arange(number, dtype=np.float64)[:, None]
    column = np.arange(number, dtype=np.float64)[None, :]
    phases = 2.0 * np.pi * rows * column / number
    factor = np.sqrt(2.0 / number)
    middle = np.cos(np.pi * rows) / np.sqrt(number)
    matrix = np.where(column < number / 2, factor * np.cos(phases), factor * np.sin(phases))
    matrix = np.where(column == number / 2, middle, matrix)
    return np.where(column == 0, 1.0 / np.sqrt(number), matrix)


def contract_matrix(full_count, reduced):
    selected = np.arange(reduced)
    selected = np.where(selected <= reduced // 2, selected, selected + full_count - reduced)
    chosen = mode_matrix(full_count)[:, selected]
    return np.sqrt(reduced / full_count) * (mode_matrix(reduced) @ chosen.T)


def step_matrices(number):
    index = np.arange(number, dtype=np.float64)
    frequency = 2.0 * (number / INVERSE_TEMP) * np.sin(np.pi * index / number)
    friction = np.where(index == 0, CENTROID_FRICTION, 2.0 * frequency)
    damping = np.exp(-friction * TIME_STEP)
    kicking = np.sqrt((1.0 - damping * damping) / INVERSE_TEMP)
    cosine = np.cos(frequency * TIME_STEP)
    sine = np.sin(frequency * TIME_STEP)
    drift = np.where(index == 0, TIME_STEP, sine / np.where(index == 0, 1.0, frequency))
    modes = mode_matrix(number)

    def over_beads(diagonal):
        return (modes * diagonal[None, :]) @ modes.T

    return np.array(
        [
            [over_beads(cosine), over_beads(drift * damping), over_beads(drift * kicking)],
            [
                over_beads(-frequency * sine),
                over_beads(cosine * damping),
                over_beads(cosine * kicking),
            ],
        ]
    )


def partner_lists(domain_cells):
    lists = []
    for one in range(domain_cells):
        near = []
        for two in range(domain_cells):
            step_y, step_z = two // GZ - one // GZ, two % GZ - one % GZ
            if abs(step_y) <= 1 and abs(step_z) <= 1:
                near.append((two, step_y, step_z))
        later = [entry for entry in near if entry[0] > one]
        lists.append(later + [(two + domain_cells, y, z) for two, y, z in near])
    starts = np.cumsum([0] + [len(entries) for entries in lists]).astype(np.int32)
    return starts, np.array([value for entries in lists for entry in entries for value in entry], np.int32)


def pair_weight(h, radius_sq, terms, longer):
    inverse = pl.reciprocal(h, approx=True)
    if longer:
        quotient = terms[0] * inverse
        sixth = quotient * quotient * quotient
        outer = jnp.maximum(1.0 - radius_sq, 0.0)
        inner = jnp.maximum(1.0 - 4.0 * radius_sq, 0.0)
        switch = outer * outer - inner * inner
        slope = outer - 4.0 * inner
        return sixth * (
            (6.0 * sixth - 3.0) * (switch * inverse) + (2.0 * sixth - 2.0) * slope
        )
    quotient = terms[1] * inverse
    twice = quotient * quotient * quotient
    edge = jnp.maximum(terms[2] * inverse - 1.0, 2.0)
    bracket = edge * (twice - 1.0) - twice
    return (twice * bracket) * ((edge - 2.0) * h)


def weight_factor(longer):
    return 8.0 if longer else 64.0 / 3.0


def columns(block):
    few, lanes = block.shape
    return jnp.concatenate([block, jnp.zeros((8 - few, lanes), F32)], axis=0).T


def spread_rows(position, params, cell, rows_ref, size_ref):
    beads, lanes = position.shape[0], position.shape[-1]
    sizes = columns(params[cell, 0:2, :])
    for kind in range(2):
        size_ref[cell, kind] = jnp.broadcast_to(sizes[:, kind : kind + 1], (lanes, lanes))
    for bead in range(beads):
        block = columns(position[bead, cell])
        for axis in range(3):
            rows_ref[cell, bead, axis] = jnp.broadcast_to(
                block[:, axis : axis + 1], (lanes, lanes)
            )


def meet(longer, cell, first, partners, refs):
    lanes_ref, sizes_ref, rows_ref, size_ref, total_ref, back_ref = refs
    beads, lanes = lanes_ref.shape[0], lanes_ref.shape[-1]
    here = pl.ds(first, SPAN)
    row_half, row_root = size_ref[cell, 0, here, :], size_ref[cell, 1, here, :]
    known = []
    for partner, _, _ in partners:
        half = row_half + sizes_ref[partner, 0:1, :]
        s2 = half * half
        terms = (s2,) if longer else (s2, CUBE_ROOT_TWO * s2, 0.75 + 3.0 * s2)
        known.append((s2, terms, row_root * sizes_ref[partner, 1:2, :]))
    for bead in range(beads):
        rows = [rows_ref[cell, bead, axis, here, :] for axis in range(3)]
        back = [None, None, None]
        for (partner, step_y, step_z), (s2, terms, depth) in zip(partners, known):
            place = lanes_ref[bead, partner]
            apart = [
                place[0:1] - rows[0], (place[1:2] + step_y) - rows[1], (place[2:3] + step_z) - rows[2]
            ]
            radius_sq = apart[0] * apart[0] + apart[1] * apart[1] + apart[2] * apart[2]
            weight = depth * pair_weight(radius_sq + s2, radius_sq, terms, longer)
            for axis in range(3):
                push = weight * apart[axis]
                back[axis] = push if back[axis] is None else back[axis] + push
                if total_ref is not None:
                    total_ref[partner, bead, axis] += jnp.sum(
                        push.reshape(SPAN // 8, 8, lanes), axis=0
                    )
        for axis in range(3):
            if total_ref is None:
                back_ref[cell, bead, axis, here, :] = back[axis]
            else:
                back_ref[cell, bead, axis, here, :] += back[axis]


def fold_back(back_ref, cell, bead):
    lanes = back_ref.shape[-1]
    column = lax.broadcasted_iota(jnp.int32, (lanes, 8), 1)
    sums = [jnp.sum(back_ref[cell, bead, axis], axis=1, keepdims=True) for axis in range(3)]
    block = jnp.where(
        column == 0, sums[0], jnp.where(column == 1, sums[1], jnp.where(column == 2, sums[2], 0.0))
    )
    return block.T[0:3]


def fold_total(total_ref, cell, bead):
    return jnp.concatenate(
        [jnp.sum(total_ref[cell, bead, axis], axis=0, keepdims=True) for axis in range(3)], axis=0
    )


def pairs_kernel(
    longer, parts, starts, partners, occupied, position, params, next_position, next_params,
    force_ref, other_ref, lanes_ref, sizes_ref, rows_ref, size_ref, total_ref, back_ref,
):
    beads, cells, _, lanes = position.shape
    factor = weight_factor(longer)
    together = max(1, 4 // beads)
    axis_row = lax.broadcasted_iota(jnp.int32, (3, lanes), 0)
    layer = jnp.where(axis_row == 0, 1.0, 0.0)
    for bead in range(beads):
        lanes_ref[bead, 0:cells] = position[bead]
        lanes_ref[bead, cells : 2 * cells] = next_position[bead] + layer[None]
    sizes_ref[0:cells] = params[:, 0:2, :]
    sizes_ref[cells : 2 * cells] = next_params[:, 0:2, :]
    total_ref[...] = jnp.zeros_like(total_ref)

    def spread(index, carry):
        for shift in range(together):
            spread_rows(position, params, index * together + shift, rows_ref, size_ref)
        return carry

    lax.fori_loop(0, cells // together, spread, 0)
    refs = (lanes_ref, sizes_ref, rows_ref, size_ref)

    def entry_of(entry):
        return (
            partners[3 * entry],
            partners[3 * entry + 1].astype(F32),
            partners[3 * entry + 2].astype(F32),
        )

    def per_cell(cell, carry):
        begin, end = starts[cell], starts[cell + 1]
        odd = lax.rem(end - begin, 2)

        def per_span(index, carry):
            firsts = [
                pl.multiple_of((index * parts + part) * SPAN, SPAN) for part in range(parts)
            ]
            for first in firsts:
                meet(longer, cell, first, [(cell, 0.0, 0.0)], refs + (None, back_ref))

            def single(entry, carry):
                for first in firsts:
                    meet(longer, cell, first, [entry_of(entry)], refs + (total_ref, back_ref))
                return carry

            def double(step, carry):
                entry = begin + odd + 2 * step
                both = [entry_of(entry), entry_of(entry + 1)]
                for first in firsts:
                    meet(longer, cell, first, both, refs + (total_ref, back_ref))
                return carry

            carry = lax.fori_loop(begin, begin + odd, single, carry)
            return lax.fori_loop(0, lax.div(end - begin, 2), double, carry)

        span = SPAN * parts
        return lax.fori_loop(0, lax.div(occupied[cell] + (span - 1), span), per_span, carry)

    lax.fori_loop(0, cells, per_cell, 0)

    def finish(index, carry):
        for shift in range(together):
            cell = index * together + shift
            alive = params[cell, 1:2, :] > 0.0
            for bead in range(beads):
                total = fold_total(total_ref, cell, bead) - fold_back(back_ref, cell, bead)
                force_ref[bead, cell] = jnp.where(alive, factor * total, 0.0)
                other_ref[bead, cell] = factor * fold_total(total_ref, cell + cells, bead)
        return carry

    lax.fori_loop(0, cells // together, finish, 0)


def octant_key(x, y, z, alive):
    zed = jnp.where(z >= 0.5, 1.0, 0.0)
    gray = jnp.where(y >= 0.5, 3.0 - zed, zed)
    return jnp.where(alive, jnp.where(x >= 0.5, 7.0 - gray, gray), 8.0)


def reach_lists(domain_cells):
    octants = []
    for bit_x in range(2):
        for bit_y in range(2):
            for bit_z in range(2):
                gray = 3 - bit_z if bit_y else bit_z
                octants.append((7 - gray if bit_x else gray, (bit_x, bit_y, bit_z)))
    brief, wide = [], []
    for one in range(domain_cells):
        entries = []
        for layer in range(2):
            for two in range(domain_cells):
                step = (layer, two // GZ - one // GZ, two % GZ - one % GZ)
                if abs(step[1]) > 1 or abs(step[2]) > 1 or (layer == 0 and two <= one):
                    continue
                keys = [
                    key
                    for key, bits in octants
                    if all(move == 0 or bit == (move > 0) for move, bit in zip(step, bits))
                ]
                entries.append(
                    (two + layer * domain_cells, step[1], step[2], min(keys), max(keys) + 1)
                )
        brief.append([entry for entry in entries if entry[4] - entry[3] == 1])
        wide.append([entry for entry in entries if entry[4] - entry[3] > 1])
    tables = []
    for lists in (brief, wide):
        starts = np.cumsum([0] + [len(entries) for entries in lists]).astype(np.int32)
        tables.append(starts)
        tables.append(
            np.array([value for entries in lists for entry in entries for value in entry], np.int32)
        )
    return tables


def split_three(value):
    high = value.astype(BF16).astype(F32)
    rest = value - high
    middle = rest.astype(BF16).astype(F32)
    return high, middle, rest - middle


def order_kernel(position, params, out_ref):
    beads, cells, _, lanes = position.shape
    row = lax.broadcasted_iota(jnp.int32, (lanes, lanes), 0)
    column = lax.broadcasted_iota(jnp.int32, (lanes, lanes), 1)
    before = jnp.where(row < column, 1.0, 0.0).astype(BF16)
    counter = jnp.concatenate([before, jnp.ones((lanes, lanes), BF16)], axis=0)
    kind = lax.broadcasted_iota(jnp.int32, (16, lanes), 0).astype(F32)
    place_row = row.astype(F32)

    def per_cell(cell, carry):
        sizes = params[cell, 0:2, :]
        for bead in range(beads):
            place = position[bead, cell]
            key = octant_key(place[0:1], place[1:2], place[2:3], sizes[1:2] > 0.0)
            same = jnp.where(key == kind, 1.0, 0.0)
            less = jnp.where(key < kind, 1.0, 0.0)
            counts = lax.dot_general(
                jnp.concatenate([same, less], axis=1).astype(BF16),
                counter,
                (((1,), (0,)), ((), ())),
                preferred_element_type=F32,
            )
            rank = jnp.sum(same * counts, axis=0, keepdims=True)
            chosen = jnp.where(rank == place_row, 1.0, 0.0).astype(BF16)
            block = jnp.concatenate([place, sizes, jnp.zeros((3, lanes), F32)], axis=0)
            moved = lax.dot_general(
                jnp.concatenate(split_three(block), axis=0).astype(BF16),
                chosen,
                (((1,), (1,)), ((), ())),
                preferred_element_type=F32,
            )
            out_ref[bead, cell, 0:5, :] = (moved[0:8] + moved[8:16] + moved[16:24])[0:5]
            out_ref[bead, cell, 5:6, :] = rank
            out_ref[bead, cell, 6:8, :] = jnp.zeros((2, lanes), F32)
        return carry

    lax.fori_loop(0, cells, per_cell, 0)


def meet_run(span, firsts, partner, step_y, step_z, lanes_ref, sizes_ref, rows_ref, total_ref, back_ref):
    beads, lanes = lanes_ref.shape[0], lanes_ref.shape[-1]
    lane_half, lane_root = sizes_ref[partner, 0:1, :], sizes_ref[partner, 1:2, :]
    for bead in range(beads):
        here = pl.ds(firsts[bead], span)
        half = rows_ref[bead, 3, here, :] + lane_half
        s2 = half * half
        terms = (s2, CUBE_ROOT_TWO * s2, 0.75 + 3.0 * s2)
        place = lanes_ref[bead, partner]
        apart = [
            place[0:1] - rows_ref[bead, 0, here, :],
            (place[1:2] + step_y) - rows_ref[bead, 1, here, :],
            (place[2:3] + step_z) - rows_ref[bead, 2, here, :],
        ]
        radius_sq = apart[0] * apart[0] + apart[1] * apart[1] + apart[2] * apart[2]
        depth = rows_ref[bead, 4, here, :] * lane_root
        weight = depth * pair_weight(radius_sq + s2, radius_sq, terms, False)
        for axis in range(3):
            push = weight * apart[axis]
            if total_ref is None:
                back_ref[bead, axis, here, :] = push
            else:
                back_ref[bead, axis, here, :] += push
                total_ref[partner, bead, axis] += jnp.sum(
                    push.reshape(span // 8, 8, lanes), axis=0
                )


def reach_kernel(
    brief_starts, brief, wide_starts, wide, bounds, position, params, next_position, next_params,
    ordered, force_ref, other_ref, lanes_ref, sizes_ref, rows_ref, total_ref, back_ref,
):
    beads, cells, _, lanes = position.shape
    factor = weight_factor(False)
    axis_row = lax.broadcasted_iota(jnp.int32, (3, lanes), 0)
    layer = jnp.where(axis_row == 0, 1.0, 0.0)
    for bead in range(beads):
        lanes_ref[bead, 0:cells] = position[bead]
        lanes_ref[bead, cells : 2 * cells] = next_position[bead] + layer[None]
    sizes_ref[0:cells] = params[:, 0:2, :]
    sizes_ref[cells : 2 * cells] = next_params[:, 0:2, :]
    total_ref[...] = jnp.zeros_like(total_ref)
    rows_ref[:, :, lanes:, :] = jnp.zeros((beads, 5, SPAN, lanes), F32)
    row = lax.broadcasted_iota(jnp.int32, (lanes, lanes), 0).astype(F32)
    slot = lax.broadcasted_iota(jnp.int32, (8, lanes), 1)
    refs = (lanes_ref, sizes_ref, rows_ref)

    def per_cell(cell, carry):
        for bead in range(beads):
            block = ordered[bead, cell].T
            for axis in range(5):
                rows_ref[bead, axis, 0:lanes, :] = jnp.broadcast_to(
                    block[:, axis : axis + 1], (lanes, lanes)
                )

        def bound(bead, octant):
            return bounds[(bead * cells + cell) * 9 + octant]

        alive = bound(0, 8)

        def itself(index, carry):
            first = pl.multiple_of(index * SPAN, SPAN)
            meet_run(SPAN, [first] * beads, cell, 0.0, 0.0, *refs, None, back_ref)
            return carry

        lax.fori_loop(0, lax.div(alive + (SPAN - 1), SPAN), itself, 0)

        for span, starts, table in ((SPAN // 2, brief_starts, brief), (SPAN, wide_starts, wide)):

            def per_entry(entry, carry):
                partner = table[5 * entry]
                step_y = table[5 * entry + 1].astype(F32)
                step_z = table[5 * entry + 2].astype(F32)
                begins = [bound(bead, table[5 * entry + 3]) for bead in range(beads)]
                longest = bound(0, table[5 * entry + 4]) - begins[0]
                for bead in range(1, beads):
                    longest = jnp.maximum(
                        longest, bound(bead, table[5 * entry + 4]) - begins[bead]
                    )

                def per_span(index, carry):
                    firsts = [jnp.minimum(begin + index * span, lanes) for begin in begins]
                    meet_run(span, firsts, partner, step_y, step_z, *refs, total_ref, back_ref)
                    return carry

                return lax.fori_loop(0, lax.div(longest + (span - 1), span), per_span, carry)

            lax.fori_loop(starts[cell], starts[cell + 1], per_entry, 0)

        column = lax.broadcasted_iota(jnp.int32, (lanes, 8), 1)
        for bead in range(beads):
            sums = [
                jnp.sum(back_ref[bead, axis, 0:lanes, :], axis=1, keepdims=True)
                for axis in range(3)
            ]
            block = jnp.where(
                column == 0,
                sums[0],
                jnp.where(column == 1, sums[1], jnp.where(column == 2, sums[2], 0.0)),
            ).T
            block = jnp.where(slot < alive, block, 0.0)
            chosen = jnp.where(ordered[bead, cell, 5:6, :] == row, 1.0, 0.0).astype(BF16)
            moved = lax.dot_general(
                jnp.concatenate(split_three(block), axis=0).astype(BF16),
                chosen,
                (((1,), (0,)), ((), ())),
                preferred_element_type=F32,
            )
            force_ref[bead, cell] = (moved[0:8] + moved[8:16] + moved[16:24])[0:3]
        return carry

    lax.fori_loop(0, cells, per_cell, 0)

    def finish(cell, carry):
        for bead in range(beads):
            total = fold_total(total_ref, cell, bead) - force_ref[bead, cell]
            force_ref[bead, cell] = factor * total
            other_ref[bead, cell] = factor * fold_total(total_ref, cell + cells, bead)
        return carry

    lax.fori_loop(0, cells, finish, 0)


def short_forces(position, params, next_position, next_params, ordered, bounds):
    beads, cells, _, lanes = position.shape
    tables = [jnp.asarray(table) for table in reach_lists(cells)]
    forces = jax.ShapeDtypeStruct((beads, cells, 3, lanes), F32)
    return call(
        reach_kernel,
        (*tables, bounds, position, params, next_position, next_params, ordered),
        5,
        (forces, forces),
        [
            pltpu.VMEM((beads, 2 * cells, 3, lanes), F32),
            pltpu.VMEM((2 * cells, 2, lanes), F32),
            pltpu.VMEM((beads, 5, lanes + SPAN, lanes), F32),
            pltpu.VMEM((2 * cells, beads, 3, 8, lanes), F32),
            pltpu.VMEM((beads, 3, lanes + SPAN, lanes), F32),
        ],
        PAIR_FLOPS * beads * 70,
    )


def call(kernel, inputs, smem, outputs, scratch, flops):
    return pl.pallas_call(
        kernel,
        out_shape=outputs,
        in_specs=[
            pl.BlockSpec(memory_space=pltpu.SMEM if place < smem else pltpu.VMEM)
            for place in range(len(inputs))
        ],
        scratch_shapes=scratch,
        compiler_params=pltpu.CompilerParams(vmem_limit_bytes=VMEM_LIMIT),
        cost_estimate=pl.CostEstimate(flops=flops, bytes_accessed=1 << 18, transcendentals=0),
    )(*inputs)


PAIR_FLOPS = 40 * 128 * 128


def pair_forces(position, params, occupied, next_position, next_params, longer):
    beads, cells, _, lanes = position.shape
    starts, entries = partner_lists(cells)
    forces = jax.ShapeDtypeStruct((beads, cells, 3, lanes), F32)
    return call(
        functools.partial(pairs_kernel, longer, lanes // SPAN if longer else 1),
        (
            jnp.asarray(starts), jnp.asarray(entries), occupied, position, params, next_position,
            next_params,
        ),
        3,
        (forces, forces),
        [
            pltpu.VMEM((beads, 2 * cells, 3, lanes), F32),
            pltpu.VMEM((2 * cells, 2, lanes), F32),
            pltpu.VMEM((cells, beads, 3, lanes, lanes), F32),
            pltpu.VMEM((cells, 2, lanes, lanes), F32),
            pltpu.VMEM((2 * cells, beads, 3, 8, lanes), F32),
            pltpu.VMEM((cells, beads, 3, lanes, lanes), F32),
        ],
        PAIR_FLOPS * beads * (len(entries) // 3 + cells),
    )


def kick_kernel(
    piece_rows, groups, table, rank, position, momenta, noise, force, back, params, partial_ref, piece_ref
):
    beads, cells = position.shape[:2]
    holders = piece_ref.shape[0]
    reduced = table.shape[0]
    first = rank[0] * beads
    if holders * piece_rows > 3 * cells:
        piece_ref[...] = jnp.zeros_like(piece_ref)
    for cell in range(cells):
        mass = params[cell, 2:3, :]
        per_mass = 1.0 / mass
        per_root = lax.rsqrt(mass)
        per_root = per_root * (1.5 - 0.5 * mass * per_root * per_root)
        inputs = []
        for bead in range(beads):
            kicked = momenta[bead, cell] + 0.5 * TIME_STEP * (force[bead, cell] + back[bead, cell])
            inputs.append((position[bead, cell], kicked * per_mass, noise[bead, cell] * per_root))
        for bead in range(beads):
            for kind in range(3):
                base = (kind * beads + bead) * piece_rows
                if piece_rows % 3 == 0:
                    owner, row = divmod(3 * cell, piece_rows)
                    piece_ref[owner, base + row : base + row + 3, :] = inputs[bead][kind]
                else:
                    for axis in range(3):
                        owner, row = divmod(3 * cell + axis, piece_rows)
                        piece_ref[owner, base + row : base + row + 1, :] = inputs[bead][kind][
                            axis : axis + 1
                        ]
        for group in range(reduced):
            total = None
            for bead in range(beads):
                for kind in range(3):
                    term = table[group, kind * holders * beads + first + bead] * inputs[bead][kind]
                    total = term if total is None else total + term
            for copy in range(groups):
                partial_ref[group * groups + copy, 3 * cell : 3 * cell + 3, :] = total


def move_kernel(piece_rows, beads, matrix, arrived, out_ref, gathered):
    holders = arrived.shape[0]
    taken = 3 * beads
    given = 2 * beads
    for row in range(piece_rows):
        for holder in range(holders):
            gathered[row, holder * taken : (holder + 1) * taken, :] = arrived[
                holder, pl.ds(row, taken, stride=piece_rows), :
            ]
        moved = lax.dot_general(
            matrix[...],
            gathered[row],
            (((1,), (0,)), ((), ())),
            precision=lax.Precision.HIGHEST,
            preferred_element_type=F32,
        )
        for holder in range(holders):
            out_ref[holder, row * given : (row + 1) * given, :] = moved[
                holder * given : (holder + 1) * given
            ]


def finish_kernel(piece_rows, groups, table, rank, moved, slow, params, position_ref, momentum_ref):
    beads, cells = position_ref.shape[:2]
    given = 2 * beads
    reduced = table.shape[0]
    first = rank[0] * beads
    for cell in range(cells):
        mass = params[cell, 2:3, :]
        for bead in range(beads):
            def taken(kind):
                if piece_rows % 3 == 0:
                    owner, row = divmod(3 * cell, piece_rows)
                    return moved[owner, pl.ds(row * given + kind * beads + bead, 3, stride=given), :]
                rows = []
                for axis in range(3):
                    owner, row = divmod(3 * cell + axis, piece_rows)
                    place = row * given + kind * beads + bead
                    rows.append(moved[owner, place : place + 1, :])
                return jnp.concatenate(rows, axis=0)

            position_ref[bead, cell] = taken(0)
            total = mass * taken(1)
            for group in range(reduced):
                total = total + table[group, first + bead] * slow[
                    group * groups, 3 * cell : 3 * cell + 3, :
                ]
            momentum_ref[bead, cell] = total


def shards(positions, momenta, noise, atom_types, occupancy, type_sigma, type_eps, type_mass):
    beads, cells, _, lanes = positions.shape
    holders = lax.axis_size("bead")
    domains = lax.axis_size("space")
    rank = lax.axis_index("bead")
    total_beads = beads * holders
    rows = 3 * cells
    piece_rows = -(-rows // holders)
    held = max(1, PC // holders)
    groups = max(1, holders // PC)
    contract = contract_matrix(total_beads, PC)
    steps = step_matrices(total_beads)
    rank_table = rank.astype(jnp.int32).reshape(1)
    one_back = [((i + 1) % domains, i) for i in range(domains)]
    one_on = [(i, (i + 1) % domains) for i in range(domains)]

    codes = jnp.arange(type_sigma.shape[0])
    onehot = atom_types[..., None] == codes
    living = jnp.arange(lanes)[None, :] < occupancy[:, None]
    half_sigma = 0.5 * jnp.sum(jnp.where(onehot, type_sigma, 0.0), -1)
    root_eps = jnp.sqrt(jnp.sum(jnp.where(onehot, type_eps, 0.0), -1))
    mass = jnp.sum(jnp.where(onehot, type_mass, 0.0), -1)
    params = jnp.stack([half_sigma, jnp.where(living, root_eps, 0.0), mass], 1)

    stacked = jnp.concatenate([positions, params[None]], 0)
    next_stacked = lax.ppermute(stacked, "space", one_back)
    next_params = next_stacked[beads]
    ordered = call(
        order_kernel,
        (positions, params),
        0,
        jax.ShapeDtypeStruct((beads, cells, 8, lanes), F32),
        [],
        1 << 22,
    )
    key = octant_key(positions[:, :, 0], positions[:, :, 1], positions[:, :, 2], living[None])
    bounds = jnp.sum(
        (key[:, :, None, :] < jnp.arange(9, dtype=F32)[:, None]).astype(jnp.int32), -1
    )
    force, back = short_forces(
        positions, params, next_stacked[:beads], next_params, ordered, bounds.reshape(-1)
    )
    back = lax.ppermute(back, "space", one_on)

    position_map = np.concatenate([contract @ steps[0, kind] for kind in range(3)], axis=1)
    partial, pieces = call(
        functools.partial(kick_kernel, piece_rows, groups),
        (
            jnp.asarray(position_map, F32), rank_table, positions, momenta, noise, force, back,
            params,
        ),
        2,
        (
            jax.ShapeDtypeStruct((PC * groups, rows, lanes), F32),
            jax.ShapeDtypeStruct((holders, 3 * beads * piece_rows, lanes), F32),
        ),
        [],
        1 << 22,
    )
    arrived = lax.all_to_all(
        partial.reshape(holders, held * rows, lanes), "bead", split_axis=0, concat_axis=0, tiled=True
    )
    contracted = jnp.sum(arrived, 0).reshape(held, cells, 3, lanes)
    next_contracted = lax.ppermute(contracted, "space", one_back)
    pieces = lax.all_to_all(pieces, "bead", split_axis=0, concat_axis=0, tiled=True)
    slow, slow_back = pair_forces(
        contracted, params, occupancy, next_contracted, next_params, True
    )
    slow = slow + lax.ppermute(slow_back, "space", one_on)

    order = steps.reshape(2, 3, holders, beads, holders, beads).transpose(2, 0, 3, 4, 1, 5)
    order = order.reshape(2 * total_beads, 3 * total_beads)
    moved = call(
        functools.partial(move_kernel, piece_rows, beads),
        (jnp.asarray(order, F32), pieces),
        0,
        jax.ShapeDtypeStruct((holders, 2 * beads * piece_rows, lanes), F32),
        [pltpu.VMEM((piece_rows, 3 * total_beads, lanes), F32)],
        1 << 23,
    )
    moved_rows = 2 * beads * piece_rows
    sent = jnp.concatenate(
        [
            moved,
            jnp.broadcast_to(slow.reshape(1, held * rows, lanes), (holders, held * rows, lanes)),
        ],
        1,
    )
    got = lax.all_to_all(sent, "bead", split_axis=0, concat_axis=0, tiled=True)
    spread = 0.5 * TIME_STEP * (total_beads / PC) * contract
    shape = jax.ShapeDtypeStruct(positions.shape, F32)
    return call(
        functools.partial(finish_kernel, piece_rows, groups),
        (
            jnp.asarray(spread, F32), rank_table, got[:, :moved_rows],
            got[:, moved_rows:].reshape(holders * held, rows, lanes), params,
        ),
        2,
        (shape, shape),
        [],
        1 << 20,
    )


def solution(mesh):
    placed = (
        P("bead", "space", None, None),
        P("bead", "space", None, None),
        P("bead", "space", None, None),
        P("space", None),
        P("space"),
        P(),
        P(),
        P(),
    )
    return jax.shard_map(
        shards,
        mesh=mesh,
        in_specs=placed,
        out_specs=(P("bead", "space", None, None), P("bead", "space", None, None)),
        check_vma=False,
    )
```

```python
import functools

import jax
import jax.numpy as jnp
import numpy as np
from jax import lax
from jax.experimental import pallas as pl
from jax.experimental.pallas import tpu as pltpu
from jax.sharding import PartitionSpec as P

PC = 8
GY = 4
GZ = 4

TIME_STEP = 0.05
INVERSE_TEMP = 32.0
CENTROID_FRICTION = 1.0
INNER_CUT = 0.5
OUTER_CUT = 1.0
CUBE_ROOT_TWO = 2.0 ** (1.0 / 3.0)
F32 = jnp.float32
BF16 = jnp.bfloat16
ORDER_CELLS = 2
GROUP = 4
SPAN = 32
RUN_SPANS = (SPAN // 2, SPAN, 2 * SPAN)
VMEM_LIMIT = 48 * 1024 * 1024


def mode_matrix(number):
    rows = np.arange(number, dtype=np.float64)[:, None]
    column = np.arange(number, dtype=np.float64)[None, :]
    phases = 2.0 * np.pi * rows * column / number
    factor = np.sqrt(2.0 / number)
    middle = np.cos(np.pi * rows) / np.sqrt(number)
    matrix = np.where(column < number / 2, factor * np.cos(phases), factor * np.sin(phases))
    matrix = np.where(column == number / 2, middle, matrix)
    return np.where(column == 0, 1.0 / np.sqrt(number), matrix)


def contract_matrix(full_count, reduced):
    selected = np.arange(reduced)
    selected = np.where(selected <= reduced // 2, selected, selected + full_count - reduced)
    chosen = mode_matrix(full_count)[:, selected]
    return np.sqrt(reduced / full_count) * (mode_matrix(reduced) @ chosen.T)


def step_matrices(number):
    index = np.arange(number, dtype=np.float64)
    frequency = 2.0 * (number / INVERSE_TEMP) * np.sin(np.pi * index / number)
    friction = np.where(index == 0, CENTROID_FRICTION, 2.0 * frequency)
    damping = np.exp(-friction * TIME_STEP)
    kicking = np.sqrt((1.0 - damping * damping) / INVERSE_TEMP)
    cosine = np.cos(frequency * TIME_STEP)
    sine = np.sin(frequency * TIME_STEP)
    drift = np.where(index == 0, TIME_STEP, sine / np.where(index == 0, 1.0, frequency))
    modes = mode_matrix(number)

    def over_beads(diagonal):
        return (modes * diagonal[None, :]) @ modes.T

    return np.array(
        [
            [over_beads(cosine), over_beads(drift * damping), over_beads(drift * kicking)],
            [
                over_beads(-frequency * sine),
                over_beads(cosine * damping),
                over_beads(cosine * kicking),
            ],
        ]
    )


def partner_lists(domain_cells):
    lists = []
    for one in range(domain_cells):
        near = []
        for two in range(domain_cells):
            step_y, step_z = two // GZ - one // GZ, two % GZ - one % GZ
            if abs(step_y) <= 1 and abs(step_z) <= 1:
                near.append((two, step_y, step_z))
        later = [entry for entry in near if entry[0] > one]
        lists.append(later + [(two + domain_cells, y, z) for two, y, z in near])
    starts = np.cumsum([0] + [len(entries) for entries in lists]).astype(np.int32)
    return starts, np.array([value for entries in lists for entry in entries for value in entry], np.int32)


def pair_weight(h, radius_sq, terms, longer):
    inverse = pl.reciprocal(h, approx=True)
    if longer:
        quotient = terms[1] * inverse
        twice = quotient * quotient * quotient
        outer = jnp.maximum(1.0 - radius_sq, 0.0)
        inner = jnp.maximum(1.0 - 4.0 * radius_sq, 0.0)
        switch = outer * outer - inner * inner
        slope = outer - 4.0 * inner
        return twice * ((twice - 1.0) * (3.0 * (switch * inverse) + slope) - slope)
    quotient = terms[1] * inverse
    twice = quotient * quotient * quotient
    edge = jnp.maximum(terms[2] * inverse - 1.0, 2.0)
    bracket = edge * (twice - 1.0) - twice
    return (twice * bracket) * ((edge - 2.0) * h)


def weight_factor(longer):
    return 4.0 if longer else 64.0 / 3.0


def columns(block):
    few, lanes = block.shape
    return jnp.concatenate([block, jnp.zeros((8 - few, lanes), F32)], axis=0).T


def spread_rows(position, params, cell, rows_ref, size_ref):
    beads, lanes = position.shape[0], position.shape[-1]
    sizes = columns(params[cell, 0:2, :])
    for kind in range(2):
        size_ref[cell, kind] = jnp.broadcast_to(sizes[:, kind : kind + 1], (lanes, lanes))
    for bead in range(beads):
        block = columns(position[bead, cell])
        for axis in range(3):
            rows_ref[cell, bead, axis] = jnp.broadcast_to(
                block[:, axis : axis + 1], (lanes, lanes)
            )


def meet(longer, cell, first, partners, refs):
    lanes_ref, sizes_ref, rows_ref, size_ref, total_ref, back_ref = refs
    beads, lanes = lanes_ref.shape[0], lanes_ref.shape[-1]
    here = pl.ds(first, SPAN)
    row_half, row_root = size_ref[cell, 0, here, :], size_ref[cell, 1, here, :]
    known = []
    for partner, _, _ in partners:
        half = row_half + sizes_ref[partner, 0:1, :]
        s2 = half * half
        terms = (s2, CUBE_ROOT_TWO * s2, None if longer else 0.75 + 3.0 * s2)
        known.append((s2, terms, row_root * sizes_ref[partner, 1:2, :]))
    for bead in range(beads):
        rows = [rows_ref[cell, bead, axis, here, :] for axis in range(3)]
        back = [None, None, None]
        for (partner, step_y, step_z), (s2, terms, depth) in zip(partners, known):
            place = lanes_ref[bead, partner]
            apart = [
                place[0:1] - rows[0], (place[1:2] + step_y) - rows[1], (place[2:3] + step_z) - rows[2]
            ]
            radius_sq = apart[0] * apart[0] + apart[1] * apart[1] + apart[2] * apart[2]
            weight = depth * pair_weight(radius_sq + s2, radius_sq, terms, longer)
            for axis in range(3):
                push = weight * apart[axis]
                back[axis] = push if back[axis] is None else back[axis] + push
                if total_ref is not None:
                    total_ref[partner, bead, axis] += jnp.sum(
                        push.reshape(SPAN // 8, 8, lanes), axis=0
                    )
        for axis in range(3):
            if total_ref is None:
                back_ref[cell, bead, axis, here, :] = back[axis]
            else:
                back_ref[cell, bead, axis, here, :] += back[axis]


def fold_back(back_ref, cell, bead):
    lanes = back_ref.shape[-1]
    column = lax.broadcasted_iota(jnp.int32, (lanes, 8), 1)
    sums = [jnp.sum(back_ref[cell, bead, axis], axis=1, keepdims=True) for axis in range(3)]
    block = jnp.where(
        column == 0, sums[0], jnp.where(column == 1, sums[1], jnp.where(column == 2, sums[2], 0.0))
    )
    return block.T[0:3]


def fold_total(total_ref, cell, bead):
    return jnp.concatenate(
        [jnp.sum(total_ref[cell, bead, axis], axis=0, keepdims=True) for axis in range(3)], axis=0
    )


def pairs_kernel(
    longer, parts, starts, partners, occupied, position, params, next_position, next_params,
    force_ref, other_ref, lanes_ref, sizes_ref, rows_ref, size_ref, total_ref, back_ref,
):
    beads, cells, _, lanes = position.shape
    factor = weight_factor(longer)
    together = max(1, 4 // beads)
    axis_row = lax.broadcasted_iota(jnp.int32, (3, lanes), 0)
    layer = jnp.where(axis_row == 0, 1.0, 0.0)
    for bead in range(beads):
        lanes_ref[bead, 0:cells] = position[bead]
        lanes_ref[bead, cells : 2 * cells] = next_position[bead] + layer[None]
    sizes_ref[0:cells] = params[:, 0:2, :]
    sizes_ref[cells : 2 * cells] = next_params[:, 0:2, :]
    total_ref[...] = jnp.zeros_like(total_ref)

    def spread(index, carry):
        for shift in range(together):
            spread_rows(position, params, index * together + shift, rows_ref, size_ref)
        return carry

    lax.fori_loop(0, cells // together, spread, 0)
    refs = (lanes_ref, sizes_ref, rows_ref, size_ref)

    def entry_of(entry):
        return (
            partners[3 * entry],
            partners[3 * entry + 1].astype(F32),
            partners[3 * entry + 2].astype(F32),
        )

    def per_cell(cell, carry):
        begin, end = starts[cell], starts[cell + 1]
        odd = lax.rem(end - begin, 2)

        def per_span(index, carry):
            firsts = [
                pl.multiple_of((index * parts + part) * SPAN, SPAN) for part in range(parts)
            ]
            for first in firsts:
                meet(longer, cell, first, [(cell, 0.0, 0.0)], refs + (None, back_ref))

            def single(entry, carry):
                for first in firsts:
                    meet(longer, cell, first, [entry_of(entry)], refs + (total_ref, back_ref))
                return carry

            def double(step, carry):
                entry = begin + odd + 2 * step
                both = [entry_of(entry), entry_of(entry + 1)]
                for first in firsts:
                    meet(longer, cell, first, both, refs + (total_ref, back_ref))
                return carry

            carry = lax.fori_loop(begin, begin + odd, single, carry)
            return lax.fori_loop(0, lax.div(end - begin, 2), double, carry)

        span = SPAN * parts
        return lax.fori_loop(0, lax.div(occupied[cell] + (span - 1), span), per_span, carry)

    lax.fori_loop(0, cells, per_cell, 0)

    def finish(index, carry):
        for shift in range(together):
            cell = index * together + shift
            alive = params[cell, 1:2, :] > 0.0
            for bead in range(beads):
                total = fold_total(total_ref, cell, bead) - fold_back(back_ref, cell, bead)
                force_ref[bead, cell] = jnp.where(alive, factor * total, 0.0)
                other_ref[bead, cell] = factor * fold_total(total_ref, cell + cells, bead)
        return carry

    lax.fori_loop(0, cells // together, finish, 0)


def octant_key(x, y, z, alive):
    zed = jnp.where(z >= 0.5, 1.0, 0.0)
    gray = jnp.where(y >= 0.5, 3.0 - zed, zed)
    return jnp.where(alive, jnp.where(x >= 0.5, 7.0 - gray, gray), 8.0)


def reach_lists(domain_cells):
    octants = []
    for bit_x in range(2):
        for bit_y in range(2):
            for bit_z in range(2):
                gray = 3 - bit_z if bit_y else bit_z
                octants.append((7 - gray if bit_x else gray, (bit_x, bit_y, bit_z)))
    classes = {span: [[] for _ in range(domain_cells)] for span in RUN_SPANS}
    for one in range(domain_cells):
        for layer in range(2):
            for two in range(domain_cells):
                step = (layer, two // GZ - one // GZ, two % GZ - one % GZ)
                if abs(step[1]) > 1 or abs(step[2]) > 1 or (layer == 0 and two <= one):
                    continue
                keys = [
                    key
                    for key, bits in octants
                    if all(move == 0 or bit == (move > 0) for move, bit in zip(step, bits))
                ]
                length = max(keys) + 1 - min(keys)
                span = {1: SPAN // 2, 4: 2 * SPAN}.get(length, SPAN)
                classes[span][one].append(
                    (two + layer * domain_cells, step[1], step[2], min(keys), max(keys) + 1)
                )
    tables = []
    for span in RUN_SPANS:
        lists = classes[span]
        starts = np.cumsum([0] + [len(entries) for entries in lists]).astype(np.int32)
        tables.append(starts)
        tables.append(
            np.array([value for entries in lists for entry in entries for value in entry], np.int32)
        )
    return tables


def split_three(value):
    high = value.astype(BF16).astype(F32)
    rest = value - high
    middle = rest.astype(BF16).astype(F32)
    return high, middle, rest - middle


def order_kernel(position, params, column_ref, rank_ref):
    beads, cells, _, lanes = position.shape
    row = lax.broadcasted_iota(jnp.int32, (lanes, lanes), 0)
    column = lax.broadcasted_iota(jnp.int32, (lanes, lanes), 1)
    before = jnp.where(row < column, 1.0, 0.0).astype(BF16)
    counter = jnp.concatenate([before, jnp.ones((lanes, lanes), BF16)], axis=0)
    kind = lax.broadcasted_iota(jnp.int32, (16, lanes), 0).astype(F32)
    place_row = row.astype(F32)

    def per_cell(index, carry):
        for shift in range(ORDER_CELLS):
            cell = index * ORDER_CELLS + shift
            sizes = params[cell, 0:2, :]
            for bead in range(beads):
                place = position[bead, cell]
                key = octant_key(place[0:1], place[1:2], place[2:3], sizes[1:2] > 0.0)
                same = jnp.where(key == kind, 1.0, 0.0)
                less = jnp.where(key < kind, 1.0, 0.0)
                counts = lax.dot_general(
                    jnp.concatenate([same, less], axis=1).astype(BF16),
                    counter,
                    (((1,), (0,)), ((), ())),
                    preferred_element_type=F32,
                )
                rank = jnp.sum(same * counts, axis=0, keepdims=True)
                chosen = jnp.where(rank == place_row, 1.0, 0.0).astype(BF16)
                block = jnp.concatenate([place, sizes, jnp.zeros((3, lanes), F32)], axis=0)
                splits = jnp.concatenate(split_three(block), axis=0).astype(BF16)
                column_ref[bead, cell] = lax.dot_general(
                    chosen, splits, (((1,), (1,)), ((), ())), preferred_element_type=F32
                ).astype(BF16)
                rank_ref[bead, cell] = rank
        return carry

    lax.fori_loop(0, cells // ORDER_CELLS, per_cell, 0)


def meet_run(span, local, firsts, partner, step_y, step_z, lanes_ref, sizes_ref, rows_ref, total_ref, back_ref):
    beads, lanes = lanes_ref.shape[0], lanes_ref.shape[-1]
    lane_half, lane_root = sizes_ref[partner, 0:1, :], sizes_ref[partner, 1:2, :]
    part = min(span, SPAN)
    for start in range(0, span, part):
        for bead in range(beads):
            here = pl.ds(firsts[bead] + start, part)
            half = rows_ref[local, bead, 3, here, :] + lane_half
            s2 = half * half
            terms = (s2, CUBE_ROOT_TWO * s2, 0.75 + 3.0 * s2)
            place = lanes_ref[bead, partner]
            apart = [
                place[0:1] - rows_ref[local, bead, 0, here, :],
                (place[1:2] + step_y) - rows_ref[local, bead, 1, here, :],
                (place[2:3] + step_z) - rows_ref[local, bead, 2, here, :],
            ]
            radius_sq = apart[0] * apart[0] + apart[1] * apart[1] + apart[2] * apart[2]
            depth = rows_ref[local, bead, 4, here, :] * lane_root
            weight = depth * pair_weight(radius_sq + s2, radius_sq, terms, False)
            for axis in range(3):
                push = weight * apart[axis]
                if total_ref is None:
                    back_ref[local, bead, axis, here, :] = push
                else:
                    back_ref[local, bead, axis, here, :] += push
                    total_ref[partner, bead, axis] += jnp.sum(
                        push.reshape(part // 8, 8, lanes), axis=0
                    )


def reach_kernel(*refs):
    runs = [refs[2 * place : 2 * place + 2] for place in range(len(RUN_SPANS))]
    (
        bounds, position, params, next_position, next_params, ordered, ranks, force_ref,
        other_ref, lanes_ref, sizes_ref, rows_ref, total_ref, back_ref,
    ) = refs[2 * len(RUN_SPANS) :]
    beads, cells, _, lanes = position.shape
    factor = weight_factor(False)
    axis_row = lax.broadcasted_iota(jnp.int32, (3, lanes), 0)
    layer = jnp.where(axis_row == 0, 1.0, 0.0)
    for bead in range(beads):
        lanes_ref[bead, 0:cells] = position[bead]
        lanes_ref[bead, cells : 2 * cells] = next_position[bead] + layer[None]
    sizes_ref[0:cells] = params[:, 0:2, :]
    sizes_ref[cells : 2 * cells] = next_params[:, 0:2, :]
    total_ref[...] = jnp.zeros_like(total_ref)
    spare = rows_ref.shape[3] - lanes
    rows_ref[:, :, :, lanes:, :] = jnp.zeros((GROUP, beads, 5, spare, lanes), F32)
    row = lax.broadcasted_iota(jnp.int32, (lanes, lanes), 0).astype(F32)
    slot = lax.broadcasted_iota(jnp.int32, (8, lanes), 1)
    split_row = lax.broadcasted_iota(jnp.int32, (8, 5 * lanes), 0)
    wide_column = lax.broadcasted_iota(jnp.int32, (8, 5 * lanes), 1)
    taken = jnp.where(
        (wide_column >= split_row * lanes) & (wide_column < (split_row + 1) * lanes), 1.0, 0.0
    )
    selector = jnp.concatenate([taken, taken, taken], axis=0).astype(BF16)
    fold_column = lax.broadcasted_iota(jnp.int32, (2 * lanes, 8), 1)
    folders = [jnp.where(fold_column == axis, 1.0, 0.0).astype(BF16) for axis in range(3)]

    def per_group(group, carry):
        for local in range(GROUP):
            for bead in range(beads):
                wide = jnp.dot(
                    ordered[bead, group * GROUP + local], selector, preferred_element_type=F32
                )
                for axis in range(5):
                    rows_ref[local, bead, axis, 0:lanes, :] = wide[
                        :, axis * lanes : (axis + 1) * lanes
                    ]

        def per_cell(local, carry):
            cell = group * GROUP + local

            def bound(bead, octant):
                return bounds[(bead * cells + cell) * 9 + octant]

            def itself(index, carry):
                first = pl.multiple_of(index * SPAN, SPAN)
                meet_run(
                    SPAN, local, [first] * beads, cell, 0.0, 0.0, lanes_ref, sizes_ref, rows_ref,
                    None, back_ref,
                )
                return carry

            lax.fori_loop(0, lax.div(bound(0, 8) + (SPAN - 1), SPAN), itself, 0)

            for span, (starts, table) in zip(RUN_SPANS, runs):

                def per_entry(entry, carry, span=span, table=table):
                    partner = table[5 * entry]
                    step_y = table[5 * entry + 1].astype(F32)
                    step_z = table[5 * entry + 2].astype(F32)
                    begins = [bound(bead, table[5 * entry + 3]) for bead in range(beads)]
                    longest = bound(0, table[5 * entry + 4]) - begins[0]
                    for bead in range(1, beads):
                        longest = jnp.maximum(
                            longest, bound(bead, table[5 * entry + 4]) - begins[bead]
                        )

                    def per_span(index, carry):
                        firsts = [jnp.minimum(begin + index * span, lanes) for begin in begins]
                        meet_run(
                            span, local, firsts, partner, step_y, step_z, lanes_ref, sizes_ref,
                            rows_ref, total_ref, back_ref,
                        )
                        return carry

                    return lax.fori_loop(0, lax.div(longest + (span - 1), span), per_span, carry)

                lax.fori_loop(starts[cell], starts[cell + 1], per_entry, 0)
            return carry

        lax.fori_loop(0, GROUP, per_cell, 0)

        for local in range(GROUP):
            cell = group * GROUP + local
            alive = bounds[cell * 9 + 8]
            for bead in range(beads):
                sums = None
                for axis in range(3):
                    value = back_ref[local, bead, axis, 0:lanes, :]
                    high = value.astype(BF16)
                    low = (value - high.astype(F32)).astype(BF16)
                    term = jnp.dot(
                        jnp.concatenate([high, low], axis=1),
                        folders[axis],
                        preferred_element_type=F32,
                    )
                    sums = term if sums is None else sums + term
                block = jnp.where(slot < alive, sums.T, 0.0)
                chosen = jnp.where(ranks[bead, cell] == row, 1.0, 0.0).astype(BF16)
                moved = jnp.dot(
                    jnp.concatenate(split_three(block), axis=0).astype(BF16),
                    chosen,
                    preferred_element_type=F32,
                )
                force_ref[bead, cell] = (moved[0:8] + moved[8:16] + moved[16:24])[0:3]
        return carry

    lax.fori_loop(0, cells // GROUP, per_group, 0)

    def finish(cell, carry):
        for bead in range(beads):
            total = fold_total(total_ref, cell, bead) - force_ref[bead, cell]
            force_ref[bead, cell] = factor * total
            other_ref[bead, cell] = factor * fold_total(total_ref, cell + cells, bead)
        return carry

    lax.fori_loop(0, cells, finish, 0)


def short_forces(position, params, next_position, next_params, ordered, ranks, bounds):
    beads, cells, _, lanes = position.shape
    tables = [jnp.asarray(table) for table in reach_lists(cells)]
    forces = jax.ShapeDtypeStruct((beads, cells, 3, lanes), F32)
    return call(
        reach_kernel,
        (*tables, bounds, position, params, next_position, next_params, ordered, ranks),
        len(tables) + 1,
        (forces, forces),
        [
            pltpu.VMEM((beads, 2 * cells, 3, lanes), F32),
            pltpu.VMEM((2 * cells, 2, lanes), F32),
            pltpu.VMEM((GROUP, beads, 5, lanes + RUN_SPANS[-1], lanes), F32),
            pltpu.VMEM((2 * cells, beads, 3, 8, lanes), F32),
            pltpu.VMEM((GROUP, beads, 3, lanes + RUN_SPANS[-1], lanes), F32),
        ],
        PAIR_FLOPS * beads * 70,
    )


def call(kernel, inputs, smem, outputs, scratch, flops):
    return pl.pallas_call(
        kernel,
        out_shape=outputs,
        in_specs=[
            pl.BlockSpec(memory_space=pltpu.SMEM if place < smem else pltpu.VMEM)
            for place in range(len(inputs))
        ],
        scratch_shapes=scratch,
        compiler_params=pltpu.CompilerParams(vmem_limit_bytes=VMEM_LIMIT),
        cost_estimate=pl.CostEstimate(flops=flops, bytes_accessed=1 << 18, transcendentals=0),
    )(*inputs)


PAIR_FLOPS = 40 * 128 * 128


def pair_forces(position, params, occupied, next_position, next_params, longer):
    beads, cells, _, lanes = position.shape
    starts, entries = partner_lists(cells)
    forces = jax.ShapeDtypeStruct((beads, cells, 3, lanes), F32)
    return call(
        functools.partial(pairs_kernel, longer, lanes // SPAN if longer else 1),
        (
            jnp.asarray(starts), jnp.asarray(entries), occupied, position, params, next_position,
            next_params,
        ),
        3,
        (forces, forces),
        [
            pltpu.VMEM((beads, 2 * cells, 3, lanes), F32),
            pltpu.VMEM((2 * cells, 2, lanes), F32),
            pltpu.VMEM((cells, beads, 3, lanes, lanes), F32),
            pltpu.VMEM((cells, 2, lanes, lanes), F32),
            pltpu.VMEM((2 * cells, beads, 3, 8, lanes), F32),
            pltpu.VMEM((cells, beads, 3, lanes, lanes), F32),
        ],
        PAIR_FLOPS * beads * (len(entries) // 3 + cells),
    )


def kick_kernel(
    piece_rows, groups, table, rank, position, momenta, noise, force, back, params, partial_ref, piece_ref
):
    beads, cells = position.shape[:2]
    holders = piece_ref.shape[0]
    reduced = table.shape[0]
    first = rank[0] * beads
    if holders * piece_rows > 3 * cells:
        piece_ref[...] = jnp.zeros_like(piece_ref)
    for cell in range(cells):
        mass = params[cell, 2:3, :]
        per_mass = 1.0 / mass
        per_root = lax.rsqrt(mass)
        per_root = per_root * (1.5 - 0.5 * mass * per_root * per_root)
        inputs = []
        for bead in range(beads):
            kicked = momenta[bead, cell] + 0.5 * TIME_STEP * (force[bead, cell] + back[bead, cell])
            inputs.append((position[bead, cell], kicked * per_mass, noise[bead, cell] * per_root))
        for bead in range(beads):
            for kind in range(3):
                base = (kind * beads + bead) * piece_rows
                if piece_rows % 3 == 0:
                    owner, row = divmod(3 * cell, piece_rows)
                    piece_ref[owner, base + row : base + row + 3, :] = inputs[bead][kind]
                else:
                    for axis in range(3):
                        owner, row = divmod(3 * cell + axis, piece_rows)
                        piece_ref[owner, base + row : base + row + 1, :] = inputs[bead][kind][
                            axis : axis + 1
                        ]
        for group in range(reduced):
            total = None
            for bead in range(beads):
                for kind in range(3):
                    term = table[group, kind * holders * beads + first + bead] * inputs[bead][kind]
                    total = term if total is None else total + term
            for copy in range(groups):
                partial_ref[group * groups + copy, 3 * cell : 3 * cell + 3, :] = total


def move_kernel(piece_rows, beads, matrix, arrived, out_ref, gathered):
    holders = arrived.shape[0]
    taken = 3 * beads
    given = 2 * beads
    for row in range(piece_rows):
        for holder in range(holders):
            gathered[row, holder * taken : (holder + 1) * taken, :] = arrived[
                holder, pl.ds(row, taken, stride=piece_rows), :
            ]
        moved = lax.dot_general(
            matrix[...],
            gathered[row],
            (((1,), (0,)), ((), ())),
            precision=lax.Precision.HIGHEST,
            preferred_element_type=F32,
        )
        for holder in range(holders):
            out_ref[holder, row * given : (row + 1) * given, :] = moved[
                holder * given : (holder + 1) * given
            ]


def finish_kernel(piece_rows, groups, table, rank, moved, slow, params, position_ref, momentum_ref):
    beads, cells = position_ref.shape[:2]
    given = 2 * beads
    reduced = table.shape[0]
    first = rank[0] * beads
    for cell in range(cells):
        mass = params[cell, 2:3, :]
        for bead in range(beads):
            def taken(kind):
                if piece_rows % 3 == 0:
                    owner, row = divmod(3 * cell, piece_rows)
                    return moved[owner, pl.ds(row * given + kind * beads + bead, 3, stride=given), :]
                rows = []
                for axis in range(3):
                    owner, row = divmod(3 * cell + axis, piece_rows)
                    place = row * given + kind * beads + bead
                    rows.append(moved[owner, place : place + 1, :])
                return jnp.concatenate(rows, axis=0)

            position_ref[bead, cell] = taken(0)
            total = mass * taken(1)
            for group in range(reduced):
                total = total + table[group, first + bead] * slow[
                    group * groups, 3 * cell : 3 * cell + 3, :
                ]
            momentum_ref[bead, cell] = total


def shards(positions, momenta, noise, atom_types, occupancy, type_sigma, type_eps, type_mass):
    beads, cells, _, lanes = positions.shape
    holders = lax.axis_size("bead")
    domains = lax.axis_size("space")
    rank = lax.axis_index("bead")
    total_beads = beads * holders
    rows = 3 * cells
    piece_rows = -(-rows // holders)
    held = max(1, PC // holders)
    groups = max(1, holders // PC)
    contract = contract_matrix(total_beads, PC)
    steps = step_matrices(total_beads)
    rank_table = rank.astype(jnp.int32).reshape(1)
    one_back = [((i + 1) % domains, i) for i in range(domains)]
    one_on = [(i, (i + 1) % domains) for i in range(domains)]

    codes = jnp.arange(type_sigma.shape[0])
    onehot = atom_types[..., None] == codes
    living = jnp.arange(lanes)[None, :] < occupancy[:, None]
    half_sigma = 0.5 * jnp.sum(jnp.where(onehot, type_sigma, 0.0), -1)
    root_eps = jnp.sqrt(jnp.sum(jnp.where(onehot, type_eps, 0.0), -1))
    mass = jnp.sum(jnp.where(onehot, type_mass, 0.0), -1)
    params = jnp.stack([half_sigma, jnp.where(living, root_eps, 0.0), mass], 1)

    stacked = jnp.concatenate([positions, params[None]], 0)
    next_stacked = lax.ppermute(stacked, "space", one_back)
    next_params = next_stacked[beads]
    ordered, ranks = call(
        order_kernel,
        (positions, params),
        0,
        (
            jax.ShapeDtypeStruct((beads, cells, lanes, 24), BF16),
            jax.ShapeDtypeStruct((beads, cells, 1, lanes), F32),
        ),
        [],
        1 << 22,
    )
    key = octant_key(positions[:, :, 0], positions[:, :, 1], positions[:, :, 2], living[None])
    bounds = jnp.sum(
        (key[:, :, None, :] < jnp.arange(9, dtype=F32)[:, None]).astype(jnp.int32), -1
    )
    force, back = short_forces(
        positions, params, next_stacked[:beads], next_params, ordered, ranks,
        bounds.reshape(-1),
    )
    back = lax.ppermute(back, "space", one_on)

    position_map = np.concatenate([contract @ steps[0, kind] for kind in range(3)], axis=1)
    partial, pieces = call(
        functools.partial(kick_kernel, piece_rows, groups),
        (
            jnp.asarray(position_map, F32), rank_table, positions, momenta, noise, force, back,
            params,
        ),
        2,
        (
            jax.ShapeDtypeStruct((PC * groups, rows, lanes), F32),
            jax.ShapeDtypeStruct((holders, 3 * beads * piece_rows, lanes), F32),
        ),
        [],
        1 << 22,
    )
    arrived = lax.all_to_all(
        partial.reshape(holders, held * rows, lanes), "bead", split_axis=0, concat_axis=0, tiled=True
    )
    contracted = jnp.sum(arrived, 0).reshape(held, cells, 3, lanes)
    next_contracted = lax.ppermute(contracted, "space", one_back)
    pieces = lax.all_to_all(pieces, "bead", split_axis=0, concat_axis=0, tiled=True)
    slow, slow_back = pair_forces(
        contracted, params, occupancy, next_contracted, next_params, True
    )
    slow = slow + lax.ppermute(slow_back, "space", one_on)

    order = steps.reshape(2, 3, holders, beads, holders, beads).transpose(2, 0, 3, 4, 1, 5)
    order = order.reshape(2 * total_beads, 3 * total_beads)
    moved = call(
        functools.partial(move_kernel, piece_rows, beads),
        (jnp.asarray(order, F32), pieces),
        0,
        jax.ShapeDtypeStruct((holders, 2 * beads * piece_rows, lanes), F32),
        [pltpu.VMEM((piece_rows, 3 * total_beads, lanes), F32)],
        1 << 23,
    )
    moved_rows = 2 * beads * piece_rows
    sent = jnp.concatenate(
        [
            moved,
            jnp.broadcast_to(slow.reshape(1, held * rows, lanes), (holders, held * rows, lanes)),
        ],
        1,
    )
    got = lax.all_to_all(sent, "bead", split_axis=0, concat_axis=0, tiled=True)
    spread = 0.5 * TIME_STEP * (total_beads / PC) * contract
    shape = jax.ShapeDtypeStruct(positions.shape, F32)
    return call(
        functools.partial(finish_kernel, piece_rows, groups),
        (
            jnp.asarray(spread, F32), rank_table, got[:, :moved_rows],
            got[:, moved_rows:].reshape(holders * held, rows, lanes), params,
        ),
        2,
        (shape, shape),
        [],
        1 << 20,
    )


def solution(mesh):
    placed = (
        P("bead", "space", None, None),
        P("bead", "space", None, None),
        P("bead", "space", None, None),
        P("space", None),
        P("space"),
        P(),
        P(),
        P(),
    )
    return jax.shard_map(
        shards,
        mesh=mesh,
        in_specs=placed,
        out_specs=(P("bead", "space", None, None), P("bead", "space", None, None)),
        check_vma=False,
    )
```

```python
import functools

import jax
import jax.numpy as jnp
import numpy as np
from jax import lax
from jax.experimental import pallas as pl
from jax.experimental.pallas import tpu as pltpu
from jax.sharding import PartitionSpec as P

PC = 8
GY = 4
GZ = 4

TIME_STEP = 0.05
INVERSE_TEMP = 32.0
CENTROID_FRICTION = 1.0
INNER_CUT = 0.5
OUTER_CUT = 1.0
CUBE_ROOT_TWO = 2.0 ** (1.0 / 3.0)
F32 = jnp.float32
BF16 = jnp.bfloat16
SPAN = 32
GROUP = 4
STEPS = ((SPAN // 2, 4), (SPAN // 2, 2), (SPAN // 2, 1), (SPAN, 2), (SPAN, 1))
VMEM_LIMIT = 48 * 1024 * 1024


def mode_matrix(number):
    rows = np.arange(number, dtype=np.float64)[:, None]
    column = np.arange(number, dtype=np.float64)[None, :]
    phases = 2.0 * np.pi * rows * column / number
    factor = np.sqrt(2.0 / number)
    middle = np.cos(np.pi * rows) / np.sqrt(number)
    matrix = np.where(column < number / 2, factor * np.cos(phases), factor * np.sin(phases))
    matrix = np.where(column == number / 2, middle, matrix)
    return np.where(column == 0, 1.0 / np.sqrt(number), matrix)


def contract_matrix(full_count, reduced):
    selected = np.arange(reduced)
    selected = np.where(selected <= reduced // 2, selected, selected + full_count - reduced)
    chosen = mode_matrix(full_count)[:, selected]
    return np.sqrt(reduced / full_count) * (mode_matrix(reduced) @ chosen.T)


def step_matrices(number):
    index = np.arange(number, dtype=np.float64)
    frequency = 2.0 * (number / INVERSE_TEMP) * np.sin(np.pi * index / number)
    friction = np.where(index == 0, CENTROID_FRICTION, 2.0 * frequency)
    damping = np.exp(-friction * TIME_STEP)
    kicking = np.sqrt((1.0 - damping * damping) / INVERSE_TEMP)
    cosine = np.cos(frequency * TIME_STEP)
    sine = np.sin(frequency * TIME_STEP)
    drift = np.where(index == 0, TIME_STEP, sine / np.where(index == 0, 1.0, frequency))
    modes = mode_matrix(number)

    def over_beads(diagonal):
        return (modes * diagonal[None, :]) @ modes.T

    return np.array(
        [
            [over_beads(cosine), over_beads(drift * damping), over_beads(drift * kicking)],
            [
                over_beads(-frequency * sine),
                over_beads(cosine * damping),
                over_beads(cosine * kicking),
            ],
        ]
    )


def partner_lists(domain_cells):
    lists = []
    for one in range(domain_cells):
        near = []
        for two in range(domain_cells):
            step_y, step_z = two // GZ - one // GZ, two % GZ - one % GZ
            if abs(step_y) <= 1 and abs(step_z) <= 1:
                near.append((two, step_y, step_z))
        later = [entry for entry in near if entry[0] > one]
        lists.append(later + [(two + domain_cells, y, z) for two, y, z in near])
    starts = np.cumsum([0] + [len(entries) for entries in lists]).astype(np.int32)
    return starts, np.array([value for entries in lists for entry in entries for value in entry], np.int32)


def pair_weight(h, radius_sq, terms, longer):
    inverse = pl.reciprocal(h, approx=True)
    if longer:
        quotient = terms[1] * inverse
        twice = quotient * quotient * quotient
        outer = jnp.maximum(1.0 - radius_sq, 0.0)
        inner = jnp.maximum(1.0 - 4.0 * radius_sq, 0.0)
        switch = outer * outer - inner * inner
        slope = outer - 4.0 * inner
        return twice * ((twice - 1.0) * (3.0 * (switch * inverse) + slope) - slope)
    quotient = terms[1] * inverse
    twice = quotient * quotient * quotient
    edge = jnp.maximum(terms[2] * inverse - 1.0, 2.0)
    bracket = edge * (twice - 1.0) - twice
    return (twice * bracket) * ((edge - 2.0) * h)


def weight_factor(longer):
    return 4.0 if longer else 64.0 / 3.0


def columns(block):
    few, lanes = block.shape
    return jnp.concatenate([block, jnp.zeros((8 - few, lanes), F32)], axis=0).T


def spread_rows(position, params, cell, rows_ref, size_ref):
    beads, lanes = position.shape[0], position.shape[-1]
    sizes = columns(params[cell, 0:2, :])
    for kind in range(2):
        size_ref[cell, kind] = jnp.broadcast_to(sizes[:, kind : kind + 1], (lanes, lanes))
    for bead in range(beads):
        block = columns(position[bead, cell])
        for axis in range(3):
            rows_ref[cell, bead, axis] = jnp.broadcast_to(
                block[:, axis : axis + 1], (lanes, lanes)
            )


def meet(longer, cell, first, partners, refs):
    lanes_ref, sizes_ref, rows_ref, size_ref, total_ref, back_ref = refs
    beads, lanes = lanes_ref.shape[0], lanes_ref.shape[-1]
    here = pl.ds(first, SPAN)
    row_half, row_root = size_ref[cell, 0, here, :], size_ref[cell, 1, here, :]
    known = []
    for partner, _, _ in partners:
        half = row_half + sizes_ref[partner, 0:1, :]
        s2 = half * half
        terms = (s2, CUBE_ROOT_TWO * s2, None if longer else 0.75 + 3.0 * s2)
        known.append((s2, terms, row_root * sizes_ref[partner, 1:2, :]))
    for bead in range(beads):
        rows = [rows_ref[cell, bead, axis, here, :] for axis in range(3)]
        back = [None, None, None]
        for (partner, step_y, step_z), (s2, terms, depth) in zip(partners, known):
            place = lanes_ref[bead, partner]
            apart = [
                place[0:1] - rows[0], (place[1:2] + step_y) - rows[1], (place[2:3] + step_z) - rows[2]
            ]
            radius_sq = apart[0] * apart[0] + apart[1] * apart[1] + apart[2] * apart[2]
            weight = depth * pair_weight(radius_sq + s2, radius_sq, terms, longer)
            for axis in range(3):
                push = weight * apart[axis]
                back[axis] = push if back[axis] is None else back[axis] + push
                if total_ref is not None:
                    total_ref[partner, bead, axis] += jnp.sum(
                        push.reshape(SPAN // 8, 8, lanes), axis=0
                    )
        for axis in range(3):
            if total_ref is None:
                back_ref[cell, bead, axis, here, :] = back[axis]
            else:
                back_ref[cell, bead, axis, here, :] += back[axis]


def fold_back(back_ref, cell, bead):
    lanes = back_ref.shape[-1]
    column = lax.broadcasted_iota(jnp.int32, (lanes, 8), 1)
    sums = [jnp.sum(back_ref[cell, bead, axis], axis=1, keepdims=True) for axis in range(3)]
    block = jnp.where(
        column == 0, sums[0], jnp.where(column == 1, sums[1], jnp.where(column == 2, sums[2], 0.0))
    )
    return block.T[0:3]


def fold_total(total_ref, cell, bead):
    return jnp.concatenate(
        [jnp.sum(total_ref[cell, bead, axis], axis=0, keepdims=True) for axis in range(3)], axis=0
    )


def pairs_kernel(
    longer, parts, plan, occupied, position, params, next_position, next_params,
    force_ref, other_ref, lanes_ref, sizes_ref, rows_ref, size_ref, total_ref, back_ref,
):
    beads, cells, _, lanes = position.shape
    factor = weight_factor(longer)
    together = max(1, 4 // beads)
    axis_row = lax.broadcasted_iota(jnp.int32, (3, lanes), 0)
    layer = jnp.where(axis_row == 0, 1.0, 0.0)
    for bead in range(beads):
        lanes_ref[bead, 0:cells] = position[bead]
        lanes_ref[bead, cells : 2 * cells] = next_position[bead] + layer[None]
    sizes_ref[0:cells] = params[:, 0:2, :]
    sizes_ref[cells : 2 * cells] = next_params[:, 0:2, :]
    total_ref[...] = jnp.zeros_like(total_ref)

    def spread(index, carry):
        for shift in range(together):
            spread_rows(position, params, index * together + shift, rows_ref, size_ref)
        return carry

    lax.fori_loop(0, cells // together, spread, 0)
    refs = (lanes_ref, sizes_ref, rows_ref, size_ref)

    def entry_of(entry):
        return (
            plan[cells + 1 + 3 * entry],
            plan[cells + 2 + 3 * entry].astype(F32),
            plan[cells + 3 + 3 * entry].astype(F32),
        )

    def per_cell(cell, carry):
        begin, end = plan[cell], plan[cell + 1]
        odd = lax.rem(end - begin, 2)

        def per_span(index, carry):
            firsts = [
                pl.multiple_of((index * parts + part) * SPAN, SPAN) for part in range(parts)
            ]
            for first in firsts:
                meet(longer, cell, first, [(cell, 0.0, 0.0)], refs + (None, back_ref))

            def single(entry, carry):
                for first in firsts:
                    meet(longer, cell, first, [entry_of(entry)], refs + (total_ref, back_ref))
                return carry

            def double(step, carry):
                entry = begin + odd + 2 * step
                both = [entry_of(entry), entry_of(entry + 1)]
                for first in firsts:
                    meet(longer, cell, first, both, refs + (total_ref, back_ref))
                return carry

            carry = lax.fori_loop(begin, begin + odd, single, carry)
            return lax.fori_loop(0, lax.div(end - begin, 2), double, carry)

        span = SPAN * parts
        return lax.fori_loop(0, lax.div(occupied[cell] + (span - 1), span), per_span, carry)

    lax.fori_loop(0, cells, per_cell, 0)

    def finish(index, carry):
        for shift in range(together):
            cell = index * together + shift
            alive = params[cell, 1:2, :] > 0.0
            for bead in range(beads):
                total = fold_total(total_ref, cell, bead) - fold_back(back_ref, cell, bead)
                force_ref[bead, cell] = jnp.where(alive, factor * total, 0.0)
                other_ref[bead, cell] = factor * fold_total(total_ref, cell + cells, bead)
        return carry

    lax.fori_loop(0, cells // together, finish, 0)


def octant_key(x, y, z, alive):
    zed = jnp.where(z >= 0.5, 1.0, 0.0)
    gray = jnp.where(y >= 0.5, 3.0 - zed, zed)
    return jnp.where(alive, jnp.where(x >= 0.5, 7.0 - gray, gray), 8.0)


def reach_lists(domain_cells):
    octants = []
    for bit_x in range(2):
        for bit_y in range(2):
            for bit_z in range(2):
                gray = 3 - bit_z if bit_y else bit_z
                octants.append((7 - gray if bit_x else gray, (bit_x, bit_y, bit_z)))
    classes = [[[] for _ in range(domain_cells)] for _ in STEPS]
    for one in range(domain_cells):
        runs = {}
        for layer in range(2):
            for two in range(domain_cells):
                step = (layer, two // GZ - one // GZ, two % GZ - one % GZ)
                if abs(step[1]) > 1 or abs(step[2]) > 1 or (layer == 0 and two <= one):
                    continue
                keys = [
                    key
                    for key, bits in octants
                    if all(move == 0 or bit == (move > 0) for move, bit in zip(step, bits))
                ]
                entry = (two + layer * domain_cells, step[1], step[2], min(keys), max(keys) + 1)
                runs.setdefault(entry[4] - entry[3], []).append(entry)
        for length, entries in sorted(runs.items()):
            entries.sort(key=lambda entry: entry[3:])
            span = SPAN // 2 if length == 1 else SPAN
            for place, (rows, count) in enumerate(STEPS):
                if rows == span:
                    whole = len(entries) // count * count
                    classes[place][one] += entries[:whole]
                    entries = entries[whole:]
    starts, values = [], []
    for lists in classes:
        for entries in lists:
            starts.append(len(values) // 5)
            values += [value for entry in entries for value in entry]
        starts.append(len(values) // 5)
    return np.array(starts, np.int32), np.array(values, np.int32)


def split_three(value):
    high = value.astype(BF16).astype(F32)
    rest = value - high
    middle = rest.astype(BF16).astype(F32)
    return high, middle, rest - middle


def order_kernel(position, params, out_ref):
    beads, cells, _, lanes = position.shape
    row = lax.broadcasted_iota(jnp.int32, (lanes, lanes), 0)
    column = lax.broadcasted_iota(jnp.int32, (lanes, lanes), 1)
    before = jnp.where(row < column, 1.0, 0.0).astype(BF16)
    counter = jnp.concatenate([before, jnp.ones((lanes, lanes), BF16)], axis=0)
    kind = lax.broadcasted_iota(jnp.int32, (16, lanes), 0).astype(F32)
    place_row = row.astype(F32)

    def per_cell(index, carry):
        for shift, bead in [(shift, bead) for shift in range(GROUP) for bead in range(beads)]:
            cell = index * GROUP + shift
            sizes = params[cell, 0:2, :]
            place = position[bead, cell]
            key = octant_key(place[0:1], place[1:2], place[2:3], sizes[1:2] > 0.0)
            same = jnp.where(key == kind, 1.0, 0.0)
            less = jnp.where(key < kind, 1.0, 0.0)
            counts = lax.dot_general(
                jnp.concatenate([same, less], axis=1).astype(BF16),
                counter,
                (((1,), (0,)), ((), ())),
                preferred_element_type=F32,
            )
            rank = jnp.sum(same * counts, axis=0, keepdims=True)
            chosen = jnp.where(rank == place_row, 1.0, 0.0).astype(BF16)
            block = jnp.concatenate([place, sizes, jnp.zeros((3, lanes), F32)], axis=0)
            moved = lax.dot_general(
                jnp.concatenate(split_three(block), axis=0).astype(BF16),
                chosen,
                (((1,), (1,)), ((), ())),
                preferred_element_type=F32,
            )
            out_ref[bead, cell, 0:5, :] = (moved[0:8] + moved[8:16] + moved[16:24])[0:5]
            out_ref[bead, cell, 5:6, :] = rank
            out_ref[bead, cell, 6:8, :] = jnp.zeros((2, lanes), F32)
        return carry

    lax.fori_loop(0, cells // GROUP, per_cell, 0)


def meet_runs(span, local, runs, lanes_ref, sizes_ref, rows_ref, total_ref, back_ref):
    beads, lanes = lanes_ref.shape[0], lanes_ref.shape[-1]
    for bead in range(beads):
        for firsts, partner, step_y, step_z in runs:
            here = pl.ds(firsts[bead], span)
            half = rows_ref[local, bead, 3, here, :] + sizes_ref[partner, 0:1, :]
            s2 = half * half
            terms = (s2, CUBE_ROOT_TWO * s2, 0.75 + 3.0 * s2)
            place = lanes_ref[bead, partner]
            apart = [
                place[0:1] - rows_ref[local, bead, 0, here, :],
                (place[1:2] + step_y) - rows_ref[local, bead, 1, here, :],
                (place[2:3] + step_z) - rows_ref[local, bead, 2, here, :],
            ]
            radius_sq = apart[0] * apart[0] + apart[1] * apart[1] + apart[2] * apart[2]
            depth = rows_ref[local, bead, 4, here, :] * sizes_ref[partner, 1:2, :]
            weight = depth * pair_weight(radius_sq + s2, radius_sq, terms, False)
            for axis in range(3):
                push = weight * apart[axis]
                if total_ref is None:
                    back_ref[local, bead, axis, here, :] = push
                else:
                    back_ref[local, bead, axis, here, :] += push
                    total_ref[partner, bead, axis] += jnp.sum(
                        push.reshape(span // 8, 8, lanes), axis=0
                    )


def reach_kernel(
    plan, position, params, next_position, next_params, ordered, force_ref, other_ref, lanes_ref,
    sizes_ref, rows_ref, total_ref, back_ref,
):
    beads, cells, _, lanes = position.shape
    entries_at = len(STEPS) * (cells + 1)
    bounds_at = plan.shape[0] - beads * cells * 9
    factor = weight_factor(False)
    axis_row = lax.broadcasted_iota(jnp.int32, (3, lanes), 0)
    layer = jnp.where(axis_row == 0, 1.0, 0.0)
    for bead in range(beads):
        lanes_ref[bead, 0:cells] = position[bead]
        lanes_ref[bead, cells : 2 * cells] = next_position[bead] + layer[None]
    sizes_ref[0:cells] = params[:, 0:2, :]
    sizes_ref[cells : 2 * cells] = next_params[:, 0:2, :]
    total_ref[...] = jnp.zeros_like(total_ref)
    rows_ref[:, :, :, lanes:, :] = jnp.zeros((GROUP, beads, 5, SPAN, lanes), F32)
    row = lax.broadcasted_iota(jnp.int32, (lanes, lanes), 0).astype(F32)
    slot = lax.broadcasted_iota(jnp.int32, (8, lanes), 1)
    column = lax.broadcasted_iota(jnp.int32, (lanes, 8), 1)
    refs = (lanes_ref, sizes_ref, rows_ref)
    every = [(local, bead) for local in range(GROUP) for bead in range(beads)]

    def per_group(group, carry):
        for local, bead in every:
            block = ordered[bead, group * GROUP + local].T
            for axis in range(5):
                rows_ref[local, bead, axis, 0:lanes, :] = jnp.broadcast_to(
                    block[:, axis : axis + 1], (lanes, lanes)
                )

        def per_cell(local, carry):
            cell = group * GROUP + local

            def bound(bead, octant):
                return plan[bounds_at + (bead * cells + cell) * 9 + octant]

            def itself(index, carry):
                first = pl.multiple_of(index * SPAN, SPAN)
                run = ([first] * beads, cell, 0.0, 0.0)
                meet_runs(SPAN, local, [run], *refs, None, back_ref)
                return carry

            lax.fori_loop(0, lax.div(bound(0, 8) + (SPAN - 1), SPAN), itself, 0)

            for place, (span, count) in enumerate(STEPS):
                begin = plan[place * (cells + 1) + cell]
                end = plan[place * (cells + 1) + cell + 1]

                def per_step(step, carry, span=span, count=count, begin=begin):
                    runs, longest = [], 0
                    for shift in range(count):
                        at = entries_at + 5 * (begin + step * count + shift)
                        begins = [bound(bead, plan[at + 3]) for bead in range(beads)]
                        for bead in range(beads):
                            longest = jnp.maximum(longest, bound(bead, plan[at + 4]) - begins[bead])
                        runs.append(
                            (begins, plan[at], plan[at + 1].astype(F32), plan[at + 2].astype(F32))
                        )

                    def per_span(index, carry):
                        moved = [
                            ([jnp.minimum(first + index * span, lanes) for first in begins], *rest)
                            for begins, *rest in runs
                        ]
                        meet_runs(span, local, moved, *refs, total_ref, back_ref)
                        return carry

                    return lax.fori_loop(0, lax.div(longest + (span - 1), span), per_span, carry)

                lax.fori_loop(0, lax.div(end - begin, count), per_step, 0)
            return carry

        lax.fori_loop(0, GROUP, per_cell, 0)

        for local, bead in every:
            cell = group * GROUP + local
            alive = plan[bounds_at + cell * 9 + 8]
            sums = [
                jnp.sum(back_ref[local, bead, axis, 0:lanes, :], axis=1, keepdims=True)
                for axis in range(3)
            ]
            block = jnp.where(
                column == 0,
                sums[0],
                jnp.where(column == 1, sums[1], jnp.where(column == 2, sums[2], 0.0)),
            ).T
            block = jnp.where(slot < alive, block, 0.0)
            chosen = jnp.where(ordered[bead, cell, 5:6, :] == row, 1.0, 0.0).astype(BF16)
            moved = lax.dot_general(
                jnp.concatenate(split_three(block), axis=0).astype(BF16),
                chosen,
                (((1,), (0,)), ((), ())),
                preferred_element_type=F32,
            )
            force_ref[bead, cell] = (moved[0:8] + moved[8:16] + moved[16:24])[0:3]
        return carry

    lax.fori_loop(0, cells // GROUP, per_group, 0)

    def finish(index, carry):
        for shift, bead in every:
            cell = index * GROUP + shift
            total = fold_total(total_ref, cell, bead) - force_ref[bead, cell]
            force_ref[bead, cell] = factor * total
            other_ref[bead, cell] = factor * fold_total(total_ref, cell + cells, bead)
        return carry

    lax.fori_loop(0, cells // GROUP, finish, 0)


def short_forces(position, params, next_position, next_params, ordered, bounds):
    beads, cells, _, lanes = position.shape
    starts, entries = reach_lists(cells)
    plan = jnp.concatenate([jnp.asarray(starts), jnp.asarray(entries), bounds])
    forces = jax.ShapeDtypeStruct((beads, cells, 3, lanes), F32)
    return call(
        reach_kernel,
        (plan, position, params, next_position, next_params, ordered),
        1,
        (forces, forces),
        [
            pltpu.VMEM((beads, 2 * cells, 3, lanes), F32),
            pltpu.VMEM((2 * cells, 2, lanes), F32),
            pltpu.VMEM((GROUP, beads, 5, lanes + SPAN, lanes), F32),
            pltpu.VMEM((2 * cells, beads, 3, 8, lanes), F32),
            pltpu.VMEM((GROUP, beads, 3, lanes + SPAN, lanes), F32),
        ],
        PAIR_FLOPS * beads * 70,
    )


def call(kernel, inputs, smem, outputs, scratch, flops):
    return pl.pallas_call(
        kernel,
        out_shape=outputs,
        in_specs=[
            pl.BlockSpec(memory_space=pltpu.SMEM if place < smem else pltpu.VMEM)
            for place in range(len(inputs))
        ],
        scratch_shapes=scratch,
        compiler_params=pltpu.CompilerParams(vmem_limit_bytes=VMEM_LIMIT),
        cost_estimate=pl.CostEstimate(flops=flops, bytes_accessed=1 << 18, transcendentals=0),
    )(*inputs)


PAIR_FLOPS = 40 * 128 * 128


def pair_forces(position, params, occupied, next_position, next_params, longer):
    beads, cells, _, lanes = position.shape
    starts, entries = partner_lists(cells)
    forces = jax.ShapeDtypeStruct((beads, cells, 3, lanes), F32)
    return call(
        functools.partial(pairs_kernel, longer, lanes // SPAN if longer else 1),
        (
            jnp.asarray(np.concatenate([starts, entries])), occupied, position, params,
            next_position, next_params,
        ),
        2,
        (forces, forces),
        [
            pltpu.VMEM((beads, 2 * cells, 3, lanes), F32),
            pltpu.VMEM((2 * cells, 2, lanes), F32),
            pltpu.VMEM((cells, beads, 3, lanes, lanes), F32),
            pltpu.VMEM((cells, 2, lanes, lanes), F32),
            pltpu.VMEM((2 * cells, beads, 3, 8, lanes), F32),
            pltpu.VMEM((cells, beads, 3, lanes, lanes), F32),
        ],
        PAIR_FLOPS * beads * (len(entries) // 3 + cells),
    )


def kick_kernel(
    piece_rows, groups, table, rank, position, momenta, noise, force, back, params, partial_ref, piece_ref
):
    beads, cells = position.shape[:2]
    holders = piece_ref.shape[0]
    reduced = table.shape[0]
    first = rank[0] * beads
    if holders * piece_rows > 3 * cells:
        piece_ref[...] = jnp.zeros_like(piece_ref)
    for cell in range(cells):
        mass = params[cell, 2:3, :]
        per_mass = 1.0 / mass
        per_root = lax.rsqrt(mass)
        per_root = per_root * (1.5 - 0.5 * mass * per_root * per_root)
        inputs = []
        for bead in range(beads):
            kicked = momenta[bead, cell] + 0.5 * TIME_STEP * (force[bead, cell] + back[bead, cell])
            inputs.append((position[bead, cell], kicked * per_mass, noise[bead, cell] * per_root))
        for bead in range(beads):
            for kind in range(3):
                base = (kind * beads + bead) * piece_rows
                if piece_rows % 3 == 0:
                    owner, row = divmod(3 * cell, piece_rows)
                    piece_ref[owner, base + row : base + row + 3, :] = inputs[bead][kind]
                else:
                    for axis in range(3):
                        owner, row = divmod(3 * cell + axis, piece_rows)
                        piece_ref[owner, base + row : base + row + 1, :] = inputs[bead][kind][
                            axis : axis + 1
                        ]
        for group in range(reduced):
            total = None
            for bead in range(beads):
                for kind in range(3):
                    term = table[group, kind * holders * beads + first + bead] * inputs[bead][kind]
                    total = term if total is None else total + term
            for copy in range(groups):
                partial_ref[group * groups + copy, 3 * cell : 3 * cell + 3, :] = total


def move_kernel(piece_rows, beads, matrix, arrived, out_ref, gathered):
    holders = arrived.shape[0]
    taken = 3 * beads
    given = 2 * beads
    for row in range(piece_rows):
        for holder in range(holders):
            gathered[row, holder * taken : (holder + 1) * taken, :] = arrived[
                holder, pl.ds(row, taken, stride=piece_rows), :
            ]
        moved = lax.dot_general(
            matrix[...],
            gathered[row],
            (((1,), (0,)), ((), ())),
            precision=lax.Precision.HIGHEST,
            preferred_element_type=F32,
        )
        for holder in range(holders):
            out_ref[holder, row * given : (row + 1) * given, :] = moved[
                holder * given : (holder + 1) * given
            ]


def finish_kernel(piece_rows, groups, table, rank, moved, slow, params, position_ref, momentum_ref):
    beads, cells = position_ref.shape[:2]
    given = 2 * beads
    reduced = table.shape[0]
    first = rank[0] * beads
    for cell in range(cells):
        mass = params[cell, 2:3, :]
        for bead in range(beads):
            def taken(kind):
                if piece_rows % 3 == 0:
                    owner, row = divmod(3 * cell, piece_rows)
                    return moved[owner, pl.ds(row * given + kind * beads + bead, 3, stride=given), :]
                rows = []
                for axis in range(3):
                    owner, row = divmod(3 * cell + axis, piece_rows)
                    place = row * given + kind * beads + bead
                    rows.append(moved[owner, place : place + 1, :])
                return jnp.concatenate(rows, axis=0)

            position_ref[bead, cell] = taken(0)
            total = mass * taken(1)
            for group in range(reduced):
                total = total + table[group, first + bead] * slow[
                    group * groups, 3 * cell : 3 * cell + 3, :
                ]
            momentum_ref[bead, cell] = total


def shards(positions, momenta, noise, atom_types, occupancy, type_sigma, type_eps, type_mass):
    beads, cells, _, lanes = positions.shape
    holders = lax.axis_size("bead")
    domains = lax.axis_size("space")
    rank = lax.axis_index("bead")
    total_beads = beads * holders
    rows = 3 * cells
    piece_rows = -(-rows // holders)
    held = max(1, PC // holders)
    groups = max(1, holders // PC)
    contract = contract_matrix(total_beads, PC)
    steps = step_matrices(total_beads)
    rank_table = rank.astype(jnp.int32).reshape(1)
    one_back = [((i + 1) % domains, i) for i in range(domains)]
    one_on = [(i, (i + 1) % domains) for i in range(domains)]

    codes = jnp.arange(type_sigma.shape[0])
    onehot = atom_types[..., None] == codes
    living = jnp.arange(lanes)[None, :] < occupancy[:, None]
    half_sigma = 0.5 * jnp.sum(jnp.where(onehot, type_sigma, 0.0), -1)
    root_eps = jnp.sqrt(jnp.sum(jnp.where(onehot, type_eps, 0.0), -1))
    mass = jnp.sum(jnp.where(onehot, type_mass, 0.0), -1)
    params = jnp.stack([half_sigma, jnp.where(living, root_eps, 0.0), mass], 1)

    stacked = jnp.concatenate([positions, params[None]], 0)
    next_stacked = lax.ppermute(stacked, "space", one_back)
    next_params = next_stacked[beads]
    ordered = call(
        order_kernel,
        (positions, params),
        0,
        jax.ShapeDtypeStruct((beads, cells, 8, lanes), F32),
        [],
        1 << 22,
    )
    key = octant_key(positions[:, :, 0], positions[:, :, 1], positions[:, :, 2], living[None])
    bounds = jnp.sum(
        (key[:, :, None, :] < jnp.arange(9, dtype=F32)[:, None]).astype(jnp.int32), -1
    )
    force, back = short_forces(
        positions, params, next_stacked[:beads], next_params, ordered, bounds.reshape(-1)
    )
    back = lax.ppermute(back, "space", one_on)

    position_map = np.concatenate([contract @ steps[0, kind] for kind in range(3)], axis=1)
    partial, pieces = call(
        functools.partial(kick_kernel, piece_rows, groups),
        (
            jnp.asarray(position_map, F32), rank_table, positions, momenta, noise, force, back,
            params,
        ),
        2,
        (
            jax.ShapeDtypeStruct((PC * groups, rows, lanes), F32),
            jax.ShapeDtypeStruct((holders, 3 * beads * piece_rows, lanes), F32),
        ),
        [],
        1 << 22,
    )
    arrived = lax.all_to_all(
        partial.reshape(holders, held * rows, lanes), "bead", split_axis=0, concat_axis=0, tiled=True
    )
    contracted = jnp.sum(arrived, 0).reshape(held, cells, 3, lanes)
    next_contracted = lax.ppermute(contracted, "space", one_back)
    pieces = lax.all_to_all(pieces, "bead", split_axis=0, concat_axis=0, tiled=True)
    slow, slow_back = pair_forces(
        contracted, params, occupancy, next_contracted, next_params, True
    )
    slow = slow + lax.ppermute(slow_back, "space", one_on)

    order = steps.reshape(2, 3, holders, beads, holders, beads).transpose(2, 0, 3, 4, 1, 5)
    order = order.reshape(2 * total_beads, 3 * total_beads)
    moved = call(
        functools.partial(move_kernel, piece_rows, beads),
        (jnp.asarray(order, F32), pieces),
        0,
        jax.ShapeDtypeStruct((holders, 2 * beads * piece_rows, lanes), F32),
        [pltpu.VMEM((piece_rows, 3 * total_beads, lanes), F32)],
        1 << 23,
    )
    moved_rows = 2 * beads * piece_rows
    sent = jnp.concatenate(
        [
            moved,
            jnp.broadcast_to(slow.reshape(1, held * rows, lanes), (holders, held * rows, lanes)),
        ],
        1,
    )
    got = lax.all_to_all(sent, "bead", split_axis=0, concat_axis=0, tiled=True)
    spread = 0.5 * TIME_STEP * (total_beads / PC) * contract
    shape = jax.ShapeDtypeStruct(positions.shape, F32)
    return call(
        functools.partial(finish_kernel, piece_rows, groups),
        (
            jnp.asarray(spread, F32), rank_table, got[:, :moved_rows],
            got[:, moved_rows:].reshape(holders * held, rows, lanes), params,
        ),
        2,
        (shape, shape),
        [],
        1 << 20,
    )


def solution(mesh):
    placed = (
        P("bead", "space", None, None),
        P("bead", "space", None, None),
        P("bead", "space", None, None),
        P("space", None),
        P("space"),
        P(),
        P(),
        P(),
    )
    return jax.shard_map(
        shards,
        mesh=mesh,
        in_specs=placed,
        out_specs=(P("bead", "space", None, None), P("bead", "space", None, None)),
        check_vma=False,
    )
```

```python
import functools

import jax
import jax.numpy as jnp
import numpy as np
from jax import lax
from jax.experimental import pallas as pl
from jax.experimental.pallas import tpu as pltpu
from jax.sharding import PartitionSpec as P

PC = 8
GY = 4
GZ = 4

TIME_STEP = 0.05
INVERSE_TEMP = 32.0
CENTROID_FRICTION = 1.0
INNER_CUT = 0.5
OUTER_CUT = 1.0
CUBE_ROOT_TWO = 2.0 ** (1.0 / 3.0)
F32 = jnp.float32
BF16 = jnp.bfloat16
SPAN = 32
GROUP = 4
STEPS = ((24, 4), (24, 2), (24, 1), (40, 2), (40, 1), (32, 2), (32, 1))
RUN_ROWS = {1: 24, 2: 40}
SPARE = 40
VMEM_LIMIT = 48 * 1024 * 1024


def mode_matrix(number):
    rows = np.arange(number, dtype=np.float64)[:, None]
    column = np.arange(number, dtype=np.float64)[None, :]
    phases = 2.0 * np.pi * rows * column / number
    factor = np.sqrt(2.0 / number)
    middle = np.cos(np.pi * rows) / np.sqrt(number)
    matrix = np.where(column < number / 2, factor * np.cos(phases), factor * np.sin(phases))
    matrix = np.where(column == number / 2, middle, matrix)
    return np.where(column == 0, 1.0 / np.sqrt(number), matrix)


def contract_matrix(full_count, reduced):
    selected = np.arange(reduced)
    selected = np.where(selected <= reduced // 2, selected, selected + full_count - reduced)
    chosen = mode_matrix(full_count)[:, selected]
    return np.sqrt(reduced / full_count) * (mode_matrix(reduced) @ chosen.T)


def step_matrices(number):
    index = np.arange(number, dtype=np.float64)
    frequency = 2.0 * (number / INVERSE_TEMP) * np.sin(np.pi * index / number)
    friction = np.where(index == 0, CENTROID_FRICTION, 2.0 * frequency)
    damping = np.exp(-friction * TIME_STEP)
    kicking = np.sqrt((1.0 - damping * damping) / INVERSE_TEMP)
    cosine = np.cos(frequency * TIME_STEP)
    sine = np.sin(frequency * TIME_STEP)
    drift = np.where(index == 0, TIME_STEP, sine / np.where(index == 0, 1.0, frequency))
    modes = mode_matrix(number)

    def over_beads(diagonal):
        return (modes * diagonal[None, :]) @ modes.T

    return np.array(
        [
            [over_beads(cosine), over_beads(drift * damping), over_beads(drift * kicking)],
            [
                over_beads(-frequency * sine),
                over_beads(cosine * damping),
                over_beads(cosine * kicking),
            ],
        ]
    )


def partner_lists(domain_cells):
    lists = []
    for one in range(domain_cells):
        near = []
        for two in range(domain_cells):
            step_y, step_z = two // GZ - one // GZ, two % GZ - one % GZ
            if abs(step_y) <= 1 and abs(step_z) <= 1:
                near.append((two, step_y, step_z))
        later = [entry for entry in near if entry[0] > one]
        lists.append(later + [(two + domain_cells, y, z) for two, y, z in near])
    starts = np.cumsum([0] + [len(entries) for entries in lists]).astype(np.int32)
    return starts, np.array([value for entries in lists for entry in entries for value in entry], np.int32)


def pair_weight(h, radius_sq, terms, longer):
    inverse = pl.reciprocal(h, approx=True)
    if longer:
        quotient = terms[1] * inverse
        twice = quotient * quotient * quotient
        outer = jnp.maximum(1.0 - radius_sq, 0.0)
        inner = jnp.maximum(1.0 - 4.0 * radius_sq, 0.0)
        switch = outer * outer - inner * inner
        slope = outer - 4.0 * inner
        return twice * ((twice - 1.0) * (3.0 * (switch * inverse) + slope) - slope)
    quotient = terms[1] * inverse
    twice = quotient * quotient * quotient
    edge = jnp.maximum(terms[2] * inverse - 1.0, 2.0)
    bracket = edge * (twice - 1.0) - twice
    return (twice * bracket) * ((edge - 2.0) * h)


def weight_factor(longer):
    return 4.0 if longer else 64.0 / 3.0


def columns(block):
    few, lanes = block.shape
    return jnp.concatenate([block, jnp.zeros((8 - few, lanes), F32)], axis=0).T


def spread_rows(position, params, cell, rows_ref, size_ref):
    beads, lanes = position.shape[0], position.shape[-1]
    sizes = columns(params[cell, 0:2, :])
    for kind in range(2):
        size_ref[cell, kind] = jnp.broadcast_to(sizes[:, kind : kind + 1], (lanes, lanes))
    for bead in range(beads):
        block = columns(position[bead, cell])
        for axis in range(3):
            rows_ref[cell, bead, axis] = jnp.broadcast_to(
                block[:, axis : axis + 1], (lanes, lanes)
            )


def meet(longer, cell, first, partners, refs):
    lanes_ref, sizes_ref, rows_ref, size_ref, total_ref, back_ref = refs
    beads, lanes = lanes_ref.shape[0], lanes_ref.shape[-1]
    here = pl.ds(first, SPAN)
    tall = (SPAN // 8, 8, lanes)
    row_half = size_ref[cell, 0, here, :].reshape(tall)
    row_root = size_ref[cell, 1, here, :].reshape(tall)
    known = []
    for partner, _, _ in partners:
        half = row_half + sizes_ref[partner, 0]
        s2 = half * half
        terms = (s2, CUBE_ROOT_TWO * s2, None if longer else 0.75 + 3.0 * s2)
        known.append((s2, terms, row_root * sizes_ref[partner, 1]))
    for bead in range(beads):
        rows = [rows_ref[cell, bead, axis, here, :].reshape(tall) for axis in range(3)]
        back = [None, None, None]
        for (partner, step_y, step_z), (s2, terms, depth) in zip(partners, known):
            apart = [
                lanes_ref[bead, partner, 0] - rows[0],
                (lanes_ref[bead, partner, 1] + step_y) - rows[1],
                (lanes_ref[bead, partner, 2] + step_z) - rows[2],
            ]
            radius_sq = apart[0] * apart[0] + apart[1] * apart[1] + apart[2] * apart[2]
            weight = depth * pair_weight(radius_sq + s2, radius_sq, terms, longer)
            for axis in range(3):
                push = weight * apart[axis]
                back[axis] = push if back[axis] is None else back[axis] + push
                if total_ref is not None:
                    total_ref[partner, bead, axis] += jnp.sum(push, axis=0)
        for axis in range(3):
            value = back[axis].reshape(SPAN, lanes)
            if total_ref is None:
                back_ref[cell, bead, axis, here, :] = value
            else:
                back_ref[cell, bead, axis, here, :] += value


def repeat_lanes(position, params, next_position, next_params, lanes_ref, sizes_ref):
    beads, cells, _, lanes = position.shape

    def per_cell(cell, carry):
        for layer, place, values in ((0, position, params), (1, next_position, next_params)):
            for kind in range(2):
                sizes_ref[layer * cells + cell, kind] = jnp.broadcast_to(
                    values[cell, kind : kind + 1, :], (8, lanes)
                )
            for bead in range(beads):
                for axis in range(3):
                    row = place[bead, cell, axis : axis + 1, :]
                    row = row + 1.0 if layer == 1 and axis == 0 else row
                    lanes_ref[bead, layer * cells + cell, axis] = jnp.broadcast_to(row, (8, lanes))
        return carry

    lax.fori_loop(0, cells, per_cell, 0)


def fold_back(back_ref, cell, bead):
    lanes = back_ref.shape[-1]
    column = lax.broadcasted_iota(jnp.int32, (lanes, 8), 1)
    sums = [jnp.sum(back_ref[cell, bead, axis], axis=1, keepdims=True) for axis in range(3)]
    block = jnp.where(
        column == 0, sums[0], jnp.where(column == 1, sums[1], jnp.where(column == 2, sums[2], 0.0))
    )
    return block.T[0:3]


def fold_total(total_ref, cell, bead):
    return jnp.concatenate(
        [jnp.sum(total_ref[cell, bead, axis], axis=0, keepdims=True) for axis in range(3)], axis=0
    )


def pairs_kernel(
    longer, parts, plan, occupied, position, params, next_position, next_params,
    force_ref, other_ref, lanes_ref, sizes_ref, rows_ref, size_ref, total_ref, back_ref,
):
    beads, cells, _, lanes = position.shape
    factor = weight_factor(longer)
    together = max(1, 4 // beads)
    repeat_lanes(position, params, next_position, next_params, lanes_ref, sizes_ref)
    total_ref[...] = jnp.zeros_like(total_ref)

    def spread(index, carry):
        for shift in range(together):
            spread_rows(position, params, index * together + shift, rows_ref, size_ref)
        return carry

    lax.fori_loop(0, cells // together, spread, 0)
    refs = (lanes_ref, sizes_ref, rows_ref, size_ref)

    def entry_of(entry):
        return (
            plan[cells + 1 + 3 * entry],
            plan[cells + 2 + 3 * entry].astype(F32),
            plan[cells + 3 + 3 * entry].astype(F32),
        )

    def per_cell(cell, carry):
        begin, end = plan[cell], plan[cell + 1]
        odd = lax.rem(end - begin, 2)

        def per_span(index, carry):
            firsts = [
                pl.multiple_of((index * parts + part) * SPAN, SPAN) for part in range(parts)
            ]
            for first in firsts:
                meet(longer, cell, first, [(cell, 0.0, 0.0)], refs + (None, back_ref))

            def single(entry, carry):
                for first in firsts:
                    meet(longer, cell, first, [entry_of(entry)], refs + (total_ref, back_ref))
                return carry

            def double(step, carry):
                entry = begin + odd + 2 * step
                both = [entry_of(entry), entry_of(entry + 1)]
                for first in firsts:
                    meet(longer, cell, first, both, refs + (total_ref, back_ref))
                return carry

            carry = lax.fori_loop(begin, begin + odd, single, carry)
            return lax.fori_loop(0, lax.div(end - begin, 2), double, carry)

        span = SPAN * parts
        return lax.fori_loop(0, lax.div(occupied[cell] + (span - 1), span), per_span, carry)

    lax.fori_loop(0, cells, per_cell, 0)

    def finish(index, carry):
        for shift in range(together):
            cell = index * together + shift
            alive = params[cell, 1:2, :] > 0.0
            for bead in range(beads):
                total = fold_total(total_ref, cell, bead) - fold_back(back_ref, cell, bead)
                force_ref[bead, cell] = jnp.where(alive, factor * total, 0.0)
                other_ref[bead, cell] = factor * fold_total(total_ref, cell + cells, bead)
        return carry

    lax.fori_loop(0, cells // together, finish, 0)


def octant_key(x, y, z, alive):
    zed = jnp.where(z >= 0.5, 1.0, 0.0)
    gray = jnp.where(y >= 0.5, 3.0 - zed, zed)
    return jnp.where(alive, jnp.where(x >= 0.5, 7.0 - gray, gray), 8.0)


def reach_lists(domain_cells):
    octants = []
    for bit_x in range(2):
        for bit_y in range(2):
            for bit_z in range(2):
                gray = 3 - bit_z if bit_y else bit_z
                octants.append((7 - gray if bit_x else gray, (bit_x, bit_y, bit_z)))
    classes = [[[] for _ in range(domain_cells)] for _ in STEPS]
    for one in range(domain_cells):
        runs = {}
        for layer in range(2):
            for two in range(domain_cells):
                step = (layer, two // GZ - one // GZ, two % GZ - one % GZ)
                if abs(step[1]) > 1 or abs(step[2]) > 1 or (layer == 0 and two <= one):
                    continue
                keys = [
                    key
                    for key, bits in octants
                    if all(move == 0 or bit == (move > 0) for move, bit in zip(step, bits))
                ]
                entry = (two + layer * domain_cells, step[1], step[2], min(keys), max(keys) + 1)
                runs.setdefault(entry[4] - entry[3], []).append(entry)
        for length, entries in sorted(runs.items()):
            entries.sort(key=lambda entry: entry[3:])
            span = RUN_ROWS.get(length, SPAN)
            for place, (rows, count) in enumerate(STEPS):
                if rows == span:
                    whole = len(entries) // count * count
                    classes[place][one] += entries[:whole]
                    entries = entries[whole:]
    starts, values = [], []
    for lists in classes:
        for entries in lists:
            starts.append(len(values) // 5)
            values += [value for entry in entries for value in entry]
        starts.append(len(values) // 5)
    return np.array(starts, np.int32), np.array(values, np.int32)


def split_three(value):
    high = value.astype(BF16).astype(F32)
    rest = value - high
    middle = rest.astype(BF16).astype(F32)
    return high, middle, rest - middle


def order_kernel(position, params, out_ref):
    beads, cells, _, lanes = position.shape
    row = lax.broadcasted_iota(jnp.int32, (lanes, lanes), 0)
    column = lax.broadcasted_iota(jnp.int32, (lanes, lanes), 1)
    before = jnp.where(row < column, 1.0, 0.0).astype(BF16)
    counter = jnp.concatenate([before, jnp.ones((lanes, lanes), BF16)], axis=0)
    kind = lax.broadcasted_iota(jnp.int32, (16, lanes), 0).astype(F32)
    place_row = row.astype(F32)

    def per_cell(index, carry):
        for shift, bead in [(shift, bead) for shift in range(GROUP) for bead in range(beads)]:
            cell = index * GROUP + shift
            sizes = params[cell, 0:2, :]
            place = position[bead, cell]
            key = octant_key(place[0:1], place[1:2], place[2:3], sizes[1:2] > 0.0)
            same = jnp.where(key == kind, 1.0, 0.0)
            less = jnp.where(key < kind, 1.0, 0.0)
            counts = lax.dot_general(
                jnp.concatenate([same, less], axis=1).astype(BF16),
                counter,
                (((1,), (0,)), ((), ())),
                preferred_element_type=F32,
            )
            rank = jnp.sum(same * counts, axis=0, keepdims=True)
            chosen = jnp.where(rank == place_row, 1.0, 0.0).astype(BF16)
            block = jnp.concatenate([place, sizes, jnp.zeros((3, lanes), F32)], axis=0)
            moved = lax.dot_general(
                jnp.concatenate(split_three(block), axis=0).astype(BF16),
                chosen,
                (((1,), (1,)), ((), ())),
                preferred_element_type=F32,
            )
            out_ref[bead, cell, 0:5, :] = (moved[0:8] + moved[8:16] + moved[16:24])[0:5]
            out_ref[bead, cell, 5:6, :] = rank
            out_ref[bead, cell, 6:8, :] = jnp.zeros((2, lanes), F32)
        return carry

    lax.fori_loop(0, cells // GROUP, per_cell, 0)


def meet_runs(span, local, runs, lanes_ref, sizes_ref, rows_ref, total_ref, back_ref):
    beads, lanes = lanes_ref.shape[0], lanes_ref.shape[-1]
    for bead in range(beads):
        for firsts, partner, step_y, step_z in runs:
            here = pl.ds(firsts[bead], span)
            rows = [
                rows_ref[local, bead, kind, here, :].reshape(span // 8, 8, lanes)
                for kind in range(5)
            ]
            half = rows[3] + sizes_ref[partner, 0]
            s2 = half * half
            terms = (s2, CUBE_ROOT_TWO * s2, 0.75 + 3.0 * s2)
            apart = [
                lanes_ref[bead, partner, 0] - rows[0],
                (lanes_ref[bead, partner, 1] + step_y) - rows[1],
                (lanes_ref[bead, partner, 2] + step_z) - rows[2],
            ]
            radius_sq = apart[0] * apart[0] + apart[1] * apart[1] + apart[2] * apart[2]
            depth = rows[4] * sizes_ref[partner, 1]
            weight = depth * pair_weight(radius_sq + s2, radius_sq, terms, False)
            for axis in range(3):
                push = weight * apart[axis]
                flat_push = push.reshape(span, lanes)
                if total_ref is None:
                    back_ref[local, bead, axis, here, :] = flat_push
                else:
                    back_ref[local, bead, axis, here, :] += flat_push
                    total_ref[partner, bead, axis] += jnp.sum(push, axis=0)


def reach_kernel(
    plan, position, params, next_position, next_params, ordered, force_ref, other_ref, lanes_ref,
    sizes_ref, rows_ref, total_ref, back_ref,
):
    beads, cells, _, lanes = position.shape
    entries_at = len(STEPS) * (cells + 1)
    bounds_at = plan.shape[0] - beads * cells * 9
    factor = weight_factor(False)
    repeat_lanes(position, params, next_position, next_params, lanes_ref, sizes_ref)
    total_ref[...] = jnp.zeros_like(total_ref)
    rows_ref[:, :, :, lanes:, :] = jnp.zeros((GROUP, beads, 5, SPARE, lanes), F32)
    row = lax.broadcasted_iota(jnp.int32, (lanes, lanes), 0).astype(F32)
    slot = lax.broadcasted_iota(jnp.int32, (8, lanes), 1)
    column = lax.broadcasted_iota(jnp.int32, (lanes, 8), 1)
    refs = (lanes_ref, sizes_ref, rows_ref)
    every = [(local, bead) for local in range(GROUP) for bead in range(beads)]

    def per_group(group, carry):
        for local, bead in every:
            block = ordered[bead, group * GROUP + local].T
            for axis in range(5):
                rows_ref[local, bead, axis, 0:lanes, :] = jnp.broadcast_to(
                    block[:, axis : axis + 1], (lanes, lanes)
                )

        def per_cell(local, carry):
            cell = group * GROUP + local

            def bound(bead, octant):
                return plan[bounds_at + (bead * cells + cell) * 9 + octant]

            def itself(index, carry):
                first = pl.multiple_of(index * SPAN, SPAN)
                run = ([first] * beads, cell, 0.0, 0.0)
                meet_runs(SPAN, local, [run], *refs, None, back_ref)
                return carry

            lax.fori_loop(0, lax.div(bound(0, 8) + (SPAN - 1), SPAN), itself, 0)

            for place, (span, count) in enumerate(STEPS):
                begin = plan[place * (cells + 1) + cell]
                end = plan[place * (cells + 1) + cell + 1]

                def per_step(step, carry, span=span, count=count, begin=begin):
                    runs, longest = [], 0
                    for shift in range(count):
                        at = entries_at + 5 * (begin + step * count + shift)
                        begins = [
                            lax.bitwise_and(bound(bead, plan[at + 3]), -8) for bead in range(beads)
                        ]
                        for bead in range(beads):
                            longest = jnp.maximum(longest, bound(bead, plan[at + 4]) - begins[bead])
                        runs.append(
                            (begins, plan[at], plan[at + 1].astype(F32), plan[at + 2].astype(F32))
                        )

                    def per_span(index, carry):
                        moved = [
                            (
                                [
                                    pl.multiple_of(jnp.minimum(first + index * span, lanes), 8)
                                    for first in begins
                                ],
                                *rest,
                            )
                            for begins, *rest in runs
                        ]
                        meet_runs(span, local, moved, *refs, total_ref, back_ref)
                        return carry

                    return lax.fori_loop(0, lax.div(longest + (span - 1), span), per_span, carry)

                lax.fori_loop(0, lax.div(end - begin, count), per_step, 0)
            return carry

        lax.fori_loop(0, GROUP, per_cell, 0)

        for local, bead in every:
            cell = group * GROUP + local
            alive = plan[bounds_at + cell * 9 + 8]
            sums = [
                jnp.sum(back_ref[local, bead, axis, 0:lanes, :], axis=1, keepdims=True)
                for axis in range(3)
            ]
            block = jnp.where(
                column == 0,
                sums[0],
                jnp.where(column == 1, sums[1], jnp.where(column == 2, sums[2], 0.0)),
            ).T
            block = jnp.where(slot < alive, block, 0.0)
            chosen = jnp.where(ordered[bead, cell, 5:6, :] == row, 1.0, 0.0).astype(BF16)
            moved = lax.dot_general(
                jnp.concatenate(split_three(block), axis=0).astype(BF16),
                chosen,
                (((1,), (0,)), ((), ())),
                preferred_element_type=F32,
            )
            force_ref[bead, cell] = (moved[0:8] + moved[8:16] + moved[16:24])[0:3]
        return carry

    lax.fori_loop(0, cells // GROUP, per_group, 0)

    def finish(index, carry):
        for shift, bead in every:
            cell = index * GROUP + shift
            total = fold_total(total_ref, cell, bead) - force_ref[bead, cell]
            force_ref[bead, cell] = factor * total
            other_ref[bead, cell] = factor * fold_total(total_ref, cell + cells, bead)
        return carry

    lax.fori_loop(0, cells // GROUP, finish, 0)


def short_forces(position, params, next_position, next_params, ordered, bounds):
    beads, cells, _, lanes = position.shape
    starts, entries = reach_lists(cells)
    plan = jnp.concatenate([jnp.asarray(starts), jnp.asarray(entries), bounds])
    forces = jax.ShapeDtypeStruct((beads, cells, 3, lanes), F32)
    return call(
        reach_kernel,
        (plan, position, params, next_position, next_params, ordered),
        1,
        (forces, forces),
        [
            pltpu.VMEM((beads, 2 * cells, 3, 8, lanes), F32),
            pltpu.VMEM((2 * cells, 2, 8, lanes), F32),
            pltpu.VMEM((GROUP, beads, 5, lanes + SPARE, lanes), F32),
            pltpu.VMEM((2 * cells, beads, 3, 8, lanes), F32),
            pltpu.VMEM((GROUP, beads, 3, lanes + SPARE, lanes), F32),
        ],
        PAIR_FLOPS * beads * 70,
    )


def call(kernel, inputs, smem, outputs, scratch, flops):
    return pl.pallas_call(
        kernel,
        out_shape=outputs,
        in_specs=[
            pl.BlockSpec(memory_space=pltpu.SMEM if place < smem else pltpu.VMEM)
            for place in range(len(inputs))
        ],
        scratch_shapes=scratch,
        compiler_params=pltpu.CompilerParams(vmem_limit_bytes=VMEM_LIMIT),
        cost_estimate=pl.CostEstimate(flops=flops, bytes_accessed=1 << 18, transcendentals=0),
    )(*inputs)


PAIR_FLOPS = 40 * 128 * 128


def pair_forces(position, params, occupied, next_position, next_params, longer):
    beads, cells, _, lanes = position.shape
    starts, entries = partner_lists(cells)
    forces = jax.ShapeDtypeStruct((beads, cells, 3, lanes), F32)
    return call(
        functools.partial(pairs_kernel, longer, lanes // SPAN if longer else 1),
        (
            jnp.asarray(np.concatenate([starts, entries])), occupied, position, params,
            next_position, next_params,
        ),
        2,
        (forces, forces),
        [
            pltpu.VMEM((beads, 2 * cells, 3, 8, lanes), F32),
            pltpu.VMEM((2 * cells, 2, 8, lanes), F32),
            pltpu.VMEM((cells, beads, 3, lanes, lanes), F32),
            pltpu.VMEM((cells, 2, lanes, lanes), F32),
            pltpu.VMEM((2 * cells, beads, 3, 8, lanes), F32),
            pltpu.VMEM((cells, beads, 3, lanes, lanes), F32),
        ],
        PAIR_FLOPS * beads * (len(entries) // 3 + cells),
    )


def kick_kernel(
    piece_rows, groups, table, rank, position, momenta, noise, force, back, params, partial_ref, piece_ref
):
    beads, cells = position.shape[:2]
    holders = piece_ref.shape[0]
    reduced = table.shape[0]
    first = rank[0] * beads
    if holders * piece_rows > 3 * cells:
        piece_ref[...] = jnp.zeros_like(piece_ref)
    for cell in range(cells):
        mass = params[cell, 2:3, :]
        per_mass = 1.0 / mass
        per_root = lax.rsqrt(mass)
        per_root = per_root * (1.5 - 0.5 * mass * per_root * per_root)
        inputs = []
        for bead in range(beads):
            kicked = momenta[bead, cell] + 0.5 * TIME_STEP * (force[bead, cell] + back[bead, cell])
            inputs.append((position[bead, cell], kicked * per_mass, noise[bead, cell] * per_root))
        for bead in range(beads):
            for kind in range(3):
                base = (kind * beads + bead) * piece_rows
                if piece_rows % 3 == 0:
                    owner, row = divmod(3 * cell, piece_rows)
                    piece_ref[owner, base + row : base + row + 3, :] = inputs[bead][kind]
                else:
                    for axis in range(3):
                        owner, row = divmod(3 * cell + axis, piece_rows)
                        piece_ref[owner, base + row : base + row + 1, :] = inputs[bead][kind][
                            axis : axis + 1
                        ]
        for group in range(reduced):
            total = None
            for bead in range(beads):
                for kind in range(3):
                    term = table[group, kind * holders * beads + first + bead] * inputs[bead][kind]
                    total = term if total is None else total + term
            for copy in range(groups):
                partial_ref[group * groups + copy, 3 * cell : 3 * cell + 3, :] = total


def move_kernel(piece_rows, beads, matrix, arrived, out_ref, gathered):
    holders = arrived.shape[0]
    taken = 3 * beads
    given = 2 * beads
    for row in range(piece_rows):
        for holder in range(holders):
            gathered[row, holder * taken : (holder + 1) * taken, :] = arrived[
                holder, pl.ds(row, taken, stride=piece_rows), :
            ]
        moved = lax.dot_general(
            matrix[...],
            gathered[row],
            (((1,), (0,)), ((), ())),
            precision=lax.Precision.HIGHEST,
            preferred_element_type=F32,
        )
        for holder in range(holders):
            out_ref[holder, row * given : (row + 1) * given, :] = moved[
                holder * given : (holder + 1) * given
            ]


def finish_kernel(piece_rows, groups, table, rank, moved, slow, params, position_ref, momentum_ref):
    beads, cells = position_ref.shape[:2]
    given = 2 * beads
    reduced = table.shape[0]
    first = rank[0] * beads
    for cell in range(cells):
        mass = params[cell, 2:3, :]
        for bead in range(beads):
            def taken(kind):
                if piece_rows % 3 == 0:
                    owner, row = divmod(3 * cell, piece_rows)
                    return moved[owner, pl.ds(row * given + kind * beads + bead, 3, stride=given), :]
                rows = []
                for axis in range(3):
                    owner, row = divmod(3 * cell + axis, piece_rows)
                    place = row * given + kind * beads + bead
                    rows.append(moved[owner, place : place + 1, :])
                return jnp.concatenate(rows, axis=0)

            position_ref[bead, cell] = taken(0)
            total = mass * taken(1)
            for group in range(reduced):
                total = total + table[group, first + bead] * slow[
                    group * groups, 3 * cell : 3 * cell + 3, :
                ]
            momentum_ref[bead, cell] = total


def shards(positions, momenta, noise, atom_types, occupancy, type_sigma, type_eps, type_mass):
    beads, cells, _, lanes = positions.shape
    holders = lax.axis_size("bead")
    domains = lax.axis_size("space")
    rank = lax.axis_index("bead")
    total_beads = beads * holders
    rows = 3 * cells
    piece_rows = -(-rows // holders)
    held = max(1, PC // holders)
    groups = max(1, holders // PC)
    contract = contract_matrix(total_beads, PC)
    steps = step_matrices(total_beads)
    rank_table = rank.astype(jnp.int32).reshape(1)
    one_back = [((i + 1) % domains, i) for i in range(domains)]
    one_on = [(i, (i + 1) % domains) for i in range(domains)]

    codes = jnp.arange(type_sigma.shape[0])
    onehot = atom_types[..., None] == codes
    living = jnp.arange(lanes)[None, :] < occupancy[:, None]
    half_sigma = 0.5 * jnp.sum(jnp.where(onehot, type_sigma, 0.0), -1)
    root_eps = jnp.sqrt(jnp.sum(jnp.where(onehot, type_eps, 0.0), -1))
    mass = jnp.sum(jnp.where(onehot, type_mass, 0.0), -1)
    params = jnp.stack([half_sigma, jnp.where(living, root_eps, 0.0), mass], 1)

    stacked = jnp.concatenate([positions, params[None]], 0)
    next_stacked = lax.ppermute(stacked, "space", one_back)
    next_params = next_stacked[beads]
    ordered = call(
        order_kernel,
        (positions, params),
        0,
        jax.ShapeDtypeStruct((beads, cells, 8, lanes), F32),
        [],
        1 << 22,
    )
    key = octant_key(positions[:, :, 0], positions[:, :, 1], positions[:, :, 2], living[None])
    bounds = jnp.sum(
        (key[:, :, None, :] < jnp.arange(9, dtype=F32)[:, None]).astype(jnp.int32), -1
    )
    force, back = short_forces(
        positions, params, next_stacked[:beads], next_params, ordered, bounds.reshape(-1)
    )
    back = lax.ppermute(back, "space", one_on)

    position_map = np.concatenate([contract @ steps[0, kind] for kind in range(3)], axis=1)
    partial, pieces = call(
        functools.partial(kick_kernel, piece_rows, groups),
        (
            jnp.asarray(position_map, F32), rank_table, positions, momenta, noise, force, back,
            params,
        ),
        2,
        (
            jax.ShapeDtypeStruct((PC * groups, rows, lanes), F32),
            jax.ShapeDtypeStruct((holders, 3 * beads * piece_rows, lanes), F32),
        ),
        [],
        1 << 22,
    )
    arrived = lax.all_to_all(
        partial.reshape(holders, held * rows, lanes), "bead", split_axis=0, concat_axis=0, tiled=True
    )
    contracted = jnp.sum(arrived, 0).reshape(held, cells, 3, lanes)
    next_contracted = lax.ppermute(contracted, "space", one_back)
    pieces = lax.all_to_all(pieces, "bead", split_axis=0, concat_axis=0, tiled=True)
    slow, slow_back = pair_forces(
        contracted, params, occupancy, next_contracted, next_params, True
    )
    slow = slow + lax.ppermute(slow_back, "space", one_on)

    order = steps.reshape(2, 3, holders, beads, holders, beads).transpose(2, 0, 3, 4, 1, 5)
    order = order.reshape(2 * total_beads, 3 * total_beads)
    moved = call(
        functools.partial(move_kernel, piece_rows, beads),
        (jnp.asarray(order, F32), pieces),
        0,
        jax.ShapeDtypeStruct((holders, 2 * beads * piece_rows, lanes), F32),
        [pltpu.VMEM((piece_rows, 3 * total_beads, lanes), F32)],
        1 << 23,
    )
    moved_rows = 2 * beads * piece_rows
    sent = jnp.concatenate(
        [
            moved,
            jnp.broadcast_to(slow.reshape(1, held * rows, lanes), (holders, held * rows, lanes)),
        ],
        1,
    )
    got = lax.all_to_all(sent, "bead", split_axis=0, concat_axis=0, tiled=True)
    spread = 0.5 * TIME_STEP * (total_beads / PC) * contract
    shape = jax.ShapeDtypeStruct(positions.shape, F32)
    return call(
        functools.partial(finish_kernel, piece_rows, groups),
        (
            jnp.asarray(spread, F32), rank_table, got[:, :moved_rows],
            got[:, moved_rows:].reshape(holders * held, rows, lanes), params,
        ),
        2,
        (shape, shape),
        [],
        1 << 20,
    )


def solution(mesh):
    placed = (
        P("bead", "space", None, None),
        P("bead", "space", None, None),
        P("bead", "space", None, None),
        P("space", None),
        P("space"),
        P(),
        P(),
        P(),
    )
    return jax.shard_map(
        shards,
        mesh=mesh,
        in_specs=placed,
        out_specs=(P("bead", "space", None, None), P("bead", "space", None, None)),
        check_vma=False,
    )
```

```python
import functools

import jax
import jax.numpy as jnp
import numpy as np
from jax import lax
from jax.experimental import pallas as pl
from jax.experimental.pallas import tpu as pltpu
from jax.sharding import PartitionSpec as P

PC = 8
GY = 4
GZ = 4

TIME_STEP = 0.05
INVERSE_TEMP = 32.0
CENTROID_FRICTION = 1.0
INNER_CUT = 0.5
OUTER_CUT = 1.0
CUBE_ROOT_TWO = 2.0 ** (1.0 / 3.0)
F32 = jnp.float32
BF16 = jnp.bfloat16
SPAN = 32
GROUP = 4
STEPS = ((24, 4), (24, 2), (24, 1), (40, 2), (40, 1), (32, 2), (32, 1))
RUN_ROWS = {1: 24, 2: 40}
SPARE = 40
VMEM_LIMIT = 48 * 1024 * 1024


def mode_matrix(number):
    rows = np.arange(number, dtype=np.float64)[:, None]
    column = np.arange(number, dtype=np.float64)[None, :]
    phases = 2.0 * np.pi * rows * column / number
    factor = np.sqrt(2.0 / number)
    middle = np.cos(np.pi * rows) / np.sqrt(number)
    matrix = np.where(column < number / 2, factor * np.cos(phases), factor * np.sin(phases))
    matrix = np.where(column == number / 2, middle, matrix)
    return np.where(column == 0, 1.0 / np.sqrt(number), matrix)


def contract_matrix(full_count, reduced):
    selected = np.arange(reduced)
    selected = np.where(selected <= reduced // 2, selected, selected + full_count - reduced)
    chosen = mode_matrix(full_count)[:, selected]
    return np.sqrt(reduced / full_count) * (mode_matrix(reduced) @ chosen.T)


def step_matrices(number):
    index = np.arange(number, dtype=np.float64)
    frequency = 2.0 * (number / INVERSE_TEMP) * np.sin(np.pi * index / number)
    friction = np.where(index == 0, CENTROID_FRICTION, 2.0 * frequency)
    damping = np.exp(-friction * TIME_STEP)
    kicking = np.sqrt((1.0 - damping * damping) / INVERSE_TEMP)
    cosine = np.cos(frequency * TIME_STEP)
    sine = np.sin(frequency * TIME_STEP)
    drift = np.where(index == 0, TIME_STEP, sine / np.where(index == 0, 1.0, frequency))
    modes = mode_matrix(number)

    def over_beads(diagonal):
        return (modes * diagonal[None, :]) @ modes.T

    return np.array(
        [
            [over_beads(cosine), over_beads(drift * damping), over_beads(drift * kicking)],
            [
                over_beads(-frequency * sine),
                over_beads(cosine * damping),
                over_beads(cosine * kicking),
            ],
        ]
    )


def partner_lists(domain_cells):
    lists = []
    for one in range(domain_cells):
        near = []
        for two in range(domain_cells):
            step_y, step_z = two // GZ - one // GZ, two % GZ - one % GZ
            if abs(step_y) <= 1 and abs(step_z) <= 1:
                near.append((two, step_y, step_z))
        later = [entry for entry in near if entry[0] > one]
        lists.append(later + [(two + domain_cells, y, z) for two, y, z in near])
    starts = np.cumsum([0] + [len(entries) for entries in lists]).astype(np.int32)
    return starts, np.array([value for entries in lists for entry in entries for value in entry], np.int32)


def pair_weight(h, radius_sq, terms, longer):
    inverse = pl.reciprocal(h, approx=True)
    if longer:
        quotient = terms[1] * inverse
        twice = quotient * quotient * quotient
        outer = jnp.maximum(1.0 - radius_sq, 0.0)
        inner = jnp.maximum(1.0 - 4.0 * radius_sq, 0.0)
        switch = outer * outer - inner * inner
        slope = outer - 4.0 * inner
        return twice * ((twice - 1.0) * (3.0 * (switch * inverse) + slope) - slope)
    quotient = terms[1] * inverse
    twice = quotient * quotient * quotient
    edge = jnp.maximum(terms[2] * inverse - 1.0, 2.0)
    bracket = edge * (twice - 1.0) - twice
    return (twice * bracket) * ((edge - 2.0) * h)


def weight_factor(longer):
    return 4.0 if longer else 64.0 / 3.0


def atom_rows(block, cell):
    return [block[kind, pl.ds(cell, 1), :] for kind in range(3)]


def columns(block):
    few, lanes = block.shape
    return jnp.concatenate([block, jnp.zeros((8 - few, lanes), F32)], axis=0).T


def spread_rows(position, params, cell, rows_ref, size_ref):
    beads, lanes = position.shape[0], position.shape[-1]
    sizes = columns(jnp.concatenate(atom_rows(params, cell)[:2], axis=0))
    for kind in range(2):
        size_ref[cell, kind] = jnp.broadcast_to(sizes[:, kind : kind + 1], (lanes, lanes))
    for bead in range(beads):
        block = columns(jnp.concatenate(atom_rows(position.at[bead], cell), axis=0))
        for axis in range(3):
            rows_ref[cell, bead, axis] = jnp.broadcast_to(
                block[:, axis : axis + 1], (lanes, lanes)
            )


def meet(longer, cell, first, partners, refs):
    lanes_ref, sizes_ref, rows_ref, size_ref, total_ref, back_ref = refs
    beads, lanes = lanes_ref.shape[0], lanes_ref.shape[-1]
    here = pl.ds(first, SPAN)
    tall = (SPAN // 8, 8, lanes)
    row_half = size_ref[cell, 0, here, :].reshape(tall)
    row_root = size_ref[cell, 1, here, :].reshape(tall)
    known = []
    for partner, _, _ in partners:
        half = row_half + sizes_ref[partner, 0]
        s2 = half * half
        terms = (s2, CUBE_ROOT_TWO * s2, None if longer else 0.75 + 3.0 * s2)
        known.append((s2, terms, row_root * sizes_ref[partner, 1]))
    for bead in range(beads):
        rows = [rows_ref[cell, bead, axis, here, :].reshape(tall) for axis in range(3)]
        back = [None, None, None]
        for (partner, step_y, step_z), (s2, terms, depth) in zip(partners, known):
            apart = [
                lanes_ref[bead, partner, 0] - rows[0],
                (lanes_ref[bead, partner, 1] + step_y) - rows[1],
                (lanes_ref[bead, partner, 2] + step_z) - rows[2],
            ]
            radius_sq = apart[0] * apart[0] + apart[1] * apart[1] + apart[2] * apart[2]
            weight = depth * pair_weight(radius_sq + s2, radius_sq, terms, longer)
            for axis in range(3):
                push = weight * apart[axis]
                back[axis] = push if back[axis] is None else back[axis] + push
                if total_ref is not None:
                    total_ref[partner, bead, axis] += jnp.sum(push, axis=0)
        for axis in range(3):
            value = back[axis].reshape(SPAN, lanes)
            if total_ref is None:
                back_ref[cell, bead, axis, here, :] = value
            else:
                back_ref[cell, bead, axis, here, :] += value


def repeat_lanes(position, params, next_position, next_params, lanes_ref, sizes_ref):
    beads, _, cells, lanes = position.shape

    def per_cell(cell, carry):
        for layer, place, values in ((0, position, params), (1, next_position, next_params)):
            for kind in range(2):
                sizes_ref[layer * cells + cell, kind] = jnp.broadcast_to(
                    values[kind, pl.ds(cell, 1), :], (8, lanes)
                )
            for bead in range(beads):
                for axis in range(3):
                    row = place[bead, axis, pl.ds(cell, 1), :]
                    row = row + 1.0 if layer == 1 and axis == 0 else row
                    lanes_ref[bead, layer * cells + cell, axis] = jnp.broadcast_to(row, (8, lanes))
        return carry

    lax.fori_loop(0, cells, per_cell, 0)


def fold_back(back_ref, cell, bead):
    lanes = back_ref.shape[-1]
    column = lax.broadcasted_iota(jnp.int32, (lanes, 8), 1)
    sums = [jnp.sum(back_ref[cell, bead, axis], axis=1, keepdims=True) for axis in range(3)]
    block = jnp.where(
        column == 0, sums[0], jnp.where(column == 1, sums[1], jnp.where(column == 2, sums[2], 0.0))
    )
    return block.T[0:3]


def put_rows(out_ref, bead, cell, block):
    for axis in range(3):
        out_ref[bead, axis, pl.ds(cell, 1), :] = block[axis : axis + 1]


def fold_total(total_ref, cell, bead):
    return jnp.concatenate(
        [jnp.sum(total_ref[cell, bead, axis], axis=0, keepdims=True) for axis in range(3)], axis=0
    )


def pairs_kernel(
    longer, plan, occupied, position, params, next_position, next_params,
    force_ref, other_ref, lanes_ref, sizes_ref, rows_ref, size_ref, total_ref, back_ref,
):
    beads, _, cells, lanes = position.shape
    factor = weight_factor(longer)
    together = max(1, 4 // beads)
    repeat_lanes(position, params, next_position, next_params, lanes_ref, sizes_ref)
    total_ref[...] = jnp.zeros_like(total_ref)

    def spread(index, carry):
        for shift in range(together):
            spread_rows(position, params, index * together + shift, rows_ref, size_ref)
        return carry

    lax.fori_loop(0, cells // together, spread, 0)
    refs = (lanes_ref, sizes_ref, rows_ref, size_ref)

    def entry_of(entry):
        return (
            plan[cells + 1 + 3 * entry],
            plan[cells + 2 + 3 * entry].astype(F32),
            plan[cells + 3 + 3 * entry].astype(F32),
        )

    def per_cell(cell, carry):
        begin, end = plan[cell], plan[cell + 1]
        odd = lax.rem(end - begin, 2)

        most = lanes // SPAN
        needed = lax.div(occupied[cell] + (SPAN - 1), SPAN)
        for parts in (most - 1, most):
            firsts = [part * SPAN for part in range(parts)]

            def all_rows(_, carry, firsts=firsts):
                for first in firsts:
                    meet(longer, cell, first, [(cell, 0.0, 0.0)], refs + (None, back_ref))

                def single(entry, carry):
                    for first in firsts:
                        meet(longer, cell, first, [entry_of(entry)], refs + (total_ref, back_ref))
                    return carry

                def double(step, carry):
                    entry = begin + odd + 2 * step
                    both = [entry_of(entry), entry_of(entry + 1)]
                    for first in firsts:
                        meet(longer, cell, first, both, refs + (total_ref, back_ref))
                    return carry

                carry = lax.fori_loop(begin, begin + odd, single, carry)
                return lax.fori_loop(0, lax.div(end - begin, 2), double, carry)

            full = (needed == most).astype(jnp.int32)
            lax.fori_loop(0, full if parts == most else 1 - full, all_rows, 0)
        return carry

    lax.fori_loop(0, cells, per_cell, 0)

    def finish(index, carry):
        for shift in range(together):
            cell = index * together + shift
            alive = params[1, pl.ds(cell, 1), :] > 0.0
            for bead in range(beads):
                total = fold_total(total_ref, cell, bead) - fold_back(back_ref, cell, bead)
                put_rows(force_ref, bead, cell, jnp.where(alive, factor * total, 0.0))
                put_rows(other_ref, bead, cell, factor * fold_total(total_ref, cell + cells, bead))
        return carry

    lax.fori_loop(0, cells // together, finish, 0)


def octant_key(x, y, z, alive):
    zed = jnp.where(z >= 0.5, 1.0, 0.0)
    gray = jnp.where(y >= 0.5, 3.0 - zed, zed)
    return jnp.where(alive, jnp.where(x >= 0.5, 7.0 - gray, gray), 8.0)


def reach_lists(domain_cells):
    octants = []
    for bit_x in range(2):
        for bit_y in range(2):
            for bit_z in range(2):
                gray = 3 - bit_z if bit_y else bit_z
                octants.append((7 - gray if bit_x else gray, (bit_x, bit_y, bit_z)))
    classes = [[[] for _ in range(domain_cells)] for _ in STEPS]
    for one in range(domain_cells):
        runs = {}
        for layer in range(2):
            for two in range(domain_cells):
                step = (layer, two // GZ - one // GZ, two % GZ - one % GZ)
                if abs(step[1]) > 1 or abs(step[2]) > 1 or (layer == 0 and two <= one):
                    continue
                keys = [
                    key
                    for key, bits in octants
                    if all(move == 0 or bit == (move > 0) for move, bit in zip(step, bits))
                ]
                entry = (two + layer * domain_cells, step[1], step[2], min(keys), max(keys) + 1)
                runs.setdefault(entry[4] - entry[3], []).append(entry)
        for length, entries in sorted(runs.items()):
            entries.sort(key=lambda entry: entry[3:])
            span = RUN_ROWS.get(length, SPAN)
            for place, (rows, count) in enumerate(STEPS):
                if rows == span:
                    whole = len(entries) // count * count
                    classes[place][one] += entries[:whole]
                    entries = entries[whole:]
    starts, values = [], []
    for lists in classes:
        for entries in lists:
            starts.append(len(values) // 5)
            values += [value for entry in entries for value in entry]
        starts.append(len(values) // 5)
    return np.array(starts, np.int32), np.array(values, np.int32)


def split_three(value):
    high = value.astype(BF16).astype(F32)
    rest = value - high
    middle = rest.astype(BF16).astype(F32)
    return high, middle, rest - middle


def order_kernel(position, params, out_ref):
    beads, _, cells, lanes = position.shape
    row = lax.broadcasted_iota(jnp.int32, (lanes, lanes), 0)
    column = lax.broadcasted_iota(jnp.int32, (lanes, lanes), 1)
    before = jnp.where(row < column, 1.0, 0.0).astype(BF16)
    counter = jnp.concatenate([before, jnp.ones((lanes, lanes), BF16)], axis=0)
    kind = lax.broadcasted_iota(jnp.int32, (16, lanes), 0).astype(F32)
    place_row = row.astype(F32)

    def per_cell(index, carry):
        for shift, bead in [(shift, bead) for shift in range(GROUP) for bead in range(beads)]:
            cell = index * GROUP + shift
            sizes = atom_rows(params, cell)[:2]
            place = atom_rows(position.at[bead], cell)
            key = octant_key(*place, sizes[1] > 0.0)
            same = jnp.where(key == kind, 1.0, 0.0)
            less = jnp.where(key < kind, 1.0, 0.0)
            counts = lax.dot_general(
                jnp.concatenate([same, less], axis=1).astype(BF16),
                counter,
                (((1,), (0,)), ((), ())),
                preferred_element_type=F32,
            )
            rank = jnp.sum(same * counts, axis=0, keepdims=True)
            chosen = jnp.where(rank == place_row, 1.0, 0.0).astype(BF16)
            block = jnp.concatenate([*place, *sizes, jnp.zeros((3, lanes), F32)], axis=0)
            moved = lax.dot_general(
                jnp.concatenate(split_three(block), axis=0).astype(BF16),
                chosen,
                (((1,), (1,)), ((), ())),
                preferred_element_type=F32,
            )
            out_ref[bead, cell, 0:5, :] = (moved[0:8] + moved[8:16] + moved[16:24])[0:5]
            out_ref[bead, cell, 5:6, :] = rank
            out_ref[bead, cell, 6:8, :] = jnp.zeros((2, lanes), F32)
        return carry

    lax.fori_loop(0, cells // GROUP, per_cell, 0)


def meet_runs(span, local, runs, lanes_ref, sizes_ref, rows_ref, total_ref, back_ref):
    beads, lanes = lanes_ref.shape[0], lanes_ref.shape[-1]
    for bead in range(beads):
        for firsts, partner, step_y, step_z in runs:
            here = pl.ds(firsts[bead], span)
            rows = [
                rows_ref[local, bead, kind, here, :].reshape(span // 8, 8, lanes)
                for kind in range(5)
            ]
            half = rows[3] + sizes_ref[partner, 0]
            s2 = half * half
            terms = (s2, CUBE_ROOT_TWO * s2, 0.75 + 3.0 * s2)
            apart = [
                lanes_ref[bead, partner, 0] - rows[0],
                (lanes_ref[bead, partner, 1] + step_y) - rows[1],
                (lanes_ref[bead, partner, 2] + step_z) - rows[2],
            ]
            radius_sq = apart[0] * apart[0] + apart[1] * apart[1] + apart[2] * apart[2]
            depth = rows[4] * sizes_ref[partner, 1]
            weight = depth * pair_weight(radius_sq + s2, radius_sq, terms, False)
            for axis in range(3):
                push = weight * apart[axis]
                flat_push = push.reshape(span, lanes)
                if total_ref is None:
                    back_ref[local, bead, axis, here, :] = flat_push
                else:
                    back_ref[local, bead, axis, here, :] += flat_push
                    total_ref[partner, bead, axis] += jnp.sum(push, axis=0)


def reach_kernel(
    plan, position, params, next_position, next_params, ordered, force_ref, other_ref, lanes_ref,
    sizes_ref, rows_ref, total_ref, back_ref,
):
    beads, _, cells, lanes = position.shape
    entries_at = len(STEPS) * (cells + 1)
    bounds_at = plan.shape[0] - beads * cells * 9
    factor = weight_factor(False)
    repeat_lanes(position, params, next_position, next_params, lanes_ref, sizes_ref)
    total_ref[...] = jnp.zeros_like(total_ref)
    rows_ref[:, :, :, lanes:, :] = jnp.zeros((GROUP, beads, 5, SPARE, lanes), F32)
    row = lax.broadcasted_iota(jnp.int32, (lanes, lanes), 0).astype(F32)
    slot = lax.broadcasted_iota(jnp.int32, (8, lanes), 1)
    column = lax.broadcasted_iota(jnp.int32, (lanes, 8), 1)
    refs = (lanes_ref, sizes_ref, rows_ref)
    every = [(local, bead) for local in range(GROUP) for bead in range(beads)]

    def per_group(group, carry):
        for local, bead in every:
            block = ordered[bead, group * GROUP + local].T
            for axis in range(5):
                rows_ref[local, bead, axis, 0:lanes, :] = jnp.broadcast_to(
                    block[:, axis : axis + 1], (lanes, lanes)
                )

        def per_cell(local, carry):
            cell = group * GROUP + local

            def bound(bead, octant):
                return plan[bounds_at + (bead * cells + cell) * 9 + octant]

            def itself(index, carry):
                first = pl.multiple_of(index * SPAN, SPAN)
                run = ([first] * beads, cell, 0.0, 0.0)
                meet_runs(SPAN, local, [run], *refs, None, back_ref)
                return carry

            lax.fori_loop(0, lax.div(bound(0, 8) + (SPAN - 1), SPAN), itself, 0)

            for place, (span, count) in enumerate(STEPS):
                begin = plan[place * (cells + 1) + cell]
                end = plan[place * (cells + 1) + cell + 1]

                def per_step(step, carry, span=span, count=count, begin=begin):
                    runs, longest = [], 0
                    for shift in range(count):
                        at = entries_at + 5 * (begin + step * count + shift)
                        begins = [
                            lax.bitwise_and(bound(bead, plan[at + 3]), -8) for bead in range(beads)
                        ]
                        for bead in range(beads):
                            longest = jnp.maximum(longest, bound(bead, plan[at + 4]) - begins[bead])
                        runs.append(
                            (begins, plan[at], plan[at + 1].astype(F32), plan[at + 2].astype(F32))
                        )

                    def per_span(index, carry):
                        moved = [
                            (
                                [
                                    pl.multiple_of(jnp.minimum(first + index * span, lanes), 8)
                                    for first in begins
                                ],
                                *rest,
                            )
                            for begins, *rest in runs
                        ]
                        meet_runs(span, local, moved, *refs, total_ref, back_ref)
                        return carry

                    return lax.fori_loop(0, lax.div(longest + (span - 1), span), per_span, carry)

                lax.fori_loop(0, lax.div(end - begin, count), per_step, 0)
            return carry

        lax.fori_loop(0, GROUP, per_cell, 0)

        for local, bead in every:
            cell = group * GROUP + local
            alive = plan[bounds_at + cell * 9 + 8]
            sums = [
                jnp.sum(back_ref[local, bead, axis, 0:lanes, :], axis=1, keepdims=True)
                for axis in range(3)
            ]
            block = jnp.where(
                column == 0,
                sums[0],
                jnp.where(column == 1, sums[1], jnp.where(column == 2, sums[2], 0.0)),
            ).T
            block = jnp.where(slot < alive, block, 0.0)
            chosen = jnp.where(ordered[bead, cell, 5:6, :] == row, 1.0, 0.0).astype(BF16)
            moved = lax.dot_general(
                jnp.concatenate(split_three(block), axis=0).astype(BF16),
                chosen,
                (((1,), (0,)), ((), ())),
                preferred_element_type=F32,
            )
            put_rows(force_ref, bead, cell, (moved[0:8] + moved[8:16] + moved[16:24])[0:3])
        return carry

    lax.fori_loop(0, cells // GROUP, per_group, 0)

    def finish(index, carry):
        for shift, bead in every:
            cell = index * GROUP + shift
            held = jnp.concatenate(atom_rows(force_ref.at[bead], cell), axis=0)
            put_rows(force_ref, bead, cell, factor * (fold_total(total_ref, cell, bead) - held))
            put_rows(other_ref, bead, cell, factor * fold_total(total_ref, cell + cells, bead))
        return carry

    lax.fori_loop(0, cells // GROUP, finish, 0)


def short_forces(position, params, next_position, next_params, ordered, bounds):
    beads, _, cells, lanes = position.shape
    starts, entries = reach_lists(cells)
    plan = jnp.concatenate([jnp.asarray(starts), jnp.asarray(entries), bounds])
    forces = jax.ShapeDtypeStruct((beads, 3, cells, lanes), F32)
    return call(
        reach_kernel,
        (plan, position, params, next_position, next_params, ordered),
        1,
        (forces, forces),
        [
            pltpu.VMEM((beads, 2 * cells, 3, 8, lanes), F32),
            pltpu.VMEM((2 * cells, 2, 8, lanes), F32),
            pltpu.VMEM((GROUP, beads, 5, lanes + SPARE, lanes), F32),
            pltpu.VMEM((2 * cells, beads, 3, 8, lanes), F32),
            pltpu.VMEM((GROUP, beads, 3, lanes + SPARE, lanes), F32),
        ],
        PAIR_FLOPS * beads * 70,
    )


def call(kernel, inputs, smem, outputs, scratch, flops):
    return pl.pallas_call(
        kernel,
        out_shape=outputs,
        in_specs=[
            pl.BlockSpec(memory_space=pltpu.SMEM if place < smem else pltpu.VMEM)
            for place in range(len(inputs))
        ],
        scratch_shapes=scratch,
        compiler_params=pltpu.CompilerParams(vmem_limit_bytes=VMEM_LIMIT),
        cost_estimate=pl.CostEstimate(flops=flops, bytes_accessed=1 << 18, transcendentals=0),
    )(*inputs)


PAIR_FLOPS = 40 * 128 * 128


def pair_forces(position, params, occupied, next_position, next_params, longer):
    beads, _, cells, lanes = position.shape
    starts, entries = partner_lists(cells)
    forces = jax.ShapeDtypeStruct((beads, 3, cells, lanes), F32)
    return call(
        functools.partial(pairs_kernel, longer),
        (
            jnp.asarray(np.concatenate([starts, entries])), occupied, position, params,
            next_position, next_params,
        ),
        2,
        (forces, forces),
        [
            pltpu.VMEM((beads, 2 * cells, 3, 8, lanes), F32),
            pltpu.VMEM((2 * cells, 2, 8, lanes), F32),
            pltpu.VMEM((cells, beads, 3, lanes, lanes), F32),
            pltpu.VMEM((cells, 2, lanes, lanes), F32),
            pltpu.VMEM((2 * cells, beads, 3, 8, lanes), F32),
            pltpu.VMEM((cells, beads, 3, lanes, lanes), F32),
        ],
        PAIR_FLOPS * beads * (len(entries) // 3 + cells),
    )


def kick_kernel(
    piece_rows, groups, table, rank, position, momenta, noise, force, back, params, partial_ref,
    piece_ref, flat_ref,
):
    beads, rows, _ = position.shape
    holders = piece_ref.shape[0]
    reduced = table.shape[0]
    first = rank[0] * beads
    if holders * piece_rows > rows:
        piece_ref[...] = jnp.zeros_like(piece_ref)
    mass = params[2]
    per_root = lax.rsqrt(mass)
    per_root = per_root * (1.5 - 0.5 * mass * per_root * per_root)
    per_mass = jnp.concatenate([1.0 / mass] * 3, axis=0)
    per_root = jnp.concatenate([per_root] * 3, axis=0)
    for bead in range(beads):
        kicked = momenta[bead] + 0.5 * TIME_STEP * (force[bead] + back[bead])
        flat_ref[0, bead] = position[bead]
        flat_ref[1, bead] = kicked * per_mass
        flat_ref[2, bead] = noise[bead] * per_root
    for kind in range(3):
        for bead in range(beads):
            base = (kind * beads + bead) * piece_rows
            for owner in range(holders):
                start = owner * piece_rows
                count = min(piece_rows, rows - start)
                if count > 0:
                    piece_ref[owner, base : base + count, :] = flat_ref[
                        kind, bead, start : start + count, :
                    ]
    for group in range(reduced):
        total = None
        for kind in range(3):
            for bead in range(beads):
                term = table[group, kind * holders * beads + first + bead] * flat_ref[kind, bead]
                total = term if total is None else total + term
        for copy in range(groups):
            partial_ref[group * groups + copy] = total


def move_kernel(piece_rows, beads, matrix, arrived, out_ref, gathered):
    holders = arrived.shape[0]
    taken = 3 * beads
    given = 2 * beads
    for row in range(piece_rows):
        for holder in range(holders):
            gathered[row, holder * taken : (holder + 1) * taken, :] = arrived[
                holder, pl.ds(row, taken, stride=piece_rows), :
            ]
        moved = lax.dot_general(
            matrix[...],
            gathered[row],
            (((1,), (0,)), ((), ())),
            precision=lax.Precision.HIGHEST,
            preferred_element_type=F32,
        )
        for holder in range(holders):
            out_ref[holder, row * given : (row + 1) * given, :] = moved[
                holder * given : (holder + 1) * given
            ]


def finish_kernel(
    piece_rows, groups, table, rank, moved, slow, params, position_ref, momentum_ref, velocity_ref
):
    beads, rows, _ = position_ref.shape
    holders = moved.shape[0]
    given = 2 * beads
    reduced = table.shape[0]
    first = 3 * holders * beads + rank[0] * beads
    mass = jnp.concatenate([params[2]] * 3, axis=0)
    for bead in range(beads):
        for owner in range(holders):
            start = owner * piece_rows
            count = min(piece_rows, rows - start)
            if count > 0:
                position_ref[bead, start : start + count, :] = moved[
                    owner, pl.ds(bead, count, stride=given), :
                ]
                velocity_ref[bead, start : start + count, :] = moved[
                    owner, pl.ds(beads + bead, count, stride=given), :
                ]
    for bead in range(beads):
        total = mass * velocity_ref[bead]
        for group in range(reduced):
            total = total + table[group, first + bead] * slow[group * groups]
        momentum_ref[bead] = total


def shards(positions, momenta, noise, atom_types, occupancy, type_sigma, type_eps, type_mass):
    beads, cells, _, lanes = positions.shape
    holders = lax.axis_size("bead")
    domains = lax.axis_size("space")
    rank = lax.axis_index("bead")
    total_beads = beads * holders
    rows = 3 * cells
    piece_rows = -(-rows // holders)
    held = max(1, PC // holders)
    groups = max(1, holders // PC)
    contract = contract_matrix(total_beads, PC)
    steps = step_matrices(total_beads)
    rank_table = rank.astype(jnp.int32).reshape(1)
    one_back = [((i + 1) % domains, i) for i in range(domains)]
    one_on = [(i, (i + 1) % domains) for i in range(domains)]

    codes = jnp.arange(type_sigma.shape[0])
    onehot = atom_types[..., None] == codes
    living = jnp.arange(lanes)[None, :] < occupancy[:, None]
    half_sigma = 0.5 * jnp.sum(jnp.where(onehot, type_sigma, 0.0), -1)
    root_eps = jnp.sqrt(jnp.sum(jnp.where(onehot, type_eps, 0.0), -1))
    mass = jnp.sum(jnp.where(onehot, type_mass, 0.0), -1)
    params = jnp.stack([half_sigma, jnp.where(living, root_eps, 0.0), mass], 0)
    positions, momenta, noise = (
        value.transpose(0, 2, 1, 3) for value in (positions, momenta, noise)
    )

    stacked = jnp.concatenate([positions, params[None]], 0)
    next_stacked = lax.ppermute(stacked, "space", one_back)
    next_params = next_stacked[beads]
    ordered = call(
        order_kernel,
        (positions, params),
        0,
        jax.ShapeDtypeStruct((beads, cells, 8, lanes), F32),
        [],
        1 << 22,
    )
    key = octant_key(positions[:, 0], positions[:, 1], positions[:, 2], living[None])
    bounds = jnp.sum(
        (key[:, :, None, :] < jnp.arange(9, dtype=F32)[:, None]).astype(jnp.int32), -1
    )
    force, back = short_forces(
        positions, params, next_stacked[:beads], next_params, ordered, bounds.reshape(-1)
    )
    back = lax.ppermute(back, "space", one_on)

    spread = 0.5 * TIME_STEP * (total_beads / PC) * contract
    table = np.concatenate([contract @ steps[0, kind] for kind in range(3)] + [spread], axis=1)
    table = jnp.asarray(table, F32)

    def flat(value):
        return value.reshape(-1, rows, lanes)

    partial, pieces = call(
        functools.partial(kick_kernel, piece_rows, groups),
        (
            table, rank_table, flat(positions), flat(momenta), flat(noise), flat(force), flat(back),
            params,
        ),
        2,
        (
            jax.ShapeDtypeStruct((PC * groups, rows, lanes), F32),
            jax.ShapeDtypeStruct((holders, 3 * beads * piece_rows, lanes), F32),
        ),
        [pltpu.VMEM((3, beads, rows, lanes), F32)],
        1 << 22,
    )
    arrived = lax.all_to_all(
        partial.reshape(holders, held * rows, lanes), "bead", split_axis=0, concat_axis=0, tiled=True
    )
    contracted = jnp.sum(arrived, 0).reshape(held, 3, cells, lanes)
    next_contracted = lax.ppermute(contracted, "space", one_back)
    pieces = lax.all_to_all(pieces, "bead", split_axis=0, concat_axis=0, tiled=True)
    slow, slow_back = pair_forces(
        contracted, params, occupancy, next_contracted, next_params, True
    )
    slow = slow + lax.ppermute(slow_back, "space", one_on)

    order = steps.reshape(2, 3, holders, beads, holders, beads).transpose(2, 0, 3, 4, 1, 5)
    order = order.reshape(2 * total_beads, 3 * total_beads)
    moved = call(
        functools.partial(move_kernel, piece_rows, beads),
        (jnp.asarray(order, F32), pieces),
        0,
        jax.ShapeDtypeStruct((holders, 2 * beads * piece_rows, lanes), F32),
        [pltpu.VMEM((piece_rows, 3 * total_beads, lanes), F32)],
        1 << 23,
    )
    moved_rows = 2 * beads * piece_rows
    sent = jnp.concatenate(
        [
            moved,
            jnp.broadcast_to(slow.reshape(1, held * rows, lanes), (holders, held * rows, lanes)),
        ],
        1,
    )
    got = lax.all_to_all(sent, "bead", split_axis=0, concat_axis=0, tiled=True)
    result = jax.ShapeDtypeStruct((beads, rows, lanes), F32)
    new_positions, new_momenta = call(
        functools.partial(finish_kernel, piece_rows, groups),
        (
            table, rank_table, got[:, :moved_rows],
            got[:, moved_rows:].reshape(holders * held, rows, lanes), params,
        ),
        2,
        (result, result),
        [pltpu.VMEM((beads, rows, lanes), F32)],
        1 << 20,
    )

    def cells_first(value):
        return value.reshape(beads, 3, cells, lanes).transpose(0, 2, 1, 3)

    return cells_first(new_positions), cells_first(new_momenta)


def solution(mesh):
    placed = (
        P("bead", "space", None, None),
        P("bead", "space", None, None),
        P("bead", "space", None, None),
        P("space", None),
        P("space"),
        P(),
        P(),
        P(),
    )
    return jax.shard_map(
        shards,
        mesh=mesh,
        in_specs=placed,
        out_specs=(P("bead", "space", None, None), P("bead", "space", None, None)),
        check_vma=False,
    )
```

```python
import functools

import jax
import jax.numpy as jnp
import numpy as np
from jax import lax
from jax.experimental import pallas as pl
from jax.experimental.pallas import tpu as pltpu
from jax.sharding import PartitionSpec as P

PC = 8
GY = 4
GZ = 4

TIME_STEP = 0.05
INVERSE_TEMP = 32.0
CENTROID_FRICTION = 1.0
INNER_CUT = 0.5
OUTER_CUT = 1.0
CUBE_ROOT_TWO = 2.0 ** (1.0 / 3.0)
F32 = jnp.float32
BF16 = jnp.bfloat16
SPAN = 32
GROUP = 4
STEPS = ((24, 4), (24, 2), (24, 1), (40, 2), (40, 1), (32, 2), (32, 1))
RUN_ROWS = {1: 24, 2: 40}
SPARE = 40
LEAST_LIVE = 64
VMEM_LIMIT = 48 * 1024 * 1024


def mode_matrix(number):
    rows = np.arange(number, dtype=np.float64)[:, None]
    column = np.arange(number, dtype=np.float64)[None, :]
    phases = 2.0 * np.pi * rows * column / number
    factor = np.sqrt(2.0 / number)
    middle = np.cos(np.pi * rows) / np.sqrt(number)
    matrix = np.where(column < number / 2, factor * np.cos(phases), factor * np.sin(phases))
    matrix = np.where(column == number / 2, middle, matrix)
    return np.where(column == 0, 1.0 / np.sqrt(number), matrix)


def contract_matrix(full_count, reduced):
    selected = np.arange(reduced)
    selected = np.where(selected <= reduced // 2, selected, selected + full_count - reduced)
    chosen = mode_matrix(full_count)[:, selected]
    return np.sqrt(reduced / full_count) * (mode_matrix(reduced) @ chosen.T)


def step_matrices(number):
    index = np.arange(number, dtype=np.float64)
    frequency = 2.0 * (number / INVERSE_TEMP) * np.sin(np.pi * index / number)
    friction = np.where(index == 0, CENTROID_FRICTION, 2.0 * frequency)
    damping = np.exp(-friction * TIME_STEP)
    kicking = np.sqrt((1.0 - damping * damping) / INVERSE_TEMP)
    cosine = np.cos(frequency * TIME_STEP)
    sine = np.sin(frequency * TIME_STEP)
    drift = np.where(index == 0, TIME_STEP, sine / np.where(index == 0, 1.0, frequency))
    modes = mode_matrix(number)

    def over_beads(diagonal):
        return (modes * diagonal[None, :]) @ modes.T

    return np.array(
        [
            [over_beads(cosine), over_beads(drift * damping), over_beads(drift * kicking)],
            [
                over_beads(-frequency * sine),
                over_beads(cosine * damping),
                over_beads(cosine * kicking),
            ],
        ]
    )


def partner_lists(domain_cells):
    lists = []
    for one in range(domain_cells):
        near = []
        for two in range(domain_cells):
            step_y, step_z = two // GZ - one // GZ, two % GZ - one % GZ
            if abs(step_y) <= 1 and abs(step_z) <= 1:
                near.append((two, step_y, step_z))
        later = [entry for entry in near if entry[0] > one]
        lists.append(later + [(two + domain_cells, y, z) for two, y, z in near])
    starts = np.cumsum([0] + [len(entries) for entries in lists]).astype(np.int32)
    return starts, np.array([value for entries in lists for entry in entries for value in entry], np.int32)


def long_weight(h, radius_sq, s2):
    inverse = pl.reciprocal(h, approx=True)
    quotient = (CUBE_ROOT_TWO * s2) * inverse
    twice = quotient * quotient * quotient
    outer = jnp.maximum(1.0 - radius_sq, 0.0)
    inner = jnp.maximum(1.0 - 4.0 * radius_sq, 0.0)
    switch = outer * outer - inner * inner
    slope = outer - 4.0 * inner
    return twice * ((twice - 1.0) * (3.0 * (switch * inverse) + slope) - slope)


def short_weight(h, s2):
    inverse = pl.reciprocal(h, approx=True)
    quotient = s2 * inverse
    sixth = quotient * quotient * quotient
    lifted = jnp.maximum((quotient + inverse) - 2.0 / 3.0, 1.0 / 3.0)
    bracket = (sixth - 0.5) * lifted - 1.0 / 6.0
    return (sixth * bracket) * ((lifted - 1.0 / 3.0) * h)


LONG_FACTOR = 4.0
SHORT_SCALE = 1.0 / INNER_CUT
SHORT_FACTOR = 192.0 / SHORT_SCALE


def atom_rows(block, cell):
    return [block[kind, pl.ds(cell, 1), :] for kind in range(3)]


def columns(block):
    few, lanes = block.shape
    return jnp.concatenate([block, jnp.zeros((8 - few, lanes), F32)], axis=0).T


def spread_rows(position, params, cell, rows_ref, size_ref):
    beads, lanes = position.shape[0], position.shape[-1]
    sizes = columns(jnp.concatenate(atom_rows(params, cell)[:2], axis=0))
    for kind in range(2):
        size_ref[cell, kind] = jnp.broadcast_to(sizes[:, kind : kind + 1], (lanes, lanes))
    for bead in range(beads):
        block = columns(jnp.concatenate(atom_rows(position.at[bead], cell), axis=0))
        for axis in range(3):
            rows_ref[cell, bead, axis] = jnp.broadcast_to(
                block[:, axis : axis + 1], (lanes, lanes)
            )


def meet(cell, first, partners, refs):
    lanes_ref, sizes_ref, rows_ref, size_ref, total_ref, back_ref = refs
    beads, lanes = lanes_ref.shape[0], lanes_ref.shape[-1]
    here = pl.ds(first, SPAN)
    tall = (SPAN // 8, 8, lanes)
    row_half = size_ref[cell, 0, here, :].reshape(tall)
    row_root = size_ref[cell, 1, here, :].reshape(tall)
    known = []
    for partner, _, _ in partners:
        half = row_half + sizes_ref[partner, 0]
        s2 = half * half
        known.append((s2, row_root * sizes_ref[partner, 1]))
    for bead in range(beads):
        rows = [rows_ref[cell, bead, axis, here, :].reshape(tall) for axis in range(3)]
        back = [None, None, None]
        for (partner, step_y, step_z), (s2, depth) in zip(partners, known):
            apart = [
                lanes_ref[bead, partner, 0] - rows[0],
                (lanes_ref[bead, partner, 1] + step_y) - rows[1],
                (lanes_ref[bead, partner, 2] + step_z) - rows[2],
            ]
            radius_sq = apart[0] * apart[0] + apart[1] * apart[1] + apart[2] * apart[2]
            weight = depth * long_weight(radius_sq + s2, radius_sq, s2)
            for axis in range(3):
                push = weight * apart[axis]
                back[axis] = push if back[axis] is None else back[axis] + push
                if total_ref is not None:
                    total_ref[partner, bead, axis] += jnp.sum(push, axis=0)
        for axis in range(3):
            value = back[axis].reshape(SPAN, lanes)
            if total_ref is None:
                back_ref[cell, bead, axis, here, :] = value
            else:
                back_ref[cell, bead, axis, here, :] += value


def repeat_lanes(scale, position, params, next_position, next_params, lanes_ref, sizes_ref):
    beads, _, cells, lanes = position.shape

    def per_cell(cell, carry):
        for layer, place, values in ((0, position, params), (1, next_position, next_params)):
            for kind in range(2):
                row = values[kind, pl.ds(cell, 1), :]
                row = scale * row if kind == 0 else row
                sizes_ref[layer * cells + cell, kind] = jnp.broadcast_to(row, (8, lanes))
            for bead in range(beads):
                for axis in range(3):
                    row = place[bead, axis, pl.ds(cell, 1), :]
                    row = scale * (row + 1.0 if layer == 1 and axis == 0 else row)
                    lanes_ref[bead, layer * cells + cell, axis] = jnp.broadcast_to(row, (8, lanes))
        return carry

    lax.fori_loop(0, cells, per_cell, 0)


def fold_back(back_ref, cell, bead):
    lanes = back_ref.shape[-1]
    column = lax.broadcasted_iota(jnp.int32, (lanes, 8), 1)
    sums = [jnp.sum(back_ref[cell, bead, axis], axis=1, keepdims=True) for axis in range(3)]
    block = jnp.where(
        column == 0, sums[0], jnp.where(column == 1, sums[1], jnp.where(column == 2, sums[2], 0.0))
    )
    return block.T[0:3]


def put_rows(out_ref, bead, cell, block):
    for axis in range(3):
        out_ref[bead, axis, pl.ds(cell, 1), :] = block[axis : axis + 1]


def fold_total(total_ref, cell, bead):
    return jnp.concatenate(
        [jnp.sum(total_ref[cell, bead, axis], axis=0, keepdims=True) for axis in range(3)], axis=0
    )


def pairs_kernel(
    plan, occupied, position, params, next_position, next_params,
    force_ref, other_ref, lanes_ref, sizes_ref, rows_ref, size_ref, total_ref, back_ref,
):
    beads, _, cells, lanes = position.shape
    factor = LONG_FACTOR
    together = max(1, 4 // beads)
    repeat_lanes(1.0, position, params, next_position, next_params, lanes_ref, sizes_ref)
    total_ref[...] = jnp.zeros_like(total_ref)

    def spread(index, carry):
        for shift in range(together):
            spread_rows(position, params, index * together + shift, rows_ref, size_ref)
        return carry

    lax.fori_loop(0, cells // together, spread, 0)
    refs = (lanes_ref, sizes_ref, rows_ref, size_ref)

    def entry_of(entry):
        return (
            plan[cells + 1 + 3 * entry],
            plan[cells + 2 + 3 * entry].astype(F32),
            plan[cells + 3 + 3 * entry].astype(F32),
        )

    def per_cell(cell, carry):
        begin, end = plan[cell], plan[cell + 1]
        odd = lax.rem(end - begin, 2)

        most = lanes // SPAN
        needed = lax.div(occupied[cell] + (SPAN - 1), SPAN)
        for parts in (most - 1, most):
            firsts = [part * SPAN for part in range(parts)]

            def all_rows(_, carry, firsts=firsts):
                for first in firsts:
                    meet(cell, first, [(cell, 0.0, 0.0)], refs + (None, back_ref))

                def single(entry, carry):
                    for first in firsts:
                        meet(cell, first, [entry_of(entry)], refs + (total_ref, back_ref))
                    return carry

                def double(step, carry):
                    entry = begin + odd + 2 * step
                    both = [entry_of(entry), entry_of(entry + 1)]
                    for first in firsts:
                        meet(cell, first, both, refs + (total_ref, back_ref))
                    return carry

                carry = lax.fori_loop(begin, begin + odd, single, carry)
                return lax.fori_loop(0, lax.div(end - begin, 2), double, carry)

            full = (needed == most).astype(jnp.int32)
            lax.fori_loop(0, full if parts == most else 1 - full, all_rows, 0)
        return carry

    lax.fori_loop(0, cells, per_cell, 0)

    def finish(index, carry):
        for shift in range(together):
            cell = index * together + shift
            alive = params[1, pl.ds(cell, 1), :] > 0.0
            for bead in range(beads):
                total = fold_total(total_ref, cell, bead) - fold_back(back_ref, cell, bead)
                put_rows(force_ref, bead, cell, jnp.where(alive, factor * total, 0.0))
                put_rows(other_ref, bead, cell, factor * fold_total(total_ref, cell + cells, bead))
        return carry

    lax.fori_loop(0, cells // together, finish, 0)


def octant_key(x, y, z, alive):
    zed = jnp.where(z >= 0.5, 1.0, 0.0)
    gray = jnp.where(y >= 0.5, 3.0 - zed, zed)
    return jnp.where(alive, jnp.where(x >= 0.5, 7.0 - gray, gray), 8.0)


def reach_lists(domain_cells):
    octants = []
    for bit_x in range(2):
        for bit_y in range(2):
            for bit_z in range(2):
                gray = 3 - bit_z if bit_y else bit_z
                octants.append((7 - gray if bit_x else gray, (bit_x, bit_y, bit_z)))
    classes = [[[] for _ in range(domain_cells)] for _ in STEPS]
    for one in range(domain_cells):
        runs = {}
        for layer in range(2):
            for two in range(domain_cells):
                step = (layer, two // GZ - one // GZ, two % GZ - one % GZ)
                if abs(step[1]) > 1 or abs(step[2]) > 1 or (layer == 0 and two <= one):
                    continue
                keys = [
                    key
                    for key, bits in octants
                    if all(move == 0 or bit == (move > 0) for move, bit in zip(step, bits))
                ]
                entry = (two + layer * domain_cells, step[1], step[2], min(keys), max(keys) + 1)
                runs.setdefault(entry[4] - entry[3], []).append(entry)
        for length, entries in sorted(runs.items()):
            entries.sort(key=lambda entry: entry[3:])
            span = RUN_ROWS.get(length, SPAN)
            for place, (rows, count) in enumerate(STEPS):
                if rows == span:
                    whole = len(entries) // count * count
                    classes[place][one] += entries[:whole]
                    entries = entries[whole:]
    starts, values = [], []
    for lists in classes:
        for entries in lists:
            starts.append(len(values) // 5)
            values += [value for entry in entries for value in entry]
        starts.append(len(values) // 5)
    return np.array(starts, np.int32), np.array(values, np.int32)


def split_three(value):
    high = value.astype(BF16).astype(F32)
    rest = value - high
    middle = rest.astype(BF16).astype(F32)
    return high, middle, rest - middle


def order_kernel(position, params, out_ref):
    beads, _, cells, lanes = position.shape
    row = lax.broadcasted_iota(jnp.int32, (lanes, lanes), 0)
    column = lax.broadcasted_iota(jnp.int32, (lanes, lanes), 1)
    before = jnp.where(row < column, 1.0, 0.0).astype(BF16)
    counter = jnp.concatenate([before, jnp.ones((lanes, lanes), BF16)], axis=0)
    kind = lax.broadcasted_iota(jnp.int32, (16, lanes), 0).astype(F32)
    place_row = row.astype(F32)

    def per_cell(index, carry):
        for shift, bead in [(shift, bead) for shift in range(GROUP) for bead in range(beads)]:
            cell = index * GROUP + shift
            sizes = atom_rows(params, cell)[:2]
            place = atom_rows(position.at[bead], cell)
            key = octant_key(*place, sizes[1] > 0.0)
            same = jnp.where(key == kind, 1.0, 0.0)
            less = jnp.where(key < kind, 1.0, 0.0)
            counts = lax.dot_general(
                jnp.concatenate([same, less], axis=1).astype(BF16),
                counter,
                (((1,), (0,)), ((), ())),
                preferred_element_type=F32,
            )
            rank = jnp.sum(same * counts, axis=0, keepdims=True)
            chosen = jnp.where(rank == place_row, 1.0, 0.0).astype(BF16)
            scaled = [SHORT_SCALE * value for value in (*place, sizes[0])]
            block = jnp.concatenate([*scaled, sizes[1], jnp.zeros((3, lanes), F32)], axis=0)
            moved = lax.dot_general(
                jnp.concatenate(split_three(block), axis=0).astype(BF16),
                chosen,
                (((1,), (1,)), ((), ())),
                preferred_element_type=F32,
            )
            out_ref[bead, cell, 0:5, :] = (moved[0:8] + moved[8:16] + moved[16:24])[0:5]
            out_ref[bead, cell, 5:6, :] = rank
            out_ref[bead, cell, 6:8, :] = jnp.zeros((2, lanes), F32)
        return carry

    lax.fori_loop(0, cells // GROUP, per_cell, 0)


def meet_runs(span, local, runs, lanes_ref, sizes_ref, rows_ref, total_ref, back_ref):
    beads, lanes = lanes_ref.shape[0], lanes_ref.shape[-1]
    for bead in range(beads):
        for firsts, partner, step_y, step_z in runs:
            here = pl.ds(firsts[bead], span)
            rows = [
                rows_ref[local, bead, kind, here, :].reshape(span // 8, 8, lanes)
                for kind in range(5)
            ]
            half = rows[3] + sizes_ref[partner, 0]
            s2 = half * half
            apart = [
                lanes_ref[bead, partner, 0] - rows[0],
                (lanes_ref[bead, partner, 1] + step_y) - rows[1],
                (lanes_ref[bead, partner, 2] + step_z) - rows[2],
            ]
            radius_sq = apart[0] * apart[0] + apart[1] * apart[1] + apart[2] * apart[2]
            depth = rows[4] * sizes_ref[partner, 1]
            weight = depth * short_weight(radius_sq + s2, s2)
            for axis in range(3):
                push = weight * apart[axis]
                flat_push = push.reshape(span, lanes)
                if total_ref is None:
                    back_ref[local, bead, axis, here, :] = flat_push
                else:
                    back_ref[local, bead, axis, here, :] += flat_push
                    total_ref[partner, bead, axis] += jnp.sum(push, axis=0)


def reach_kernel(
    plan, position, params, next_position, next_params, ordered, force_ref, other_ref, lanes_ref,
    sizes_ref, rows_ref, total_ref, back_ref,
):
    beads, _, cells, lanes = position.shape
    entries_at = len(STEPS) * (cells + 1)
    bounds_at = plan.shape[0] - beads * cells * 9
    factor = SHORT_FACTOR
    repeat_lanes(SHORT_SCALE, position, params, next_position, next_params, lanes_ref, sizes_ref)
    total_ref[...] = jnp.zeros_like(total_ref)
    rows_ref[:, :, :, lanes:, :] = jnp.zeros((GROUP, beads, 5, SPARE, lanes), F32)
    row = lax.broadcasted_iota(jnp.int32, (lanes, lanes), 0).astype(F32)
    slot = lax.broadcasted_iota(jnp.int32, (8, lanes), 1)
    column = lax.broadcasted_iota(jnp.int32, (lanes, 8), 1)
    refs = (lanes_ref, sizes_ref, rows_ref)
    every = [(local, bead) for local in range(GROUP) for bead in range(beads)]

    def per_group(group, carry):
        for local, bead in every:
            block = ordered[bead, group * GROUP + local].T
            for axis in range(5):
                rows_ref[local, bead, axis, 0:lanes, :] = jnp.broadcast_to(
                    block[:, axis : axis + 1], (lanes, lanes)
                )
            if bead == beads - 1:
                for first in range(0, LEAST_LIVE, SPAN):
                    run = ([first] * beads, group * GROUP + local, 0.0, 0.0)
                    meet_runs(SPAN, local, [run], *refs, None, back_ref)

        def per_cell(local, carry):
            cell = group * GROUP + local

            def bound(bead, octant):
                return plan[bounds_at + (bead * cells + cell) * 9 + octant]

            def itself(index, carry):
                first = pl.multiple_of(index * SPAN, SPAN)
                run = ([first] * beads, cell, 0.0, 0.0)
                meet_runs(SPAN, local, [run], *refs, None, back_ref)
                return carry

            lax.fori_loop(
                LEAST_LIVE // SPAN, lax.div(bound(0, 8) + (SPAN - 1), SPAN), itself, 0
            )

            for place, (span, count) in enumerate(STEPS):
                begin = plan[place * (cells + 1) + cell]
                end = plan[place * (cells + 1) + cell + 1]

                def per_step(step, carry, span=span, count=count, begin=begin):
                    runs, longest = [], 0
                    for shift in range(count):
                        at = entries_at + 5 * (begin + step * count + shift)
                        begins = [
                            lax.bitwise_and(bound(bead, plan[at + 3]), -8) for bead in range(beads)
                        ]
                        for bead in range(beads):
                            longest = jnp.maximum(longest, bound(bead, plan[at + 4]) - begins[bead])
                        runs.append(
                            (
                                begins, plan[at], SHORT_SCALE * plan[at + 1].astype(F32),
                                SHORT_SCALE * plan[at + 2].astype(F32),
                            )
                        )

                    def per_span(index, carry):
                        moved = [
                            (
                                [
                                    pl.multiple_of(jnp.minimum(first + index * span, lanes), 8)
                                    for first in begins
                                ],
                                *rest,
                            )
                            for begins, *rest in runs
                        ]
                        meet_runs(span, local, moved, *refs, total_ref, back_ref)
                        return carry

                    return lax.fori_loop(0, lax.div(longest + (span - 1), span), per_span, carry)

                lax.fori_loop(0, lax.div(end - begin, count), per_step, 0)
            return carry

        lax.fori_loop(0, GROUP, per_cell, 0)

        for local, bead in every:
            cell = group * GROUP + local
            alive = plan[bounds_at + cell * 9 + 8]
            sums = [
                jnp.sum(back_ref[local, bead, axis, 0:lanes, :], axis=1, keepdims=True)
                for axis in range(3)
            ]
            block = jnp.where(
                column == 0,
                sums[0],
                jnp.where(column == 1, sums[1], jnp.where(column == 2, sums[2], 0.0)),
            ).T
            block = jnp.where(slot < alive, block, 0.0)
            chosen = jnp.where(ordered[bead, cell, 5:6, :] == row, 1.0, 0.0).astype(BF16)
            moved = lax.dot_general(
                jnp.concatenate(split_three(block), axis=0).astype(BF16),
                chosen,
                (((1,), (0,)), ((), ())),
                preferred_element_type=F32,
            )
            put_rows(force_ref, bead, cell, (moved[0:8] + moved[8:16] + moved[16:24])[0:3])
        return carry

    lax.fori_loop(0, cells // GROUP, per_group, 0)

    def finish(index, carry):
        for shift, bead in every:
            cell = index * GROUP + shift
            held = jnp.concatenate(atom_rows(force_ref.at[bead], cell), axis=0)
            put_rows(force_ref, bead, cell, factor * (fold_total(total_ref, cell, bead) - held))
            put_rows(other_ref, bead, cell, factor * fold_total(total_ref, cell + cells, bead))
        return carry

    lax.fori_loop(0, cells // GROUP, finish, 0)


def short_forces(position, params, next_position, next_params, ordered, bounds):
    beads, _, cells, lanes = position.shape
    starts, entries = reach_lists(cells)
    plan = jnp.concatenate([jnp.asarray(starts), jnp.asarray(entries), bounds])
    forces = jax.ShapeDtypeStruct((beads, 3, cells, lanes), F32)
    return call(
        reach_kernel,
        (plan, position, params, next_position, next_params, ordered),
        1,
        (forces, forces),
        [
            pltpu.VMEM((beads, 2 * cells, 3, 8, lanes), F32),
            pltpu.VMEM((2 * cells, 2, 8, lanes), F32),
            pltpu.VMEM((GROUP, beads, 5, lanes + SPARE, lanes), F32),
            pltpu.VMEM((2 * cells, beads, 3, 8, lanes), F32),
            pltpu.VMEM((GROUP, beads, 3, lanes + SPARE, lanes), F32),
        ],
        PAIR_FLOPS * beads * 70,
    )


def call(kernel, inputs, smem, outputs, scratch, flops):
    return pl.pallas_call(
        kernel,
        out_shape=outputs,
        in_specs=[
            pl.BlockSpec(memory_space=pltpu.SMEM if place < smem else pltpu.VMEM)
            for place in range(len(inputs))
        ],
        scratch_shapes=scratch,
        compiler_params=pltpu.CompilerParams(vmem_limit_bytes=VMEM_LIMIT),
        cost_estimate=pl.CostEstimate(flops=flops, bytes_accessed=1 << 18, transcendentals=0),
    )(*inputs)


PAIR_FLOPS = 40 * 128 * 128


def pair_forces(position, params, occupied, next_position, next_params):
    beads, _, cells, lanes = position.shape
    starts, entries = partner_lists(cells)
    forces = jax.ShapeDtypeStruct((beads, 3, cells, lanes), F32)
    return call(
        pairs_kernel,
        (
            jnp.asarray(np.concatenate([starts, entries])), occupied, position, params,
            next_position, next_params,
        ),
        2,
        (forces, forces),
        [
            pltpu.VMEM((beads, 2 * cells, 3, 8, lanes), F32),
            pltpu.VMEM((2 * cells, 2, 8, lanes), F32),
            pltpu.VMEM((cells, beads, 3, lanes, lanes), F32),
            pltpu.VMEM((cells, 2, lanes, lanes), F32),
            pltpu.VMEM((2 * cells, beads, 3, 8, lanes), F32),
            pltpu.VMEM((cells, beads, 3, lanes, lanes), F32),
        ],
        PAIR_FLOPS * beads * (len(entries) // 3 + cells),
    )


def kick_kernel(
    piece_rows, groups, table, rank, position, momenta, noise, force, back, params, partial_ref,
    piece_ref, flat_ref,
):
    beads, rows, _ = position.shape
    holders = piece_ref.shape[0]
    reduced = table.shape[0]
    first = rank[0] * beads
    if holders * piece_rows > rows:
        piece_ref[...] = jnp.zeros_like(piece_ref)
    mass = params[2]
    per_root = lax.rsqrt(mass)
    per_root = per_root * (1.5 - 0.5 * mass * per_root * per_root)
    per_mass = jnp.concatenate([1.0 / mass] * 3, axis=0)
    per_root = jnp.concatenate([per_root] * 3, axis=0)
    for bead in range(beads):
        kicked = momenta[bead] + 0.5 * TIME_STEP * (force[bead] + back[bead])
        flat_ref[0, bead] = position[bead]
        flat_ref[1, bead] = kicked * per_mass
        flat_ref[2, bead] = noise[bead] * per_root
    for kind in range(3):
        for bead in range(beads):
            base = (kind * beads + bead) * piece_rows
            for owner in range(holders):
                start = owner * piece_rows
                count = min(piece_rows, rows - start)
                if count > 0:
                    piece_ref[owner, base : base + count, :] = flat_ref[
                        kind, bead, start : start + count, :
                    ]
    for group in range(reduced):
        total = None
        for kind in range(3):
            for bead in range(beads):
                term = table[group, kind * holders * beads + first + bead] * flat_ref[kind, bead]
                total = term if total is None else total + term
        for copy in range(groups):
            partial_ref[group * groups + copy] = total


def move_kernel(piece_rows, beads, matrix, arrived, out_ref, gathered):
    holders = arrived.shape[0]
    taken = 3 * beads
    given = 2 * beads
    for row in range(piece_rows):
        for holder in range(holders):
            gathered[row, holder * taken : (holder + 1) * taken, :] = arrived[
                holder, pl.ds(row, taken, stride=piece_rows), :
            ]
        moved = lax.dot_general(
            matrix[...],
            gathered[row],
            (((1,), (0,)), ((), ())),
            precision=lax.Precision.HIGHEST,
            preferred_element_type=F32,
        )
        for holder in range(holders):
            out_ref[holder, row * given : (row + 1) * given, :] = moved[
                holder * given : (holder + 1) * given
            ]


def finish_kernel(
    piece_rows, groups, table, rank, moved, slow, params, position_ref, momentum_ref, velocity_ref
):
    beads, rows, _ = position_ref.shape
    holders = moved.shape[0]
    given = 2 * beads
    reduced = table.shape[0]
    first = 3 * holders * beads + rank[0] * beads
    mass = jnp.concatenate([params[2]] * 3, axis=0)
    for bead in range(beads):
        for owner in range(holders):
            start = owner * piece_rows
            count = min(piece_rows, rows - start)
            if count > 0:
                position_ref[bead, start : start + count, :] = moved[
                    owner, pl.ds(bead, count, stride=given), :
                ]
                velocity_ref[bead, start : start + count, :] = moved[
                    owner, pl.ds(beads + bead, count, stride=given), :
                ]
    for bead in range(beads):
        total = mass * velocity_ref[bead]
        for group in range(reduced):
            total = total + table[group, first + bead] * slow[group * groups]
        momentum_ref[bead] = total


def shards(positions, momenta, noise, atom_types, occupancy, type_sigma, type_eps, type_mass):
    beads, cells, _, lanes = positions.shape
    holders = lax.axis_size("bead")
    domains = lax.axis_size("space")
    rank = lax.axis_index("bead")
    total_beads = beads * holders
    rows = 3 * cells
    piece_rows = -(-rows // holders)
    held = max(1, PC // holders)
    groups = max(1, holders // PC)
    contract = contract_matrix(total_beads, PC)
    steps = step_matrices(total_beads)
    rank_table = rank.astype(jnp.int32).reshape(1)
    one_back = [((i + 1) % domains, i) for i in range(domains)]
    one_on = [(i, (i + 1) % domains) for i in range(domains)]

    codes = jnp.arange(type_sigma.shape[0])
    onehot = atom_types[..., None] == codes
    living = jnp.arange(lanes)[None, :] < occupancy[:, None]
    half_sigma = 0.5 * jnp.sum(jnp.where(onehot, type_sigma, 0.0), -1)
    root_eps = jnp.sqrt(jnp.sum(jnp.where(onehot, type_eps, 0.0), -1))
    mass = jnp.sum(jnp.where(onehot, type_mass, 0.0), -1)
    params = jnp.stack([half_sigma, jnp.where(living, root_eps, 0.0), mass], 0)
    positions, momenta, noise = (
        value.transpose(0, 2, 1, 3) for value in (positions, momenta, noise)
    )

    stacked = jnp.concatenate([positions, params[None]], 0)
    next_stacked = lax.ppermute(stacked, "space", one_back)
    next_params = next_stacked[beads]
    ordered = call(
        order_kernel,
        (positions, params),
        0,
        jax.ShapeDtypeStruct((beads, cells, 8, lanes), F32),
        [],
        1 << 22,
    )
    key = octant_key(positions[:, 0], positions[:, 1], positions[:, 2], living[None])
    bounds = jnp.sum(
        (key[:, :, None, :] < jnp.arange(9, dtype=F32)[:, None]).astype(jnp.int32), -1
    )
    force, back = short_forces(
        positions, params, next_stacked[:beads], next_params, ordered, bounds.reshape(-1)
    )
    back = lax.ppermute(back, "space", one_on)

    spread = 0.5 * TIME_STEP * (total_beads / PC) * contract
    table = np.concatenate([contract @ steps[0, kind] for kind in range(3)] + [spread], axis=1)
    table = jnp.asarray(table, F32)

    def flat(value):
        return value.reshape(-1, rows, lanes)

    partial, pieces = call(
        functools.partial(kick_kernel, piece_rows, groups),
        (
            table, rank_table, flat(positions), flat(momenta), flat(noise), flat(force), flat(back),
            params,
        ),
        2,
        (
            jax.ShapeDtypeStruct((PC * groups, rows, lanes), F32),
            jax.ShapeDtypeStruct((holders, 3 * beads * piece_rows, lanes), F32),
        ),
        [pltpu.VMEM((3, beads, rows, lanes), F32)],
        1 << 22,
    )
    arrived = lax.all_to_all(
        partial.reshape(holders, held * rows, lanes), "bead", split_axis=0, concat_axis=0, tiled=True
    )
    contracted = jnp.sum(arrived, 0).reshape(held, 3, cells, lanes)
    contracted, pieces = lax.optimization_barrier((contracted, pieces))
    next_contracted = lax.ppermute(contracted, "space", one_back)
    pieces = lax.all_to_all(pieces, "bead", split_axis=0, concat_axis=0, tiled=True)
    slow, slow_back = pair_forces(
        contracted, params, occupancy, next_contracted, next_params
    )
    slow = slow + lax.ppermute(slow_back, "space", one_on)

    order = steps.reshape(2, 3, holders, beads, holders, beads).transpose(2, 0, 3, 4, 1, 5)
    order = order.reshape(2 * total_beads, 3 * total_beads)
    moved = call(
        functools.partial(move_kernel, piece_rows, beads),
        (jnp.asarray(order, F32), pieces),
        0,
        jax.ShapeDtypeStruct((holders, 2 * beads * piece_rows, lanes), F32),
        [pltpu.VMEM((piece_rows, 3 * total_beads, lanes), F32)],
        1 << 23,
    )
    moved_rows = 2 * beads * piece_rows
    sent = jnp.concatenate(
        [
            moved,
            jnp.broadcast_to(slow.reshape(1, held * rows, lanes), (holders, held * rows, lanes)),
        ],
        1,
    )
    got = lax.all_to_all(sent, "bead", split_axis=0, concat_axis=0, tiled=True)
    result = jax.ShapeDtypeStruct((beads, rows, lanes), F32)
    new_positions, new_momenta = call(
        functools.partial(finish_kernel, piece_rows, groups),
        (
            table, rank_table, got[:, :moved_rows],
            got[:, moved_rows:].reshape(holders * held, rows, lanes), params,
        ),
        2,
        (result, result),
        [pltpu.VMEM((beads, rows, lanes), F32)],
        1 << 20,
    )

    def cells_first(value):
        return value.reshape(beads, 3, cells, lanes).transpose(0, 2, 1, 3)

    return cells_first(new_positions), cells_first(new_momenta)


def solution(mesh):
    placed = (
        P("bead", "space", None, None),
        P("bead", "space", None, None),
        P("bead", "space", None, None),
        P("space", None),
        P("space"),
        P(),
        P(),
        P(),
    )
    return jax.shard_map(
        shards,
        mesh=mesh,
        in_specs=placed,
        out_specs=(P("bead", "space", None, None), P("bead", "space", None, None)),
        check_vma=False,
    )
```

```python
import functools

import jax
import jax.numpy as jnp
import numpy as np
from jax import lax
from jax.experimental import pallas as pl
from jax.experimental.pallas import tpu as pltpu
from jax.sharding import PartitionSpec as P

PC = 8
GY = 4
GZ = 4

TIME_STEP = 0.05
INVERSE_TEMP = 32.0
CENTROID_FRICTION = 1.0
INNER_CUT = 0.5
OUTER_CUT = 1.0
CUBE_ROOT_TWO = 2.0 ** (1.0 / 3.0)
F32 = jnp.float32
BF16 = jnp.bfloat16
SPAN = 32
GROUP = 4
STEPS = ((24, 4), (24, 2), (24, 1), (40, 2), (40, 1), (32, 2), (32, 1))
RUN_ROWS = {1: 24, 2: 40}
SPARE = 40
EARLY_ROWS = 96
VMEM_LIMIT = 48 * 1024 * 1024


def mode_matrix(number):
    rows = np.arange(number, dtype=np.float64)[:, None]
    column = np.arange(number, dtype=np.float64)[None, :]
    phases = 2.0 * np.pi * rows * column / number
    factor = np.sqrt(2.0 / number)
    middle = np.cos(np.pi * rows) / np.sqrt(number)
    matrix = np.where(column < number / 2, factor * np.cos(phases), factor * np.sin(phases))
    matrix = np.where(column == number / 2, middle, matrix)
    return np.where(column == 0, 1.0 / np.sqrt(number), matrix)


def contract_matrix(full_count, reduced):
    selected = np.arange(reduced)
    selected = np.where(selected <= reduced // 2, selected, selected + full_count - reduced)
    chosen = mode_matrix(full_count)[:, selected]
    return np.sqrt(reduced / full_count) * (mode_matrix(reduced) @ chosen.T)


def step_matrices(number):
    index = np.arange(number, dtype=np.float64)
    frequency = 2.0 * (number / INVERSE_TEMP) * np.sin(np.pi * index / number)
    friction = np.where(index == 0, CENTROID_FRICTION, 2.0 * frequency)
    damping = np.exp(-friction * TIME_STEP)
    kicking = np.sqrt((1.0 - damping * damping) / INVERSE_TEMP)
    cosine = np.cos(frequency * TIME_STEP)
    sine = np.sin(frequency * TIME_STEP)
    drift = np.where(index == 0, TIME_STEP, sine / np.where(index == 0, 1.0, frequency))
    modes = mode_matrix(number)

    def over_beads(diagonal):
        return (modes * diagonal[None, :]) @ modes.T

    return np.array(
        [
            [over_beads(cosine), over_beads(drift * damping), over_beads(drift * kicking)],
            [
                over_beads(-frequency * sine),
                over_beads(cosine * damping),
                over_beads(cosine * kicking),
            ],
        ]
    )


def partner_lists(domain_cells):
    lists = []
    for one in range(domain_cells):
        near = []
        for two in range(domain_cells):
            step_y, step_z = two // GZ - one // GZ, two % GZ - one % GZ
            if abs(step_y) <= 1 and abs(step_z) <= 1:
                near.append((two, step_y, step_z))
        later = [entry for entry in near if entry[0] > one]
        lists.append(later + [(two + domain_cells, y, z) for two, y, z in near])
    starts = np.cumsum([0] + [len(entries) for entries in lists]).astype(np.int32)
    return starts, np.array([value for entries in lists for entry in entries for value in entry], np.int32)


def long_weight(h, radius_sq, s2):
    inverse = pl.reciprocal(h, approx=True)
    quotient = (CUBE_ROOT_TWO * s2) * inverse
    twice = quotient * quotient * quotient
    outer = jnp.maximum(1.0 - radius_sq, 0.0)
    inner = jnp.maximum(1.0 - 4.0 * radius_sq, 0.0)
    switch = outer * outer - inner * inner
    slope = outer - 4.0 * inner
    return twice * ((twice - 1.0) * (3.0 * (switch * inverse) + slope) - slope)


def short_weight(h, s2):
    inverse = pl.reciprocal(h, approx=True)
    quotient = s2 * inverse
    sixth = quotient * quotient * quotient
    lifted = jnp.maximum((quotient + inverse) - 2.0 / 3.0, 1.0 / 3.0)
    bracket = (sixth - 0.5) * lifted - 1.0 / 6.0
    return (sixth * bracket) * ((lifted - 1.0 / 3.0) * h)


LONG_FACTOR = 4.0
SHORT_SCALE = 1.0 / INNER_CUT
SHORT_FACTOR = 192.0 / SHORT_SCALE


def atom_rows(block, cell):
    return [block[kind, pl.ds(cell, 1), :] for kind in range(3)]


def columns(block):
    few, lanes = block.shape
    return jnp.concatenate([block, jnp.zeros((8 - few, lanes), F32)], axis=0).T


def spread_rows(position, params, cell, rows_ref, size_ref):
    beads, lanes = position.shape[0], position.shape[-1]
    sizes = columns(jnp.concatenate(atom_rows(params, cell)[:2], axis=0))
    for kind in range(2):
        size_ref[cell, kind] = jnp.broadcast_to(sizes[:, kind : kind + 1], (lanes, lanes))
    for bead in range(beads):
        block = columns(jnp.concatenate(atom_rows(position.at[bead], cell), axis=0))
        for axis in range(3):
            rows_ref[cell, bead, axis] = jnp.broadcast_to(
                block[:, axis : axis + 1], (lanes, lanes)
            )


def meet(cell, first, partners, refs):
    lanes_ref, sizes_ref, rows_ref, size_ref, total_ref, back_ref = refs
    beads, lanes = lanes_ref.shape[0], lanes_ref.shape[-1]
    here = pl.ds(first, SPAN)
    tall = (SPAN // 8, 8, lanes)
    row_half = size_ref[cell, 0, here, :].reshape(tall)
    row_root = size_ref[cell, 1, here, :].reshape(tall)
    known = []
    for partner, _, _ in partners:
        half = row_half + sizes_ref[partner, 0]
        s2 = half * half
        known.append((s2, row_root * sizes_ref[partner, 1]))
    for bead in range(beads):
        rows = [rows_ref[cell, bead, axis, here, :].reshape(tall) for axis in range(3)]
        back = [None, None, None]
        for (partner, step_y, step_z), (s2, depth) in zip(partners, known):
            apart = [
                lanes_ref[bead, partner, 0] - rows[0],
                (lanes_ref[bead, partner, 1] + step_y) - rows[1],
                (lanes_ref[bead, partner, 2] + step_z) - rows[2],
            ]
            radius_sq = apart[0] * apart[0] + apart[1] * apart[1] + apart[2] * apart[2]
            weight = depth * long_weight(radius_sq + s2, radius_sq, s2)
            for axis in range(3):
                push = weight * apart[axis]
                back[axis] = push if back[axis] is None else back[axis] + push
                if total_ref is not None:
                    total_ref[partner, bead, axis] += jnp.sum(push, axis=0)
        for axis in range(3):
            value = back[axis].reshape(SPAN, lanes)
            if total_ref is None:
                back_ref[cell, bead, axis, here, :] = value
            else:
                back_ref[cell, bead, axis, here, :] += value


def repeat_lanes(scale, position, params, next_position, next_params, lanes_ref, sizes_ref):
    beads, _, cells, lanes = position.shape

    def per_cell(cell, carry):
        for layer, place, values in ((0, position, params), (1, next_position, next_params)):
            for kind in range(2):
                row = values[kind, pl.ds(cell, 1), :]
                row = scale * row if kind == 0 else row
                sizes_ref[layer * cells + cell, kind] = jnp.broadcast_to(row, (8, lanes))
            for bead in range(beads):
                for axis in range(3):
                    row = place[bead, axis, pl.ds(cell, 1), :]
                    row = scale * (row + 1.0 if layer == 1 and axis == 0 else row)
                    lanes_ref[bead, layer * cells + cell, axis] = jnp.broadcast_to(row, (8, lanes))
        return carry

    lax.fori_loop(0, cells, per_cell, 0)


def fold_back(back_ref, cell, bead):
    lanes = back_ref.shape[-1]
    column = lax.broadcasted_iota(jnp.int32, (lanes, 8), 1)
    sums = [jnp.sum(back_ref[cell, bead, axis], axis=1, keepdims=True) for axis in range(3)]
    block = jnp.where(
        column == 0, sums[0], jnp.where(column == 1, sums[1], jnp.where(column == 2, sums[2], 0.0))
    )
    return block.T[0:3]


def put_rows(out_ref, bead, cell, block):
    for axis in range(3):
        out_ref[bead, axis, pl.ds(cell, 1), :] = block[axis : axis + 1]


def fold_total(total_ref, cell, bead):
    return jnp.concatenate(
        [jnp.sum(total_ref[cell, bead, axis], axis=0, keepdims=True) for axis in range(3)], axis=0
    )


def pairs_kernel(
    plan, occupied, position, params, next_position, next_params,
    force_ref, other_ref, lanes_ref, sizes_ref, rows_ref, size_ref, total_ref, back_ref,
):
    beads, _, cells, lanes = position.shape
    factor = LONG_FACTOR
    together = max(1, 4 // beads)
    repeat_lanes(1.0, position, params, next_position, next_params, lanes_ref, sizes_ref)
    total_ref[...] = jnp.zeros_like(total_ref)

    refs = (lanes_ref, sizes_ref, rows_ref, size_ref)

    def spread(index, carry):
        for shift in range(together):
            cell = index * together + shift
            spread_rows(position, params, cell, rows_ref, size_ref)
            for first in range(0, EARLY_ROWS, SPAN):
                meet(cell, first, [(cell, 0.0, 0.0)], refs + (None, back_ref))
        return carry

    lax.fori_loop(0, cells // together, spread, 0)

    def entry_of(entry):
        return (
            plan[cells + 1 + 3 * entry],
            plan[cells + 2 + 3 * entry].astype(F32),
            plan[cells + 3 + 3 * entry].astype(F32),
        )

    def per_cell(cell, carry):
        begin, end = plan[cell], plan[cell + 1]
        odd = lax.rem(end - begin, 2)

        most = lanes // SPAN
        needed = lax.div(occupied[cell] + (SPAN - 1), SPAN)
        for parts in (most - 1, most):
            firsts = [part * SPAN for part in range(parts)]

            def all_rows(_, carry, firsts=firsts):
                for first in firsts:
                    if first >= EARLY_ROWS:
                        meet(cell, first, [(cell, 0.0, 0.0)], refs + (None, back_ref))

                def single(entry, carry):
                    for first in firsts:
                        meet(cell, first, [entry_of(entry)], refs + (total_ref, back_ref))
                    return carry

                def double(step, carry):
                    entry = begin + odd + 2 * step
                    both = [entry_of(entry), entry_of(entry + 1)]
                    for first in firsts:
                        meet(cell, first, both, refs + (total_ref, back_ref))
                    return carry

                carry = lax.fori_loop(begin, begin + odd, single, carry)
                return lax.fori_loop(0, lax.div(end - begin, 2), double, carry)

            full = (needed == most).astype(jnp.int32)
            lax.fori_loop(0, full if parts == most else 1 - full, all_rows, 0)
        return carry

    lax.fori_loop(0, cells, per_cell, 0)

    def finish(index, carry):
        for shift in range(together):
            cell = index * together + shift
            alive = params[1, pl.ds(cell, 1), :] > 0.0
            for bead in range(beads):
                total = fold_total(total_ref, cell, bead) - fold_back(back_ref, cell, bead)
                put_rows(force_ref, bead, cell, jnp.where(alive, factor * total, 0.0))
                put_rows(other_ref, bead, cell, factor * fold_total(total_ref, cell + cells, bead))
        return carry

    lax.fori_loop(0, cells // together, finish, 0)


def octant_key(x, y, z, alive):
    zed = jnp.where(z >= 0.5, 1.0, 0.0)
    gray = jnp.where(y >= 0.5, 3.0 - zed, zed)
    return jnp.where(alive, jnp.where(x >= 0.5, 7.0 - gray, gray), 8.0)


def reach_lists(domain_cells):
    octants = []
    for bit_x in range(2):
        for bit_y in range(2):
            for bit_z in range(2):
                gray = 3 - bit_z if bit_y else bit_z
                octants.append((7 - gray if bit_x else gray, (bit_x, bit_y, bit_z)))
    classes = [[[] for _ in range(domain_cells)] for _ in STEPS]
    for one in range(domain_cells):
        runs = {}
        for layer in range(2):
            for two in range(domain_cells):
                step = (layer, two // GZ - one // GZ, two % GZ - one % GZ)
                if abs(step[1]) > 1 or abs(step[2]) > 1 or (layer == 0 and two <= one):
                    continue
                keys = [
                    key
                    for key, bits in octants
                    if all(move == 0 or bit == (move > 0) for move, bit in zip(step, bits))
                ]
                entry = (two + layer * domain_cells, step[1], step[2], min(keys), max(keys) + 1)
                runs.setdefault(entry[4] - entry[3], []).append(entry)
        for length, entries in sorted(runs.items()):
            entries.sort(key=lambda entry: entry[3:])
            span = RUN_ROWS.get(length, SPAN)
            for place, (rows, count) in enumerate(STEPS):
                if rows == span:
                    whole = len(entries) // count * count
                    classes[place][one] += entries[:whole]
                    entries = entries[whole:]
    starts, values = [], []
    for lists in classes:
        for entries in lists:
            starts.append(len(values) // 5)
            values += [value for entry in entries for value in entry]
        starts.append(len(values) // 5)
    return np.array(starts, np.int32), np.array(values, np.int32)


def split_three(value):
    high = value.astype(BF16).astype(F32)
    rest = value - high
    middle = rest.astype(BF16).astype(F32)
    return high, middle, rest - middle


def order_kernel(position, params, out_ref):
    beads, _, cells, lanes = position.shape
    row = lax.broadcasted_iota(jnp.int32, (lanes, lanes), 0)
    column = lax.broadcasted_iota(jnp.int32, (lanes, lanes), 1)
    before = jnp.where(row < column, 1.0, 0.0).astype(BF16)
    counter = jnp.concatenate([before, jnp.ones((lanes, lanes), BF16)], axis=0)
    kind = lax.broadcasted_iota(jnp.int32, (16, lanes), 0).astype(F32)
    place_row = row.astype(F32)

    def per_cell(index, carry):
        for shift, bead in [(shift, bead) for shift in range(GROUP) for bead in range(beads)]:
            cell = index * GROUP + shift
            sizes = atom_rows(params, cell)[:2]
            place = atom_rows(position.at[bead], cell)
            key = octant_key(*place, sizes[1] > 0.0)
            same = jnp.where(key == kind, 1.0, 0.0)
            less = jnp.where(key < kind, 1.0, 0.0)
            counts = lax.dot_general(
                jnp.concatenate([same, less], axis=1).astype(BF16),
                counter,
                (((1,), (0,)), ((), ())),
                preferred_element_type=F32,
            )
            rank = jnp.sum(same * counts, axis=0, keepdims=True)
            chosen = jnp.where(rank == place_row, 1.0, 0.0).astype(BF16)
            scaled = [SHORT_SCALE * value for value in (*place, sizes[0])]
            block = jnp.concatenate([*scaled, sizes[1], jnp.zeros((3, lanes), F32)], axis=0)
            moved = lax.dot_general(
                jnp.concatenate(split_three(block), axis=0).astype(BF16),
                chosen,
                (((1,), (1,)), ((), ())),
                preferred_element_type=F32,
            )
            out_ref[bead, cell, 0:5, :] = (moved[0:8] + moved[8:16] + moved[16:24])[0:5]
            out_ref[bead, cell, 5:6, :] = rank
            out_ref[bead, cell, 6:8, :] = jnp.zeros((2, lanes), F32)
        return carry

    lax.fori_loop(0, cells // GROUP, per_cell, 0)


def meet_runs(span, local, runs, lanes_ref, sizes_ref, rows_ref, total_ref, back_ref):
    beads, lanes = lanes_ref.shape[0], lanes_ref.shape[-1]
    for bead in range(beads):
        for firsts, partner, step_y, step_z in runs:
            here = pl.ds(firsts[bead], span)
            rows = [
                rows_ref[local, bead, kind, here, :].reshape(span // 8, 8, lanes)
                for kind in range(5)
            ]
            half = rows[3] + sizes_ref[partner, 0]
            s2 = half * half
            apart = [
                lanes_ref[bead, partner, 0] - rows[0],
                (lanes_ref[bead, partner, 1] + step_y) - rows[1],
                (lanes_ref[bead, partner, 2] + step_z) - rows[2],
            ]
            radius_sq = apart[0] * apart[0] + apart[1] * apart[1] + apart[2] * apart[2]
            depth = rows[4] * sizes_ref[partner, 1]
            weight = depth * short_weight(radius_sq + s2, s2)
            for axis in range(3):
                push = weight * apart[axis]
                flat_push = push.reshape(span, lanes)
                if total_ref is None:
                    back_ref[local, bead, axis, here, :] = flat_push
                else:
                    back_ref[local, bead, axis, here, :] += flat_push
                    total_ref[partner, bead, axis] += jnp.sum(push, axis=0)


def reach_kernel(
    plan, position, params, next_position, next_params, ordered, force_ref, other_ref, lanes_ref,
    sizes_ref, rows_ref, total_ref, back_ref,
):
    beads, _, cells, lanes = position.shape
    entries_at = len(STEPS) * (cells + 1)
    bounds_at = plan.shape[0] - beads * cells * 9
    factor = SHORT_FACTOR
    repeat_lanes(SHORT_SCALE, position, params, next_position, next_params, lanes_ref, sizes_ref)
    total_ref[...] = jnp.zeros_like(total_ref)
    rows_ref[:, :, :, lanes:, :] = jnp.zeros((GROUP, beads, 5, SPARE, lanes), F32)
    row = lax.broadcasted_iota(jnp.int32, (lanes, lanes), 0).astype(F32)
    slot = lax.broadcasted_iota(jnp.int32, (8, lanes), 1)
    column = lax.broadcasted_iota(jnp.int32, (lanes, 8), 1)
    refs = (lanes_ref, sizes_ref, rows_ref)
    every = [(local, bead) for local in range(GROUP) for bead in range(beads)]

    def per_group(group, carry):
        for local, bead in every:
            block = ordered[bead, group * GROUP + local].T
            for axis in range(5):
                rows_ref[local, bead, axis, 0:lanes, :] = jnp.broadcast_to(
                    block[:, axis : axis + 1], (lanes, lanes)
                )
            if bead == beads - 1:
                for first in range(0, EARLY_ROWS, SPAN):
                    run = ([first] * beads, group * GROUP + local, 0.0, 0.0)
                    meet_runs(SPAN, local, [run], *refs, None, back_ref)

        def per_cell(local, carry):
            cell = group * GROUP + local

            def bound(bead, octant):
                return plan[bounds_at + (bead * cells + cell) * 9 + octant]

            def itself(index, carry):
                first = pl.multiple_of(index * SPAN, SPAN)
                run = ([first] * beads, cell, 0.0, 0.0)
                meet_runs(SPAN, local, [run], *refs, None, back_ref)
                return carry

            lax.fori_loop(
                EARLY_ROWS // SPAN, lax.div(bound(0, 8) + (SPAN - 1), SPAN), itself, 0
            )

            for place, (span, count) in enumerate(STEPS):
                begin = plan[place * (cells + 1) + cell]
                end = plan[place * (cells + 1) + cell + 1]

                def per_step(step, carry, span=span, count=count, begin=begin):
                    runs, longest = [], 0
                    for shift in range(count):
                        at = entries_at + 5 * (begin + step * count + shift)
                        begins = [
                            lax.bitwise_and(bound(bead, plan[at + 3]), -8) for bead in range(beads)
                        ]
                        for bead in range(beads):
                            longest = jnp.maximum(longest, bound(bead, plan[at + 4]) - begins[bead])
                        runs.append(
                            (
                                begins, plan[at], SHORT_SCALE * plan[at + 1].astype(F32),
                                SHORT_SCALE * plan[at + 2].astype(F32),
                            )
                        )

                    def per_span(index, carry):
                        moved = [
                            (
                                [
                                    pl.multiple_of(jnp.minimum(first + index * span, lanes), 8)
                                    for first in begins
                                ],
                                *rest,
                            )
                            for begins, *rest in runs
                        ]
                        meet_runs(span, local, moved, *refs, total_ref, back_ref)
                        return carry

                    return lax.fori_loop(0, lax.div(longest + (span - 1), span), per_span, carry)

                lax.fori_loop(0, lax.div(end - begin, count), per_step, 0)
            return carry

        lax.fori_loop(0, GROUP, per_cell, 0)

        for local, bead in every:
            cell = group * GROUP + local
            alive = plan[bounds_at + cell * 9 + 8]
            sums = [
                jnp.sum(back_ref[local, bead, axis, 0:lanes, :], axis=1, keepdims=True)
                for axis in range(3)
            ]
            block = jnp.where(
                column == 0,
                sums[0],
                jnp.where(column == 1, sums[1], jnp.where(column == 2, sums[2], 0.0)),
            ).T
            block = jnp.where(slot < alive, block, 0.0)
            chosen = jnp.where(ordered[bead, cell, 5:6, :] == row, 1.0, 0.0).astype(BF16)
            moved = lax.dot_general(
                jnp.concatenate(split_three(block), axis=0).astype(BF16),
                chosen,
                (((1,), (0,)), ((), ())),
                preferred_element_type=F32,
            )
            put_rows(force_ref, bead, cell, (moved[0:8] + moved[8:16] + moved[16:24])[0:3])
        return carry

    lax.fori_loop(0, cells // GROUP, per_group, 0)

    def finish(index, carry):
        for shift, bead in every:
            cell = index * GROUP + shift
            held = jnp.concatenate(atom_rows(force_ref.at[bead], cell), axis=0)
            put_rows(force_ref, bead, cell, factor * (fold_total(total_ref, cell, bead) - held))
            put_rows(other_ref, bead, cell, factor * fold_total(total_ref, cell + cells, bead))
        return carry

    lax.fori_loop(0, cells // GROUP, finish, 0)


def short_forces(position, params, next_position, next_params, ordered, bounds):
    beads, _, cells, lanes = position.shape
    starts, entries = reach_lists(cells)
    plan = jnp.concatenate([jnp.asarray(starts), jnp.asarray(entries), bounds])
    forces = jax.ShapeDtypeStruct((beads, 3, cells, lanes), F32)
    return call(
        reach_kernel,
        (plan, position, params, next_position, next_params, ordered),
        1,
        (forces, forces),
        [
            pltpu.VMEM((beads, 2 * cells, 3, 8, lanes), F32),
            pltpu.VMEM((2 * cells, 2, 8, lanes), F32),
            pltpu.VMEM((GROUP, beads, 5, lanes + SPARE, lanes), F32),
            pltpu.VMEM((2 * cells, beads, 3, 8, lanes), F32),
            pltpu.VMEM((GROUP, beads, 3, lanes + SPARE, lanes), F32),
        ],
        PAIR_FLOPS * beads * 70,
    )


def call(kernel, inputs, smem, outputs, scratch, flops, fetched=()):
    def space(place):
        if place in fetched:
            return pltpu.HBM
        return pltpu.SMEM if place < smem else pltpu.VMEM

    return pl.pallas_call(
        kernel,
        out_shape=outputs,
        in_specs=[pl.BlockSpec(memory_space=space(place)) for place in range(len(inputs))],
        scratch_shapes=scratch,
        compiler_params=pltpu.CompilerParams(vmem_limit_bytes=VMEM_LIMIT),
        cost_estimate=pl.CostEstimate(flops=flops, bytes_accessed=1 << 18, transcendentals=0),
    )(*inputs)


PAIR_FLOPS = 40 * 128 * 128


def pair_forces(position, params, occupied, next_position, next_params):
    beads, _, cells, lanes = position.shape
    starts, entries = partner_lists(cells)
    forces = jax.ShapeDtypeStruct((beads, 3, cells, lanes), F32)
    return call(
        pairs_kernel,
        (
            jnp.asarray(np.concatenate([starts, entries])), occupied, position, params,
            next_position, next_params,
        ),
        2,
        (forces, forces),
        [
            pltpu.VMEM((beads, 2 * cells, 3, 8, lanes), F32),
            pltpu.VMEM((2 * cells, 2, 8, lanes), F32),
            pltpu.VMEM((cells, beads, 3, lanes, lanes), F32),
            pltpu.VMEM((cells, 2, lanes, lanes), F32),
            pltpu.VMEM((2 * cells, beads, 3, 8, lanes), F32),
            pltpu.VMEM((cells, beads, 3, lanes, lanes), F32),
        ],
        PAIR_FLOPS * beads * (len(entries) // 3 + cells),
    )


def kick_kernel(
    piece_rows, groups, rank, table_hbm, position, momenta, noise, force, back, params, partial_ref,
    piece_ref, flat_ref, table, done,
):
    fetch = pltpu.make_async_copy(table_hbm, table, done)
    fetch.start()
    beads, rows, _ = position.shape
    holders = piece_ref.shape[0]
    reduced = table.shape[0]
    first = rank[0] * beads
    if holders * piece_rows > rows:
        piece_ref[...] = jnp.zeros_like(piece_ref)
    mass = params[2]
    per_root = lax.rsqrt(mass)
    per_root = per_root * (1.5 - 0.5 * mass * per_root * per_root)
    per_mass = jnp.concatenate([1.0 / mass] * 3, axis=0)
    per_root = jnp.concatenate([per_root] * 3, axis=0)
    for bead in range(beads):
        kicked = momenta[bead] + 0.5 * TIME_STEP * (force[bead] + back[bead])
        flat_ref[0, bead] = position[bead]
        flat_ref[1, bead] = kicked * per_mass
        flat_ref[2, bead] = noise[bead] * per_root
    for kind in range(3):
        for bead in range(beads):
            base = (kind * beads + bead) * piece_rows
            for owner in range(holders):
                start = owner * piece_rows
                count = min(piece_rows, rows - start)
                if count > 0:
                    piece_ref[owner, base : base + count, :] = flat_ref[
                        kind, bead, start : start + count, :
                    ]
    fetch.wait()
    for group in range(reduced):
        total = None
        for kind in range(3):
            for bead in range(beads):
                term = table[group, kind * holders * beads + first + bead] * flat_ref[kind, bead]
                total = term if total is None else total + term
        for copy in range(groups):
            partial_ref[group * groups + copy] = total


def move_kernel(piece_rows, beads, matrix_hbm, arrived, out_ref, gathered, matrix, done):
    fetch = pltpu.make_async_copy(matrix_hbm, matrix, done)
    fetch.start()
    holders = arrived.shape[0]
    taken = 3 * beads
    given = 2 * beads
    for row in range(piece_rows):
        for holder in range(holders):
            gathered[row, holder * taken : (holder + 1) * taken, :] = arrived[
                holder, pl.ds(row, taken, stride=piece_rows), :
            ]
    fetch.wait()
    for row in range(piece_rows):
        moved = lax.dot_general(
            matrix[...],
            gathered[row],
            (((1,), (0,)), ((), ())),
            precision=lax.Precision.HIGHEST,
            preferred_element_type=F32,
        )
        for holder in range(holders):
            out_ref[holder, row * given : (row + 1) * given, :] = moved[
                holder * given : (holder + 1) * given
            ]


def finish_kernel(
    piece_rows, groups, rank, table_hbm, moved, slow, params, position_ref, momentum_ref,
    velocity_ref, table, done,
):
    fetch = pltpu.make_async_copy(table_hbm, table, done)
    fetch.start()
    beads, rows, _ = position_ref.shape
    holders = moved.shape[0]
    given = 2 * beads
    reduced = table.shape[0]
    first = 3 * holders * beads + rank[0] * beads
    mass = jnp.concatenate([params[2]] * 3, axis=0)
    for bead in range(beads):
        for owner in range(holders):
            start = owner * piece_rows
            count = min(piece_rows, rows - start)
            if count > 0:
                position_ref[bead, start : start + count, :] = moved[
                    owner, pl.ds(bead, count, stride=given), :
                ]
                velocity_ref[bead, start : start + count, :] = moved[
                    owner, pl.ds(beads + bead, count, stride=given), :
                ]
    fetch.wait()
    for bead in range(beads):
        total = mass * velocity_ref[bead]
        for group in range(reduced):
            total = total + table[group, first + bead] * slow[group * groups]
        momentum_ref[bead] = total


def shards(positions, momenta, noise, atom_types, occupancy, type_sigma, type_eps, type_mass):
    beads, cells, _, lanes = positions.shape
    holders = lax.axis_size("bead")
    domains = lax.axis_size("space")
    rank = lax.axis_index("bead")
    total_beads = beads * holders
    rows = 3 * cells
    piece_rows = -(-rows // holders)
    held = max(1, PC // holders)
    groups = max(1, holders // PC)
    contract = contract_matrix(total_beads, PC)
    steps = step_matrices(total_beads)
    rank_table = rank.astype(jnp.int32).reshape(1)
    one_back = [((i + 1) % domains, i) for i in range(domains)]
    one_on = [(i, (i + 1) % domains) for i in range(domains)]

    codes = jnp.arange(type_sigma.shape[0])
    onehot = atom_types[..., None] == codes
    living = jnp.arange(lanes)[None, :] < occupancy[:, None]
    half_sigma = 0.5 * jnp.sum(jnp.where(onehot, type_sigma, 0.0), -1)
    root_eps = jnp.sqrt(jnp.sum(jnp.where(onehot, type_eps, 0.0), -1))
    mass = jnp.sum(jnp.where(onehot, type_mass, 0.0), -1)
    params = jnp.stack([half_sigma, jnp.where(living, root_eps, 0.0), mass], 0)
    positions, momenta, noise = (
        value.transpose(0, 2, 1, 3) for value in (positions, momenta, noise)
    )

    stacked = jnp.concatenate([positions, params[None]], 0)
    next_stacked = lax.ppermute(stacked, "space", one_back)
    next_params = next_stacked[beads]
    ordered = call(
        order_kernel,
        (positions, params),
        0,
        jax.ShapeDtypeStruct((beads, cells, 8, lanes), F32),
        [],
        1 << 22,
    )
    key = octant_key(positions[:, 0], positions[:, 1], positions[:, 2], living[None])
    bounds = jnp.sum(
        (key[:, :, None, :] < jnp.arange(9, dtype=F32)[:, None]).astype(jnp.int32), -1
    )
    force, back = short_forces(
        positions, params, next_stacked[:beads], next_params, ordered, bounds.reshape(-1)
    )
    back = lax.ppermute(back, "space", one_on)

    spread = 0.5 * TIME_STEP * (total_beads / PC) * contract
    table = np.concatenate([contract @ steps[0, kind] for kind in range(3)] + [spread], axis=1)
    table = jnp.asarray(table, F32)

    def flat(value):
        return value.reshape(-1, rows, lanes)

    partial, pieces = call(
        functools.partial(kick_kernel, piece_rows, groups),
        (
            rank_table, table, flat(positions), flat(momenta), flat(noise), flat(force), flat(back),
            params,
        ),
        1,
        (
            jax.ShapeDtypeStruct((PC * groups, rows, lanes), F32),
            jax.ShapeDtypeStruct((holders, 3 * beads * piece_rows, lanes), F32),
        ),
        [
            pltpu.VMEM((3, beads, rows, lanes), F32), pltpu.SMEM(table.shape, F32),
            pltpu.SemaphoreType.DMA,
        ],
        1 << 22,
        (1,),
    )
    arrived = lax.all_to_all(
        partial.reshape(holders, held * rows, lanes), "bead", split_axis=0, concat_axis=0, tiled=True
    )
    contracted = jnp.sum(arrived, 0).reshape(held, 3, cells, lanes)
    contracted, pieces = lax.optimization_barrier((contracted, pieces))
    next_contracted = lax.ppermute(contracted, "space", one_back)
    pieces = lax.all_to_all(pieces, "bead", split_axis=0, concat_axis=0, tiled=True)
    slow, slow_back = pair_forces(
        contracted, params, occupancy, next_contracted, next_params
    )
    slow = slow + lax.ppermute(slow_back, "space", one_on)

    order = steps.reshape(2, 3, holders, beads, holders, beads).transpose(2, 0, 3, 4, 1, 5)
    order = order.reshape(2 * total_beads, 3 * total_beads)
    moved = call(
        functools.partial(move_kernel, piece_rows, beads),
        (jnp.asarray(order, F32), pieces),
        0,
        jax.ShapeDtypeStruct((holders, 2 * beads * piece_rows, lanes), F32),
        [
            pltpu.VMEM((piece_rows, 3 * total_beads, lanes), F32), pltpu.VMEM(order.shape, F32),
            pltpu.SemaphoreType.DMA,
        ],
        1 << 23,
        (0,),
    )
    moved_rows = 2 * beads * piece_rows
    sent = jnp.concatenate(
        [
            moved,
            jnp.broadcast_to(slow.reshape(1, held * rows, lanes), (holders, held * rows, lanes)),
        ],
        1,
    )
    got = lax.all_to_all(sent, "bead", split_axis=0, concat_axis=0, tiled=True)
    result = jax.ShapeDtypeStruct((beads, rows, lanes), F32)
    new_positions, new_momenta = call(
        functools.partial(finish_kernel, piece_rows, groups),
        (
            rank_table, table, got[:, :moved_rows],
            got[:, moved_rows:].reshape(holders * held, rows, lanes), params,
        ),
        1,
        (result, result),
        [
            pltpu.VMEM((beads, rows, lanes), F32), pltpu.SMEM(table.shape, F32),
            pltpu.SemaphoreType.DMA,
        ],
        1 << 20,
        (1,),
    )

    def cells_first(value):
        return value.reshape(beads, 3, cells, lanes).transpose(0, 2, 1, 3)

    return cells_first(new_positions), cells_first(new_momenta)


def solution(mesh):
    placed = (
        P("bead", "space", None, None),
        P("bead", "space", None, None),
        P("bead", "space", None, None),
        P("space", None),
        P("space"),
        P(),
        P(),
        P(),
    )
    return jax.shard_map(
        shards,
        mesh=mesh,
        in_specs=placed,
        out_specs=(P("bead", "space", None, None), P("bead", "space", None, None)),
        check_vma=False,
    )
```

```python
import functools

import jax
import jax.numpy as jnp
import numpy as np
from jax import lax
from jax.experimental import pallas as pl
from jax.experimental.pallas import tpu as pltpu
from jax.sharding import PartitionSpec as P

PC = 8
GY = 4
GZ = 4

TIME_STEP = 0.05
INVERSE_TEMP = 32.0
CENTROID_FRICTION = 1.0
INNER_CUT = 0.5
OUTER_CUT = 1.0
CUBE_ROOT_TWO = 2.0 ** (1.0 / 3.0)
F32 = jnp.float32
BF16 = jnp.bfloat16
SPAN = 32
GROUP = 4
STEPS = ((24, 4), (24, 2), (24, 1), (40, 2), (40, 1), (32, 2), (32, 1))
RUN_ROWS = {1: 24, 2: 40}
SPARE = 40
EARLY_ROWS = 96
VMEM_LIMIT = 48 * 1024 * 1024


def mode_matrix(number):
    rows = np.arange(number, dtype=np.float64)[:, None]
    column = np.arange(number, dtype=np.float64)[None, :]
    phases = 2.0 * np.pi * rows * column / number
    factor = np.sqrt(2.0 / number)
    middle = np.cos(np.pi * rows) / np.sqrt(number)
    matrix = np.where(column < number / 2, factor * np.cos(phases), factor * np.sin(phases))
    matrix = np.where(column == number / 2, middle, matrix)
    return np.where(column == 0, 1.0 / np.sqrt(number), matrix)


def contract_matrix(full_count, reduced):
    selected = np.arange(reduced)
    selected = np.where(selected <= reduced // 2, selected, selected + full_count - reduced)
    chosen = mode_matrix(full_count)[:, selected]
    return np.sqrt(reduced / full_count) * (mode_matrix(reduced) @ chosen.T)


def step_matrices(number):
    index = np.arange(number, dtype=np.float64)
    frequency = 2.0 * (number / INVERSE_TEMP) * np.sin(np.pi * index / number)
    friction = np.where(index == 0, CENTROID_FRICTION, 2.0 * frequency)
    damping = np.exp(-friction * TIME_STEP)
    kicking = np.sqrt((1.0 - damping * damping) / INVERSE_TEMP)
    cosine = np.cos(frequency * TIME_STEP)
    sine = np.sin(frequency * TIME_STEP)
    drift = np.where(index == 0, TIME_STEP, sine / np.where(index == 0, 1.0, frequency))
    modes = mode_matrix(number)

    def over_beads(diagonal):
        return (modes * diagonal[None, :]) @ modes.T

    return np.array(
        [
            [over_beads(cosine), over_beads(drift * damping), over_beads(drift * kicking)],
            [
                over_beads(-frequency * sine),
                over_beads(cosine * damping),
                over_beads(cosine * kicking),
            ],
        ]
    )


def partner_lists(domain_cells):
    lists = []
    for one in range(domain_cells):
        near = []
        for two in range(domain_cells):
            step_y, step_z = two // GZ - one // GZ, two % GZ - one % GZ
            if abs(step_y) <= 1 and abs(step_z) <= 1:
                near.append((two, step_y, step_z))
        later = [entry for entry in near if entry[0] > one]
        lists.append(later + [(two + domain_cells, y, z) for two, y, z in near])
    starts = np.cumsum([0] + [len(entries) for entries in lists]).astype(np.int32)
    return starts, np.array([value for entries in lists for entry in entries for value in entry], np.int32)


def long_weight(h, radius_sq, s2):
    inverse = pl.reciprocal(h, approx=True)
    quotient = (CUBE_ROOT_TWO * s2) * inverse
    twice = quotient * quotient * quotient
    outer = jnp.maximum(1.0 - radius_sq, 0.0)
    inner = jnp.maximum(1.0 - 4.0 * radius_sq, 0.0)
    switch = outer * outer - inner * inner
    slope = outer - 4.0 * inner
    return twice * ((twice - 1.0) * (3.0 * (switch * inverse) + slope) - slope)


def short_weight(h, s2):
    inverse = pl.reciprocal(h, approx=True)
    quotient = s2 * inverse
    sixth = quotient * quotient * quotient
    lifted = jnp.maximum((quotient + inverse) - 2.0 / 3.0, 1.0 / 3.0)
    bracket = (sixth - 0.5) * lifted - 1.0 / 6.0
    return (sixth * bracket) * ((lifted - 1.0 / 3.0) * h)


LONG_FACTOR = 4.0
SHORT_SCALE = 1.0 / INNER_CUT
SHORT_FACTOR = 192.0 / SHORT_SCALE


def atom_rows(block, cell):
    return [block[kind, pl.ds(cell, 1), :] for kind in range(3)]


def columns(block):
    few, lanes = block.shape
    return jnp.concatenate([block, jnp.zeros((8 - few, lanes), F32)], axis=0).T


def spread_rows(position, params, cell, rows_ref, size_ref):
    beads, lanes = position.shape[0], position.shape[-1]
    sizes = columns(jnp.concatenate(atom_rows(params, cell)[:2], axis=0))
    for kind in range(2):
        size_ref[cell, kind] = jnp.broadcast_to(sizes[:, kind : kind + 1], (lanes, lanes))
    for bead in range(beads):
        block = columns(jnp.concatenate(atom_rows(position.at[bead], cell), axis=0))
        for axis in range(3):
            rows_ref[cell, bead, axis] = jnp.broadcast_to(
                block[:, axis : axis + 1], (lanes, lanes)
            )


def meet(cell, first, partners, refs):
    lanes_ref, sizes_ref, rows_ref, size_ref, total_ref, back_ref = refs
    beads, lanes = lanes_ref.shape[0], lanes_ref.shape[-1]
    here = pl.ds(first, SPAN)
    tall = (SPAN // 8, 8, lanes)
    row_half = size_ref[cell, 0, here, :].reshape(tall)
    row_root = size_ref[cell, 1, here, :].reshape(tall)
    known = []
    for partner, _, _ in partners:
        half = row_half + sizes_ref[partner, 0]
        s2 = half * half
        known.append((s2, row_root * sizes_ref[partner, 1]))
    for bead in range(beads):
        rows = [rows_ref[cell, bead, axis, here, :].reshape(tall) for axis in range(3)]
        back = [None, None, None]
        for (partner, step_y, step_z), (s2, depth) in zip(partners, known):
            apart = [
                lanes_ref[bead, partner, 0] - rows[0],
                (lanes_ref[bead, partner, 1] + step_y) - rows[1],
                (lanes_ref[bead, partner, 2] + step_z) - rows[2],
            ]
            radius_sq = apart[0] * apart[0] + apart[1] * apart[1] + apart[2] * apart[2]
            weight = depth * long_weight(radius_sq + s2, radius_sq, s2)
            for axis in range(3):
                push = weight * apart[axis]
                back[axis] = push if back[axis] is None else back[axis] + push
                if total_ref is not None:
                    total_ref[partner, bead, axis] += jnp.sum(push, axis=0)
        for axis in range(3):
            value = back[axis].reshape(SPAN, lanes)
            if total_ref is None:
                back_ref[cell, bead, axis, here, :] = value
            else:
                back_ref[cell, bead, axis, here, :] += value


def repeat_lanes(scale, position, params, next_position, next_params, lanes_ref, sizes_ref):
    beads, _, cells, lanes = position.shape

    def per_cell(cell, carry):
        for layer, place, values in ((0, position, params), (1, next_position, next_params)):
            for kind in range(2):
                row = values[kind, pl.ds(cell, 1), :]
                row = scale * row if kind == 0 else row
                sizes_ref[layer * cells + cell, kind] = jnp.broadcast_to(row, (8, lanes))
            for bead in range(beads):
                for axis in range(3):
                    row = place[bead, axis, pl.ds(cell, 1), :]
                    row = scale * (row + 1.0 if layer == 1 and axis == 0 else row)
                    lanes_ref[bead, layer * cells + cell, axis] = jnp.broadcast_to(row, (8, lanes))
        return carry

    lax.fori_loop(0, cells, per_cell, 0)


def fold_back(back_ref, cell, bead):
    lanes = back_ref.shape[-1]
    column = lax.broadcasted_iota(jnp.int32, (lanes, 8), 1)
    sums = [jnp.sum(back_ref[cell, bead, axis], axis=1, keepdims=True) for axis in range(3)]
    block = jnp.where(
        column == 0, sums[0], jnp.where(column == 1, sums[1], jnp.where(column == 2, sums[2], 0.0))
    )
    return block.T[0:3]


def put_rows(out_ref, bead, cell, block):
    for axis in range(3):
        out_ref[bead, axis, pl.ds(cell, 1), :] = block[axis : axis + 1]


def fold_total(total_ref, cell, bead):
    return jnp.concatenate(
        [jnp.sum(total_ref[cell, bead, axis], axis=0, keepdims=True) for axis in range(3)], axis=0
    )


def pairs_kernel(
    plan, occupied, position, params, next_position, next_params,
    force_ref, other_ref, lanes_ref, sizes_ref, rows_ref, size_ref, total_ref, back_ref,
):
    beads, _, cells, lanes = position.shape
    factor = LONG_FACTOR
    together = max(1, 4 // beads)
    repeat_lanes(1.0, position, params, next_position, next_params, lanes_ref, sizes_ref)
    total_ref[...] = jnp.zeros_like(total_ref)

    refs = (lanes_ref, sizes_ref, rows_ref, size_ref)

    def spread(index, carry):
        for shift in range(together):
            cell = index * together + shift
            spread_rows(position, params, cell, rows_ref, size_ref)
            for first in range(0, EARLY_ROWS, SPAN):
                meet(cell, first, [(cell, 0.0, 0.0)], refs + (None, back_ref))
        return carry

    lax.fori_loop(0, cells // together, spread, 0)

    def entry_of(entry):
        return (
            plan[cells + 1 + 3 * entry],
            plan[cells + 2 + 3 * entry].astype(F32),
            plan[cells + 3 + 3 * entry].astype(F32),
        )

    def per_cell(cell, carry):
        begin, end = plan[cell], plan[cell + 1]
        odd = lax.rem(end - begin, 2)

        most = lanes // SPAN
        needed = lax.div(occupied[cell] + (SPAN - 1), SPAN)
        for parts in (most - 1, most):
            firsts = [part * SPAN for part in range(parts)]

            def all_rows(_, carry, firsts=firsts):
                for first in firsts:
                    if first >= EARLY_ROWS:
                        meet(cell, first, [(cell, 0.0, 0.0)], refs + (None, back_ref))

                def single(entry, carry):
                    for first in firsts:
                        meet(cell, first, [entry_of(entry)], refs + (total_ref, back_ref))
                    return carry

                def double(step, carry):
                    entry = begin + odd + 2 * step
                    both = [entry_of(entry), entry_of(entry + 1)]
                    for first in firsts:
                        meet(cell, first, both, refs + (total_ref, back_ref))
                    return carry

                carry = lax.fori_loop(begin, begin + odd, single, carry)
                return lax.fori_loop(0, lax.div(end - begin, 2), double, carry)

            full = (needed == most).astype(jnp.int32)
            lax.fori_loop(0, full if parts == most else 1 - full, all_rows, 0)
        return carry

    lax.fori_loop(0, cells, per_cell, 0)

    def finish(index, carry):
        for shift in range(together):
            cell = index * together + shift
            alive = params[1, pl.ds(cell, 1), :] > 0.0
            for bead in range(beads):
                total = fold_total(total_ref, cell, bead) - fold_back(back_ref, cell, bead)
                put_rows(force_ref, bead, cell, jnp.where(alive, factor * total, 0.0))
                put_rows(other_ref, bead, cell, factor * fold_total(total_ref, cell + cells, bead))
        return carry

    lax.fori_loop(0, cells // together, finish, 0)


def octant_key(x, y, z, alive):
    zed = jnp.where(z >= 0.5, 1.0, 0.0)
    gray = jnp.where(y >= 0.5, 3.0 - zed, zed)
    return jnp.where(alive, jnp.where(x >= 0.5, 7.0 - gray, gray), 8.0)


def reach_lists(domain_cells):
    octants = []
    for bit_x in range(2):
        for bit_y in range(2):
            for bit_z in range(2):
                gray = 3 - bit_z if bit_y else bit_z
                octants.append((7 - gray if bit_x else gray, (bit_x, bit_y, bit_z)))
    classes = [[[] for _ in range(domain_cells)] for _ in STEPS]
    for one in range(domain_cells):
        runs = {}
        for layer in range(2):
            for two in range(domain_cells):
                step = (layer, two // GZ - one // GZ, two % GZ - one % GZ)
                if abs(step[1]) > 1 or abs(step[2]) > 1 or (layer == 0 and two <= one):
                    continue
                keys = [
                    key
                    for key, bits in octants
                    if all(move == 0 or bit == (move > 0) for move, bit in zip(step, bits))
                ]
                entry = (two + layer * domain_cells, step[1], step[2], min(keys), max(keys) + 1)
                runs.setdefault(entry[4] - entry[3], []).append(entry)
        for length, entries in sorted(runs.items()):
            entries.sort(key=lambda entry: entry[3:])
            span = RUN_ROWS.get(length, SPAN)
            for place, (rows, count) in enumerate(STEPS):
                if rows == span:
                    whole = len(entries) // count * count
                    classes[place][one] += entries[:whole]
                    entries = entries[whole:]
    starts, values = [], []
    for lists in classes:
        for entries in lists:
            starts.append(len(values) // 5)
            values += [value for entry in entries for value in entry]
        starts.append(len(values) // 5)
    return np.array(starts, np.int32), np.array(values, np.int32)


def split_three(value):
    high = value.astype(BF16).astype(F32)
    rest = value - high
    middle = rest.astype(BF16).astype(F32)
    return high, middle, rest - middle


def order_kernel(position, params, table, matrix, out_ref, table_out, matrix_out):
    beads, _, cells, lanes = position.shape
    table_out[...] = table[...]
    matrix_out[...] = matrix[...]
    row = lax.broadcasted_iota(jnp.int32, (lanes, lanes), 0)
    column = lax.broadcasted_iota(jnp.int32, (lanes, lanes), 1)
    before = jnp.where(row < column, 1.0, 0.0).astype(BF16)
    counter = jnp.concatenate([before, jnp.ones((lanes, lanes), BF16)], axis=0)
    kind = lax.broadcasted_iota(jnp.int32, (16, lanes), 0).astype(F32)
    place_row = row.astype(F32)
    every = [(shift, bead) for shift in range(GROUP) for bead in range(beads)]

    def per_group(index, carry):
        blocks, sames, marks = [], [], []
        for shift, bead in every:
            cell = index * GROUP + shift
            sizes = atom_rows(params, cell)[:2]
            place = atom_rows(position.at[bead], cell)
            key = octant_key(*place, sizes[1] > 0.0)
            same = jnp.where(key == kind, 1.0, 0.0)
            less = jnp.where(key < kind, 1.0, 0.0)
            scaled = [SHORT_SCALE * value for value in (*place, sizes[0])]
            blocks.append(
                jnp.concatenate([*scaled, sizes[1], jnp.zeros((3, lanes), F32)], axis=0)
            )
            sames.append(same)
            marks.append(jnp.concatenate([same, less], axis=1))
        counts = jnp.dot(
            jnp.concatenate(marks, axis=0).astype(BF16), counter, preferred_element_type=F32
        )
        for place, (shift, bead) in enumerate(every):
            cell = index * GROUP + shift
            rank = jnp.sum(
                sames[place] * counts[16 * place : 16 * place + 16], axis=0, keepdims=True
            )
            chosen = jnp.where(rank == place_row, 1.0, 0.0).astype(BF16)
            moved = lax.dot_general(
                jnp.concatenate(split_three(blocks[place]), axis=0).astype(BF16),
                chosen,
                (((1,), (1,)), ((), ())),
                preferred_element_type=F32,
            )
            out_ref[bead, cell, 0:5, :] = (moved[0:8] + moved[8:16] + moved[16:24])[0:5]
            out_ref[bead, cell, 5:6, :] = rank
            out_ref[bead, cell, 6:8, :] = jnp.zeros((2, lanes), F32)
        return carry

    lax.fori_loop(0, cells // GROUP, per_group, 0)


def meet_runs(span, local, runs, lanes_ref, sizes_ref, rows_ref, total_ref, back_ref):
    beads, lanes = lanes_ref.shape[0], lanes_ref.shape[-1]
    for bead in range(beads):
        for firsts, partner, step_y, step_z in runs:
            here = pl.ds(firsts[bead], span)
            rows = [
                rows_ref[local, bead, kind, here, :].reshape(span // 8, 8, lanes)
                for kind in range(5)
            ]
            half = rows[3] + sizes_ref[partner, 0]
            s2 = half * half
            apart = [
                lanes_ref[bead, partner, 0] - rows[0],
                (lanes_ref[bead, partner, 1] + step_y) - rows[1],
                (lanes_ref[bead, partner, 2] + step_z) - rows[2],
            ]
            radius_sq = apart[0] * apart[0] + apart[1] * apart[1] + apart[2] * apart[2]
            depth = rows[4] * sizes_ref[partner, 1]
            weight = depth * short_weight(radius_sq + s2, s2)
            for axis in range(3):
                push = weight * apart[axis]
                flat_push = push.reshape(span, lanes)
                if total_ref is None:
                    back_ref[local, bead, axis, here, :] = flat_push
                else:
                    back_ref[local, bead, axis, here, :] += flat_push
                    total_ref[partner, bead, axis] += jnp.sum(push, axis=0)


def reach_kernel(
    plan, position, params, next_position, next_params, ordered, force_ref, other_ref, lanes_ref,
    sizes_ref, rows_ref, total_ref, back_ref,
):
    beads, _, cells, lanes = position.shape
    entries_at = len(STEPS) * (cells + 1)
    bounds_at = plan.shape[0] - beads * cells * 9
    factor = SHORT_FACTOR
    repeat_lanes(SHORT_SCALE, position, params, next_position, next_params, lanes_ref, sizes_ref)
    total_ref[...] = jnp.zeros_like(total_ref)
    rows_ref[:, :, :, lanes:, :] = jnp.zeros((GROUP, beads, 5, SPARE, lanes), F32)
    row = lax.broadcasted_iota(jnp.int32, (lanes, lanes), 0).astype(F32)
    slot = lax.broadcasted_iota(jnp.int32, (8, lanes), 1)
    column = lax.broadcasted_iota(jnp.int32, (lanes, 8), 1)
    refs = (lanes_ref, sizes_ref, rows_ref)
    every = [(local, bead) for local in range(GROUP) for bead in range(beads)]

    def per_group(group, carry):
        for local, bead in every:
            block = ordered[bead, group * GROUP + local].T
            for axis in range(5):
                rows_ref[local, bead, axis, 0:lanes, :] = jnp.broadcast_to(
                    block[:, axis : axis + 1], (lanes, lanes)
                )
            if bead == beads - 1:
                for first in range(0, EARLY_ROWS, SPAN):
                    run = ([first] * beads, group * GROUP + local, 0.0, 0.0)
                    meet_runs(SPAN, local, [run], *refs, None, back_ref)

        def per_cell(local, carry):
            cell = group * GROUP + local

            def bound(bead, octant):
                return plan[bounds_at + (bead * cells + cell) * 9 + octant]

            def itself(index, carry):
                first = pl.multiple_of(index * SPAN, SPAN)
                run = ([first] * beads, cell, 0.0, 0.0)
                meet_runs(SPAN, local, [run], *refs, None, back_ref)
                return carry

            lax.fori_loop(
                EARLY_ROWS // SPAN, lax.div(bound(0, 8) + (SPAN - 1), SPAN), itself, 0
            )

            for place, (span, count) in enumerate(STEPS):
                begin = plan[place * (cells + 1) + cell]
                end = plan[place * (cells + 1) + cell + 1]

                def per_step(step, carry, span=span, count=count, begin=begin):
                    runs, longest = [], 0
                    for shift in range(count):
                        at = entries_at + 5 * (begin + step * count + shift)
                        begins = [
                            lax.bitwise_and(bound(bead, plan[at + 3]), -8) for bead in range(beads)
                        ]
                        for bead in range(beads):
                            longest = jnp.maximum(longest, bound(bead, plan[at + 4]) - begins[bead])
                        runs.append(
                            (
                                begins, plan[at], SHORT_SCALE * plan[at + 1].astype(F32),
                                SHORT_SCALE * plan[at + 2].astype(F32),
                            )
                        )

                    def per_span(index, carry):
                        moved = [
                            (
                                [
                                    pl.multiple_of(jnp.minimum(first + index * span, lanes), 8)
                                    for first in begins
                                ],
                                *rest,
                            )
                            for begins, *rest in runs
                        ]
                        meet_runs(span, local, moved, *refs, total_ref, back_ref)
                        return carry

                    return lax.fori_loop(0, lax.div(longest + (span - 1), span), per_span, carry)

                lax.fori_loop(0, lax.div(end - begin, count), per_step, 0)
            return carry

        lax.fori_loop(0, GROUP, per_cell, 0)

        for local, bead in every:
            cell = group * GROUP + local
            alive = plan[bounds_at + cell * 9 + 8]
            sums = [
                jnp.sum(back_ref[local, bead, axis, 0:lanes, :], axis=1, keepdims=True)
                for axis in range(3)
            ]
            block = jnp.where(
                column == 0,
                sums[0],
                jnp.where(column == 1, sums[1], jnp.where(column == 2, sums[2], 0.0)),
            ).T
            block = jnp.where(slot < alive, block, 0.0)
            chosen = jnp.where(ordered[bead, cell, 5:6, :] == row, 1.0, 0.0).astype(BF16)
            moved = lax.dot_general(
                jnp.concatenate(split_three(block), axis=0).astype(BF16),
                chosen,
                (((1,), (0,)), ((), ())),
                preferred_element_type=F32,
            )
            put_rows(force_ref, bead, cell, (moved[0:8] + moved[8:16] + moved[16:24])[0:3])
        return carry

    lax.fori_loop(0, cells // GROUP, per_group, 0)

    def finish(index, carry):
        for shift, bead in every:
            cell = index * GROUP + shift
            held = jnp.concatenate(atom_rows(force_ref.at[bead], cell), axis=0)
            put_rows(force_ref, bead, cell, factor * (fold_total(total_ref, cell, bead) - held))
            put_rows(other_ref, bead, cell, factor * fold_total(total_ref, cell + cells, bead))
        return carry

    lax.fori_loop(0, cells // GROUP, finish, 0)


def short_forces(position, params, next_position, next_params, ordered, bounds):
    beads, _, cells, lanes = position.shape
    starts, entries = reach_lists(cells)
    plan = jnp.concatenate([jnp.asarray(starts), jnp.asarray(entries), bounds])
    forces = jax.ShapeDtypeStruct((beads, 3, cells, lanes), F32)
    return call(
        reach_kernel,
        (plan, position, params, next_position, next_params, ordered),
        1,
        (forces, forces),
        [
            pltpu.VMEM((beads, 2 * cells, 3, 8, lanes), F32),
            pltpu.VMEM((2 * cells, 2, 8, lanes), F32),
            pltpu.VMEM((GROUP, beads, 5, lanes + SPARE, lanes), F32),
            pltpu.VMEM((2 * cells, beads, 3, 8, lanes), F32),
            pltpu.VMEM((GROUP, beads, 3, lanes + SPARE, lanes), F32),
        ],
        PAIR_FLOPS * beads * 70,
    )


def call(kernel, inputs, smem, outputs, scratch, flops, fetched=()):
    def space(place):
        if place in fetched:
            return pltpu.HBM
        return pltpu.SMEM if place < smem else pltpu.VMEM

    return pl.pallas_call(
        kernel,
        out_shape=outputs,
        in_specs=[pl.BlockSpec(memory_space=space(place)) for place in range(len(inputs))],
        scratch_shapes=scratch,
        compiler_params=pltpu.CompilerParams(vmem_limit_bytes=VMEM_LIMIT),
        cost_estimate=pl.CostEstimate(flops=flops, bytes_accessed=1 << 18, transcendentals=0),
    )(*inputs)


PAIR_FLOPS = 40 * 128 * 128


def pair_forces(position, params, occupied, next_position, next_params):
    beads, _, cells, lanes = position.shape
    starts, entries = partner_lists(cells)
    forces = jax.ShapeDtypeStruct((beads, 3, cells, lanes), F32)
    return call(
        pairs_kernel,
        (
            jnp.asarray(np.concatenate([starts, entries])), occupied, position, params,
            next_position, next_params,
        ),
        2,
        (forces, forces),
        [
            pltpu.VMEM((beads, 2 * cells, 3, 8, lanes), F32),
            pltpu.VMEM((2 * cells, 2, 8, lanes), F32),
            pltpu.VMEM((cells, beads, 3, lanes, lanes), F32),
            pltpu.VMEM((cells, 2, lanes, lanes), F32),
            pltpu.VMEM((2 * cells, beads, 3, 8, lanes), F32),
            pltpu.VMEM((cells, beads, 3, lanes, lanes), F32),
        ],
        PAIR_FLOPS * beads * (len(entries) // 3 + cells),
    )


def kick_kernel(
    piece_rows, groups, rank, table_hbm, position, momenta, noise, force, back, params, partial_ref,
    piece_ref, flat_ref, table, done,
):
    fetch = pltpu.make_async_copy(table_hbm, table, done)
    fetch.start()
    beads, rows, _ = position.shape
    holders = piece_ref.shape[0]
    reduced = table.shape[0]
    first = rank[0] * beads
    if holders * piece_rows > rows:
        piece_ref[...] = jnp.zeros_like(piece_ref)
    mass = params[2]
    per_root = lax.rsqrt(mass)
    per_root = per_root * (1.5 - 0.5 * mass * per_root * per_root)
    per_mass = jnp.concatenate([1.0 / mass] * 3, axis=0)
    per_root = jnp.concatenate([per_root] * 3, axis=0)
    for bead in range(beads):
        kicked = momenta[bead] + 0.5 * TIME_STEP * (force[bead] + back[bead])
        flat_ref[0, bead] = position[bead]
        flat_ref[1, bead] = kicked * per_mass
        flat_ref[2, bead] = noise[bead] * per_root
    for kind in range(3):
        for bead in range(beads):
            base = (kind * beads + bead) * piece_rows
            for owner in range(holders):
                start = owner * piece_rows
                count = min(piece_rows, rows - start)
                if count > 0:
                    piece_ref[owner, base : base + count, :] = flat_ref[
                        kind, bead, start : start + count, :
                    ]
    fetch.wait()
    for group in range(reduced):
        total = None
        for kind in range(3):
            for bead in range(beads):
                term = table[group, kind * holders * beads + first + bead] * flat_ref[kind, bead]
                total = term if total is None else total + term
        for copy in range(groups):
            partial_ref[group * groups + copy] = total


def move_kernel(piece_rows, beads, matrix_hbm, arrived, out_ref, gathered, matrix, done):
    fetch = pltpu.make_async_copy(matrix_hbm, matrix, done)
    fetch.start()
    holders = arrived.shape[0]
    taken = 3 * beads
    given = 2 * beads
    for row in range(piece_rows):
        for holder in range(holders):
            gathered[row, holder * taken : (holder + 1) * taken, :] = arrived[
                holder, pl.ds(row, taken, stride=piece_rows), :
            ]
    fetch.wait()
    for row in range(piece_rows):
        moved = lax.dot_general(
            matrix[...],
            gathered[row],
            (((1,), (0,)), ((), ())),
            precision=lax.Precision.HIGHEST,
            preferred_element_type=F32,
        )
        for holder in range(holders):
            out_ref[holder, row * given : (row + 1) * given, :] = moved[
                holder * given : (holder + 1) * given
            ]


def finish_kernel(
    piece_rows, groups, rank, table_hbm, moved, slow, params, position_ref, momentum_ref,
    velocity_ref, table, done,
):
    fetch = pltpu.make_async_copy(table_hbm, table, done)
    fetch.start()
    beads, rows, _ = position_ref.shape
    holders = moved.shape[0]
    given = 2 * beads
    reduced = table.shape[0]
    first = 3 * holders * beads + rank[0] * beads
    mass = jnp.concatenate([params[2]] * 3, axis=0)
    for bead in range(beads):
        for owner in range(holders):
            start = owner * piece_rows
            count = min(piece_rows, rows - start)
            if count > 0:
                position_ref[bead, start : start + count, :] = moved[
                    owner, pl.ds(bead, count, stride=given), :
                ]
                velocity_ref[bead, start : start + count, :] = moved[
                    owner, pl.ds(beads + bead, count, stride=given), :
                ]
    fetch.wait()
    for bead in range(beads):
        total = mass * velocity_ref[bead]
        for group in range(reduced):
            total = total + table[group, first + bead] * slow[group * groups]
        momentum_ref[bead] = total


def shards(positions, momenta, noise, atom_types, occupancy, type_sigma, type_eps, type_mass):
    beads, cells, _, lanes = positions.shape
    holders = lax.axis_size("bead")
    domains = lax.axis_size("space")
    rank = lax.axis_index("bead")
    total_beads = beads * holders
    rows = 3 * cells
    piece_rows = -(-rows // holders)
    held = max(1, PC // holders)
    groups = max(1, holders // PC)
    contract = contract_matrix(total_beads, PC)
    steps = step_matrices(total_beads)
    rank_table = rank.astype(jnp.int32).reshape(1)
    one_back = [((i + 1) % domains, i) for i in range(domains)]
    one_on = [(i, (i + 1) % domains) for i in range(domains)]

    codes = jnp.arange(type_sigma.shape[0])
    onehot = atom_types[..., None] == codes
    living = jnp.arange(lanes)[None, :] < occupancy[:, None]
    half_sigma = 0.5 * jnp.sum(jnp.where(onehot, type_sigma, 0.0), -1)
    root_eps = jnp.sqrt(jnp.sum(jnp.where(onehot, type_eps, 0.0), -1))
    mass = jnp.sum(jnp.where(onehot, type_mass, 0.0), -1)
    params = jnp.stack([half_sigma, jnp.where(living, root_eps, 0.0), mass], 0)
    positions, momenta, noise = (
        value.transpose(0, 2, 1, 3) for value in (positions, momenta, noise)
    )

    stacked = jnp.concatenate([positions, params[None]], 0)
    next_stacked = lax.ppermute(stacked, "space", one_back)
    next_params = next_stacked[beads]
    spread = 0.5 * TIME_STEP * (total_beads / PC) * contract
    table = np.concatenate([contract @ steps[0, kind] for kind in range(3)] + [spread], axis=1)
    order = steps.reshape(2, 3, holders, beads, holders, beads).transpose(2, 0, 3, 4, 1, 5)
    order = order.reshape(2 * total_beads, 3 * total_beads)
    ordered, table, order = call(
        order_kernel,
        (positions, params, jnp.asarray(table, F32), jnp.asarray(order, F32)),
        0,
        (
            jax.ShapeDtypeStruct((beads, cells, 8, lanes), F32),
            jax.ShapeDtypeStruct(table.shape, F32),
            jax.ShapeDtypeStruct(order.shape, F32),
        ),
        [],
        1 << 22,
    )
    key = octant_key(positions[:, 0], positions[:, 1], positions[:, 2], living[None])
    bounds = jnp.sum(
        (key[:, :, None, :] < jnp.arange(9, dtype=F32)[:, None]).astype(jnp.int32), -1
    )
    force, back = short_forces(
        positions, params, next_stacked[:beads], next_params, ordered, bounds.reshape(-1)
    )
    back = lax.ppermute(back, "space", one_on)

    def flat(value):
        return value.reshape(-1, rows, lanes)

    partial, pieces = call(
        functools.partial(kick_kernel, piece_rows, groups),
        (
            rank_table, table, flat(positions), flat(momenta), flat(noise), flat(force), flat(back),
            params,
        ),
        1,
        (
            jax.ShapeDtypeStruct((PC * groups, rows, lanes), F32),
            jax.ShapeDtypeStruct((holders, 3 * beads * piece_rows, lanes), F32),
        ),
        [
            pltpu.VMEM((3, beads, rows, lanes), F32), pltpu.SMEM(table.shape, F32),
            pltpu.SemaphoreType.DMA,
        ],
        1 << 22,
        (1,),
    )
    arrived = lax.all_to_all(
        partial.reshape(holders, held * rows, lanes), "bead", split_axis=0, concat_axis=0, tiled=True
    )
    contracted = jnp.sum(arrived, 0).reshape(held, 3, cells, lanes)
    contracted, pieces = lax.optimization_barrier((contracted, pieces))
    next_contracted = lax.ppermute(contracted, "space", one_back)
    pieces = lax.all_to_all(pieces, "bead", split_axis=0, concat_axis=0, tiled=True)
    slow, slow_back = pair_forces(
        contracted, params, occupancy, next_contracted, next_params
    )
    slow = slow + lax.ppermute(slow_back, "space", one_on)

    moved = call(
        functools.partial(move_kernel, piece_rows, beads),
        (order, pieces),
        0,
        jax.ShapeDtypeStruct((holders, 2 * beads * piece_rows, lanes), F32),
        [
            pltpu.VMEM((piece_rows, 3 * total_beads, lanes), F32), pltpu.VMEM(order.shape, F32),
            pltpu.SemaphoreType.DMA,
        ],
        1 << 23,
        (0,),
    )
    moved_rows = 2 * beads * piece_rows
    sent = jnp.concatenate(
        [
            moved,
            jnp.broadcast_to(slow.reshape(1, held * rows, lanes), (holders, held * rows, lanes)),
        ],
        1,
    )
    got = lax.all_to_all(sent, "bead", split_axis=0, concat_axis=0, tiled=True)
    result = jax.ShapeDtypeStruct((beads, rows, lanes), F32)
    new_positions, new_momenta = call(
        functools.partial(finish_kernel, piece_rows, groups),
        (
            rank_table, table, got[:, :moved_rows],
            got[:, moved_rows:].reshape(holders * held, rows, lanes), params,
        ),
        1,
        (result, result),
        [
            pltpu.VMEM((beads, rows, lanes), F32), pltpu.SMEM(table.shape, F32),
            pltpu.SemaphoreType.DMA,
        ],
        1 << 20,
        (1,),
    )

    def cells_first(value):
        return value.reshape(beads, 3, cells, lanes).transpose(0, 2, 1, 3)

    return cells_first(new_positions), cells_first(new_momenta)


def solution(mesh):
    placed = (
        P("bead", "space", None, None),
        P("bead", "space", None, None),
        P("bead", "space", None, None),
        P("space", None),
        P("space"),
        P(),
        P(),
        P(),
    )
    return jax.shard_map(
        shards,
        mesh=mesh,
        in_specs=placed,
        out_specs=(P("bead", "space", None, None), P("bead", "space", None, None)),
        check_vma=False,
    )
```

```python
import functools

import jax
import jax.numpy as jnp
import numpy as np
from jax import lax
from jax.experimental import pallas as pl
from jax.experimental.pallas import tpu as pltpu
from jax.sharding import PartitionSpec as P

PC = 8
GY = 4
GZ = 4

TIME_STEP = 0.05
INVERSE_TEMP = 32.0
CENTROID_FRICTION = 1.0
INNER_CUT = 0.5
OUTER_CUT = 1.0
CUBE_ROOT_TWO = 2.0 ** (1.0 / 3.0)
F32 = jnp.float32
BF16 = jnp.bfloat16
SPAN = 32
GROUP = 4
STEPS = ((24, 4), (24, 2), (24, 1), (40, 2), (40, 1), (32, 2), (32, 1), (96, 1))
RUN_ROWS = {1: 24, 2: 40, 6: 96}
SPARE = 96
VMEM_LIMIT = 48 * 1024 * 1024


def mode_matrix(number):
    rows = np.arange(number, dtype=np.float64)[:, None]
    column = np.arange(number, dtype=np.float64)[None, :]
    phases = 2.0 * np.pi * rows * column / number
    factor = np.sqrt(2.0 / number)
    middle = np.cos(np.pi * rows) / np.sqrt(number)
    matrix = np.where(column < number / 2, factor * np.cos(phases), factor * np.sin(phases))
    matrix = np.where(column == number / 2, middle, matrix)
    return np.where(column == 0, 1.0 / np.sqrt(number), matrix)


def contract_matrix(full_count, reduced):
    selected = np.arange(reduced)
    selected = np.where(selected <= reduced // 2, selected, selected + full_count - reduced)
    chosen = mode_matrix(full_count)[:, selected]
    return np.sqrt(reduced / full_count) * (mode_matrix(reduced) @ chosen.T)


def step_matrices(number):
    index = np.arange(number, dtype=np.float64)
    frequency = 2.0 * (number / INVERSE_TEMP) * np.sin(np.pi * index / number)
    friction = np.where(index == 0, CENTROID_FRICTION, 2.0 * frequency)
    damping = np.exp(-friction * TIME_STEP)
    kicking = np.sqrt((1.0 - damping * damping) / INVERSE_TEMP)
    cosine = np.cos(frequency * TIME_STEP)
    sine = np.sin(frequency * TIME_STEP)
    drift = np.where(index == 0, TIME_STEP, sine / np.where(index == 0, 1.0, frequency))
    modes = mode_matrix(number)

    def over_beads(diagonal):
        return (modes * diagonal[None, :]) @ modes.T

    return np.array(
        [
            [over_beads(cosine), over_beads(drift * damping), over_beads(drift * kicking)],
            [
                over_beads(-frequency * sine),
                over_beads(cosine * damping),
                over_beads(cosine * kicking),
            ],
        ]
    )


def partner_lists(domain_cells):
    lists = []
    for one in range(domain_cells):
        near = []
        for two in range(domain_cells):
            step_y, step_z = two // GZ - one // GZ, two % GZ - one % GZ
            if abs(step_y) <= 1 and abs(step_z) <= 1:
                near.append((two, step_y, step_z))
        later = [entry for entry in near if entry[0] > one]
        lists.append(later + [(two + domain_cells, y, z) for two, y, z in near])
    starts = np.cumsum([0] + [len(entries) for entries in lists]).astype(np.int32)
    return starts, np.array([value for entries in lists for entry in entries for value in entry], np.int32)


def long_weight(h, radius_sq, s2):
    inverse = pl.reciprocal(h, approx=True)
    quotient = (CUBE_ROOT_TWO * s2) * inverse
    twice = quotient * quotient * quotient
    outer = jnp.maximum(1.0 - radius_sq, 0.0)
    inner = jnp.maximum(1.0 - 4.0 * radius_sq, 0.0)
    switch = outer * outer - inner * inner
    slope = outer - 4.0 * inner
    return twice * ((twice - 1.0) * (3.0 * (switch * inverse) + slope) - slope)


def short_weight(h, s2):
    inverse = pl.reciprocal(h, approx=True)
    quotient = s2 * inverse
    sixth = quotient * quotient * quotient
    lifted = jnp.maximum((quotient + inverse) - 2.0 / 3.0, 1.0 / 3.0)
    bracket = (sixth - 0.5) * lifted - 1.0 / 6.0
    return (sixth * bracket) * ((lifted - 1.0 / 3.0) * h)


LONG_FACTOR = 4.0
SHORT_SCALE = 1.0 / INNER_CUT
SHORT_FACTOR = 192.0 / SHORT_SCALE


def atom_rows(block, cell):
    return [block[kind, pl.ds(cell, 1), :] for kind in range(3)]


def columns(block):
    few, lanes = block.shape
    return jnp.concatenate([block, jnp.zeros((8 - few, lanes), F32)], axis=0).T


def spread_rows(position, params, cell, rows_ref, size_ref):
    beads, lanes = position.shape[0], position.shape[-1]
    sizes = columns(jnp.concatenate(atom_rows(params, cell)[:2], axis=0))
    for kind in range(2):
        size_ref[cell, kind] = jnp.broadcast_to(sizes[:, kind : kind + 1], (lanes, lanes))
    for bead in range(beads):
        block = columns(jnp.concatenate(atom_rows(position.at[bead], cell), axis=0))
        for axis in range(3):
            rows_ref[cell, bead, axis] = jnp.broadcast_to(
                block[:, axis : axis + 1], (lanes, lanes)
            )


def meet(cell, first, partners, refs):
    lanes_ref, sizes_ref, rows_ref, size_ref, total_ref, back_ref = refs
    beads, lanes = lanes_ref.shape[0], lanes_ref.shape[-1]
    here = pl.ds(first, SPAN)
    tall = (SPAN // 8, 8, lanes)
    row_half = size_ref[cell, 0, here, :].reshape(tall)
    row_root = size_ref[cell, 1, here, :].reshape(tall)
    known = []
    for partner, _, _ in partners:
        half = row_half + sizes_ref[partner, 0]
        s2 = half * half
        known.append((s2, row_root * sizes_ref[partner, 1]))
    for bead in range(beads):
        rows = [rows_ref[cell, bead, axis, here, :].reshape(tall) for axis in range(3)]
        back = [None, None, None]
        for (partner, step_y, step_z), (s2, depth) in zip(partners, known):
            apart = [
                lanes_ref[bead, partner, 0] - rows[0],
                (lanes_ref[bead, partner, 1] + step_y) - rows[1],
                (lanes_ref[bead, partner, 2] + step_z) - rows[2],
            ]
            radius_sq = apart[0] * apart[0] + apart[1] * apart[1] + apart[2] * apart[2]
            weight = depth * long_weight(radius_sq + s2, radius_sq, s2)
            for axis in range(3):
                push = weight * apart[axis]
                back[axis] = push if back[axis] is None else back[axis] + push
                if total_ref is not None:
                    total_ref[partner, bead, axis] += jnp.sum(push, axis=0)
        for axis in range(3):
            value = back[axis].reshape(SPAN, lanes)
            if total_ref is None:
                back_ref[cell, bead, axis, here, :] = value
            else:
                back_ref[cell, bead, axis, here, :] += value


def repeat_lanes(scale, position, params, next_position, next_params, lanes_ref, sizes_ref):
    beads, _, cells, lanes = position.shape

    def per_cell(cell, carry):
        for layer, place, values in ((0, position, params), (1, next_position, next_params)):
            for kind in range(2):
                row = values[kind, pl.ds(cell, 1), :]
                row = scale * row if kind == 0 else row
                sizes_ref[layer * cells + cell, kind] = jnp.broadcast_to(row, (8, lanes))
            for bead in range(beads):
                for axis in range(3):
                    row = place[bead, axis, pl.ds(cell, 1), :]
                    row = scale * (row + 1.0 if layer == 1 and axis == 0 else row)
                    lanes_ref[bead, layer * cells + cell, axis] = jnp.broadcast_to(row, (8, lanes))
        return carry

    lax.fori_loop(0, cells, per_cell, 0)


def fold_back(back_ref, cell, bead):
    lanes = back_ref.shape[-1]
    column = lax.broadcasted_iota(jnp.int32, (lanes, 8), 1)
    sums = [jnp.sum(back_ref[cell, bead, axis], axis=1, keepdims=True) for axis in range(3)]
    block = jnp.where(
        column == 0, sums[0], jnp.where(column == 1, sums[1], jnp.where(column == 2, sums[2], 0.0))
    )
    return block.T[0:3]


def put_rows(out_ref, bead, cell, block):
    for axis in range(3):
        out_ref[bead, axis, pl.ds(cell, 1), :] = block[axis : axis + 1]


def fold_total(total_ref, cell, bead):
    return jnp.concatenate(
        [jnp.sum(total_ref[cell, bead, axis], axis=0, keepdims=True) for axis in range(3)], axis=0
    )


def pairs_kernel(
    plan, occupied, position, params, next_position, next_params,
    force_ref, other_ref, lanes_ref, sizes_ref, rows_ref, size_ref, total_ref, back_ref,
):
    beads, _, cells, lanes = position.shape
    factor = LONG_FACTOR
    together = max(1, 4 // beads)
    repeat_lanes(1.0, position, params, next_position, next_params, lanes_ref, sizes_ref)
    total_ref[...] = jnp.zeros_like(total_ref)

    refs = (lanes_ref, sizes_ref, rows_ref, size_ref)

    def spread(index, carry):
        for shift in range(together):
            cell = index * together + shift
            spread_rows(position, params, cell, rows_ref, size_ref)
            for first in range(0, lanes, SPAN):
                meet(cell, first, [(cell, 0.0, 0.0)], refs + (None, back_ref))
        return carry

    lax.fori_loop(0, cells // together, spread, 0)

    def entry_of(entry):
        return (
            plan[cells + 1 + 3 * entry],
            plan[cells + 2 + 3 * entry].astype(F32),
            plan[cells + 3 + 3 * entry].astype(F32),
        )

    def per_cell(cell, carry):
        begin, end = plan[cell], plan[cell + 1]
        odd = lax.rem(end - begin, 2)

        most = lanes // SPAN
        needed = lax.div(occupied[cell] + (SPAN - 1), SPAN)
        for parts in (most - 1, most):
            firsts = [part * SPAN for part in range(parts)]

            def all_rows(_, carry, firsts=firsts):
                def single(entry, carry):
                    for first in firsts:
                        meet(cell, first, [entry_of(entry)], refs + (total_ref, back_ref))
                    return carry

                def double(step, carry):
                    entry = begin + odd + 2 * step
                    both = [entry_of(entry), entry_of(entry + 1)]
                    for first in firsts:
                        meet(cell, first, both, refs + (total_ref, back_ref))
                    return carry

                carry = lax.fori_loop(begin, begin + odd, single, carry)
                return lax.fori_loop(0, lax.div(end - begin, 2), double, carry)

            full = (needed == most).astype(jnp.int32)
            lax.fori_loop(0, full if parts == most else 1 - full, all_rows, 0)
        return carry

    lax.fori_loop(0, cells, per_cell, 0)

    def finish(index, carry):
        for shift in range(together):
            cell = index * together + shift
            alive = params[1, pl.ds(cell, 1), :] > 0.0
            for bead in range(beads):
                total = fold_total(total_ref, cell, bead) - fold_back(back_ref, cell, bead)
                put_rows(force_ref, bead, cell, jnp.where(alive, factor * total, 0.0))
                put_rows(other_ref, bead, cell, factor * fold_total(total_ref, cell + cells, bead))
        return carry

    lax.fori_loop(0, cells // together, finish, 0)


def octant_key(x, y, z, alive):
    zed = jnp.where(z >= 0.5, 1.0, 0.0)
    gray = jnp.where(y >= 0.5, 3.0 - zed, zed)
    return jnp.where(alive, jnp.where(x >= 0.5, 7.0 - gray, gray), 8.0)


def reach_lists(domain_cells):
    octants = []
    for bit_x in range(2):
        for bit_y in range(2):
            for bit_z in range(2):
                gray = 3 - bit_z if bit_y else bit_z
                octants.append((7 - gray if bit_x else gray, (bit_x, bit_y, bit_z)))
    classes = [[[] for _ in range(domain_cells)] for _ in STEPS]
    for one in range(domain_cells):
        runs = {}
        for layer in range(2):
            for two in range(domain_cells):
                step = (layer, two // GZ - one // GZ, two % GZ - one % GZ)
                if abs(step[1]) > 1 or abs(step[2]) > 1 or (layer == 0 and two <= one):
                    continue
                keys = [
                    key
                    for key, bits in octants
                    if all(move == 0 or bit == (move > 0) for move, bit in zip(step, bits))
                ]
                entry = (two + layer * domain_cells, step[1], step[2], min(keys), max(keys) + 1)
                runs.setdefault(entry[4] - entry[3], []).append(entry)
        for length, entries in sorted(runs.items()):
            entries.sort(key=lambda entry: entry[3:])
            span = RUN_ROWS.get(length, SPAN)
            for place, (rows, count) in enumerate(STEPS):
                if rows == span:
                    whole = len(entries) // count * count
                    classes[place][one] += entries[:whole]
                    entries = entries[whole:]
    starts, values = [], []
    for lists in classes:
        for entries in lists:
            starts.append(len(values) // 5)
            values += [value for entry in entries for value in entry]
        starts.append(len(values) // 5)
    return np.array(starts, np.int32), np.array(values, np.int32)


def split_three(value):
    high = value.astype(BF16).astype(F32)
    rest = value - high
    middle = rest.astype(BF16).astype(F32)
    return high, middle, rest - middle


def order_kernel(position, params, table, matrix, out_ref, table_out, matrix_out):
    beads, _, cells, lanes = position.shape
    table_out[...] = table[...]
    matrix_out[...] = matrix[...]
    row = lax.broadcasted_iota(jnp.int32, (lanes, lanes), 0)
    column = lax.broadcasted_iota(jnp.int32, (lanes, lanes), 1)
    before = jnp.where(row < column, 1.0, 0.0).astype(BF16)
    counter = jnp.concatenate([before, jnp.ones((lanes, lanes), BF16)], axis=0)
    kind = lax.broadcasted_iota(jnp.int32, (16, lanes), 0).astype(F32)
    place_row = row.astype(F32)
    every = [(shift, bead) for shift in range(GROUP) for bead in range(beads)]

    def per_group(index, carry):
        blocks, sames, marks = [], [], []
        for shift, bead in every:
            cell = index * GROUP + shift
            sizes = atom_rows(params, cell)[:2]
            place = atom_rows(position.at[bead], cell)
            key = octant_key(*place, sizes[1] > 0.0)
            same = jnp.where(key == kind, 1.0, 0.0)
            less = jnp.where(key < kind, 1.0, 0.0)
            scaled = [SHORT_SCALE * value for value in (*place, sizes[0])]
            blocks.append(
                jnp.concatenate([*scaled, sizes[1], jnp.zeros((3, lanes), F32)], axis=0)
            )
            sames.append(same)
            marks.append(jnp.concatenate([same, less], axis=1))
        counts = jnp.dot(
            jnp.concatenate(marks, axis=0).astype(BF16), counter, preferred_element_type=F32
        )
        for place, (shift, bead) in enumerate(every):
            cell = index * GROUP + shift
            rank = jnp.sum(
                sames[place] * counts[16 * place : 16 * place + 16], axis=0, keepdims=True
            )
            chosen = jnp.where(rank == place_row, 1.0, 0.0).astype(BF16)
            moved = lax.dot_general(
                jnp.concatenate(split_three(blocks[place]), axis=0).astype(BF16),
                chosen,
                (((1,), (1,)), ((), ())),
                preferred_element_type=F32,
            )
            out_ref[bead, cell, 0:5, :] = (moved[0:8] + moved[8:16] + moved[16:24])[0:5]
            out_ref[bead, cell, 5:6, :] = rank
            out_ref[bead, cell, 6:8, :] = jnp.zeros((2, lanes), F32)
        return carry

    lax.fori_loop(0, cells // GROUP, per_group, 0)


def meet_runs(span, local, runs, lanes_ref, sizes_ref, rows_ref, total_ref, back_ref):
    beads, lanes = lanes_ref.shape[0], lanes_ref.shape[-1]
    if span > 2 * SPAN:
        for start in range(0, span, SPAN):
            later = [([first + start for first in firsts], *rest) for firsts, *rest in runs]
            meet_runs(
                SPAN, local, later, lanes_ref, sizes_ref, rows_ref, total_ref, back_ref
            )
        return
    for bead in range(beads):
        for firsts, partner, step_y, step_z in runs:
            first = firsts[bead]
            here = pl.ds(first if isinstance(first, int) else pl.multiple_of(first, 8), span)
            rows = [
                rows_ref[local, bead, kind, here, :].reshape(span // 8, 8, lanes)
                for kind in range(5)
            ]
            half = rows[3] + sizes_ref[partner, 0]
            s2 = half * half
            apart = [
                lanes_ref[bead, partner, 0] - rows[0],
                (lanes_ref[bead, partner, 1] + step_y) - rows[1],
                (lanes_ref[bead, partner, 2] + step_z) - rows[2],
            ]
            radius_sq = apart[0] * apart[0] + apart[1] * apart[1] + apart[2] * apart[2]
            depth = rows[4] * sizes_ref[partner, 1]
            weight = depth * short_weight(radius_sq + s2, s2)
            for axis in range(3):
                push = weight * apart[axis]
                flat_push = push.reshape(span, lanes)
                if total_ref is None:
                    back_ref[local, bead, axis, here, :] = flat_push
                else:
                    back_ref[local, bead, axis, here, :] += flat_push
                    total_ref[partner, bead, axis] += jnp.sum(push, axis=0)


def reach_kernel(
    plan, position, params, next_position, next_params, ordered, force_ref, other_ref, lanes_ref,
    sizes_ref, rows_ref, total_ref, back_ref,
):
    beads, _, cells, lanes = position.shape
    entries_at = len(STEPS) * (cells + 1)
    bounds_at = plan.shape[0] - beads * cells * 9
    factor = SHORT_FACTOR
    repeat_lanes(SHORT_SCALE, position, params, next_position, next_params, lanes_ref, sizes_ref)
    total_ref[...] = jnp.zeros_like(total_ref)
    rows_ref[:, :, :, lanes:, :] = jnp.zeros((GROUP, beads, 5, SPARE, lanes), F32)
    row = lax.broadcasted_iota(jnp.int32, (lanes, lanes), 0).astype(F32)
    slot = lax.broadcasted_iota(jnp.int32, (8, lanes), 1)
    column = lax.broadcasted_iota(jnp.int32, (lanes, 8), 1)
    refs = (lanes_ref, sizes_ref, rows_ref)
    every = [(local, bead) for local in range(GROUP) for bead in range(beads)]

    def per_group(group, carry):
        for local, bead in every:
            block = ordered[bead, group * GROUP + local].T
            for axis in range(5):
                rows_ref[local, bead, axis, 0:lanes, :] = jnp.broadcast_to(
                    block[:, axis : axis + 1], (lanes, lanes)
                )
            if bead == beads - 1:
                for first in range(0, lanes, SPAN):
                    run = ([first] * beads, group * GROUP + local, 0.0, 0.0)
                    meet_runs(SPAN, local, [run], *refs, None, back_ref)

        def per_cell(local, carry):
            cell = group * GROUP + local

            def bound(bead, octant):
                return plan[bounds_at + (bead * cells + cell) * 9 + octant]

            for place, (span, count) in enumerate(STEPS):
                begin = plan[place * (cells + 1) + cell]
                end = plan[place * (cells + 1) + cell + 1]

                def per_step(step, carry, span=span, count=count, begin=begin):
                    runs, longest = [], 0
                    for shift in range(count):
                        at = entries_at + 5 * (begin + step * count + shift)
                        begins = [
                            lax.bitwise_and(bound(bead, plan[at + 3]), -8) for bead in range(beads)
                        ]
                        for bead in range(beads):
                            longest = jnp.maximum(longest, bound(bead, plan[at + 4]) - begins[bead])
                        runs.append(
                            (
                                begins, plan[at], SHORT_SCALE * plan[at + 1].astype(F32),
                                SHORT_SCALE * plan[at + 2].astype(F32),
                            )
                        )

                    def per_span(index, carry):
                        moved = [
                            (
                                [
                                    pl.multiple_of(jnp.minimum(first + index * span, lanes), 8)
                                    for first in begins
                                ],
                                *rest,
                            )
                            for begins, *rest in runs
                        ]
                        meet_runs(span, local, moved, *refs, total_ref, back_ref)
                        return carry

                    return lax.fori_loop(0, lax.div(longest + (span - 1), span), per_span, carry)

                lax.fori_loop(0, lax.div(end - begin, count), per_step, 0)
            return carry

        lax.fori_loop(0, GROUP, per_cell, 0)

        for local, bead in every:
            cell = group * GROUP + local
            alive = plan[bounds_at + cell * 9 + 8]
            sums = [
                jnp.sum(back_ref[local, bead, axis, 0:lanes, :], axis=1, keepdims=True)
                for axis in range(3)
            ]
            block = jnp.where(
                column == 0,
                sums[0],
                jnp.where(column == 1, sums[1], jnp.where(column == 2, sums[2], 0.0)),
            ).T
            block = jnp.where(slot < alive, block, 0.0)
            chosen = jnp.where(ordered[bead, cell, 5:6, :] == row, 1.0, 0.0).astype(BF16)
            moved = lax.dot_general(
                jnp.concatenate(split_three(block), axis=0).astype(BF16),
                chosen,
                (((1,), (0,)), ((), ())),
                preferred_element_type=F32,
            )
            put_rows(force_ref, bead, cell, (moved[0:8] + moved[8:16] + moved[16:24])[0:3])
        return carry

    lax.fori_loop(0, cells // GROUP, per_group, 0)

    def finish(index, carry):
        for shift, bead in every:
            cell = index * GROUP + shift
            held = jnp.concatenate(atom_rows(force_ref.at[bead], cell), axis=0)
            put_rows(force_ref, bead, cell, factor * (fold_total(total_ref, cell, bead) - held))
            put_rows(other_ref, bead, cell, factor * fold_total(total_ref, cell + cells, bead))
        return carry

    lax.fori_loop(0, cells // GROUP, finish, 0)


def short_forces(position, params, next_position, next_params, ordered, bounds):
    beads, _, cells, lanes = position.shape
    starts, entries = reach_lists(cells)
    plan = jnp.concatenate([jnp.asarray(starts), jnp.asarray(entries), bounds])
    forces = jax.ShapeDtypeStruct((beads, 3, cells, lanes), F32)
    return call(
        reach_kernel,
        (plan, position, params, next_position, next_params, ordered),
        1,
        (forces, forces),
        [
            pltpu.VMEM((beads, 2 * cells, 3, 8, lanes), F32),
            pltpu.VMEM((2 * cells, 2, 8, lanes), F32),
            pltpu.VMEM((GROUP, beads, 5, lanes + SPARE, lanes), F32),
            pltpu.VMEM((2 * cells, beads, 3, 8, lanes), F32),
            pltpu.VMEM((GROUP, beads, 3, lanes + SPARE, lanes), F32),
        ],
        PAIR_FLOPS * beads * 70,
    )


def call(kernel, inputs, smem, outputs, scratch, flops, fetched=()):
    def space(place):
        if place in fetched:
            return pltpu.HBM
        return pltpu.SMEM if place < smem else pltpu.VMEM

    return pl.pallas_call(
        kernel,
        out_shape=outputs,
        in_specs=[pl.BlockSpec(memory_space=space(place)) for place in range(len(inputs))],
        scratch_shapes=scratch,
        compiler_params=pltpu.CompilerParams(vmem_limit_bytes=VMEM_LIMIT),
        cost_estimate=pl.CostEstimate(flops=flops, bytes_accessed=1 << 18, transcendentals=0),
    )(*inputs)


PAIR_FLOPS = 40 * 128 * 128


def pair_forces(position, params, occupied, next_position, next_params):
    beads, _, cells, lanes = position.shape
    starts, entries = partner_lists(cells)
    forces = jax.ShapeDtypeStruct((beads, 3, cells, lanes), F32)
    return call(
        pairs_kernel,
        (
            jnp.asarray(np.concatenate([starts, entries])), occupied, position, params,
            next_position, next_params,
        ),
        2,
        (forces, forces),
        [
            pltpu.VMEM((beads, 2 * cells, 3, 8, lanes), F32),
            pltpu.VMEM((2 * cells, 2, 8, lanes), F32),
            pltpu.VMEM((cells, beads, 3, lanes, lanes), F32),
            pltpu.VMEM((cells, 2, lanes, lanes), F32),
            pltpu.VMEM((2 * cells, beads, 3, 8, lanes), F32),
            pltpu.VMEM((cells, beads, 3, lanes, lanes), F32),
        ],
        PAIR_FLOPS * beads * (len(entries) // 3 + cells),
    )


def kick_kernel(
    piece_rows, groups, rank, table_hbm, position, momenta, noise, force, back, params, partial_ref,
    piece_ref, flat_ref, table, done,
):
    fetch = pltpu.make_async_copy(table_hbm, table, done)
    fetch.start()
    beads, rows, _ = position.shape
    holders = piece_ref.shape[0]
    reduced = table.shape[0]
    first = rank[0] * beads
    if holders * piece_rows > rows:
        piece_ref[...] = jnp.zeros_like(piece_ref)
    mass = params[2]
    per_root = lax.rsqrt(mass)
    per_root = per_root * (1.5 - 0.5 * mass * per_root * per_root)
    per_mass = jnp.concatenate([1.0 / mass] * 3, axis=0)
    per_root = jnp.concatenate([per_root] * 3, axis=0)
    for bead in range(beads):
        kicked = momenta[bead] + 0.5 * TIME_STEP * (force[bead] + back[bead])
        flat_ref[0, bead] = position[bead]
        flat_ref[1, bead] = kicked * per_mass
        flat_ref[2, bead] = noise[bead] * per_root
    for kind in range(3):
        for bead in range(beads):
            base = (kind * beads + bead) * piece_rows
            for owner in range(holders):
                start = owner * piece_rows
                count = min(piece_rows, rows - start)
                if count > 0:
                    piece_ref[owner, base : base + count, :] = flat_ref[
                        kind, bead, start : start + count, :
                    ]
    fetch.wait()
    for group in range(reduced):
        total = None
        for kind in range(3):
            for bead in range(beads):
                term = table[group, kind * holders * beads + first + bead] * flat_ref[kind, bead]
                total = term if total is None else total + term
        for copy in range(groups):
            partial_ref[group * groups + copy] = total


def move_kernel(piece_rows, beads, matrix_hbm, arrived, out_ref, gathered, matrix, done):
    fetch = pltpu.make_async_copy(matrix_hbm, matrix, done)
    fetch.start()
    holders = arrived.shape[0]
    taken = 3 * beads
    given = 2 * beads
    for row in range(piece_rows):
        for holder in range(holders):
            gathered[row, holder * taken : (holder + 1) * taken, :] = arrived[
                holder, pl.ds(row, taken, stride=piece_rows), :
            ]
    fetch.wait()
    for row in range(piece_rows):
        moved = lax.dot_general(
            matrix[...],
            gathered[row],
            (((1,), (0,)), ((), ())),
            precision=lax.Precision.HIGHEST,
            preferred_element_type=F32,
        )
        for holder in range(holders):
            out_ref[holder, row * given : (row + 1) * given, :] = moved[
                holder * given : (holder + 1) * given
            ]


def finish_kernel(
    piece_rows, groups, rank, table_hbm, moved, slow, params, position_ref, momentum_ref,
    velocity_ref, table, done,
):
    fetch = pltpu.make_async_copy(table_hbm, table, done)
    fetch.start()
    beads, rows, _ = position_ref.shape
    holders = moved.shape[0]
    given = 2 * beads
    reduced = table.shape[0]
    first = 3 * holders * beads + rank[0] * beads
    mass = jnp.concatenate([params[2]] * 3, axis=0)
    for bead in range(beads):
        for owner in range(holders):
            start = owner * piece_rows
            count = min(piece_rows, rows - start)
            if count > 0:
                position_ref[bead, start : start + count, :] = moved[
                    owner, pl.ds(bead, count, stride=given), :
                ]
                velocity_ref[bead, start : start + count, :] = moved[
                    owner, pl.ds(beads + bead, count, stride=given), :
                ]
    fetch.wait()
    for bead in range(beads):
        total = mass * velocity_ref[bead]
        for group in range(reduced):
            total = total + table[group, first + bead] * slow[group * groups]
        momentum_ref[bead] = total


def shards(positions, momenta, noise, atom_types, occupancy, type_sigma, type_eps, type_mass):
    beads, cells, _, lanes = positions.shape
    holders = lax.axis_size("bead")
    domains = lax.axis_size("space")
    rank = lax.axis_index("bead")
    total_beads = beads * holders
    rows = 3 * cells
    piece_rows = -(-rows // holders)
    held = max(1, PC // holders)
    groups = max(1, holders // PC)
    contract = contract_matrix(total_beads, PC)
    steps = step_matrices(total_beads)
    rank_table = rank.astype(jnp.int32).reshape(1)
    one_back = [((i + 1) % domains, i) for i in range(domains)]
    one_on = [(i, (i + 1) % domains) for i in range(domains)]

    codes = jnp.arange(type_sigma.shape[0])
    onehot = atom_types[..., None] == codes
    living = jnp.arange(lanes)[None, :] < occupancy[:, None]
    half_sigma = 0.5 * jnp.sum(jnp.where(onehot, type_sigma, 0.0), -1)
    root_eps = jnp.sqrt(jnp.sum(jnp.where(onehot, type_eps, 0.0), -1))
    mass = jnp.sum(jnp.where(onehot, type_mass, 0.0), -1)
    params = jnp.stack([half_sigma, jnp.where(living, root_eps, 0.0), mass], 0)
    positions, momenta, noise = (
        value.transpose(0, 2, 1, 3) for value in (positions, momenta, noise)
    )

    stacked = jnp.concatenate([positions, params[None]], 0)
    next_stacked = lax.ppermute(stacked, "space", one_back)
    next_params = next_stacked[beads]
    spread = 0.5 * TIME_STEP * (total_beads / PC) * contract
    table = np.concatenate([contract @ steps[0, kind] for kind in range(3)] + [spread], axis=1)
    order = steps.reshape(2, 3, holders, beads, holders, beads).transpose(2, 0, 3, 4, 1, 5)
    order = order.reshape(2 * total_beads, 3 * total_beads)
    ordered, table, order = call(
        order_kernel,
        (positions, params, jnp.asarray(table, F32), jnp.asarray(order, F32)),
        0,
        (
            jax.ShapeDtypeStruct((beads, cells, 8, lanes), F32),
            jax.ShapeDtypeStruct(table.shape, F32),
            jax.ShapeDtypeStruct(order.shape, F32),
        ),
        [],
        1 << 22,
    )
    key = octant_key(positions[:, 0], positions[:, 1], positions[:, 2], living[None])
    bounds = jnp.sum(
        (key[:, :, None, :] < jnp.arange(9, dtype=F32)[:, None]).astype(jnp.int32), -1
    )
    force, back = short_forces(
        positions, params, next_stacked[:beads], next_params, ordered, bounds.reshape(-1)
    )
    back = lax.ppermute(back, "space", one_on)

    def flat(value):
        return value.reshape(-1, rows, lanes)

    partial, pieces = call(
        functools.partial(kick_kernel, piece_rows, groups),
        (
            rank_table, table, flat(positions), flat(momenta), flat(noise), flat(force), flat(back),
            params,
        ),
        1,
        (
            jax.ShapeDtypeStruct((PC * groups, rows, lanes), F32),
            jax.ShapeDtypeStruct((holders, 3 * beads * piece_rows, lanes), F32),
        ),
        [
            pltpu.VMEM((3, beads, rows, lanes), F32), pltpu.SMEM(table.shape, F32),
            pltpu.SemaphoreType.DMA,
        ],
        1 << 22,
        (1,),
    )
    arrived = lax.all_to_all(
        partial.reshape(holders, held * rows, lanes), "bead", split_axis=0, concat_axis=0, tiled=True
    )
    contracted = jnp.sum(arrived, 0).reshape(held, 3, cells, lanes)
    contracted, pieces = lax.optimization_barrier((contracted, pieces))
    next_contracted = lax.ppermute(contracted, "space", one_back)
    pieces = lax.all_to_all(pieces, "bead", split_axis=0, concat_axis=0, tiled=True)
    slow, slow_back = pair_forces(
        contracted, params, occupancy, next_contracted, next_params
    )
    slow = slow + lax.ppermute(slow_back, "space", one_on)

    moved = call(
        functools.partial(move_kernel, piece_rows, beads),
        (order, pieces),
        0,
        jax.ShapeDtypeStruct((holders, 2 * beads * piece_rows, lanes), F32),
        [
            pltpu.VMEM((piece_rows, 3 * total_beads, lanes), F32), pltpu.VMEM(order.shape, F32),
            pltpu.SemaphoreType.DMA,
        ],
        1 << 23,
        (0,),
    )
    moved_rows = 2 * beads * piece_rows
    sent = jnp.concatenate(
        [
            moved,
            jnp.broadcast_to(slow.reshape(1, held * rows, lanes), (holders, held * rows, lanes)),
        ],
        1,
    )
    got = lax.all_to_all(sent, "bead", split_axis=0, concat_axis=0, tiled=True)
    result = jax.ShapeDtypeStruct((beads, rows, lanes), F32)
    new_positions, new_momenta = call(
        functools.partial(finish_kernel, piece_rows, groups),
        (
            rank_table, table, got[:, :moved_rows],
            got[:, moved_rows:].reshape(holders * held, rows, lanes), params,
        ),
        1,
        (result, result),
        [
            pltpu.VMEM((beads, rows, lanes), F32), pltpu.SMEM(table.shape, F32),
            pltpu.SemaphoreType.DMA,
        ],
        1 << 20,
        (1,),
    )

    def cells_first(value):
        return value.reshape(beads, 3, cells, lanes).transpose(0, 2, 1, 3)

    return cells_first(new_positions), cells_first(new_momenta)


def solution(mesh):
    placed = (
        P("bead", "space", None, None),
        P("bead", "space", None, None),
        P("bead", "space", None, None),
        P("space", None),
        P("space"),
        P(),
        P(),
        P(),
    )
    return jax.shard_map(
        shards,
        mesh=mesh,
        in_specs=placed,
        out_specs=(P("bead", "space", None, None), P("bead", "space", None, None)),
        check_vma=False,
    )
```

```python
import functools

import jax
import jax.numpy as jnp
import numpy as np
from jax import lax
from jax.experimental import pallas as pl
from jax.experimental.pallas import tpu as pltpu
from jax.sharding import PartitionSpec as P

PC = 8
GY = 4
GZ = 4

TIME_STEP = 0.05
INVERSE_TEMP = 32.0
CENTROID_FRICTION = 1.0
INNER_CUT = 0.5
OUTER_CUT = 1.0
CUBE_ROOT_TWO = 2.0 ** (1.0 / 3.0)
F32 = jnp.float32
BF16 = jnp.bfloat16
SPAN = 32
GROUP = 4
STEPS = ((24, 4), (24, 2), (24, 1), (40, 2), (40, 1), (32, 2), (32, 1))
RUN_ROWS = {1: 24, 2: 40}
SPARE = 40
EARLY_ROWS = 96
VMEM_LIMIT = 48 * 1024 * 1024


def mode_matrix(number):
    rows = np.arange(number, dtype=np.float64)[:, None]
    column = np.arange(number, dtype=np.float64)[None, :]
    phases = 2.0 * np.pi * rows * column / number
    factor = np.sqrt(2.0 / number)
    middle = np.cos(np.pi * rows) / np.sqrt(number)
    matrix = np.where(column < number / 2, factor * np.cos(phases), factor * np.sin(phases))
    matrix = np.where(column == number / 2, middle, matrix)
    return np.where(column == 0, 1.0 / np.sqrt(number), matrix)


def contract_matrix(full_count, reduced):
    selected = np.arange(reduced)
    selected = np.where(selected <= reduced // 2, selected, selected + full_count - reduced)
    chosen = mode_matrix(full_count)[:, selected]
    return np.sqrt(reduced / full_count) * (mode_matrix(reduced) @ chosen.T)


def step_matrices(number):
    index = np.arange(number, dtype=np.float64)
    frequency = 2.0 * (number / INVERSE_TEMP) * np.sin(np.pi * index / number)
    friction = np.where(index == 0, CENTROID_FRICTION, 2.0 * frequency)
    damping = np.exp(-friction * TIME_STEP)
    kicking = np.sqrt((1.0 - damping * damping) / INVERSE_TEMP)
    cosine = np.cos(frequency * TIME_STEP)
    sine = np.sin(frequency * TIME_STEP)
    drift = np.where(index == 0, TIME_STEP, sine / np.where(index == 0, 1.0, frequency))
    modes = mode_matrix(number)

    def over_beads(diagonal):
        return (modes * diagonal[None, :]) @ modes.T

    return np.array(
        [
            [over_beads(cosine), over_beads(drift * damping), over_beads(drift * kicking)],
            [
                over_beads(-frequency * sine),
                over_beads(cosine * damping),
                over_beads(cosine * kicking),
            ],
        ]
    )


def partner_lists(domain_cells):
    lists = []
    for one in range(domain_cells):
        near = []
        for two in range(domain_cells):
            step_y, step_z = two // GZ - one // GZ, two % GZ - one % GZ
            if abs(step_y) <= 1 and abs(step_z) <= 1:
                near.append((two, step_y, step_z))
        later = [entry for entry in near if entry[0] > one]
        lists.append(later + [(two + domain_cells, y, z) for two, y, z in near])
    starts = np.cumsum([0] + [len(entries) for entries in lists]).astype(np.int32)
    return starts, np.array([value for entries in lists for entry in entries for value in entry], np.int32)


def long_weight(h, radius_sq, s2):
    inverse = pl.reciprocal(h, approx=True)
    quotient = (CUBE_ROOT_TWO * s2) * inverse
    twice = quotient * quotient * quotient
    outer = jnp.maximum(1.0 - radius_sq, 0.0)
    inner = jnp.maximum(1.0 - 4.0 * radius_sq, 0.0)
    switch = outer * outer - inner * inner
    slope = outer - 4.0 * inner
    return twice * ((twice - 1.0) * (3.0 * (switch * inverse) + slope) - slope)


def short_weight(h, s2):
    inverse = pl.reciprocal(h, approx=True)
    quotient = s2 * inverse
    sixth = quotient * quotient * quotient
    lifted = jnp.maximum((quotient + inverse) - 2.0 / 3.0, 1.0 / 3.0)
    bracket = (sixth - 0.5) * lifted - 1.0 / 6.0
    return (sixth * bracket) * ((lifted - 1.0 / 3.0) * h)


LONG_FACTOR = 4.0
SHORT_SCALE = 1.0 / INNER_CUT
SHORT_FACTOR = 192.0 / SHORT_SCALE


def atom_rows(block, cell):
    return [block[kind, pl.ds(cell, 1), :] for kind in range(3)]


def columns(block):
    few, lanes = block.shape
    return jnp.concatenate([block, jnp.zeros((8 - few, lanes), F32)], axis=0).T


def spread_rows(position, params, cell, rows_ref, size_ref):
    beads, lanes = position.shape[0], position.shape[-1]
    sizes = columns(jnp.concatenate(atom_rows(params, cell)[:2], axis=0))
    for kind in range(2):
        size_ref[cell, kind] = jnp.broadcast_to(sizes[:, kind : kind + 1], (lanes, lanes))
    for bead in range(beads):
        block = columns(jnp.concatenate(atom_rows(position.at[bead], cell), axis=0))
        for axis in range(3):
            rows_ref[cell, bead, axis] = jnp.broadcast_to(
                block[:, axis : axis + 1], (lanes, lanes)
            )


def meet(cell, first, partners, refs):
    lanes_ref, sizes_ref, rows_ref, size_ref, total_ref, back_ref = refs
    beads, lanes = lanes_ref.shape[0], lanes_ref.shape[-1]
    here = pl.ds(first, SPAN)
    tall = (SPAN // 8, 8, lanes)
    row_half = size_ref[cell, 0, here, :].reshape(tall)
    row_root = size_ref[cell, 1, here, :].reshape(tall)
    known = []
    for partner, _, _ in partners:
        half = row_half + sizes_ref[partner, 0]
        s2 = half * half
        known.append((s2, row_root * sizes_ref[partner, 1]))
    for bead in range(beads):
        rows = [rows_ref[cell, bead, axis, here, :].reshape(tall) for axis in range(3)]
        back = [None, None, None]
        for (partner, step_y, step_z), (s2, depth) in zip(partners, known):
            apart = [
                lanes_ref[bead, partner, 0] - rows[0],
                (lanes_ref[bead, partner, 1] + step_y) - rows[1],
                (lanes_ref[bead, partner, 2] + step_z) - rows[2],
            ]
            radius_sq = apart[0] * apart[0] + apart[1] * apart[1] + apart[2] * apart[2]
            weight = depth * long_weight(radius_sq + s2, radius_sq, s2)
            for axis in range(3):
                push = weight * apart[axis]
                back[axis] = push if back[axis] is None else back[axis] + push
                if total_ref is not None:
                    total_ref[partner, bead, axis] += jnp.sum(push, axis=0)
        for axis in range(3):
            value = back[axis].reshape(SPAN, lanes)
            if total_ref is None:
                back_ref[cell, bead, axis, here, :] = value
            else:
                back_ref[cell, bead, axis, here, :] += value


def repeat_lanes(scale, position, params, next_position, next_params, lanes_ref, sizes_ref):
    beads, _, cells, lanes = position.shape

    def per_cell(cell, carry):
        for layer, place, values in ((0, position, params), (1, next_position, next_params)):
            for kind in range(2):
                row = values[kind, pl.ds(cell, 1), :]
                row = scale * row if kind == 0 else row
                sizes_ref[layer * cells + cell, kind] = jnp.broadcast_to(row, (8, lanes))
            for bead in range(beads):
                for axis in range(3):
                    row = place[bead, axis, pl.ds(cell, 1), :]
                    row = scale * (row + 1.0 if layer == 1 and axis == 0 else row)
                    lanes_ref[bead, layer * cells + cell, axis] = jnp.broadcast_to(row, (8, lanes))
        return carry

    lax.fori_loop(0, cells, per_cell, 0)


def fold_back(back_ref, cell, bead):
    lanes = back_ref.shape[-1]
    column = lax.broadcasted_iota(jnp.int32, (lanes, 8), 1)
    sums = [jnp.sum(back_ref[cell, bead, axis], axis=1, keepdims=True) for axis in range(3)]
    block = jnp.where(
        column == 0, sums[0], jnp.where(column == 1, sums[1], jnp.where(column == 2, sums[2], 0.0))
    )
    return block.T[0:3]


def put_rows(out_ref, bead, cell, block):
    for axis in range(3):
        out_ref[bead, axis, pl.ds(cell, 1), :] = block[axis : axis + 1]


def fold_total(total_ref, cell, bead):
    return jnp.concatenate(
        [jnp.sum(total_ref[cell, bead, axis], axis=0, keepdims=True) for axis in range(3)], axis=0
    )


def pairs_kernel(
    plan, occupied, position, params, next_position, next_params,
    force_ref, other_ref, lanes_ref, sizes_ref, rows_ref, size_ref, total_ref, back_ref,
):
    beads, _, cells, lanes = position.shape
    factor = LONG_FACTOR
    together = max(1, 4 // beads)
    repeat_lanes(1.0, position, params, next_position, next_params, lanes_ref, sizes_ref)
    total_ref[...] = jnp.zeros_like(total_ref)

    refs = (lanes_ref, sizes_ref, rows_ref, size_ref)

    def spread(index, carry):
        for shift in range(together):
            cell = index * together + shift
            spread_rows(position, params, cell, rows_ref, size_ref)
            for first in range(0, lanes, SPAN):
                meet(cell, first, [(cell, 0.0, 0.0)], refs + (None, back_ref))
        return carry

    lax.fori_loop(0, cells // together, spread, 0)

    def entry_of(entry):
        return (
            plan[cells + 1 + 3 * entry],
            plan[cells + 2 + 3 * entry].astype(F32),
            plan[cells + 3 + 3 * entry].astype(F32),
        )

    def per_cell(cell, carry):
        begin, end = plan[cell], plan[cell + 1]
        odd = lax.rem(end - begin, 2)

        most = lanes // SPAN
        needed = lax.div(occupied[cell] + (SPAN - 1), SPAN)
        for parts in (most - 1, most):
            firsts = [part * SPAN for part in range(parts)]

            def all_rows(_, carry, firsts=firsts):
                def single(entry, carry):
                    for first in firsts:
                        meet(cell, first, [entry_of(entry)], refs + (total_ref, back_ref))
                    return carry

                def double(step, carry):
                    entry = begin + odd + 2 * step
                    both = [entry_of(entry), entry_of(entry + 1)]
                    for first in firsts:
                        meet(cell, first, both, refs + (total_ref, back_ref))
                    return carry

                carry = lax.fori_loop(begin, begin + odd, single, carry)
                return lax.fori_loop(0, lax.div(end - begin, 2), double, carry)

            full = (needed == most).astype(jnp.int32)
            lax.fori_loop(0, full if parts == most else 1 - full, all_rows, 0)
        return carry

    lax.fori_loop(0, cells, per_cell, 0)

    def finish(index, carry):
        for shift in range(together):
            cell = index * together + shift
            alive = params[1, pl.ds(cell, 1), :] > 0.0
            for bead in range(beads):
                total = fold_total(total_ref, cell, bead) - fold_back(back_ref, cell, bead)
                put_rows(force_ref, bead, cell, jnp.where(alive, factor * total, 0.0))
                put_rows(other_ref, bead, cell, factor * fold_total(total_ref, cell + cells, bead))
        return carry

    lax.fori_loop(0, cells // together, finish, 0)


def octant_key(x, y, z, alive):
    zed = jnp.where(z >= 0.5, 1.0, 0.0)
    gray = jnp.where(y >= 0.5, 3.0 - zed, zed)
    return jnp.where(alive, jnp.where(x >= 0.5, 7.0 - gray, gray), 8.0)


def reach_lists(domain_cells):
    octants = []
    for bit_x in range(2):
        for bit_y in range(2):
            for bit_z in range(2):
                gray = 3 - bit_z if bit_y else bit_z
                octants.append((7 - gray if bit_x else gray, (bit_x, bit_y, bit_z)))
    classes = [[[] for _ in range(domain_cells)] for _ in STEPS]
    for one in range(domain_cells):
        runs = {}
        for layer in range(2):
            for two in range(domain_cells):
                step = (layer, two // GZ - one // GZ, two % GZ - one % GZ)
                if abs(step[1]) > 1 or abs(step[2]) > 1 or (layer == 0 and two <= one):
                    continue
                keys = [
                    key
                    for key, bits in octants
                    if all(move == 0 or bit == (move > 0) for move, bit in zip(step, bits))
                ]
                entry = (two + layer * domain_cells, step[1], step[2], min(keys), max(keys) + 1)
                runs.setdefault(entry[4] - entry[3], []).append(entry)
        for length, entries in sorted(runs.items()):
            entries.sort(key=lambda entry: entry[3:])
            span = RUN_ROWS.get(length, SPAN)
            for place, (rows, count) in enumerate(STEPS):
                if rows == span:
                    whole = len(entries) // count * count
                    classes[place][one] += entries[:whole]
                    entries = entries[whole:]
    starts, values = [], []
    for lists in classes:
        for entries in lists:
            starts.append(len(values) // 5)
            values += [value for entry in entries for value in entry]
        starts.append(len(values) // 5)
    return np.array(starts, np.int32), np.array(values, np.int32)


def split_three(value):
    high = value.astype(BF16).astype(F32)
    rest = value - high
    middle = rest.astype(BF16).astype(F32)
    return high, middle, rest - middle


def order_kernel(position, params, table, matrix, out_ref, table_out, matrix_out):
    beads, _, cells, lanes = position.shape
    table_out[...] = table[...]
    matrix_out[...] = matrix[...]
    row = lax.broadcasted_iota(jnp.int32, (lanes, lanes), 0)
    column = lax.broadcasted_iota(jnp.int32, (lanes, lanes), 1)
    before = jnp.where(row < column, 1.0, 0.0).astype(BF16)
    counter = jnp.concatenate([before, jnp.ones((lanes, lanes), BF16)], axis=0)
    kind = lax.broadcasted_iota(jnp.int32, (16, lanes), 0).astype(F32)
    place_row = row.astype(F32)
    every = [(shift, bead) for shift in range(GROUP) for bead in range(beads)]

    def per_group(index, carry):
        blocks, sames, marks = [], [], []
        for shift, bead in every:
            cell = index * GROUP + shift
            sizes = atom_rows(params, cell)[:2]
            place = atom_rows(position.at[bead], cell)
            key = octant_key(*place, sizes[1] > 0.0)
            same = jnp.where(key == kind, 1.0, 0.0)
            less = jnp.where(key < kind, 1.0, 0.0)
            scaled = [SHORT_SCALE * value for value in (*place, sizes[0])]
            blocks.append(
                jnp.concatenate([*scaled, sizes[1], jnp.zeros((3, lanes), F32)], axis=0)
            )
            sames.append(same)
            marks.append(jnp.concatenate([same, less], axis=1))
        counts = jnp.dot(
            jnp.concatenate(marks, axis=0).astype(BF16), counter, preferred_element_type=F32
        )
        for place, (shift, bead) in enumerate(every):
            cell = index * GROUP + shift
            rank = jnp.sum(
                sames[place] * counts[16 * place : 16 * place + 16], axis=0, keepdims=True
            )
            chosen = jnp.where(rank == place_row, 1.0, 0.0).astype(BF16)
            moved = lax.dot_general(
                jnp.concatenate(split_three(blocks[place]), axis=0).astype(BF16),
                chosen,
                (((1,), (1,)), ((), ())),
                preferred_element_type=F32,
            )
            out_ref[bead, cell, 0:5, :] = (moved[0:8] + moved[8:16] + moved[16:24])[0:5]
            out_ref[bead, cell, 5:6, :] = rank
            out_ref[bead, cell, 6:8, :] = jnp.zeros((2, lanes), F32)
        return carry

    lax.fori_loop(0, cells // GROUP, per_group, 0)


def meet_runs(span, local, runs, lanes_ref, sizes_ref, rows_ref, total_ref, back_ref):
    beads, lanes = lanes_ref.shape[0], lanes_ref.shape[-1]
    for bead in range(beads):
        for firsts, partner, step_y, step_z in runs:
            here = pl.ds(firsts[bead], span)
            rows = [
                rows_ref[local, bead, kind, here, :].reshape(span // 8, 8, lanes)
                for kind in range(5)
            ]
            half = rows[3] + sizes_ref[partner, 0]
            s2 = half * half
            apart = [
                lanes_ref[bead, partner, 0] - rows[0],
                (lanes_ref[bead, partner, 1] + step_y) - rows[1],
                (lanes_ref[bead, partner, 2] + step_z) - rows[2],
            ]
            radius_sq = apart[0] * apart[0] + apart[1] * apart[1] + apart[2] * apart[2]
            depth = rows[4] * sizes_ref[partner, 1]
            weight = depth * short_weight(radius_sq + s2, s2)
            for axis in range(3):
                push = weight * apart[axis]
                flat_push = push.reshape(span, lanes)
                if total_ref is None:
                    back_ref[local, bead, axis, here, :] = flat_push
                else:
                    back_ref[local, bead, axis, here, :] += flat_push
                    total_ref[partner, bead, axis] += jnp.sum(push, axis=0)


def reach_kernel(
    plan, position, params, next_position, next_params, ordered, force_ref, other_ref, lanes_ref,
    sizes_ref, rows_ref, total_ref, back_ref,
):
    beads, _, cells, lanes = position.shape
    entries_at = len(STEPS) * (cells + 1)
    bounds_at = plan.shape[0] - beads * cells * 9
    factor = SHORT_FACTOR
    repeat_lanes(SHORT_SCALE, position, params, next_position, next_params, lanes_ref, sizes_ref)
    total_ref[...] = jnp.zeros_like(total_ref)
    rows_ref[:, :, :, lanes:, :] = jnp.zeros((GROUP, beads, 5, SPARE, lanes), F32)
    row = lax.broadcasted_iota(jnp.int32, (lanes, lanes), 0).astype(F32)
    slot = lax.broadcasted_iota(jnp.int32, (8, lanes), 1)
    column = lax.broadcasted_iota(jnp.int32, (lanes, 8), 1)
    refs = (lanes_ref, sizes_ref, rows_ref)
    every = [(local, bead) for local in range(GROUP) for bead in range(beads)]

    def per_group(group, carry):
        for local, bead in every:
            block = ordered[bead, group * GROUP + local].T
            for axis in range(5):
                rows_ref[local, bead, axis, 0:lanes, :] = jnp.broadcast_to(
                    block[:, axis : axis + 1], (lanes, lanes)
                )
            if bead == beads - 1:
                for first in range(0, EARLY_ROWS, SPAN):
                    run = ([first] * beads, group * GROUP + local, 0.0, 0.0)
                    meet_runs(SPAN, local, [run], *refs, None, back_ref)

        def per_cell(local, carry):
            cell = group * GROUP + local

            def bound(bead, octant):
                return plan[bounds_at + (bead * cells + cell) * 9 + octant]

            def itself(index, carry):
                first = pl.multiple_of(index * SPAN, SPAN)
                run = ([first] * beads, cell, 0.0, 0.0)
                meet_runs(SPAN, local, [run], *refs, None, back_ref)
                return carry

            lax.fori_loop(
                EARLY_ROWS // SPAN, lax.div(bound(0, 8) + (SPAN - 1), SPAN), itself, 0
            )

            for place, (span, count) in enumerate(STEPS):
                begin = plan[place * (cells + 1) + cell]
                end = plan[place * (cells + 1) + cell + 1]

                def per_step(step, carry, span=span, count=count, begin=begin):
                    runs, longest = [], 0
                    for shift in range(count):
                        at = entries_at + 5 * (begin + step * count + shift)
                        begins = [
                            lax.bitwise_and(bound(bead, plan[at + 3]), -8) for bead in range(beads)
                        ]
                        for bead in range(beads):
                            longest = jnp.maximum(longest, bound(bead, plan[at + 4]) - begins[bead])
                        runs.append(
                            (
                                begins, plan[at], SHORT_SCALE * plan[at + 1].astype(F32),
                                SHORT_SCALE * plan[at + 2].astype(F32),
                            )
                        )

                    def per_span(index, carry):
                        moved = [
                            (
                                [
                                    pl.multiple_of(jnp.minimum(first + index * span, lanes), 8)
                                    for first in begins
                                ],
                                *rest,
                            )
                            for begins, *rest in runs
                        ]
                        meet_runs(span, local, moved, *refs, total_ref, back_ref)
                        return carry

                    return lax.fori_loop(0, lax.div(longest + (span - 1), span), per_span, carry)

                lax.fori_loop(0, lax.div(end - begin, count), per_step, 0)
            return carry

        lax.fori_loop(0, GROUP, per_cell, 0)

        for local, bead in every:
            cell = group * GROUP + local
            alive = plan[bounds_at + cell * 9 + 8]
            sums = [
                jnp.sum(back_ref[local, bead, axis, 0:lanes, :], axis=1, keepdims=True)
                for axis in range(3)
            ]
            block = jnp.where(
                column == 0,
                sums[0],
                jnp.where(column == 1, sums[1], jnp.where(column == 2, sums[2], 0.0)),
            ).T
            block = jnp.where(slot < alive, block, 0.0)
            chosen = jnp.where(ordered[bead, cell, 5:6, :] == row, 1.0, 0.0).astype(BF16)
            moved = lax.dot_general(
                jnp.concatenate(split_three(block), axis=0).astype(BF16),
                chosen,
                (((1,), (0,)), ((), ())),
                preferred_element_type=F32,
            )
            put_rows(force_ref, bead, cell, (moved[0:8] + moved[8:16] + moved[16:24])[0:3])
        return carry

    lax.fori_loop(0, cells // GROUP, per_group, 0)

    def finish(index, carry):
        for shift, bead in every:
            cell = index * GROUP + shift
            held = jnp.concatenate(atom_rows(force_ref.at[bead], cell), axis=0)
            put_rows(force_ref, bead, cell, factor * (fold_total(total_ref, cell, bead) - held))
            put_rows(other_ref, bead, cell, factor * fold_total(total_ref, cell + cells, bead))
        return carry

    lax.fori_loop(0, cells // GROUP, finish, 0)


def short_forces(position, params, next_position, next_params, ordered, bounds):
    beads, _, cells, lanes = position.shape
    starts, entries = reach_lists(cells)
    plan = jnp.concatenate([jnp.asarray(starts), jnp.asarray(entries), bounds])
    forces = jax.ShapeDtypeStruct((beads, 3, cells, lanes), F32)
    return call(
        reach_kernel,
        (plan, position, params, next_position, next_params, ordered),
        1,
        (forces, forces),
        [
            pltpu.VMEM((beads, 2 * cells, 3, 8, lanes), F32),
            pltpu.VMEM((2 * cells, 2, 8, lanes), F32),
            pltpu.VMEM((GROUP, beads, 5, lanes + SPARE, lanes), F32),
            pltpu.VMEM((2 * cells, beads, 3, 8, lanes), F32),
            pltpu.VMEM((GROUP, beads, 3, lanes + SPARE, lanes), F32),
        ],
        PAIR_FLOPS * beads * 70,
    )


def call(kernel, inputs, smem, outputs, scratch, flops, fetched=()):
    def space(place):
        if place in fetched:
            return pltpu.HBM
        return pltpu.SMEM if place < smem else pltpu.VMEM

    return pl.pallas_call(
        kernel,
        out_shape=outputs,
        in_specs=[pl.BlockSpec(memory_space=space(place)) for place in range(len(inputs))],
        scratch_shapes=scratch,
        compiler_params=pltpu.CompilerParams(vmem_limit_bytes=VMEM_LIMIT),
        cost_estimate=pl.CostEstimate(flops=flops, bytes_accessed=1 << 18, transcendentals=0),
    )(*inputs)


PAIR_FLOPS = 40 * 128 * 128


def pair_forces(position, params, occupied, next_position, next_params):
    beads, _, cells, lanes = position.shape
    starts, entries = partner_lists(cells)
    forces = jax.ShapeDtypeStruct((beads, 3, cells, lanes), F32)
    return call(
        pairs_kernel,
        (
            jnp.asarray(np.concatenate([starts, entries])), occupied, position, params,
            next_position, next_params,
        ),
        2,
        (forces, forces),
        [
            pltpu.VMEM((beads, 2 * cells, 3, 8, lanes), F32),
            pltpu.VMEM((2 * cells, 2, 8, lanes), F32),
            pltpu.VMEM((cells, beads, 3, lanes, lanes), F32),
            pltpu.VMEM((cells, 2, lanes, lanes), F32),
            pltpu.VMEM((2 * cells, beads, 3, 8, lanes), F32),
            pltpu.VMEM((cells, beads, 3, lanes, lanes), F32),
        ],
        PAIR_FLOPS * beads * (len(entries) // 3 + cells),
    )


def kick_kernel(
    piece_rows, groups, rank, table_hbm, position, momenta, noise, force, back, params, partial_ref,
    piece_ref, flat_ref, table, done,
):
    fetch = pltpu.make_async_copy(table_hbm, table, done)
    fetch.start()
    beads, rows, _ = position.shape
    holders = piece_ref.shape[0]
    reduced = table.shape[0]
    first = rank[0] * beads
    if holders * piece_rows > rows:
        piece_ref[...] = jnp.zeros_like(piece_ref)
    mass = params[2]
    per_root = lax.rsqrt(mass)
    per_root = per_root * (1.5 - 0.5 * mass * per_root * per_root)
    per_mass = jnp.concatenate([1.0 / mass] * 3, axis=0)
    per_root = jnp.concatenate([per_root] * 3, axis=0)
    for bead in range(beads):
        kicked = momenta[bead] + 0.5 * TIME_STEP * (force[bead] + back[bead])
        flat_ref[0, bead] = position[bead]
        flat_ref[1, bead] = kicked * per_mass
        flat_ref[2, bead] = noise[bead] * per_root
    for kind in range(3):
        for bead in range(beads):
            base = (kind * beads + bead) * piece_rows
            for owner in range(holders):
                start = owner * piece_rows
                count = min(piece_rows, rows - start)
                if count > 0:
                    piece_ref[owner, base : base + count, :] = flat_ref[
                        kind, bead, start : start + count, :
                    ]
    fetch.wait()
    for group in range(reduced):
        total = None
        for kind in range(3):
            for bead in range(beads):
                term = table[group, kind * holders * beads + first + bead] * flat_ref[kind, bead]
                total = term if total is None else total + term
        for copy in range(groups):
            partial_ref[group * groups + copy] = total


def move_kernel(piece_rows, beads, matrix_hbm, arrived, out_ref, gathered, matrix, done):
    fetch = pltpu.make_async_copy(matrix_hbm, matrix, done)
    fetch.start()
    holders = arrived.shape[0]
    taken = 3 * beads
    given = 2 * beads
    for row in range(piece_rows):
        for holder in range(holders):
            gathered[row, holder * taken : (holder + 1) * taken, :] = arrived[
                holder, pl.ds(row, taken, stride=piece_rows), :
            ]
    fetch.wait()
    for row in range(piece_rows):
        moved = lax.dot_general(
            matrix[...],
            gathered[row],
            (((1,), (0,)), ((), ())),
            precision=lax.Precision.HIGHEST,
            preferred_element_type=F32,
        )
        for holder in range(holders):
            out_ref[holder, row * given : (row + 1) * given, :] = moved[
                holder * given : (holder + 1) * given
            ]


def finish_kernel(
    piece_rows, groups, rank, table_hbm, moved, slow, params, position_ref, momentum_ref,
    velocity_ref, table, done,
):
    fetch = pltpu.make_async_copy(table_hbm, table, done)
    fetch.start()
    beads, rows, _ = position_ref.shape
    holders = moved.shape[0]
    given = 2 * beads
    reduced = table.shape[0]
    first = 3 * holders * beads + rank[0] * beads
    mass = jnp.concatenate([params[2]] * 3, axis=0)
    for bead in range(beads):
        for owner in range(holders):
            start = owner * piece_rows
            count = min(piece_rows, rows - start)
            if count > 0:
                position_ref[bead, start : start + count, :] = moved[
                    owner, pl.ds(bead, count, stride=given), :
                ]
                velocity_ref[bead, start : start + count, :] = moved[
                    owner, pl.ds(beads + bead, count, stride=given), :
                ]
    fetch.wait()
    for bead in range(beads):
        total = mass * velocity_ref[bead]
        for group in range(reduced):
            total = total + table[group, first + bead] * slow[group * groups]
        momentum_ref[bead] = total


def shards(positions, momenta, noise, atom_types, occupancy, type_sigma, type_eps, type_mass):
    beads, cells, _, lanes = positions.shape
    holders = lax.axis_size("bead")
    domains = lax.axis_size("space")
    rank = lax.axis_index("bead")
    total_beads = beads * holders
    rows = 3 * cells
    piece_rows = -(-rows // holders)
    held = max(1, PC // holders)
    groups = max(1, holders // PC)
    contract = contract_matrix(total_beads, PC)
    steps = step_matrices(total_beads)
    rank_table = rank.astype(jnp.int32).reshape(1)
    one_back = [((i + 1) % domains, i) for i in range(domains)]
    one_on = [(i, (i + 1) % domains) for i in range(domains)]

    codes = jnp.arange(type_sigma.shape[0])
    onehot = atom_types[..., None] == codes
    living = jnp.arange(lanes)[None, :] < occupancy[:, None]
    half_sigma = 0.5 * jnp.sum(jnp.where(onehot, type_sigma, 0.0), -1)
    root_eps = jnp.sqrt(jnp.sum(jnp.where(onehot, type_eps, 0.0), -1))
    mass = jnp.sum(jnp.where(onehot, type_mass, 0.0), -1)
    params = jnp.stack([half_sigma, jnp.where(living, root_eps, 0.0), mass], 0)
    positions, momenta, noise = (
        value.transpose(0, 2, 1, 3) for value in (positions, momenta, noise)
    )

    stacked = jnp.concatenate([positions, params[None]], 0)
    next_stacked = lax.ppermute(stacked, "space", one_back)
    next_params = next_stacked[beads]
    spread = 0.5 * TIME_STEP * (total_beads / PC) * contract
    table = np.concatenate([contract @ steps[0, kind] for kind in range(3)] + [spread], axis=1)
    order = steps.reshape(2, 3, holders, beads, holders, beads).transpose(2, 0, 3, 4, 1, 5)
    order = order.reshape(2 * total_beads, 3 * total_beads)
    ordered, table, order = call(
        order_kernel,
        (positions, params, jnp.asarray(table, F32), jnp.asarray(order, F32)),
        0,
        (
            jax.ShapeDtypeStruct((beads, cells, 8, lanes), F32),
            jax.ShapeDtypeStruct(table.shape, F32),
            jax.ShapeDtypeStruct(order.shape, F32),
        ),
        [],
        1 << 22,
    )
    key = octant_key(positions[:, 0], positions[:, 1], positions[:, 2], living[None])
    bounds = jnp.sum(
        (key[:, :, None, :] < jnp.arange(9, dtype=F32)[:, None]).astype(jnp.int32), -1
    )
    force, back = short_forces(
        positions, params, next_stacked[:beads], next_params, ordered, bounds.reshape(-1)
    )
    back = lax.ppermute(back, "space", one_on)

    def flat(value):
        return value.reshape(-1, rows, lanes)

    partial, pieces = call(
        functools.partial(kick_kernel, piece_rows, groups),
        (
            rank_table, table, flat(positions), flat(momenta), flat(noise), flat(force), flat(back),
            params,
        ),
        1,
        (
            jax.ShapeDtypeStruct((PC * groups, rows, lanes), F32),
            jax.ShapeDtypeStruct((holders, 3 * beads * piece_rows, lanes), F32),
        ),
        [
            pltpu.VMEM((3, beads, rows, lanes), F32), pltpu.SMEM(table.shape, F32),
            pltpu.SemaphoreType.DMA,
        ],
        1 << 22,
        (1,),
    )
    arrived = lax.all_to_all(
        partial.reshape(holders, held * rows, lanes), "bead", split_axis=0, concat_axis=0, tiled=True
    )
    contracted = jnp.sum(arrived, 0).reshape(held, 3, cells, lanes)
    contracted, pieces = lax.optimization_barrier((contracted, pieces))
    next_contracted = lax.ppermute(contracted, "space", one_back)
    pieces = lax.all_to_all(pieces, "bead", split_axis=0, concat_axis=0, tiled=True)
    slow, slow_back = pair_forces(
        contracted, params, occupancy, next_contracted, next_params
    )
    slow = slow + lax.ppermute(slow_back, "space", one_on)

    moved = call(
        functools.partial(move_kernel, piece_rows, beads),
        (order, pieces),
        0,
        jax.ShapeDtypeStruct((holders, 2 * beads * piece_rows, lanes), F32),
        [
            pltpu.VMEM((piece_rows, 3 * total_beads, lanes), F32), pltpu.VMEM(order.shape, F32),
            pltpu.SemaphoreType.DMA,
        ],
        1 << 23,
        (0,),
    )
    moved_rows = 2 * beads * piece_rows
    sent = jnp.concatenate(
        [
            moved,
            jnp.broadcast_to(slow.reshape(1, held * rows, lanes), (holders, held * rows, lanes)),
        ],
        1,
    )
    got = lax.all_to_all(sent, "bead", split_axis=0, concat_axis=0, tiled=True)
    result = jax.ShapeDtypeStruct((beads, rows, lanes), F32)
    new_positions, new_momenta = call(
        functools.partial(finish_kernel, piece_rows, groups),
        (
            rank_table, table, got[:, :moved_rows],
            got[:, moved_rows:].reshape(holders * held, rows, lanes), params,
        ),
        1,
        (result, result),
        [
            pltpu.VMEM((beads, rows, lanes), F32), pltpu.SMEM(table.shape, F32),
            pltpu.SemaphoreType.DMA,
        ],
        1 << 20,
        (1,),
    )

    def cells_first(value):
        return value.reshape(beads, 3, cells, lanes).transpose(0, 2, 1, 3)

    return cells_first(new_positions), cells_first(new_momenta)


def solution(mesh):
    placed = (
        P("bead", "space", None, None),
        P("bead", "space", None, None),
        P("bead", "space", None, None),
        P("space", None),
        P("space"),
        P(),
        P(),
        P(),
    )
    return jax.shard_map(
        shards,
        mesh=mesh,
        in_specs=placed,
        out_specs=(P("bead", "space", None, None), P("bead", "space", None, None)),
        check_vma=False,
    )
```

```python
import functools

import jax
import jax.numpy as jnp
import numpy as np
from jax import lax
from jax.experimental import pallas as pl
from jax.experimental.pallas import tpu as pltpu
from jax.sharding import PartitionSpec as P

PC = 8
GY = 4
GZ = 4

TIME_STEP = 0.05
INVERSE_TEMP = 32.0
CENTROID_FRICTION = 1.0
INNER_CUT = 0.5
OUTER_CUT = 1.0
CUBE_ROOT_TWO = 2.0 ** (1.0 / 3.0)
F32 = jnp.float32
BF16 = jnp.bfloat16
SPAN = 32
GROUP = 8
STEPS = ((24, 4), (24, 2), (24, 1), (40, 2), (40, 1), (32, 2), (32, 1))
RUN_ROWS = {1: 24, 2: 40}
SPARE = 40
EARLY_ROWS = 96
VMEM_LIMIT = 48 * 1024 * 1024


def mode_matrix(number):
    rows = np.arange(number, dtype=np.float64)[:, None]
    column = np.arange(number, dtype=np.float64)[None, :]
    phases = 2.0 * np.pi * rows * column / number
    factor = np.sqrt(2.0 / number)
    middle = np.cos(np.pi * rows) / np.sqrt(number)
    matrix = np.where(column < number / 2, factor * np.cos(phases), factor * np.sin(phases))
    matrix = np.where(column == number / 2, middle, matrix)
    return np.where(column == 0, 1.0 / np.sqrt(number), matrix)


def contract_matrix(full_count, reduced):
    selected = np.arange(reduced)
    selected = np.where(selected <= reduced // 2, selected, selected + full_count - reduced)
    chosen = mode_matrix(full_count)[:, selected]
    return np.sqrt(reduced / full_count) * (mode_matrix(reduced) @ chosen.T)


def step_matrices(number):
    index = np.arange(number, dtype=np.float64)
    frequency = 2.0 * (number / INVERSE_TEMP) * np.sin(np.pi * index / number)
    friction = np.where(index == 0, CENTROID_FRICTION, 2.0 * frequency)
    damping = np.exp(-friction * TIME_STEP)
    kicking = np.sqrt((1.0 - damping * damping) / INVERSE_TEMP)
    cosine = np.cos(frequency * TIME_STEP)
    sine = np.sin(frequency * TIME_STEP)
    drift = np.where(index == 0, TIME_STEP, sine / np.where(index == 0, 1.0, frequency))
    modes = mode_matrix(number)

    def over_beads(diagonal):
        return (modes * diagonal[None, :]) @ modes.T

    return np.array(
        [
            [over_beads(cosine), over_beads(drift * damping), over_beads(drift * kicking)],
            [
                over_beads(-frequency * sine),
                over_beads(cosine * damping),
                over_beads(cosine * kicking),
            ],
        ]
    )


def partner_lists(domain_cells):
    lists = []
    for one in range(domain_cells):
        near = []
        for two in range(domain_cells):
            step_y, step_z = two // GZ - one // GZ, two % GZ - one % GZ
            if abs(step_y) <= 1 and abs(step_z) <= 1:
                near.append((two, step_y, step_z))
        later = [entry for entry in near if entry[0] > one]
        lists.append(later + [(two + domain_cells, y, z) for two, y, z in near])
    starts = np.cumsum([0] + [len(entries) for entries in lists]).astype(np.int32)
    return starts, np.array([value for entries in lists for entry in entries for value in entry], np.int32)


def long_weight(h, radius_sq, s2):
    inverse = pl.reciprocal(h, approx=True)
    quotient = (CUBE_ROOT_TWO * s2) * inverse
    twice = quotient * quotient * quotient
    outer = jnp.maximum(1.0 - radius_sq, 0.0)
    inner = jnp.maximum(1.0 - 4.0 * radius_sq, 0.0)
    switch = outer * outer - inner * inner
    slope = outer - 4.0 * inner
    return twice * ((twice - 1.0) * (3.0 * (switch * inverse) + slope) - slope)


def short_weight(h, s2):
    inverse = pl.reciprocal(h, approx=True)
    quotient = s2 * inverse
    sixth = quotient * quotient * quotient
    lifted = jnp.maximum((quotient + inverse) - 2.0 / 3.0, 1.0 / 3.0)
    bracket = (sixth - 0.5) * lifted - 1.0 / 6.0
    return (sixth * bracket) * ((lifted - 1.0 / 3.0) * h)


LONG_FACTOR = 4.0
SHORT_SCALE = 1.0 / INNER_CUT
SHORT_FACTOR = 192.0 / SHORT_SCALE


def atom_rows(block, cell):
    return [block[kind, pl.ds(cell, 1), :] for kind in range(3)]


def columns(block):
    few, lanes = block.shape
    return jnp.concatenate([block, jnp.zeros((8 - few, lanes), F32)], axis=0).T


def spread_rows(position, params, cell, rows_ref, size_ref):
    beads, lanes = position.shape[0], position.shape[-1]
    sizes = columns(jnp.concatenate(atom_rows(params, cell)[:2], axis=0))
    for kind in range(2):
        size_ref[cell, kind] = jnp.broadcast_to(sizes[:, kind : kind + 1], (lanes, lanes))
    for bead in range(beads):
        block = columns(jnp.concatenate(atom_rows(position.at[bead], cell), axis=0))
        for axis in range(3):
            rows_ref[cell, bead, axis] = jnp.broadcast_to(
                block[:, axis : axis + 1], (lanes, lanes)
            )


def meet(cell, first, partners, refs):
    lanes_ref, sizes_ref, rows_ref, size_ref, total_ref, back_ref = refs
    beads, lanes = lanes_ref.shape[0], lanes_ref.shape[-1]
    here = pl.ds(first, SPAN)
    tall = (SPAN // 8, 8, lanes)
    row_half = size_ref[cell, 0, here, :].reshape(tall)
    row_root = size_ref[cell, 1, here, :].reshape(tall)
    known = []
    for partner, _, _ in partners:
        half = row_half + sizes_ref[partner, 0]
        s2 = half * half
        known.append((s2, row_root * sizes_ref[partner, 1]))
    for bead in range(beads):
        rows = [rows_ref[cell, bead, axis, here, :].reshape(tall) for axis in range(3)]
        back = [None, None, None]
        for (partner, step_y, step_z), (s2, depth) in zip(partners, known):
            apart = [
                lanes_ref[bead, partner, 0] - rows[0],
                (lanes_ref[bead, partner, 1] + step_y) - rows[1],
                (lanes_ref[bead, partner, 2] + step_z) - rows[2],
            ]
            radius_sq = apart[0] * apart[0] + apart[1] * apart[1] + apart[2] * apart[2]
            weight = depth * long_weight(radius_sq + s2, radius_sq, s2)
            for axis in range(3):
                push = weight * apart[axis]
                back[axis] = push if back[axis] is None else back[axis] + push
                if total_ref is not None:
                    total_ref[partner, bead, axis] += jnp.sum(push, axis=0)
        for axis in range(3):
            value = back[axis].reshape(SPAN, lanes)
            if total_ref is None:
                back_ref[cell, bead, axis, here, :] = value
            else:
                back_ref[cell, bead, axis, here, :] += value


def repeat_lanes(scale, position, params, next_position, next_params, lanes_ref, sizes_ref):
    beads, _, cells, lanes = position.shape

    def per_cell(cell, carry):
        for layer, place, values in ((0, position, params), (1, next_position, next_params)):
            for kind in range(2):
                row = values[kind, pl.ds(cell, 1), :]
                row = scale * row if kind == 0 else row
                sizes_ref[layer * cells + cell, kind] = jnp.broadcast_to(row, (8, lanes))
            for bead in range(beads):
                for axis in range(3):
                    row = place[bead, axis, pl.ds(cell, 1), :]
                    row = scale * (row + 1.0 if layer == 1 and axis == 0 else row)
                    lanes_ref[bead, layer * cells + cell, axis] = jnp.broadcast_to(row, (8, lanes))
        return carry

    lax.fori_loop(0, cells, per_cell, 0)


def fold_back(back_ref, cell, bead):
    lanes = back_ref.shape[-1]
    column = lax.broadcasted_iota(jnp.int32, (lanes, 8), 1)
    sums = [jnp.sum(back_ref[cell, bead, axis], axis=1, keepdims=True) for axis in range(3)]
    block = jnp.where(
        column == 0, sums[0], jnp.where(column == 1, sums[1], jnp.where(column == 2, sums[2], 0.0))
    )
    return block.T[0:3]


def put_rows(out_ref, bead, cell, block):
    for axis in range(3):
        out_ref[bead, axis, pl.ds(cell, 1), :] = block[axis : axis + 1]


def fold_total(total_ref, cell, bead):
    return jnp.concatenate(
        [jnp.sum(total_ref[cell, bead, axis], axis=0, keepdims=True) for axis in range(3)], axis=0
    )


def pairs_kernel(
    plan, occupied, position, params, next_position, next_params,
    force_ref, other_ref, lanes_ref, sizes_ref, rows_ref, size_ref, total_ref, back_ref,
):
    beads, _, cells, lanes = position.shape
    factor = LONG_FACTOR
    together = max(1, 4 // beads)
    repeat_lanes(1.0, position, params, next_position, next_params, lanes_ref, sizes_ref)
    total_ref[...] = jnp.zeros_like(total_ref)

    refs = (lanes_ref, sizes_ref, rows_ref, size_ref)

    def spread(index, carry):
        for shift in range(together):
            cell = index * together + shift
            spread_rows(position, params, cell, rows_ref, size_ref)
            for first in range(0, lanes, SPAN):
                meet(cell, first, [(cell, 0.0, 0.0)], refs + (None, back_ref))
        return carry

    lax.fori_loop(0, cells // together, spread, 0)

    def entry_of(entry):
        return (
            plan[cells + 1 + 3 * entry],
            plan[cells + 2 + 3 * entry].astype(F32),
            plan[cells + 3 + 3 * entry].astype(F32),
        )

    def per_cell(cell, carry):
        begin, end = plan[cell], plan[cell + 1]
        odd = lax.rem(end - begin, 2)

        most = lanes // SPAN
        needed = lax.div(occupied[cell] + (SPAN - 1), SPAN)
        for parts in (most - 1, most):
            firsts = [part * SPAN for part in range(parts)]

            def all_rows(_, carry, firsts=firsts):
                def single(entry, carry):
                    for first in firsts:
                        meet(cell, first, [entry_of(entry)], refs + (total_ref, back_ref))
                    return carry

                def double(step, carry):
                    entry = begin + odd + 2 * step
                    both = [entry_of(entry), entry_of(entry + 1)]
                    for first in firsts:
                        meet(cell, first, both, refs + (total_ref, back_ref))
                    return carry

                carry = lax.fori_loop(begin, begin + odd, single, carry)
                return lax.fori_loop(0, lax.div(end - begin, 2), double, carry)

            full = (needed == most).astype(jnp.int32)
            lax.fori_loop(0, full if parts == most else 1 - full, all_rows, 0)
        return carry

    lax.fori_loop(0, cells, per_cell, 0)

    def finish(index, carry):
        for shift in range(together):
            cell = index * together + shift
            alive = params[1, pl.ds(cell, 1), :] > 0.0
            for bead in range(beads):
                total = fold_total(total_ref, cell, bead) - fold_back(back_ref, cell, bead)
                put_rows(force_ref, bead, cell, jnp.where(alive, factor * total, 0.0))
                put_rows(other_ref, bead, cell, factor * fold_total(total_ref, cell + cells, bead))
        return carry

    lax.fori_loop(0, cells // together, finish, 0)


def octant_key(x, y, z, alive):
    zed = jnp.where(z >= 0.5, 1.0, 0.0)
    gray = jnp.where(y >= 0.5, 3.0 - zed, zed)
    return jnp.where(alive, jnp.where(x >= 0.5, 7.0 - gray, gray), 8.0)


def reach_lists(domain_cells):
    octants = []
    for bit_x in range(2):
        for bit_y in range(2):
            for bit_z in range(2):
                gray = 3 - bit_z if bit_y else bit_z
                octants.append((7 - gray if bit_x else gray, (bit_x, bit_y, bit_z)))
    classes = [[[] for _ in range(domain_cells)] for _ in STEPS]
    for one in range(domain_cells):
        runs = {}
        for layer in range(2):
            for two in range(domain_cells):
                step = (layer, two // GZ - one // GZ, two % GZ - one % GZ)
                if abs(step[1]) > 1 or abs(step[2]) > 1 or (layer == 0 and two <= one):
                    continue
                keys = [
                    key
                    for key, bits in octants
                    if all(move == 0 or bit == (move > 0) for move, bit in zip(step, bits))
                ]
                entry = (two + layer * domain_cells, step[1], step[2], min(keys), max(keys) + 1)
                runs.setdefault(entry[4] - entry[3], []).append(entry)
        for length, entries in sorted(runs.items()):
            entries.sort(key=lambda entry: entry[3:])
            span = RUN_ROWS.get(length, SPAN)
            for place, (rows, count) in enumerate(STEPS):
                if rows == span:
                    whole = len(entries) // count * count
                    classes[place][one] += entries[:whole]
                    entries = entries[whole:]
    starts, values = [], []
    for lists in classes:
        for entries in lists:
            starts.append(len(values) // 5)
            values += [value for entry in entries for value in entry]
        starts.append(len(values) // 5)
    return np.array(starts, np.int32), np.array(values, np.int32)


def split_three(value):
    high = value.astype(BF16).astype(F32)
    rest = value - high
    middle = rest.astype(BF16).astype(F32)
    return high, middle, rest - middle


def order_kernel(position, params, table, matrix, out_ref, table_out, matrix_out):
    beads, _, cells, lanes = position.shape
    table_out[...] = table[...]
    matrix_out[...] = matrix[...]
    row = lax.broadcasted_iota(jnp.int32, (lanes, lanes), 0)
    column = lax.broadcasted_iota(jnp.int32, (lanes, lanes), 1)
    before = jnp.where(row < column, 1.0, 0.0).astype(BF16)
    counter = jnp.concatenate([before, jnp.ones((lanes, lanes), BF16)], axis=0)
    kind = lax.broadcasted_iota(jnp.int32, (16, lanes), 0).astype(F32)
    place_row = row.astype(F32)
    every = [(shift, bead) for shift in range(GROUP) for bead in range(beads)]

    def per_group(index, carry):
        blocks, sames, marks = [], [], []
        for shift, bead in every:
            cell = index * GROUP + shift
            sizes = atom_rows(params, cell)[:2]
            place = atom_rows(position.at[bead], cell)
            key = octant_key(*place, sizes[1] > 0.0)
            same = jnp.where(key == kind, 1.0, 0.0)
            less = jnp.where(key < kind, 1.0, 0.0)
            scaled = [SHORT_SCALE * value for value in (*place, sizes[0])]
            blocks.append(
                jnp.concatenate([*scaled, sizes[1], jnp.zeros((3, lanes), F32)], axis=0)
            )
            sames.append(same)
            marks.append(jnp.concatenate([same, less], axis=1))
        counts = jnp.dot(
            jnp.concatenate(marks, axis=0).astype(BF16), counter, preferred_element_type=F32
        )
        for place, (shift, bead) in enumerate(every):
            cell = index * GROUP + shift
            rank = jnp.sum(
                sames[place] * counts[16 * place : 16 * place + 16], axis=0, keepdims=True
            )
            chosen = jnp.where(rank == place_row, 1.0, 0.0).astype(BF16)
            moved = lax.dot_general(
                jnp.concatenate(split_three(blocks[place]), axis=0).astype(BF16),
                chosen,
                (((1,), (1,)), ((), ())),
                preferred_element_type=F32,
            )
            out_ref[bead, cell, 0:5, :] = (moved[0:8] + moved[8:16] + moved[16:24])[0:5]
            out_ref[bead, cell, 5:6, :] = rank
            out_ref[bead, cell, 6:8, :] = jnp.zeros((2, lanes), F32)
        return carry

    lax.fori_loop(0, cells // GROUP, per_group, 0)


def meet_runs(span, local, runs, lanes_ref, sizes_ref, rows_ref, total_ref, back_ref):
    beads, lanes = lanes_ref.shape[0], lanes_ref.shape[-1]
    for bead in range(beads):
        for firsts, partner, step_y, step_z in runs:
            here = pl.ds(firsts[bead], span)
            rows = [
                rows_ref[local, bead, kind, here, :].reshape(span // 8, 8, lanes)
                for kind in range(5)
            ]
            half = rows[3] + sizes_ref[partner, 0]
            s2 = half * half
            apart = [
                lanes_ref[bead, partner, 0] - rows[0],
                (lanes_ref[bead, partner, 1] + step_y) - rows[1],
                (lanes_ref[bead, partner, 2] + step_z) - rows[2],
            ]
            radius_sq = apart[0] * apart[0] + apart[1] * apart[1] + apart[2] * apart[2]
            depth = rows[4] * sizes_ref[partner, 1]
            weight = depth * short_weight(radius_sq + s2, s2)
            for axis in range(3):
                push = weight * apart[axis]
                flat_push = push.reshape(span, lanes)
                if total_ref is None:
                    back_ref[local, bead, axis, here, :] = flat_push
                else:
                    back_ref[local, bead, axis, here, :] += flat_push
                    total_ref[partner, bead, axis] += jnp.sum(push, axis=0)


def reach_kernel(
    plan, position, params, next_position, next_params, ordered, force_ref, other_ref, lanes_ref,
    sizes_ref, rows_ref, total_ref, back_ref,
):
    beads, _, cells, lanes = position.shape
    entries_at = len(STEPS) * (cells + 1)
    bounds_at = plan.shape[0] - beads * cells * 9
    factor = SHORT_FACTOR
    repeat_lanes(SHORT_SCALE, position, params, next_position, next_params, lanes_ref, sizes_ref)
    total_ref[...] = jnp.zeros_like(total_ref)
    rows_ref[:, :, :, lanes:, :] = jnp.zeros((GROUP, beads, 5, SPARE, lanes), F32)
    row = lax.broadcasted_iota(jnp.int32, (lanes, lanes), 0).astype(F32)
    slot = lax.broadcasted_iota(jnp.int32, (8, lanes), 1)
    column = lax.broadcasted_iota(jnp.int32, (lanes, 8), 1)
    refs = (lanes_ref, sizes_ref, rows_ref)
    every = [(local, bead) for local in range(GROUP) for bead in range(beads)]

    def per_group(group, carry):
        for local, bead in every:
            block = ordered[bead, group * GROUP + local].T
            for axis in range(5):
                rows_ref[local, bead, axis, 0:lanes, :] = jnp.broadcast_to(
                    block[:, axis : axis + 1], (lanes, lanes)
                )
            if bead == beads - 1:
                for first in range(0, EARLY_ROWS, SPAN):
                    run = ([first] * beads, group * GROUP + local, 0.0, 0.0)
                    meet_runs(SPAN, local, [run], *refs, None, back_ref)

        def per_cell(local, carry):
            cell = group * GROUP + local

            def bound(bead, octant):
                return plan[bounds_at + (bead * cells + cell) * 9 + octant]

            def itself(index, carry):
                first = pl.multiple_of(index * SPAN, SPAN)
                run = ([first] * beads, cell, 0.0, 0.0)
                meet_runs(SPAN, local, [run], *refs, None, back_ref)
                return carry

            lax.fori_loop(
                EARLY_ROWS // SPAN, lax.div(bound(0, 8) + (SPAN - 1), SPAN), itself, 0
            )

            for place, (span, count) in enumerate(STEPS):
                begin = plan[place * (cells + 1) + cell]
                end = plan[place * (cells + 1) + cell + 1]

                def per_step(step, carry, span=span, count=count, begin=begin):
                    runs, longest = [], 0
                    for shift in range(count):
                        at = entries_at + 5 * (begin + step * count + shift)
                        begins = [
                            lax.bitwise_and(bound(bead, plan[at + 3]), -8) for bead in range(beads)
                        ]
                        for bead in range(beads):
                            longest = jnp.maximum(longest, bound(bead, plan[at + 4]) - begins[bead])
                        runs.append(
                            (
                                begins, plan[at], SHORT_SCALE * plan[at + 1].astype(F32),
                                SHORT_SCALE * plan[at + 2].astype(F32),
                            )
                        )

                    def per_span(index, carry):
                        moved = [
                            (
                                [
                                    pl.multiple_of(jnp.minimum(first + index * span, lanes), 8)
                                    for first in begins
                                ],
                                *rest,
                            )
                            for begins, *rest in runs
                        ]
                        meet_runs(span, local, moved, *refs, total_ref, back_ref)
                        return carry

                    return lax.fori_loop(0, lax.div(longest + (span - 1), span), per_span, carry)

                lax.fori_loop(0, lax.div(end - begin, count), per_step, 0)
            return carry

        lax.fori_loop(0, GROUP, per_cell, 0)

        for local, bead in every:
            cell = group * GROUP + local
            alive = plan[bounds_at + cell * 9 + 8]
            sums = [
                jnp.sum(back_ref[local, bead, axis, 0:lanes, :], axis=1, keepdims=True)
                for axis in range(3)
            ]
            block = jnp.where(
                column == 0,
                sums[0],
                jnp.where(column == 1, sums[1], jnp.where(column == 2, sums[2], 0.0)),
            ).T
            block = jnp.where(slot < alive, block, 0.0)
            chosen = jnp.where(ordered[bead, cell, 5:6, :] == row, 1.0, 0.0).astype(BF16)
            moved = lax.dot_general(
                jnp.concatenate(split_three(block), axis=0).astype(BF16),
                chosen,
                (((1,), (0,)), ((), ())),
                preferred_element_type=F32,
            )
            put_rows(force_ref, bead, cell, (moved[0:8] + moved[8:16] + moved[16:24])[0:3])
        return carry

    lax.fori_loop(0, cells // GROUP, per_group, 0)

    def finish(index, carry):
        for shift, bead in every:
            cell = index * GROUP + shift
            held = jnp.concatenate(atom_rows(force_ref.at[bead], cell), axis=0)
            put_rows(force_ref, bead, cell, factor * (fold_total(total_ref, cell, bead) - held))
            put_rows(other_ref, bead, cell, factor * fold_total(total_ref, cell + cells, bead))
        return carry

    lax.fori_loop(0, cells // GROUP, finish, 0)


def short_forces(position, params, next_position, next_params, ordered, bounds):
    beads, _, cells, lanes = position.shape
    starts, entries = reach_lists(cells)
    plan = jnp.concatenate([jnp.asarray(starts), jnp.asarray(entries), bounds])
    forces = jax.ShapeDtypeStruct((beads, 3, cells, lanes), F32)
    return call(
        reach_kernel,
        (plan, position, params, next_position, next_params, ordered),
        1,
        (forces, forces),
        [
            pltpu.VMEM((beads, 2 * cells, 3, 8, lanes), F32),
            pltpu.VMEM((2 * cells, 2, 8, lanes), F32),
            pltpu.VMEM((GROUP, beads, 5, lanes + SPARE, lanes), F32),
            pltpu.VMEM((2 * cells, beads, 3, 8, lanes), F32),
            pltpu.VMEM((GROUP, beads, 3, lanes + SPARE, lanes), F32),
        ],
        PAIR_FLOPS * beads * 70,
    )


def call(kernel, inputs, smem, outputs, scratch, flops, fetched=()):
    def space(place):
        if place in fetched:
            return pltpu.HBM
        return pltpu.SMEM if place < smem else pltpu.VMEM

    return pl.pallas_call(
        kernel,
        out_shape=outputs,
        in_specs=[pl.BlockSpec(memory_space=space(place)) for place in range(len(inputs))],
        scratch_shapes=scratch,
        compiler_params=pltpu.CompilerParams(vmem_limit_bytes=VMEM_LIMIT),
        cost_estimate=pl.CostEstimate(flops=flops, bytes_accessed=1 << 18, transcendentals=0),
    )(*inputs)


PAIR_FLOPS = 40 * 128 * 128


def pair_forces(position, params, occupied, next_position, next_params):
    beads, _, cells, lanes = position.shape
    starts, entries = partner_lists(cells)
    forces = jax.ShapeDtypeStruct((beads, 3, cells, lanes), F32)
    return call(
        pairs_kernel,
        (
            jnp.asarray(np.concatenate([starts, entries])), occupied, position, params,
            next_position, next_params,
        ),
        2,
        (forces, forces),
        [
            pltpu.VMEM((beads, 2 * cells, 3, 8, lanes), F32),
            pltpu.VMEM((2 * cells, 2, 8, lanes), F32),
            pltpu.VMEM((cells, beads, 3, lanes, lanes), F32),
            pltpu.VMEM((cells, 2, lanes, lanes), F32),
            pltpu.VMEM((2 * cells, beads, 3, 8, lanes), F32),
            pltpu.VMEM((cells, beads, 3, lanes, lanes), F32),
        ],
        PAIR_FLOPS * beads * (len(entries) // 3 + cells),
    )


def kick_kernel(
    piece_rows, groups, rank, table_hbm, position, momenta, noise, force, back, params, partial_ref,
    piece_ref, flat_ref, table, done,
):
    fetch = pltpu.make_async_copy(table_hbm, table, done)
    fetch.start()
    beads, rows, _ = position.shape
    holders = piece_ref.shape[0]
    reduced = table.shape[0]
    first = rank[0] * beads
    if holders * piece_rows > rows:
        piece_ref[...] = jnp.zeros_like(piece_ref)
    mass = params[2]
    per_root = lax.rsqrt(mass)
    per_root = per_root * (1.5 - 0.5 * mass * per_root * per_root)
    per_mass = jnp.concatenate([1.0 / mass] * 3, axis=0)
    per_root = jnp.concatenate([per_root] * 3, axis=0)
    for bead in range(beads):
        kicked = momenta[bead] + 0.5 * TIME_STEP * (force[bead] + back[bead])
        flat_ref[0, bead] = position[bead]
        flat_ref[1, bead] = kicked * per_mass
        flat_ref[2, bead] = noise[bead] * per_root
    for kind in range(3):
        for bead in range(beads):
            base = (kind * beads + bead) * piece_rows
            for owner in range(holders):
                start = owner * piece_rows
                count = min(piece_rows, rows - start)
                if count > 0:
                    piece_ref[owner, base : base + count, :] = flat_ref[
                        kind, bead, start : start + count, :
                    ]
    fetch.wait()
    for group in range(reduced):
        total = None
        for kind in range(3):
            for bead in range(beads):
                term = table[group, kind * holders * beads + first + bead] * flat_ref[kind, bead]
                total = term if total is None else total + term
        for copy in range(groups):
            partial_ref[group * groups + copy] = total


def move_kernel(piece_rows, beads, matrix_hbm, arrived, out_ref, gathered, matrix, done):
    fetch = pltpu.make_async_copy(matrix_hbm, matrix, done)
    fetch.start()
    holders = arrived.shape[0]
    taken = 3 * beads
    given = 2 * beads
    for row in range(piece_rows):
        for holder in range(holders):
            gathered[row, holder * taken : (holder + 1) * taken, :] = arrived[
                holder, pl.ds(row, taken, stride=piece_rows), :
            ]
    fetch.wait()
    for row in range(piece_rows):
        moved = lax.dot_general(
            matrix[...],
            gathered[row],
            (((1,), (0,)), ((), ())),
            precision=lax.Precision.HIGHEST,
            preferred_element_type=F32,
        )
        for holder in range(holders):
            out_ref[holder, row * given : (row + 1) * given, :] = moved[
                holder * given : (holder + 1) * given
            ]


def finish_kernel(
    piece_rows, groups, rank, table_hbm, moved, slow, params, position_ref, momentum_ref,
    velocity_ref, table, done,
):
    fetch = pltpu.make_async_copy(table_hbm, table, done)
    fetch.start()
    beads, rows, _ = position_ref.shape
    holders = moved.shape[0]
    given = 2 * beads
    reduced = table.shape[0]
    first = 3 * holders * beads + rank[0] * beads
    mass = jnp.concatenate([params[2]] * 3, axis=0)
    for bead in range(beads):
        for owner in range(holders):
            start = owner * piece_rows
            count = min(piece_rows, rows - start)
            if count > 0:
                position_ref[bead, start : start + count, :] = moved[
                    owner, pl.ds(bead, count, stride=given), :
                ]
                velocity_ref[bead, start : start + count, :] = moved[
                    owner, pl.ds(beads + bead, count, stride=given), :
                ]
    fetch.wait()
    for bead in range(beads):
        total = mass * velocity_ref[bead]
        for group in range(reduced):
            total = total + table[group, first + bead] * slow[group * groups]
        momentum_ref[bead] = total


def shards(positions, momenta, noise, atom_types, occupancy, type_sigma, type_eps, type_mass):
    beads, cells, _, lanes = positions.shape
    holders = lax.axis_size("bead")
    domains = lax.axis_size("space")
    rank = lax.axis_index("bead")
    total_beads = beads * holders
    rows = 3 * cells
    piece_rows = -(-rows // holders)
    held = max(1, PC // holders)
    groups = max(1, holders // PC)
    contract = contract_matrix(total_beads, PC)
    steps = step_matrices(total_beads)
    rank_table = rank.astype(jnp.int32).reshape(1)
    one_back = [((i + 1) % domains, i) for i in range(domains)]
    one_on = [(i, (i + 1) % domains) for i in range(domains)]

    codes = jnp.arange(type_sigma.shape[0])
    onehot = atom_types[..., None] == codes
    living = jnp.arange(lanes)[None, :] < occupancy[:, None]
    half_sigma = 0.5 * jnp.sum(jnp.where(onehot, type_sigma, 0.0), -1)
    root_eps = jnp.sqrt(jnp.sum(jnp.where(onehot, type_eps, 0.0), -1))
    mass = jnp.sum(jnp.where(onehot, type_mass, 0.0), -1)
    params = jnp.stack([half_sigma, jnp.where(living, root_eps, 0.0), mass], 0)
    positions, momenta, noise = (
        value.transpose(0, 2, 1, 3) for value in (positions, momenta, noise)
    )

    stacked = jnp.concatenate([positions, params[None]], 0)
    next_stacked = lax.ppermute(stacked, "space", one_back)
    next_params = next_stacked[beads]
    spread = 0.5 * TIME_STEP * (total_beads / PC) * contract
    table = np.concatenate([contract @ steps[0, kind] for kind in range(3)] + [spread], axis=1)
    order = steps.reshape(2, 3, holders, beads, holders, beads).transpose(2, 0, 3, 4, 1, 5)
    order = order.reshape(2 * total_beads, 3 * total_beads)
    ordered, table, order = call(
        order_kernel,
        (positions, params, jnp.asarray(table, F32), jnp.asarray(order, F32)),
        0,
        (
            jax.ShapeDtypeStruct((beads, cells, 8, lanes), F32),
            jax.ShapeDtypeStruct(table.shape, F32),
            jax.ShapeDtypeStruct(order.shape, F32),
        ),
        [],
        1 << 22,
    )
    key = octant_key(positions[:, 0], positions[:, 1], positions[:, 2], living[None])
    bounds = jnp.sum(
        (key[:, :, None, :] < jnp.arange(9, dtype=F32)[:, None]).astype(jnp.int32), -1
    )
    force, back = short_forces(
        positions, params, next_stacked[:beads], next_params, ordered, bounds.reshape(-1)
    )
    back = lax.ppermute(back, "space", one_on)

    def flat(value):
        return value.reshape(-1, rows, lanes)

    partial, pieces = call(
        functools.partial(kick_kernel, piece_rows, groups),
        (
            rank_table, table, flat(positions), flat(momenta), flat(noise), flat(force), flat(back),
            params,
        ),
        1,
        (
            jax.ShapeDtypeStruct((PC * groups, rows, lanes), F32),
            jax.ShapeDtypeStruct((holders, 3 * beads * piece_rows, lanes), F32),
        ),
        [
            pltpu.VMEM((3, beads, rows, lanes), F32), pltpu.SMEM(table.shape, F32),
            pltpu.SemaphoreType.DMA,
        ],
        1 << 22,
        (1,),
    )
    arrived = lax.all_to_all(
        partial.reshape(holders, held * rows, lanes), "bead", split_axis=0, concat_axis=0, tiled=True
    )
    contracted = jnp.sum(arrived, 0).reshape(held, 3, cells, lanes)
    contracted, pieces = lax.optimization_barrier((contracted, pieces))
    next_contracted = lax.ppermute(contracted, "space", one_back)
    pieces = lax.all_to_all(pieces, "bead", split_axis=0, concat_axis=0, tiled=True)
    slow, slow_back = pair_forces(
        contracted, params, occupancy, next_contracted, next_params
    )
    slow = slow + lax.ppermute(slow_back, "space", one_on)

    moved = call(
        functools.partial(move_kernel, piece_rows, beads),
        (order, pieces),
        0,
        jax.ShapeDtypeStruct((holders, 2 * beads * piece_rows, lanes), F32),
        [
            pltpu.VMEM((piece_rows, 3 * total_beads, lanes), F32), pltpu.VMEM(order.shape, F32),
            pltpu.SemaphoreType.DMA,
        ],
        1 << 23,
        (0,),
    )
    moved_rows = 2 * beads * piece_rows
    sent = jnp.concatenate(
        [
            moved,
            jnp.broadcast_to(slow.reshape(1, held * rows, lanes), (holders, held * rows, lanes)),
        ],
        1,
    )
    got = lax.all_to_all(sent, "bead", split_axis=0, concat_axis=0, tiled=True)
    result = jax.ShapeDtypeStruct((beads, rows, lanes), F32)
    new_positions, new_momenta = call(
        functools.partial(finish_kernel, piece_rows, groups),
        (
            rank_table, table, got[:, :moved_rows],
            got[:, moved_rows:].reshape(holders * held, rows, lanes), params,
        ),
        1,
        (result, result),
        [
            pltpu.VMEM((beads, rows, lanes), F32), pltpu.SMEM(table.shape, F32),
            pltpu.SemaphoreType.DMA,
        ],
        1 << 20,
        (1,),
    )

    def cells_first(value):
        return value.reshape(beads, 3, cells, lanes).transpose(0, 2, 1, 3)

    return cells_first(new_positions), cells_first(new_momenta)


def solution(mesh):
    placed = (
        P("bead", "space", None, None),
        P("bead", "space", None, None),
        P("bead", "space", None, None),
        P("space", None),
        P("space"),
        P(),
        P(),
        P(),
    )
    return jax.shard_map(
        shards,
        mesh=mesh,
        in_specs=placed,
        out_specs=(P("bead", "space", None, None), P("bead", "space", None, None)),
        check_vma=False,
    )
```
